32 devices in a mesh: lat: 4 (over z), lon: 8 (over y, x, core).
Axes of the slice: x: 2, y: 2, z: 4, core: 2. Of those that a mesh axis runs over, the one named last changes fastest.
Arguments:
- ensemble: float32 [128, 1024, 128], P('lat', 'lon'), may hold values from -6 to 6
- observed: float32 [2, 4, 8, 8], P(None, 'lat', 'lon'), may hold values from -8 to 8
- precision: float32 [2, 4, 8, 8], P(None, 'lat', 'lon'), may hold values from 0.05 to 0.5
- interp_weight: float32 [2, 4, 8, 4, 8], P(None, 'lat', 'lon'), may hold values from 0.1 to 1
- stencil: int32 [2, 4, 8, 4, 8], P(None, 'lat', 'lon'), may hold values from 0 to 4419, as said below
- owned: int32 [2, 4, 8, 8], P(None, 'lat', 'lon'), may hold values from 0 to 1, as said below
- pattern: int32 [2, 4, 8, 5, 8], P(None, 'lat', 'lon'), may hold values 0 or 1
Outputs:
- analysis: float32 [128, 1024, 128], P('lat', 'lon')
The draws below stay inside these ranges and needn't reach their ends.
Inputs may be any that keep to these rules, and one draw needn't show every extreme that they name: `stencil`: each index names one of the four corners of a 2 x 2 square of cells of the rim-extended tile, in the order (0,0), (0,1), (1,0), (1,1). In each batch and tile the owned slots come first and there is at least one; some tile owns all 8 slots in every batch.
All inputs are finite; a program needn't handle non-finite values. No bound on the sum of `pattern` on one device may be relied on, other than what follows from the above.
Results may differ from the reference program's by a relative error of at most 0.0026.
Values may be sent and summed in bfloat16 or wider, within the bound.
No kernel may reach another device: no remote copies, remote signals or barrier semaphores. Data moves between devices by JAX's collectives and lax.ppermute only.
A program may use at most 64 MiB of HBM per device.

```python
import math
import jax
import jax.numpy as jnp
from jax import lax

MEMBERS = 128
CELLS_LAT = 32
CELLS_LON = 128
OBS_DEV = 8
BATCHES = 2
REACH = 2
WIN = 5
TILES_LAT = 4
TILES_LON = 8
GRID_LAT = 128
GRID_LON = 1024


def draw_stencil(key, part):
    first_key, second_key = jax.random.split(jax.random.fold_in(key, 11))
    base_row = jax.random.randint(first_key, (BATCHES, TILES_LAT, TILES_LON, 1, OBS_DEV), 0, CELLS_LAT + 1)
    base_col = jax.random.randint(second_key, (BATCHES, TILES_LAT, TILES_LON, 1, OBS_DEV), 0, CELLS_LON + 1)
    corner = jnp.array([0, 1, CELLS_LON + 2, CELLS_LON + 3], jnp.int32).reshape(1, 1, 1, 4, 1)
    return (base_row * (CELLS_LON + 2) + base_col + corner).astype(jnp.int32)


def draw_owned(key, part):
    counts = jax.random.randint(jax.random.fold_in(key, 23), (BATCHES, TILES_LAT, TILES_LON, 1), 1, OBS_DEV + 1)
    counts = counts.at[:, 0, 0, :].set(OBS_DEV)
    slots = jnp.arange(OBS_DEV, dtype=jnp.int32).reshape(1, 1, 1, -1)
    return (slots < counts).astype(jnp.int32)


def with_ends(values, own_key, smallest, largest):
    extent = values.shape
    place = [jax.random.randint(jax.random.fold_in(own_key, axis), (), 0, extent[axis]) for axis in range(len(extent))]
    values = values.at[tuple(place)].set(smallest)
    longest = extent.index(max(extent))
    place[longest] = (place[longest] + 1) % extent[longest]
    return values.at[tuple(place)].set(largest)


def levels(own_key, dims, pieces, least, top_value):
    level = 1.0
    for position, parts in pieces:
        steps = jax.random.uniform(jax.random.fold_in(jax.random.fold_in(own_key, 6), position), (parts,), jnp.float32, least / len(pieces), top_value / len(pieces))
        level = level * jnp.repeat(jnp.exp(steps), dims[position] // parts).reshape((-1,) + (1,) * (len(dims) - 1 - position))
    return level


def gaussian(rng, shape, deviation, reach, shards=(), held_as=jnp.bfloat16):
    loudness = levels(rng, shape, shards, -0.22, 0.18) if shards else 1.0
    values = jax.random.normal(rng, shape, jnp.float32) * deviation * loudness
    return jnp.minimum(jnp.maximum(values, -reach), reach).astype(held_as)


def setup_inputs(seed: int = 0) -> dict:
    key_list = jax.random.split(jax.random.key(seed), 8)
    return {
        "ensemble": gaussian(key_list[0], (GRID_LAT, GRID_LON, MEMBERS), 1.0, 6.0, ((0, 4), (1, 8)), jnp.float32),
        "observed": gaussian(key_list[1], (BATCHES, TILES_LAT, TILES_LON, OBS_DEV), 1.5, 8.0, ((1, 4), (2, 8)), jnp.float32),
        "precision": jnp.clip(jnp.exp(math.log(0.5) - 2.3025851 * jax.random.uniform(key_list[2], (BATCHES, TILES_LAT, TILES_LON, OBS_DEV), jnp.float32) ** levels(key_list[2], (BATCHES, TILES_LAT, TILES_LON, OBS_DEV), ((1, 4), (2, 8)), -0.2, 0.2)), 0.05, 0.5),
        "interp_weight": jnp.clip(0.1 + 0.9 * jax.random.uniform(key_list[3], (BATCHES, TILES_LAT, TILES_LON, 4, OBS_DEV), jnp.float32) ** levels(key_list[3], (BATCHES, TILES_LAT, TILES_LON, 4, OBS_DEV), ((1, 4), (2, 8)), -0.2, 0.2), 0.1, 1.0),
        "stencil": draw_stencil(jax.random.fold_in(key_list[7], 71), 0),
        "owned": draw_owned(jax.random.fold_in(key_list[7], 71), 0),
        "pattern": with_ends((jax.random.randint(key_list[6], (BATCHES, TILES_LAT, TILES_LON, WIN, TILES_LON), 0, 2) < 1).astype(jnp.int32), jax.random.fold_in(key_list[6], 1), 0, 1),
    }


def square_root(gram, proj):
    members = gram.shape[-1]
    eye = jnp.eye(members, dtype=jnp.float32)
    system = gram + (members - 1.0) * eye
    factor = jnp.linalg.cholesky(system)
    lower_sol = jax.scipy.linalg.solve_triangular(factor, proj[..., None], lower=True)
    weights = jax.scipy.linalg.solve_triangular(factor, lower_sol, lower=True, trans=1)
    inverse = jax.scipy.linalg.solve_triangular(factor, jnp.broadcast_to(eye, system.shape), lower=True)
    return jnp.sqrt(members - 1.0) * jnp.swapaxes(inverse, -1, -2) + weights

def reference(ensemble, observed, precision, interp_weight, stencil, owned, pattern):
    analysis = ensemble
    tile_row = (jnp.arange(TILES_LAT, dtype=jnp.int32) * CELLS_LAT).reshape(-1, 1, 1, 1)
    tile_col = (jnp.arange(TILES_LON, dtype=jnp.int32) * CELLS_LON).reshape(1, -1, 1, 1)
    for batch_no in range(BATCHES):
        wrapped = jnp.concatenate([analysis[:, -1:], analysis, analysis[:, :1]], axis=1)
        padded = jnp.pad(wrapped, ((1, 1), (0, 0), (0, 0)))
        cells = stencil[batch_no]
        in_row = cells // (CELLS_LON + 2)
        in_col = cells % (CELLS_LON + 2)
        values = padded[tile_row + in_row, tile_col + in_col]
        prior = lax.optimization_barrier(jnp.sum(interp_weight[batch_no][..., None] * values, axis=2))
        mean_prior = lax.optimization_barrier(jnp.mean(prior, axis=-1))
        root = jnp.sqrt(precision[batch_no]) * owned[batch_no].astype(jnp.float32)
        scaled = (root[..., None] * (prior - mean_prior[..., None])).astype(jnp.bfloat16)
        innov = (root * (observed[batch_no] - mean_prior)).astype(jnp.bfloat16)
        scaled_f = scaled.astype(jnp.float32)
        innov_f = innov.astype(jnp.float32)
        blocks = jnp.einsum('acom,acon->acmn', scaled_f, scaled_f, precision=lax.Precision.HIGHEST)
        vectors = jnp.einsum('acom,aco->acm', scaled_f, innov_f, precision=lax.Precision.HIGHEST)
        pad_blocks = jnp.pad(blocks, ((REACH, REACH), (0, 0), (0, 0), (0, 0)))
        pad_vectors = jnp.pad(vectors, ((REACH, REACH), (0, 0), (0, 0)))
        marks = pattern[batch_no].astype(jnp.float32)
        gram = jnp.zeros((TILES_LAT, TILES_LON, MEMBERS, MEMBERS), jnp.float32)
        proj = jnp.zeros((TILES_LAT, TILES_LON, MEMBERS), jnp.float32)
        for offset in range(WIN):
            gram = gram + jnp.einsum('ace,aemn->acmn', marks[:, :, offset], pad_blocks[offset:offset + TILES_LAT], precision=lax.Precision.HIGHEST)
            proj = proj + jnp.einsum('ace,aem->acm', marks[:, :, offset], pad_vectors[offset:offset + TILES_LAT], precision=lax.Precision.HIGHEST)
        transform = square_root(gram, proj)
        tiles = analysis.reshape(TILES_LAT, CELLS_LAT, TILES_LON, CELLS_LON, MEMBERS)
        center = lax.optimization_barrier(jnp.mean(tiles, axis=-1, keepdims=True))
        moved = jnp.einsum('axcym,acmn->axcyn', tiles - center, transform, precision=lax.Precision.HIGHEST)
        analysis = (center + moved).reshape(GRID_LAT, GRID_LON, MEMBERS)
    return analysis
```

```python
import functools
import jax
import jax.numpy as jnp
from jax import lax
from jax.experimental import pallas as pl
from jax.experimental.pallas import tpu as pltpu
from jax.sharding import PartitionSpec as P

REACH = 2
WIN = 2 * REACH + 1
SUB = 8
LANES = 128
NEAR = tuple((da, dc) for da in (-1, 0, 1) for dc in (-1, 0, 1))
OWN = NEAR.index((0, 0))
SPAN = 64
AT_ROW, AT_COL, AT_WEIGHT, AT_OBS = (0, 8, 16, 48)
F32 = jnp.float32
BF16 = jnp.bfloat16


def packed_params(observed, precision, interp_weight, stencil, owned, width):
    batches = observed.shape[0]
    root = jnp.sqrt(precision[:, 0, 0]) * owned[:, 0, 0].astype(F32)
    corner = stencil[:, 0, 0, 0]
    weight = (interp_weight[:, 0, 0] * root[:, None, :]).reshape(batches, -1)
    pieces = [
        (corner // width).astype(F32),
        (corner % width).astype(F32),
        weight,
        root * observed[:, 0, 0],
    ]
    row = jnp.concatenate(pieces, axis=1)
    row = jnp.pad(row, ((0, 0), (0, SPAN - row.shape[1])))
    return row.reshape(1, 1, batches * SPAN)


def place_shares(out_ref, shares, lat_count, lon_count):
    my_lat, my_lon = (lax.axis_index("lat"), lax.axis_index("lon"))
    out_ref[...] = jnp.zeros_like(out_ref)
    for t, (da, dc) in enumerate(NEAR):
        lat = my_lat + da
        lon = lax.rem(my_lon + dc + lon_count, lon_count)

        @pl.when((lat >= 0) & (lat < lat_count))
        def _():
            out_ref[lat * lon_count + lon] = shares(t)


def shares_kernel(
    lat_count, lon_count, params_ref, cells_ref, first_ref, later_ref, pad, near, params, cell_sem, param_sem
):
    rows, cols = (cells_ref.shape[0], cells_ref.shape[1])
    my_lat, my_lon = (lax.axis_index("lat"), lax.axis_index("lon"))
    cell_copy = pltpu.make_async_copy(cells_ref, pad.at[pl.ds(2, rows), pl.ds(SUB, cols)], cell_sem)
    cell_copy.start()
    param_copies = []
    for t, (da, dc) in enumerate(NEAR):
        lat = jnp.clip(my_lat + da, 0, lat_count - 1)
        lon = lax.rem(my_lon + dc + lon_count, lon_count)
        copy = pltpu.make_async_copy(params_ref.at[lat * lon_count + lon], params.at[t], param_sem.at[t])
        copy.start()
        param_copies.append(copy)
    edge = jnp.zeros((2, cols + 2 * SUB, LANES), F32)
    pad[pl.ds(0, 2)] = edge
    pad[pl.ds(rows + 2, 2)] = edge
    side = jnp.zeros((rows, SUB, LANES), F32)
    pad[pl.ds(2, rows), pl.ds(0, SUB)] = side
    pad[pl.ds(2, rows), pl.ds(SUB + cols, SUB)] = side
    for copy in param_copies:
        copy.wait()
    cell_copy.wait()

    def share(batch, t, o):
        da, dc = NEAR[t]
        at = batch * SPAN + o
        row = params[t, 0, at + AT_ROW].astype(jnp.int32) - 1 + da * rows
        col = params[t, 0, at + AT_COL].astype(jnp.int32) - 1 + dc * cols
        row = jnp.clip(row, -2, rows) + 2
        col = jnp.clip(col, -2, cols) + SUB
        total = None
        for k in range(4):
            cell = pad[row + k // 2, pl.ds(col + k % 2, 1), :]
            term = params[t, 0, at + AT_WEIGHT + k * SUB] * cell
            total = term if total is None else total + term
        return total

    sub = lax.broadcasted_iota(jnp.int32, (SUB, LANES), 0)
    for batch, ref in enumerate((near, later_ref)):
        for t in range(len(NEAR)):
            for o in range(SUB):
                ref[t, pl.ds(o, 1), :] = share(batch, t, o)
        shift = jnp.zeros((SUB, LANES), F32)
        for o in range(SUB):
            shift = jnp.where(sub == o, params[OWN, 0, batch * SPAN + AT_OBS + o], shift)
        if batch == 0:
            near[OWN] = near[OWN] - shift
        else:
            later_ref[len(NEAR)] = shift
    place_shares(first_ref, lambda t: near[t], lat_count, lon_count)


def row_of(block, j):
    return jnp.broadcast_to(block[j:j + 1, :], (SUB, LANES))


def reciprocal(value):
    guess = pl.reciprocal(value, approx=True)
    return guess * (2.0 - value * guess)


def eliminate(blocks):
    count = len(blocks) - 1
    blocks = list(blocks)
    sub = lax.broadcasted_iota(jnp.int32, (SUB, LANES), 0)
    lane = lax.broadcasted_iota(jnp.int32, (SUB, LANES), 1)
    inverse = []
    for k in range(count):
        here = (lane >= k * SUB) & (lane < (k + 1) * SUB)
        column = [
            [jnp.broadcast_to(blocks[i][:, k * SUB + j:k * SUB + j + 1], (SUB, LANES)) for j in range(SUB)]
            for i in range(k, count + 1)
        ]
        diag = column[0]
        full = jnp.where(here, jnp.where(lane - k * SUB == sub, 1.0, 0.0), blocks[k])
        lower = full
        scale = jnp.zeros((SUB, LANES), F32)
        for j in range(0, SUB, 2):
            a, b, c = (row_of(diag[j], j), row_of(diag[j + 1], j), row_of(diag[j + 1], j + 1))
            det = a * c - b * b
            over_det = reciprocal(det)
            first = jnp.where(sub == j, -c, jnp.where(sub == j + 1, b, diag[j] * c - diag[j + 1] * b))
            second = jnp.where(sub == j, b, jnp.where(sub == j + 1, -a, diag[j + 1] * a - diag[j] * b))
            first, second = (first * over_det, second * over_det)
            other = (sub != j) & (sub != j + 1)
            for n in range(j + 2, SUB):
                diag[n] = jnp.where(other, diag[n], 0.0) - first * row_of(diag[n], j) - second * row_of(diag[n], j + 1)
            full = jnp.where(other, full, 0.0) - first * row_of(full, j) - second * row_of(full, j + 1)
            over_a = reciprocal(a)
            top, bottom = (row_of(lower, j), row_of(lower, j + 1))
            below = sub > j + 1
            lower = lower - jnp.where(sub == j + 1, b * over_a, jnp.where(below, first, 0.0)) * top
            lower = lower - jnp.where(below, second, 0.0) * bottom
            scale = jnp.where(sub == j, lax.rsqrt(a), jnp.where(sub == j + 1, lax.rsqrt(det * over_a), scale))
        inverse.append(jnp.where(lane < (k + 1) * SUB, lower * scale, 0.0))
        pivot = [row_of(full, j) for j in range(SUB)]
        for i in range(k + 1, count + 1):
            terms = [column[i - k][j] * pivot[j] for j in range(SUB)]
            while len(terms) > 1:
                terms = [terms[n] + terms[n + 1] for n in range(0, len(terms), 2)]
            blocks[i] = jnp.where(here, 0.0, blocks[i]) - terms[0]
    return inverse, blocks[count][:1]


def batch_map(batch, lat_count, near_ref, pattern_ref):
    lon_count = pattern_ref.shape[-1]
    held = min(WIN, lat_count)
    my_lat = lax.axis_index("lat")
    start = jnp.clip(my_lat - REACH, 0, lat_count - held)
    marks = []
    for j in range(held):
        offset = start + j - my_lat + REACH
        inside = (offset >= 0) & (offset < WIN)
        offset = jnp.clip(offset, 0, WIN - 1)
        for e in range(lon_count):
            mark = jnp.where(inside, pattern_ref[batch, 0, 0, offset, e], 0).astype(F32)
            marks.append(jnp.full((SUB, LANES), mark))
    marks = jnp.concatenate(marks, axis=0)
    value = near_ref[...].reshape(-1, LANES)
    mean = jnp.mean(value, axis=-1, keepdims=True)
    scaled = (value - mean).astype(BF16)
    innov = (-mean).astype(BF16).astype(F32)
    weighted = scaled.astype(F32) * marks
    proj = jnp.sum((weighted * innov).reshape(-1, SUB, LANES), axis=0)
    proj = jnp.sum(proj, axis=0, keepdims=True)
    gram = lax.dot_general(
        weighted.astype(BF16), scaled, (((0,), (0,)), ((), ())), preferred_element_type=F32
    )
    sub = lax.broadcasted_iota(jnp.int32, (SUB, LANES), 0)
    lane = lax.broadcasted_iota(jnp.int32, (SUB, LANES), 1)
    members = LANES
    blocks = []
    for k in range(members // SUB):
        block = gram[k * SUB:(k + 1) * SUB, :]
        blocks.append(block + jnp.where(lane - k * SUB == sub, members - 1.0, 0.0))
    blocks.append(jnp.broadcast_to(proj, (SUB, LANES)))
    inverse, weights = eliminate(blocks)
    flipped = jnp.concatenate(inverse, axis=0) * (members - 1.0) ** 0.5 - weights
    return flipped - jnp.mean(flipped, axis=-1, keepdims=True) + 1.0 / members


def exact_dot(a, b, contract_b):
    return lax.dot_general(
        a, b, (((1,), (contract_b,)), ((), ())), precision=lax.Precision.HIGHEST, preferred_element_type=F32
    )


def first_kernel(batch, lat_count, lon_count, near_ref, pattern_ref, later_ref, out_ref, map_ref, moved):
    flipped = batch_map(batch, lat_count, near_ref, pattern_ref)
    map_ref[...] = flipped
    later = later_ref[pl.ds(0, len(NEAR))].reshape(-1, LANES)
    moved[...] = exact_dot(later, flipped, 1).reshape(moved.shape)
    moved[OWN] = moved[OWN] - later_ref[len(NEAR)]
    place_shares(out_ref, lambda t: moved[t], lat_count, lon_count)


def last_kernel(
    batch, lat_count, near_ref, pattern_ref, map_ref, cells_ref, out_ref, cells, result, cell_sem, out_sem
):
    parts = out_sem.shape[0]
    rows = cells.shape[0] // parts
    copy = pltpu.make_async_copy(cells_ref, cells, cell_sem)
    copy.start()
    flipped = exact_dot(batch_map(batch, lat_count, near_ref, pattern_ref), map_ref[...], 0)
    high = flipped.astype(BF16)
    low = (flipped - high.astype(F32)).astype(BF16)
    right = jnp.concatenate(
        [jnp.concatenate([high, high], axis=1), jnp.concatenate([low, jnp.zeros_like(low)], axis=1)], axis=0
    )
    copy.wait()
    copies = []
    for n in range(parts):
        part = pl.ds(n * rows, rows)
        value = cells[part, :]
        upper = value.astype(BF16)
        rest = (value - upper.astype(F32)).astype(BF16)
        both = lax.dot_general(
            jnp.concatenate([upper, rest], axis=1), right, (((1,), (1,)), ((), ())), preferred_element_type=F32
        )
        result[part, :] = both[:, :LANES] + both[:, LANES:]
        copies.append(pltpu.make_async_copy(result.at[part], out_ref.at[part], out_sem.at[n]))
        copies[-1].start()
    for out_copy in copies:
        out_copy.wait()


def window(tiles, lat_count, lon_count):
    held = min(WIN, lat_count)
    if held == lat_count:
        return tiles
    start = jnp.clip(lax.axis_index("lat") - REACH, 0, lat_count - held)
    return lax.dynamic_slice_in_dim(tiles, start * lon_count, held * lon_count, axis=0)


def local(ensemble, observed, precision, interp_weight, stencil, owned, pattern):
    rows, cols, members = ensemble.shape
    lat_count, lon_count = (lax.axis_size("lat"), lax.axis_size("lon"))
    tiles = lat_count * lon_count
    vmem = pl.BlockSpec(memory_space=pltpu.VMEM)
    smem = pl.BlockSpec(memory_space=pltpu.SMEM)
    anywhere = pl.BlockSpec(memory_space=pl.ANY)
    limit = pltpu.CompilerParams(vmem_limit_bytes=48 * 1024 * 1024)
    mine = packed_params(observed, precision, interp_weight, stencil, owned, cols + 2)
    params = lax.all_gather(mine, ("lat", "lon"), axis=0, tiled=True)
    near_shape = (len(NEAR), SUB, LANES)
    all_shape = jax.ShapeDtypeStruct((tiles, SUB, LANES), F32)
    first, later = pl.pallas_call(
        functools.partial(shares_kernel, lat_count, lon_count),
        out_shape=(all_shape, jax.ShapeDtypeStruct((len(NEAR) + 1, SUB, LANES), F32)),
        in_specs=[anywhere, anywhere],
        out_specs=(vmem, vmem),
        scratch_shapes=[
            pltpu.VMEM((rows + 4, cols + 2 * SUB, members), F32),
            pltpu.VMEM(near_shape, F32),
            pltpu.SMEM((len(NEAR),) + mine.shape[1:], F32),
            pltpu.SemaphoreType.DMA,
            pltpu.SemaphoreType.DMA((len(NEAR),)),
        ],
        compiler_params=limit,
        name="shares",
    )(params, ensemble)
    near = window(lax.psum(first, ("lat", "lon")), lat_count, lon_count)
    moved, first_map = pl.pallas_call(
        functools.partial(first_kernel, 0, lat_count, lon_count),
        out_shape=(all_shape, jax.ShapeDtypeStruct((members, members), F32)),
        in_specs=[vmem, smem, vmem],
        out_specs=(vmem, vmem),
        scratch_shapes=[pltpu.VMEM(near_shape, F32)],
        compiler_params=limit,
        name="first_batch",
    )(near, pattern, later)
    near = window(lax.psum(moved, ("lat", "lon")), lat_count, lon_count)
    parts = 8
    result = pl.pallas_call(
        functools.partial(last_kernel, 1, lat_count),
        out_shape=jax.ShapeDtypeStruct((rows * cols, members), F32),
        in_specs=[vmem, smem, vmem, anywhere],
        out_specs=anywhere,
        scratch_shapes=[
            pltpu.VMEM((rows * cols, members), F32),
            pltpu.VMEM((rows * cols, members), F32),
            pltpu.SemaphoreType.DMA,
            pltpu.SemaphoreType.DMA((parts,)),
        ],
        compiler_params=limit,
        name="second_batch",
    )(near, pattern, first_map, ensemble.reshape(rows * cols, members))
    return result.reshape(rows, cols, members)


def solution(mesh):
    placed = (
        P("lat", "lon", None),
        P(None, "lat", "lon", None),
        P(None, "lat", "lon", None),
        P(None, "lat", "lon", None, None),
        P(None, "lat", "lon", None, None),
        P(None, "lat", "lon", None),
        P(None, "lat", "lon", None, None),
    )
    return jax.shard_map(
        local, mesh=mesh, in_specs=placed, out_specs=P("lat", "lon", None), check_vma=False
    )
```

```python
import functools
import jax
import jax.numpy as jnp
from jax import lax
from jax.experimental import pallas as pl
from jax.experimental.pallas import tpu as pltpu
from jax.sharding import PartitionSpec as P

REACH = 2
WIN = 2 * REACH + 1
SUB = 8
LANES = 128
NEAR = tuple((da, dc) for da in (-1, 0, 1) for dc in (-1, 0, 1))
OWN = NEAR.index((0, 0))
SPAN = 64
AT_ROW, AT_COL, AT_WEIGHT, AT_OBS = (0, 8, 16, 48)
F32 = jnp.float32
BF16 = jnp.bfloat16


def pack_kernel(width, observed, precision, weight, stencil, owned, out_ref):
    batches = observed.shape[0]
    lane = lax.broadcasted_iota(jnp.int32, out_ref.shape[1:], 1)
    value = jnp.zeros(out_ref.shape[1:], F32)
    variance = jnp.ones(out_ref.shape[1:], F32)
    for b in range(batches):
        for o in range(SUB):
            at = b * SPAN + o
            corner = stencil[b, 0, 0, 0, o]
            row = corner // width
            value = jnp.where(lane == at + AT_ROW, row.astype(F32), value)
            value = jnp.where(lane == at + AT_COL, (corner - row * width).astype(F32), value)
            for k in range(4):
                value = jnp.where(lane == at + AT_WEIGHT + k * SUB, weight[b, 0, 0, k, o], value)
            value = jnp.where(lane == at + AT_OBS, observed[b, 0, 0, o], value)
            spot = lane - b * SPAN
            scaled = (spot >= AT_WEIGHT) & (spot < AT_OBS + SUB) & (spot % SUB == o)
            mine = precision[b, 0, 0, o] * owned[b, 0, 0, o].astype(F32)
            variance = jnp.where(scaled, mine, variance)
    out_ref[...] = jnp.broadcast_to(value * jnp.sqrt(variance), out_ref.shape)


def place_shares(out_ref, shares, lat_count, lon_count):
    my_lat, my_lon = (lax.axis_index("lat"), lax.axis_index("lon"))
    out_ref[...] = jnp.zeros_like(out_ref)
    for t, (da, dc) in enumerate(NEAR):
        lat = my_lat + da
        lon = lax.rem(my_lon + dc + lon_count, lon_count)

        @pl.when((lat >= 0) & (lat < lat_count))
        def _():
            out_ref[lat * lon_count + lon] = shares(t)


def shares_kernel(
    lat_count, lon_count, params_ref, cells_ref, first_ref, later_ref, pad, near, params, cell_sem, param_sem
):
    rows, cols = (cells_ref.shape[0], cells_ref.shape[1])
    my_lat, my_lon = (lax.axis_index("lat"), lax.axis_index("lon"))
    cell_copy = pltpu.make_async_copy(cells_ref, pad.at[pl.ds(2, rows), pl.ds(SUB, cols)], cell_sem)
    cell_copy.start()
    param_copies = []
    for t, (da, dc) in enumerate(NEAR):
        lat = jnp.clip(my_lat + da, 0, lat_count - 1)
        lon = lax.rem(my_lon + dc + lon_count, lon_count)
        copy = pltpu.make_async_copy(params_ref.at[lat * lon_count + lon], params.at[t], param_sem.at[t])
        copy.start()
        param_copies.append(copy)
    edge = jnp.zeros((2, cols + 2 * SUB, LANES), F32)
    pad[pl.ds(0, 2)] = edge
    pad[pl.ds(rows + 2, 2)] = edge
    side = jnp.zeros((rows, SUB, LANES), F32)
    pad[pl.ds(2, rows), pl.ds(0, SUB)] = side
    pad[pl.ds(2, rows), pl.ds(SUB + cols, SUB)] = side
    for copy in param_copies:
        copy.wait()
    cell_copy.wait()

    def share(batch, t, o):
        da, dc = NEAR[t]
        at = batch * SPAN + o
        row = params[t, 0, at + AT_ROW].astype(jnp.int32) - 1 + da * rows
        col = params[t, 0, at + AT_COL].astype(jnp.int32) - 1 + dc * cols
        row = jnp.clip(row, -2, rows) + 2
        col = jnp.clip(col, -2, cols) + SUB
        total = None
        for k in range(4):
            cell = pad[row + k // 2, pl.ds(col + k % 2, 1), :]
            term = params[t, 0, at + AT_WEIGHT + k * SUB] * cell
            total = term if total is None else total + term
        return total

    sub = lax.broadcasted_iota(jnp.int32, (SUB, LANES), 0)
    for batch, ref in enumerate((near, later_ref)):
        for t in range(len(NEAR)):
            for o in range(SUB):
                ref[t, pl.ds(o, 1), :] = share(batch, t, o)
        shift = jnp.zeros((SUB, LANES), F32)
        for o in range(SUB):
            shift = jnp.where(sub == o, params[OWN, 0, batch * SPAN + AT_OBS + o], shift)
        if batch == 0:
            near[OWN] = near[OWN] - shift
        else:
            later_ref[len(NEAR)] = shift
    place_shares(first_ref, lambda t: near[t], lat_count, lon_count)


def row_of(block, j):
    return jnp.broadcast_to(block[j:j + 1, :], (SUB, LANES))


def reciprocal(value):
    guess = pl.reciprocal(value, approx=True)
    return guess * (2.0 - value * guess)


def eliminate(blocks):
    count = len(blocks) - 1
    blocks = list(blocks)
    sub = lax.broadcasted_iota(jnp.int32, (SUB, LANES), 0)
    lane = lax.broadcasted_iota(jnp.int32, (SUB, LANES), 1)
    inverse = []
    for k in range(count):
        here = (lane >= k * SUB) & (lane < (k + 1) * SUB)
        column = [
            [jnp.broadcast_to(blocks[i][:, k * SUB + j:k * SUB + j + 1], (SUB, LANES)) for j in range(SUB)]
            for i in range(k, count + 1)
        ]
        diag = column[0]
        full = jnp.where(here, jnp.where(lane - k * SUB == sub, 1.0, 0.0), blocks[k])
        lower = full
        scale = jnp.zeros((SUB, LANES), F32)
        for j in range(0, SUB, 2):
            a, b, c = (row_of(diag[j], j), row_of(diag[j + 1], j), row_of(diag[j + 1], j + 1))
            det = a * c - b * b
            over_det = reciprocal(det)
            first = jnp.where(sub == j, -c, jnp.where(sub == j + 1, b, diag[j] * c - diag[j + 1] * b))
            second = jnp.where(sub == j, b, jnp.where(sub == j + 1, -a, diag[j + 1] * a - diag[j] * b))
            first, second = (first * over_det, second * over_det)
            other = (sub != j) & (sub != j + 1)
            for n in range(j + 2, SUB):
                diag[n] = jnp.where(other, diag[n], 0.0) - first * row_of(diag[n], j) - second * row_of(diag[n], j + 1)
            full = jnp.where(other, full, 0.0) - first * row_of(full, j) - second * row_of(full, j + 1)
            over_a = reciprocal(a)
            top, bottom = (row_of(lower, j), row_of(lower, j + 1))
            below = sub > j + 1
            lower = lower - jnp.where(sub == j + 1, b * over_a, jnp.where(below, first, 0.0)) * top
            lower = lower - jnp.where(below, second, 0.0) * bottom
            scale = jnp.where(sub == j, lax.rsqrt(a), jnp.where(sub == j + 1, lax.rsqrt(det * over_a), scale))
        inverse.append(jnp.where(lane < (k + 1) * SUB, lower * scale, 0.0))
        pivot = [row_of(full, j) for j in range(SUB)]
        for i in range(k + 1, count + 1):
            terms = [column[i - k][j] * pivot[j] for j in range(SUB)]
            while len(terms) > 1:
                terms = [terms[n] + terms[n + 1] for n in range(0, len(terms), 2)]
            blocks[i] = jnp.where(here, 0.0, blocks[i]) - terms[0]
    return inverse, blocks[count][:1]


def block_kernel(shares_ref, out_ref):
    value = jnp.sum(shares_ref[...], axis=0)
    mean = jnp.mean(value, axis=-1, keepdims=True)
    innov = jnp.broadcast_to(-mean, value.shape)
    block = jnp.concatenate([value - mean, innov], axis=0).astype(BF16)
    out_ref[...] = jnp.broadcast_to(block, out_ref.shape)


def batch_map(batch, lat_count, near_ref, pattern_ref):
    lon_count = pattern_ref.shape[-1]
    held = min(WIN, lat_count)
    my_lat = lax.axis_index("lat")
    start = jnp.clip(my_lat - REACH, 0, lat_count - held)
    marks = []
    for j in range(held):
        offset = start + j - my_lat + REACH
        inside = (offset >= 0) & (offset < WIN)
        offset = jnp.clip(offset, 0, WIN - 1)
        for e in range(lon_count):
            mark = jnp.where(inside, pattern_ref[batch, 0, 0, offset, e], 0).astype(F32)
            marks.append(jnp.full((SUB, LANES), mark))
    marks = jnp.concatenate(marks, axis=0)
    near = near_ref[...].astype(F32)
    scaled = near[:, :SUB].reshape(-1, LANES)
    innov = near[:, SUB:].reshape(-1, LANES)
    weighted = scaled * marks
    scaled = scaled.astype(BF16)
    proj = jnp.sum((weighted * innov).reshape(-1, SUB, LANES), axis=0)
    proj = jnp.sum(proj, axis=0, keepdims=True)
    gram = lax.dot_general(
        weighted.astype(BF16), scaled, (((0,), (0,)), ((), ())), preferred_element_type=F32
    )
    sub = lax.broadcasted_iota(jnp.int32, (SUB, LANES), 0)
    lane = lax.broadcasted_iota(jnp.int32, (SUB, LANES), 1)
    members = LANES
    blocks = []
    for k in range(members // SUB):
        block = gram[k * SUB:(k + 1) * SUB, :]
        blocks.append(block + jnp.where(lane - k * SUB == sub, members - 1.0, 0.0))
    blocks.append(jnp.broadcast_to(proj, (SUB, LANES)))
    inverse, weights = eliminate(blocks)
    flipped = jnp.concatenate(inverse, axis=0) * (members - 1.0) ** 0.5 - weights
    return flipped - jnp.mean(flipped, axis=-1, keepdims=True) + 1.0 / members


def exact_dot(a, b, contract_b):
    return lax.dot_general(
        a, b, (((1,), (contract_b,)), ((), ())), precision=lax.Precision.HIGHEST, preferred_element_type=F32
    )


def first_kernel(batch, lat_count, lon_count, near_ref, pattern_ref, later_ref, out_ref, map_ref, moved):
    flipped = batch_map(batch, lat_count, near_ref, pattern_ref)
    map_ref[...] = flipped
    later = later_ref[pl.ds(0, len(NEAR))].reshape(-1, LANES)
    moved[...] = exact_dot(later, flipped, 1).reshape(moved.shape)
    moved[OWN] = moved[OWN] - later_ref[len(NEAR)]
    place_shares(out_ref, lambda t: moved[t], lat_count, lon_count)


def last_kernel(
    batch, lat_count, near_ref, pattern_ref, map_ref, cells_ref, out_ref, cells, result, cell_sem, out_sem
):
    parts = out_sem.shape[0]
    rows = cells.shape[0] // parts
    copy = pltpu.make_async_copy(cells_ref, cells, cell_sem)
    copy.start()
    flipped = exact_dot(batch_map(batch, lat_count, near_ref, pattern_ref), map_ref[...], 0)
    high = flipped.astype(BF16)
    low = (flipped - high.astype(F32)).astype(BF16)
    right = jnp.concatenate(
        [jnp.concatenate([high, high], axis=1), jnp.concatenate([low, jnp.zeros_like(low)], axis=1)], axis=0
    )
    copy.wait()
    copies = []
    for n in range(parts):
        part = pl.ds(n * rows, rows)
        value = cells[part, :]
        upper = value.astype(BF16)
        rest = (value - upper.astype(F32)).astype(BF16)
        both = lax.dot_general(
            jnp.concatenate([upper, rest], axis=1), right, (((1,), (1,)), ((), ())), preferred_element_type=F32
        )
        result[part, :] = both[:, :LANES] + both[:, LANES:]
        copies.append(pltpu.make_async_copy(result.at[part], out_ref.at[part], out_sem.at[n]))
        copies[-1].start()
    for out_copy in copies:
        out_copy.wait()


def window(tiles, lat_count, lon_count):
    held = min(WIN, lat_count)
    if held == lat_count:
        return tiles
    start = jnp.clip(lax.axis_index("lat") - REACH, 0, lat_count - held)
    return lax.dynamic_slice_in_dim(tiles, start * lon_count, held * lon_count, axis=0)


def local(ensemble, observed, precision, interp_weight, stencil, owned, pattern):
    rows, cols, members = ensemble.shape
    lat_count, lon_count = (lax.axis_size("lat"), lax.axis_size("lon"))
    tiles = lat_count * lon_count
    vmem = pl.BlockSpec(memory_space=pltpu.VMEM)
    smem = pl.BlockSpec(memory_space=pltpu.SMEM)
    anywhere = pl.BlockSpec(memory_space=pl.ANY)
    limit = pltpu.CompilerParams(vmem_limit_bytes=48 * 1024 * 1024)
    def exchange(slots):
        return lax.all_to_all(slots, ("lat", "lon"), split_axis=0, concat_axis=0, tiled=True)

    def gathered(shares):
        blocks = pl.pallas_call(
            block_kernel,
            out_shape=jax.ShapeDtypeStruct((tiles, 2 * SUB, LANES), BF16),
            in_specs=[vmem],
            out_specs=vmem,
            compiler_params=limit,
            name="own_block",
        )(exchange(shares))
        return window(exchange(blocks), lat_count, lon_count)

    mine = pl.pallas_call(
        functools.partial(pack_kernel, cols + 2),
        out_shape=jax.ShapeDtypeStruct((tiles, 1, observed.shape[0] * SPAN), F32),
        in_specs=[smem] * 5,
        out_specs=vmem,
        compiler_params=limit,
        name="pack",
    )(observed, precision, interp_weight, stencil, owned)
    params = exchange(mine)
    near_shape = (len(NEAR), SUB, LANES)
    all_shape = jax.ShapeDtypeStruct((tiles, SUB, LANES), F32)
    first, later = pl.pallas_call(
        functools.partial(shares_kernel, lat_count, lon_count),
        out_shape=(all_shape, jax.ShapeDtypeStruct((len(NEAR) + 1, SUB, LANES), F32)),
        in_specs=[anywhere, anywhere],
        out_specs=(vmem, vmem),
        scratch_shapes=[
            pltpu.VMEM((rows + 4, cols + 2 * SUB, members), F32),
            pltpu.VMEM(near_shape, F32),
            pltpu.SMEM((len(NEAR),) + mine.shape[1:], F32),
            pltpu.SemaphoreType.DMA,
            pltpu.SemaphoreType.DMA((len(NEAR),)),
        ],
        compiler_params=limit,
        name="shares",
    )(params, ensemble)
    near = gathered(first)
    moved, first_map = pl.pallas_call(
        functools.partial(first_kernel, 0, lat_count, lon_count),
        out_shape=(all_shape, jax.ShapeDtypeStruct((members, members), F32)),
        in_specs=[vmem, smem, vmem],
        out_specs=(vmem, vmem),
        scratch_shapes=[pltpu.VMEM(near_shape, F32)],
        compiler_params=limit,
        name="first_batch",
    )(near, pattern, later)
    near = gathered(moved)
    parts = 8
    result = pl.pallas_call(
        functools.partial(last_kernel, 1, lat_count),
        out_shape=jax.ShapeDtypeStruct((rows * cols, members), F32),
        in_specs=[vmem, smem, vmem, anywhere],
        out_specs=anywhere,
        scratch_shapes=[
            pltpu.VMEM((rows * cols, members), F32),
            pltpu.VMEM((rows * cols, members), F32),
            pltpu.SemaphoreType.DMA,
            pltpu.SemaphoreType.DMA((parts,)),
        ],
        compiler_params=limit,
        name="second_batch",
    )(near, pattern, first_map, ensemble.reshape(rows * cols, members))
    return result.reshape(rows, cols, members)


def solution(mesh):
    placed = (
        P("lat", "lon", None),
        P(None, "lat", "lon", None),
        P(None, "lat", "lon", None),
        P(None, "lat", "lon", None, None),
        P(None, "lat", "lon", None, None),
        P(None, "lat", "lon", None),
        P(None, "lat", "lon", None, None),
    )
    return jax.shard_map(
        local, mesh=mesh, in_specs=placed, out_specs=P("lat", "lon", None), check_vma=False
    )
```

```python
import functools
import jax
import jax.numpy as jnp
from jax import lax
from jax.experimental import pallas as pl
from jax.experimental.pallas import tpu as pltpu
from jax.sharding import PartitionSpec as P

REACH = 2
WIN = 2 * REACH + 1
SUB = 8
LANES = 128
NEAR = (-1, 0, 1)
AT_ROW, AT_COL, AT_OBS = (4, 5, 6)
F32 = jnp.float32
BF16 = jnp.bfloat16


def start_kernel(
    width, observed, precision, weight, stencil, owned, cells, params_ref, left_ref, right_ref,
    observed_v, precision_v, weight_v, stencil_v, owned_v, left_v, right_v, sems
):
    batches, cols = (observed.shape[0], cells.shape[1])
    pairs = (
        (observed, observed_v),
        (precision, precision_v),
        (weight, weight_v),
        (stencil, stencil_v),
        (owned, owned_v),
        (cells.at[:, pl.ds(0, SUB)], left_v),
        (cells.at[:, pl.ds(cols - SUB, SUB)], right_v),
    )
    copies = [pltpu.make_async_copy(source, target, sems.at[n]) for n, (source, target) in enumerate(pairs)]
    for copy in copies:
        copy.start()
    for copy in copies:
        copy.wait()
    params_ref[...] = jnp.zeros_like(params_ref)
    for b in range(batches):
        root = jnp.sqrt(precision_v[b, 0]) * owned_v[b, 0].astype(F32)
        corner = stencil_v[b, 0, 0, pl.ds(0, 1)].astype(F32)
        row = jnp.floor((corner + 0.5) * (1.0 / width))
        params_ref[b, pl.ds(0, 4), pl.ds(0, SUB)] = weight_v[b, 0, 0] * root
        params_ref[b, pl.ds(AT_ROW, 1), pl.ds(0, SUB)] = row
        params_ref[b, pl.ds(AT_COL, 1), pl.ds(0, SUB)] = corner - row * width
        params_ref[b, pl.ds(AT_OBS, 1), pl.ds(0, SUB)] = observed_v[b, 0] * root
    left_ref[...] = left_v[:, 0, :]
    right_ref[...] = right_v[:, SUB - 1, :]


def clear_rim(pad, rows, cols):
    edge = jnp.zeros((2, cols + 2 * SUB, LANES), F32)
    pad[pl.ds(0, 2)] = edge
    pad[pl.ds(rows + 2, 2)] = edge
    side = jnp.zeros((rows, SUB, LANES), F32)
    pad[pl.ds(2, rows), pl.ds(0, SUB)] = side
    pad[pl.ds(2, rows), pl.ds(SUB + cols, SUB)] = side


def share(pad, number, rows, cols, da, dc, o):
    row = number(AT_ROW, o).astype(jnp.int32) - 1 + da * rows
    col = number(AT_COL, o).astype(jnp.int32) - 1 + dc * cols
    row = jnp.clip(row, -2, rows) + 2
    col = jnp.clip(col, -2, cols) + SUB
    terms = [number(k, o) * pad[row + k // 2, pl.ds(col + k % 2, 1), :] for k in range(4)]
    return (terms[0] + terms[1]) + (terms[2] + terms[3])


def own_shift(number):
    sub = lax.broadcasted_iota(jnp.int32, (SUB, LANES), 0)
    shift = jnp.zeros((SUB, LANES), F32)
    for o in range(SUB):
        shift = jnp.where(sub == o, number(AT_OBS, o), shift)
    return shift


def column_kernel(mine, above, below, left, right, cells, out_ref, pad, params, sems):
    rows, cols = (cells.shape[0], cells.shape[1])
    copies = [pltpu.make_async_copy(cells, pad.at[pl.ds(2, rows), pl.ds(SUB, cols)], sems.at[0])]
    for n, block in enumerate((above, mine, below)):
        copies.append(pltpu.make_async_copy(block.at[0], params.at[n], sems.at[n + 1]))
    for copy in copies:
        copy.start()
    clear_rim(pad, rows, cols)
    for i in range(rows):
        pad[2 + i, pl.ds(SUB - 1, 1), :] = left[pl.ds(i, 1), :]
        pad[2 + i, pl.ds(SUB + cols, 1), :] = right[pl.ds(i, 1), :]
    for copy in copies:
        copy.wait()
    for n, da in enumerate(NEAR):
        number = lambda kind, o: params[n, kind, o]
        for o in range(SUB):
            out_ref[0, pl.ds(n * SUB + o, 1), :] = share(pad, number, rows, cols, da, 0, o)
        if da == 0:
            own = pl.ds(n * SUB, SUB)
            out_ref[0, own, :] = out_ref[0, own, :] - own_shift(number)
    out_ref[0, pl.ds(len(NEAR) * SUB, SUB), :] = mine[1]
    for slot in range(1, out_ref.shape[0]):
        out_ref[slot] = out_ref[0]


def window_start(lat_count, my_lat):
    return 0 if lat_count <= WIN else jnp.clip(my_lat - REACH, 0, lat_count - WIN)


def rows_kernel(lat_count, carries, shares, out_ref):
    my_lat = lax.axis_index("lat")
    start = window_start(lat_count, my_lat)
    held = min(WIN, lat_count)
    for j in range(held):
        total = jnp.zeros((SUB, LANES), F32)
        for n, da in enumerate(NEAR):
            lat = start + j - da
            part = pl.ds(n * SUB, SUB)
            if isinstance(lat, int):
                if 0 <= lat < lat_count:
                    total = total + shares[lat, part, :]
            else:
                inside = (lat >= 0) & (lat < lat_count)
                total = total + jnp.where(inside, shares[jnp.clip(lat, 0, lat_count - 1), part, :], 0.0)
        out_ref[0, pl.ds(j * SUB, SUB), :] = total
    if carries:
        lane = lax.broadcasted_iota(jnp.int32, (SUB, LANES), 1)
        packed = jnp.zeros((SUB, LANES), F32)
        for n, da in enumerate(NEAR):
            lat = jnp.clip(my_lat + da, 0, lat_count - 1)
            block = shares[lat, pl.ds(len(NEAR) * SUB, SUB), :]
            shifted = pltpu.roll(block, n * SUB, 1) if n else block
            packed = jnp.where((lane >= n * SUB) & (lane < (n + 1) * SUB), shifted, packed)
        out_ref[0, pl.ds(held * SUB, SUB), :] = packed
    for slot in range(1, out_ref.shape[0]):
        out_ref[slot] = out_ref[0]


def row_of(block, j):
    return jnp.broadcast_to(block[j:j + 1, :], (SUB, LANES))


def reciprocal(value):
    guess = pl.reciprocal(value, approx=True)
    return guess * (2.0 - value * guess)


def eliminate(blocks):
    count = len(blocks) - 1
    blocks = list(blocks)
    sub = lax.broadcasted_iota(jnp.int32, (SUB, LANES), 0)
    lane = lax.broadcasted_iota(jnp.int32, (SUB, LANES), 1)
    inverse = []
    for k in range(count):
        here = (lane >= k * SUB) & (lane < (k + 1) * SUB)
        column = [
            [jnp.broadcast_to(blocks[i][:, k * SUB + j:k * SUB + j + 1], (SUB, LANES)) for j in range(SUB)]
            for i in range(k, count + 1)
        ]
        diag = column[0]
        full = jnp.where(here, jnp.where(lane - k * SUB == sub, 1.0, 0.0), blocks[k])
        lower = full
        scale = jnp.zeros((SUB, LANES), F32)
        for j in range(0, SUB, 2):
            a, b, c = (row_of(diag[j], j), row_of(diag[j + 1], j), row_of(diag[j + 1], j + 1))
            det = a * c - b * b
            over_det = reciprocal(det)
            first = jnp.where(sub == j, -c, jnp.where(sub == j + 1, b, diag[j] * c - diag[j + 1] * b))
            second = jnp.where(sub == j, b, jnp.where(sub == j + 1, -a, diag[j + 1] * a - diag[j] * b))
            first, second = (first * over_det, second * over_det)
            other = (sub != j) & (sub != j + 1)
            for n in range(j + 2, SUB):
                diag[n] = jnp.where(other, diag[n], 0.0) - first * row_of(diag[n], j) - second * row_of(diag[n], j + 1)
            full = jnp.where(other, full, 0.0) - first * row_of(full, j) - second * row_of(full, j + 1)
            over_a = reciprocal(a)
            top, bottom = (row_of(lower, j), row_of(lower, j + 1))
            below = sub > j + 1
            lower = lower - jnp.where(sub == j + 1, b * over_a, jnp.where(below, first, 0.0)) * top
            lower = lower - jnp.where(below, second, 0.0) * bottom
            scale = jnp.where(sub == j, lax.rsqrt(a), jnp.where(sub == j + 1, lax.rsqrt(det * over_a), scale))
        inverse.append(jnp.where(lane < (k + 1) * SUB, lower * scale, 0.0))
        pivot = [row_of(full, j) for j in range(SUB)]
        for i in range(k + 1, count + 1):
            terms = [column[i - k][j] * pivot[j] for j in range(SUB)]
            while len(terms) > 1:
                terms = [terms[n] + terms[n + 1] for n in range(0, len(terms), 2)]
            blocks[i] = jnp.where(here, 0.0, blocks[i]) - terms[0]
    return inverse, blocks[count][:1]


def batch_map(batch, lat_count, near_ref, pattern_ref):
    lon_count = near_ref.shape[0]
    held = min(WIN, lat_count)
    my_lat = lax.axis_index("lat")
    start = window_start(lat_count, my_lat)
    marks = []
    for e in range(lon_count):
        for j in range(held):
            offset = start + j - my_lat + REACH
            inside = (offset >= 0) & (offset < WIN)
            mark = jnp.where(inside, pattern_ref[batch, 0, 0, jnp.clip(offset, 0, WIN - 1), e], 0)
            marks.append(jnp.full((SUB, LANES), mark.astype(F32)))
    marks = jnp.concatenate(marks, axis=0)
    value = near_ref[:, pl.ds(0, held * SUB), :].reshape(-1, LANES)
    mean = jnp.mean(value, axis=-1, keepdims=True)
    scaled = (value - mean).astype(BF16)
    innov = (-mean).astype(BF16).astype(F32)
    weighted = scaled.astype(F32) * marks
    proj = jnp.sum((weighted * innov).reshape(-1, SUB, LANES), axis=0)
    proj = jnp.sum(proj, axis=0, keepdims=True)
    gram = lax.dot_general(
        weighted.astype(BF16), scaled, (((0,), (0,)), ((), ())), preferred_element_type=F32
    )
    sub = lax.broadcasted_iota(jnp.int32, (SUB, LANES), 0)
    lane = lax.broadcasted_iota(jnp.int32, (SUB, LANES), 1)
    members = LANES
    blocks = []
    for k in range(members // SUB):
        block = gram[k * SUB:(k + 1) * SUB, :]
        blocks.append(block + jnp.where(lane - k * SUB == sub, members - 1.0, 0.0))
    blocks.append(jnp.broadcast_to(proj, (SUB, LANES)))
    inverse, weights = eliminate(blocks)
    flipped = jnp.concatenate(inverse, axis=0) * (members - 1.0) ** 0.5 - weights
    return flipped - jnp.mean(flipped, axis=-1, keepdims=True) + 1.0 / members


def exact_dot(a, b, contract_b):
    return lax.dot_general(
        a, b, (((1,), (contract_b,)), ((), ())), precision=lax.Precision.HIGHEST, preferred_element_type=F32
    )


def first_kernel(
    batch, lat_count, near_ref, pattern_ref, cells, left_ref, mid_ref, right_ref, map_ref, pad, later, params, sems
):
    rows, cols = (cells.shape[0], cells.shape[1])
    lon_count = near_ref.shape[0]
    held = min(WIN, lat_count)
    my_lon = lax.axis_index("lon")
    copies = [pltpu.make_async_copy(cells, pad.at[pl.ds(2, rows), pl.ds(SUB, cols)], sems.at[0])]
    for n, dc in enumerate(NEAR):
        lon = lax.rem(my_lon + dc + lon_count, lon_count)
        block = near_ref.at[lon, pl.ds(held * SUB, SUB)]
        copies.append(pltpu.make_async_copy(block, params.at[n], sems.at[n + 1]))
    for copy in copies:
        copy.start()
    clear_rim(pad, rows, cols)
    for copy in copies:
        copy.wait()
    for n, dc in enumerate(NEAR):
        for m, da in enumerate(NEAR):
            number = lambda kind, o: params[n, kind, m * SUB + o]
            for o in range(SUB):
                at = (n * len(NEAR) + m) * SUB + o
                later[pl.ds(at, 1), :] = share(pad, number, rows, cols, da, dc, o)
    flipped = batch_map(batch, lat_count, near_ref, pattern_ref)
    map_ref[...] = flipped
    moved = exact_dot(later[...], flipped, 1)
    size = len(NEAR) * SUB
    left_ref[...] = moved[:size]
    mid_ref[...] = moved[size:2 * size]
    right_ref[...] = moved[2 * size:]
    own = pl.ds(SUB, SUB)
    mid_ref[own, :] = mid_ref[own, :] - own_shift(lambda kind, o: params[1, kind, SUB + o])


def meet_kernel(mid, from_left, from_right, out_ref):
    total = mid[...] + from_left[...] + from_right[...]
    out_ref[...] = jnp.broadcast_to(total, out_ref.shape)


def last_kernel(
    batch, lat_count, near_ref, pattern_ref, map_ref, cells_ref, out_ref, cells, result, cell_sem, out_sem
):
    parts = out_sem.shape[0]
    rows = cells.shape[0] // parts
    copy = pltpu.make_async_copy(cells_ref, cells, cell_sem)
    copy.start()
    flipped = exact_dot(batch_map(batch, lat_count, near_ref, pattern_ref), map_ref[...], 0)
    high = flipped.astype(BF16)
    low = (flipped - high.astype(F32)).astype(BF16)
    right = jnp.concatenate(
        [jnp.concatenate([high, high], axis=1), jnp.concatenate([low, jnp.zeros_like(low)], axis=1)], axis=0
    )
    copy.wait()
    copies = []
    for n in range(parts):
        part = pl.ds(n * rows, rows)
        value = cells[part, :]
        upper = value.astype(BF16)
        rest = (value - upper.astype(F32)).astype(BF16)
        both = lax.dot_general(
            jnp.concatenate([upper, rest], axis=1), right, (((1,), (1,)), ((), ())), preferred_element_type=F32
        )
        result[part, :] = both[:, :LANES] + both[:, LANES:]
        copies.append(pltpu.make_async_copy(result.at[part], out_ref.at[part], out_sem.at[n]))
        copies[-1].start()
    for out_copy in copies:
        out_copy.wait()


def local(ensemble, observed, precision, interp_weight, stencil, owned, pattern):
    rows, cols, members = ensemble.shape
    batches = observed.shape[0]
    lat_count, lon_count = (lax.axis_size("lat"), lax.axis_size("lon"))
    held = min(WIN, lat_count)
    column = len(NEAR) * SUB
    vmem = pl.BlockSpec(memory_space=pltpu.VMEM)
    smem = pl.BlockSpec(memory_space=pltpu.SMEM)
    anywhere = pl.BlockSpec(memory_space=pl.ANY)
    hbm = pl.BlockSpec(memory_space=pltpu.HBM)
    limit = pltpu.CompilerParams(vmem_limit_bytes=48 * 1024 * 1024)

    def shape(*dims):
        return jax.ShapeDtypeStruct(dims, F32)

    def exchange(slots, axis):
        return lax.all_to_all(slots, axis, split_axis=0, concat_axis=0, tiled=True)

    def to_next(array, axis, step, count, wraps):
        route = [(i, (i + step) % count) for i in range(count) if wraps or 0 <= i + step < count]
        return lax.ppermute(array, axis, route)

    def gathered(shares, carries):
        sums = pl.pallas_call(
            functools.partial(rows_kernel, lat_count, carries),
            out_shape=shape(lon_count, (held + carries) * SUB, members),
            in_specs=[vmem],
            out_specs=vmem,
            compiler_params=limit,
            name="column_sums",
        )(exchange(shares, "lat"))
        return exchange(sums, "lon")

    small = (observed, precision, interp_weight, stencil, owned)
    mine, left, right = pl.pallas_call(
        functools.partial(start_kernel, cols + 2),
        out_shape=(shape(batches, SUB, LANES), shape(rows, members), shape(rows, members)),
        in_specs=[hbm] * 6,
        out_specs=(vmem,) * 3,
        scratch_shapes=[pltpu.VMEM(array.shape, array.dtype) for array in small]
        + [pltpu.VMEM((rows, SUB, members), F32)] * 2
        + [pltpu.SemaphoreType.DMA((7,))],
        compiler_params=limit,
        name="start",
    )(*small, ensemble)
    from_left = to_next(right, "lon", 1, lon_count, True)
    from_right = to_next(left, "lon", -1, lon_count, True)
    above = to_next(mine, "lat", 1, lat_count, False)
    below = to_next(mine, "lat", -1, lat_count, False)
    pad = pltpu.VMEM((rows + 4, cols + 2 * SUB, members), F32)
    shares = pl.pallas_call(
        column_kernel,
        out_shape=shape(lat_count, column + SUB, members),
        in_specs=[vmem] * 5 + [anywhere],
        out_specs=vmem,
        scratch_shapes=[pad, pltpu.SMEM((3, SUB, LANES), F32), pltpu.SemaphoreType.DMA((4,))],
        compiler_params=limit,
        name="column_shares",
    )(mine, above, below, from_left, from_right, ensemble)
    near = gathered(shares, True)
    part = shape(column, members)
    left, mid, right, first_map = pl.pallas_call(
        functools.partial(first_kernel, 0, lat_count),
        out_shape=(part, part, part, shape(members, members)),
        in_specs=[vmem, smem, anywhere],
        out_specs=(vmem,) * 4,
        scratch_shapes=[
            pad,
            pltpu.VMEM((len(NEAR) * column, members), F32),
            pltpu.SMEM((3, SUB, LANES), F32),
            pltpu.SemaphoreType.DMA((4,)),
        ],
        compiler_params=limit,
        name="first_batch",
    )(near, pattern, ensemble)
    from_left = to_next(right, "lon", 1, lon_count, True)
    from_right = to_next(left, "lon", -1, lon_count, True)
    shares = pl.pallas_call(
        meet_kernel,
        out_shape=shape(lat_count, column, members),
        in_specs=[vmem] * 3,
        out_specs=vmem,
        compiler_params=limit,
        name="meet",
    )(mid, from_left, from_right)
    near = gathered(shares, False)
    parts = 8
    result = pl.pallas_call(
        functools.partial(last_kernel, 1, lat_count),
        out_shape=shape(rows * cols, members),
        in_specs=[vmem, smem, vmem, anywhere],
        out_specs=anywhere,
        scratch_shapes=[
            pltpu.VMEM((rows * cols, members), F32),
            pltpu.VMEM((rows * cols, members), F32),
            pltpu.SemaphoreType.DMA,
            pltpu.SemaphoreType.DMA((parts,)),
        ],
        compiler_params=limit,
        name="second_batch",
    )(near, pattern, first_map, ensemble.reshape(rows * cols, members))
    return result.reshape(rows, cols, members)


def solution(mesh):
    placed = (
        P("lat", "lon", None),
        P(None, "lat", "lon", None),
        P(None, "lat", "lon", None),
        P(None, "lat", "lon", None, None),
        P(None, "lat", "lon", None, None),
        P(None, "lat", "lon", None),
        P(None, "lat", "lon", None, None),
    )
    return jax.shard_map(
        local, mesh=mesh, in_specs=placed, out_specs=P("lat", "lon", None), check_vma=False
    )
```

```python
import functools
import jax
import jax.numpy as jnp
from jax import lax
from jax.experimental import pallas as pl
from jax.experimental.pallas import tpu as pltpu
from jax.sharding import PartitionSpec as P

REACH = 2
WIN = 2 * REACH + 1
SUB = 8
LANES = 128
NEAR = (-1, 0, 1)
AT_ROW, AT_COL, AT_OBS = (4, 5, 6)
F32 = jnp.float32
BF16 = jnp.bfloat16


class Axis:
    def __init__(self, name, count):
        self.count, self.sizes = (count, [])
        least = 2
        while count > 1:
            if count % least == 0:
                self.sizes.append(least)
                count //= least
            else:
                least += 1
        self.names = tuple(f"{name}{n}" for n in range(len(self.sizes)))

    def index(self):
        total = 0
        for name, size in zip(self.names, self.sizes):
            total = total * size + lax.axis_index(name)
        return total

    def gather(self, block):
        for name in self.names:
            block = lax.all_gather(block, name, axis=0)
        return block.reshape((self.count,) + block.shape[len(self.names):])

    def place(self, index):
        total = 0
        for size in reversed(self.sizes):
            if isinstance(index, int):
                digit, index = (index % size, index // size)
            else:
                digit, index = (lax.rem(index, size), lax.div(index, size))
            total = total * size + digit
        return total

    def shifted(self, block, step, wraps):
        route = [(i, (i + step) % self.count) for i in range(self.count) if wraps or 0 <= i + step < self.count]
        return lax.ppermute(block, self.names, route)


def start_kernel(
    width, observed, precision, weight, stencil, owned, cells, params_ref, left_ref, right_ref,
    observed_v, precision_v, weight_v, stencil_v, owned_v, left_v, right_v, sems
):
    batches, cols = (observed.shape[0], cells.shape[1])
    pairs = (
        (observed, observed_v),
        (precision, precision_v),
        (weight, weight_v),
        (stencil, stencil_v),
        (owned, owned_v),
        (cells.at[:, pl.ds(0, SUB)], left_v),
        (cells.at[:, pl.ds(cols - SUB, SUB)], right_v),
    )
    copies = [pltpu.make_async_copy(source, target, sems.at[n]) for n, (source, target) in enumerate(pairs)]
    for copy in copies:
        copy.start()
    for copy in copies:
        copy.wait()
    params_ref[...] = jnp.zeros_like(params_ref)
    for b in range(batches):
        root = jnp.sqrt(precision_v[b, 0]) * owned_v[b, 0].astype(F32)
        corner = stencil_v[b, 0, 0, pl.ds(0, 1)].astype(F32)
        row = jnp.floor((corner + 0.5) * (1.0 / width))
        params_ref[b, pl.ds(0, 4), pl.ds(0, SUB)] = weight_v[b, 0, 0] * root
        params_ref[b, pl.ds(AT_ROW, 1), pl.ds(0, SUB)] = row
        params_ref[b, pl.ds(AT_COL, 1), pl.ds(0, SUB)] = corner - row * width
        params_ref[b, pl.ds(AT_OBS, 1), pl.ds(0, SUB)] = observed_v[b, 0] * root
    left_ref[...] = left_v[:, 0, :]
    right_ref[...] = right_v[:, SUB - 1, :]


def clear_rim(pad, rows, cols):
    edge = jnp.zeros((2, cols + 2 * SUB, LANES), F32)
    pad[pl.ds(0, 2)] = edge
    pad[pl.ds(rows + 2, 2)] = edge
    side = jnp.zeros((rows, SUB, LANES), F32)
    pad[pl.ds(2, rows), pl.ds(0, SUB)] = side
    pad[pl.ds(2, rows), pl.ds(SUB + cols, SUB)] = side


def share(pad, number, rows, cols, da, dc, o):
    row = number(AT_ROW, o).astype(jnp.int32) - 1 + da * rows
    col = number(AT_COL, o).astype(jnp.int32) - 1 + dc * cols
    row = jnp.clip(row, -2, rows) + 2
    col = jnp.clip(col, -2, cols) + SUB
    terms = [number(k, o) * pad[row + k // 2, pl.ds(col + k % 2, 1), :] for k in range(4)]
    return (terms[0] + terms[1]) + (terms[2] + terms[3])


def own_shift(number):
    sub = lax.broadcasted_iota(jnp.int32, (SUB, LANES), 0)
    shift = jnp.zeros((SUB, LANES), F32)
    for o in range(SUB):
        shift = jnp.where(sub == o, number(AT_OBS, o), shift)
    return shift


def column_kernel(mine, above, below, left, right, cells, out_ref, pad, params, sems):
    rows, cols = (cells.shape[0], cells.shape[1])
    copies = [pltpu.make_async_copy(cells, pad.at[pl.ds(2, rows), pl.ds(SUB, cols)], sems.at[0])]
    for n, block in enumerate((above, mine, below)):
        copies.append(pltpu.make_async_copy(block.at[0], params.at[n], sems.at[n + 1]))
    for copy in copies:
        copy.start()
    clear_rim(pad, rows, cols)
    for i in range(rows):
        pad[2 + i, pl.ds(SUB - 1, 1), :] = left[pl.ds(i, 1), :]
        pad[2 + i, pl.ds(SUB + cols, 1), :] = right[pl.ds(i, 1), :]
    for copy in copies:
        copy.wait()
    for n, da in enumerate(NEAR):
        number = lambda kind, o: params[n, kind, o]
        for o in range(SUB):
            out_ref[pl.ds(n * SUB + o, 1), :] = share(pad, number, rows, cols, da, 0, o)
        if da == 0:
            own = pl.ds(n * SUB, SUB)
            out_ref[own, :] = out_ref[own, :] - own_shift(number)
    out_ref[pl.ds(len(NEAR) * SUB, SUB), :] = mine[1]


def window_start(lat_count, my_lat):
    return 0 if lat_count <= WIN else jnp.clip(my_lat - REACH, 0, lat_count - WIN)


def rows_kernel(lats, carries, shares, out_ref):
    lat_count, my_lat = (lats.count, lats.index())
    start = window_start(lat_count, my_lat)
    held = min(WIN, lat_count)
    for j in range(held):
        total = jnp.zeros((SUB, LANES), F32)
        for n, da in enumerate(NEAR):
            lat = start + j - da
            part = pl.ds(n * SUB, SUB)
            if isinstance(lat, int):
                if 0 <= lat < lat_count:
                    total = total + shares[lats.place(lat), part, :]
            else:
                inside = (lat >= 0) & (lat < lat_count)
                total = total + jnp.where(inside, shares[lats.place(jnp.clip(lat, 0, lat_count - 1)), part, :], 0.0)
        out_ref[pl.ds(j * SUB, SUB), :] = total
    if carries:
        lane = lax.broadcasted_iota(jnp.int32, (SUB, LANES), 1)
        packed = jnp.zeros((SUB, LANES), F32)
        for n, da in enumerate(NEAR):
            lat = jnp.clip(my_lat + da, 0, lat_count - 1)
            block = shares[lats.place(lat), pl.ds(len(NEAR) * SUB, SUB), :]
            shifted = pltpu.roll(block, n * SUB, 1) if n else block
            packed = jnp.where((lane >= n * SUB) & (lane < (n + 1) * SUB), shifted, packed)
        out_ref[pl.ds(held * SUB, SUB), :] = packed


def row_of(block, j):
    return jnp.broadcast_to(block[j:j + 1, :], (SUB, LANES))


def reciprocal(value):
    guess = pl.reciprocal(value, approx=True)
    return guess * (2.0 - value * guess)


def eliminate(blocks):
    count = len(blocks) - 1
    blocks = list(blocks)
    sub = lax.broadcasted_iota(jnp.int32, (SUB, LANES), 0)
    lane = lax.broadcasted_iota(jnp.int32, (SUB, LANES), 1)
    inverse = []
    for k in range(count):
        here = (lane >= k * SUB) & (lane < (k + 1) * SUB)
        column = [
            [jnp.broadcast_to(blocks[i][:, k * SUB + j:k * SUB + j + 1], (SUB, LANES)) for j in range(SUB)]
            for i in range(k, count + 1)
        ]
        diag = column[0]
        full = jnp.where(here, jnp.where(lane - k * SUB == sub, 1.0, 0.0), blocks[k])
        lower = full
        scale = jnp.zeros((SUB, LANES), F32)
        for j in range(0, SUB, 2):
            a, b, c = (row_of(diag[j], j), row_of(diag[j + 1], j), row_of(diag[j + 1], j + 1))
            det = a * c - b * b
            over_det = reciprocal(det)
            first = jnp.where(sub == j, -c, jnp.where(sub == j + 1, b, diag[j] * c - diag[j + 1] * b))
            second = jnp.where(sub == j, b, jnp.where(sub == j + 1, -a, diag[j + 1] * a - diag[j] * b))
            first, second = (first * over_det, second * over_det)
            other = (sub != j) & (sub != j + 1)
            for n in range(j + 2, SUB):
                diag[n] = jnp.where(other, diag[n], 0.0) - first * row_of(diag[n], j) - second * row_of(diag[n], j + 1)
            full = jnp.where(other, full, 0.0) - first * row_of(full, j) - second * row_of(full, j + 1)
            over_a = reciprocal(a)
            top, bottom = (row_of(lower, j), row_of(lower, j + 1))
            below = sub > j + 1
            lower = lower - jnp.where(sub == j + 1, b * over_a, jnp.where(below, first, 0.0)) * top
            lower = lower - jnp.where(below, second, 0.0) * bottom
            scale = jnp.where(sub == j, lax.rsqrt(a), jnp.where(sub == j + 1, lax.rsqrt(det * over_a), scale))
        inverse.append(jnp.where(lane < (k + 1) * SUB, lower * scale, 0.0))
        pivot = [row_of(full, j) for j in range(SUB)]
        for i in range(k + 1, count + 1):
            terms = [column[i - k][j] * pivot[j] for j in range(SUB)]
            while len(terms) > 1:
                terms = [terms[n] + terms[n + 1] for n in range(0, len(terms), 2)]
            blocks[i] = jnp.where(here, 0.0, blocks[i]) - terms[0]
    return inverse, blocks[count][:1]


def batch_map(batch, lats, lons, near_ref, pattern_ref):
    held = min(WIN, lats.count)
    my_lat = lats.index()
    start = window_start(lats.count, my_lat)
    marks = []
    for e in sorted(range(lons.count), key=lons.place):
        for j in range(held):
            offset = start + j - my_lat + REACH
            inside = (offset >= 0) & (offset < WIN)
            mark = jnp.where(inside, pattern_ref[batch, 0, 0, jnp.clip(offset, 0, WIN - 1), e], 0)
            marks.append(jnp.full((SUB, LANES), mark.astype(F32)))
    marks = jnp.concatenate(marks, axis=0)
    value = near_ref[:, pl.ds(0, held * SUB), :].reshape(-1, LANES)
    mean = jnp.mean(value, axis=-1, keepdims=True)
    scaled = (value - mean).astype(BF16)
    innov = (-mean).astype(BF16).astype(F32)
    weighted = scaled.astype(F32) * marks
    proj = jnp.sum((weighted * innov).reshape(-1, SUB, LANES), axis=0)
    proj = jnp.sum(proj, axis=0, keepdims=True)
    gram = lax.dot_general(
        weighted.astype(BF16), scaled, (((0,), (0,)), ((), ())), preferred_element_type=F32
    )
    sub = lax.broadcasted_iota(jnp.int32, (SUB, LANES), 0)
    lane = lax.broadcasted_iota(jnp.int32, (SUB, LANES), 1)
    members = LANES
    blocks = []
    for k in range(members // SUB):
        block = gram[k * SUB:(k + 1) * SUB, :]
        blocks.append(block + jnp.where(lane - k * SUB == sub, members - 1.0, 0.0))
    blocks.append(jnp.broadcast_to(proj, (SUB, LANES)))
    inverse, weights = eliminate(blocks)
    flipped = jnp.concatenate(inverse, axis=0) * (members - 1.0) ** 0.5 - weights
    return flipped - jnp.mean(flipped, axis=-1, keepdims=True) + 1.0 / members


def exact_dot(a, b, contract_b):
    return lax.dot_general(
        a, b, (((1,), (contract_b,)), ((), ())), precision=lax.Precision.HIGHEST, preferred_element_type=F32
    )


def first_kernel(
    batch, lats, lons, near_ref, pattern_ref, cells, left_ref, mid_ref, right_ref, map_ref, pad, later, params, sems
):
    rows, cols = (cells.shape[0], cells.shape[1])
    held = min(WIN, lats.count)
    my_lon = lons.index()
    copies = [pltpu.make_async_copy(cells, pad.at[pl.ds(2, rows), pl.ds(SUB, cols)], sems.at[0])]
    for n, dc in enumerate(NEAR):
        lon = lax.rem(my_lon + dc + lons.count, lons.count)
        block = near_ref.at[lons.place(lon), pl.ds(held * SUB, SUB)]
        copies.append(pltpu.make_async_copy(block, params.at[n], sems.at[n + 1]))
    for copy in copies:
        copy.start()
    clear_rim(pad, rows, cols)
    for copy in copies:
        copy.wait()
    for n, dc in enumerate(NEAR):
        for m, da in enumerate(NEAR):
            number = lambda kind, o: params[n, kind, m * SUB + o]
            for o in range(SUB):
                at = (n * len(NEAR) + m) * SUB + o
                later[pl.ds(at, 1), :] = share(pad, number, rows, cols, da, dc, o)
    flipped = batch_map(batch, lats, lons, near_ref, pattern_ref)
    map_ref[...] = flipped
    moved = exact_dot(later[...], flipped, 1)
    size = len(NEAR) * SUB
    left_ref[...] = moved[:size]
    mid_ref[...] = moved[size:2 * size]
    right_ref[...] = moved[2 * size:]
    own = pl.ds(SUB, SUB)
    mid_ref[own, :] = mid_ref[own, :] - own_shift(lambda kind, o: params[1, kind, SUB + o])


def meet_kernel(mid, from_left, from_right, out_ref):
    out_ref[...] = mid[...] + from_left[...] + from_right[...]


def last_kernel(
    batch, lats, lons, near_ref, pattern_ref, map_ref, cells_ref, out_ref, cells, result, cell_sem, out_sem
):
    parts = out_sem.shape[0]
    rows = cells.shape[0] // parts
    copy = pltpu.make_async_copy(cells_ref, cells, cell_sem)
    copy.start()
    flipped = exact_dot(batch_map(batch, lats, lons, near_ref, pattern_ref), map_ref[...], 0)
    high = flipped.astype(BF16)
    low = (flipped - high.astype(F32)).astype(BF16)
    right = jnp.concatenate(
        [jnp.concatenate([high, high], axis=1), jnp.concatenate([low, jnp.zeros_like(low)], axis=1)], axis=0
    )
    copy.wait()
    copies = []
    for n in range(parts):
        part = pl.ds(n * rows, rows)
        value = cells[part, :]
        upper = value.astype(BF16)
        rest = (value - upper.astype(F32)).astype(BF16)
        both = lax.dot_general(
            jnp.concatenate([upper, rest], axis=1), right, (((1,), (1,)), ((), ())), preferred_element_type=F32
        )
        result[part, :] = both[:, :LANES] + both[:, LANES:]
        copies.append(pltpu.make_async_copy(result.at[part], out_ref.at[part], out_sem.at[n]))
        copies[-1].start()
    for out_copy in copies:
        out_copy.wait()


def local(lats, lons, ensemble, observed, precision, interp_weight, stencil, owned, pattern):
    rows, cols, members = ensemble.shape
    batches = observed.shape[0]
    held = min(WIN, lats.count)
    column = len(NEAR) * SUB
    vmem = pl.BlockSpec(memory_space=pltpu.VMEM)
    smem = pl.BlockSpec(memory_space=pltpu.SMEM)
    anywhere = pl.BlockSpec(memory_space=pl.ANY)
    hbm = pl.BlockSpec(memory_space=pltpu.HBM)
    limit = pltpu.CompilerParams(vmem_limit_bytes=48 * 1024 * 1024)

    def shape(*dims):
        return jax.ShapeDtypeStruct(dims, F32)

    def gathered(shares, carries):
        sums = pl.pallas_call(
            functools.partial(rows_kernel, lats, carries),
            out_shape=shape((held + carries) * SUB, members),
            in_specs=[vmem],
            out_specs=vmem,
            compiler_params=limit,
            name="column_sums",
        )(lats.gather(shares))
        return lons.gather(sums)

    small = (observed, precision, interp_weight, stencil, owned)
    mine, left, right = pl.pallas_call(
        functools.partial(start_kernel, cols + 2),
        out_shape=(shape(batches, SUB, LANES), shape(rows, members), shape(rows, members)),
        in_specs=[hbm] * 6,
        out_specs=(vmem,) * 3,
        scratch_shapes=[pltpu.VMEM(array.shape, array.dtype) for array in small]
        + [pltpu.VMEM((rows, SUB, members), F32)] * 2
        + [pltpu.SemaphoreType.DMA((7,))],
        compiler_params=pltpu.CompilerParams(vmem_limit_bytes=63 * 1024 * 1024),
        name="start",
    )(*small, ensemble)
    from_left = lons.shifted(right, 1, True)
    from_right = lons.shifted(left, -1, True)
    above = lats.shifted(mine, 1, False)
    below = lats.shifted(mine, -1, False)
    pad = pltpu.VMEM((rows + 4, cols + 2 * SUB, members), F32)
    shares = pl.pallas_call(
        column_kernel,
        out_shape=shape(column + SUB, members),
        in_specs=[vmem] * 5 + [anywhere],
        out_specs=vmem,
        scratch_shapes=[pad, pltpu.SMEM((3, SUB, LANES), F32), pltpu.SemaphoreType.DMA((4,))],
        compiler_params=limit,
        name="column_shares",
    )(mine, above, below, from_left, from_right, ensemble)
    near = gathered(shares, True)
    part = shape(column, members)
    left, mid, right, first_map = pl.pallas_call(
        functools.partial(first_kernel, 0, lats, lons),
        out_shape=(part, part, part, shape(members, members)),
        in_specs=[vmem, smem, anywhere],
        out_specs=(vmem,) * 4,
        scratch_shapes=[
            pad,
            pltpu.VMEM((len(NEAR) * column, members), F32),
            pltpu.SMEM((3, SUB, LANES), F32),
            pltpu.SemaphoreType.DMA((4,)),
        ],
        compiler_params=limit,
        name="first_batch",
    )(near, pattern, ensemble)
    from_left = lons.shifted(right, 1, True)
    from_right = lons.shifted(left, -1, True)
    shares = pl.pallas_call(
        meet_kernel,
        out_shape=part,
        in_specs=[vmem] * 3,
        out_specs=vmem,
        compiler_params=limit,
        name="meet",
    )(mid, from_left, from_right)
    near = gathered(shares, False)
    parts = 8
    result = pl.pallas_call(
        functools.partial(last_kernel, 1, lats, lons),
        out_shape=shape(rows * cols, members),
        in_specs=[vmem, smem, vmem, anywhere],
        out_specs=anywhere,
        scratch_shapes=[
            pltpu.VMEM((rows * cols, members), F32),
            pltpu.VMEM((rows * cols, members), F32),
            pltpu.SemaphoreType.DMA,
            pltpu.SemaphoreType.DMA((parts,)),
        ],
        compiler_params=limit,
        name="second_batch",
    )(near, pattern, first_map, ensemble.reshape(rows * cols, members))
    return result.reshape(rows, cols, members)


def solution(mesh):
    lats, lons = (Axis(name, mesh.shape[name]) for name in ("lat", "lon"))
    split = jax.sharding.Mesh(mesh.devices.reshape(lats.sizes + lons.sizes), lats.names + lons.names)
    lat, lon = (lats.names, lons.names)
    placed = (
        P(lat, lon, None),
        P(None, lat, lon, None),
        P(None, lat, lon, None),
        P(None, lat, lon, None, None),
        P(None, lat, lon, None, None),
        P(None, lat, lon, None),
        P(None, lat, lon, None, None),
    )
    return jax.shard_map(
        functools.partial(local, lats, lons),
        mesh=split,
        in_specs=placed,
        out_specs=P(lat, lon, None),
        check_vma=False,
    )
```

```python
import functools
import jax
import jax.numpy as jnp
from jax import lax
from jax.experimental import pallas as pl
from jax.experimental.pallas import tpu as pltpu
from jax.sharding import PartitionSpec as P

REACH = 2
WIN = 2 * REACH + 1
SUB = 8
LANES = 128
NEAR = (-1, 0, 1)
AT_ROW, AT_COL, AT_OBS = (4, 5, 6)
F32 = jnp.float32
BF16 = jnp.bfloat16


def start_kernel(
    width, observed, precision, weight, stencil, owned, cells, params_ref, left_ref, right_ref,
    observed_v, precision_v, weight_v, stencil_v, owned_v, left_v, right_v, sems
):
    batches, cols = (observed.shape[0], cells.shape[1])
    pairs = (
        (observed, observed_v),
        (precision, precision_v),
        (weight, weight_v),
        (stencil, stencil_v),
        (owned, owned_v),
        (cells.at[:, pl.ds(0, SUB)], left_v),
        (cells.at[:, pl.ds(cols - SUB, SUB)], right_v),
    )
    copies = [pltpu.make_async_copy(source, target, sems.at[n]) for n, (source, target) in enumerate(pairs)]
    for copy in copies:
        copy.start()
    for copy in copies:
        copy.wait()
    params_ref[...] = jnp.zeros_like(params_ref)
    for b in range(batches):
        root = jnp.sqrt(precision_v[b, 0]) * owned_v[b, 0].astype(F32)
        corner = stencil_v[b, 0, 0, pl.ds(0, 1)].astype(F32)
        row = jnp.floor((corner + 0.5) * (1.0 / width))
        params_ref[b, pl.ds(0, 4), pl.ds(0, SUB)] = weight_v[b, 0, 0] * root
        params_ref[b, pl.ds(AT_ROW, 1), pl.ds(0, SUB)] = row
        params_ref[b, pl.ds(AT_COL, 1), pl.ds(0, SUB)] = corner - row * width
        params_ref[b, pl.ds(AT_OBS, 1), pl.ds(0, SUB)] = observed_v[b, 0] * root
    left_ref[...] = left_v[:, 0, :]
    right_ref[...] = right_v[:, SUB - 1, :]


def clear_rim(pad, rows, cols):
    edge = jnp.zeros((2, cols + 2 * SUB, LANES), F32)
    pad[pl.ds(0, 2)] = edge
    pad[pl.ds(rows + 2, 2)] = edge
    side = jnp.zeros((rows, SUB, LANES), F32)
    pad[pl.ds(2, rows), pl.ds(0, SUB)] = side
    pad[pl.ds(2, rows), pl.ds(SUB + cols, SUB)] = side


def share(pad, number, rows, cols, da, dc, o):
    row = number(AT_ROW, o).astype(jnp.int32) - 1 + da * rows
    col = number(AT_COL, o).astype(jnp.int32) - 1 + dc * cols
    row = jnp.clip(row, -2, rows) + 2
    col = jnp.clip(col, -2, cols) + SUB
    terms = [number(k, o) * pad[row + k // 2, pl.ds(col + k % 2, 1), :] for k in range(4)]
    return (terms[0] + terms[1]) + (terms[2] + terms[3])


def own_shift(number):
    sub = lax.broadcasted_iota(jnp.int32, (SUB, LANES), 0)
    shift = jnp.zeros((SUB, LANES), F32)
    for o in range(SUB):
        shift = jnp.where(sub == o, number(AT_OBS, o), shift)
    return shift


def pad_kernel(cells, pad, sem):
    rows, cols = (cells.shape[0], cells.shape[1])
    copy = pltpu.make_async_copy(cells, pad.at[pl.ds(2, rows), pl.ds(SUB, cols)], sem)
    copy.start()
    clear_rim(pad, rows, cols)
    copy.wait()


def column_kernel(mine, above, below, left, right, pad, out_ref, block, sides, params, sems):
    rows, cols = (pad.shape[0] - 4, pad.shape[1] - 2 * SUB)
    copies = []
    for n, tile in enumerate((above, mine, below)):
        copies.append(pltpu.make_async_copy(tile.at[0], params.at[n], sems.at[n]))
    for copy in copies:
        copy.start()
    sides[...] = jnp.zeros_like(sides)
    sides[0, pl.ds(SUB, rows), :] = left[...]
    sides[1, pl.ds(SUB, rows), :] = right[...]
    for copy in copies:
        copy.wait()
    for n, da in enumerate(NEAR):
        number = lambda kind, o: params[n, kind, o]
        for o in range(SUB):
            total = share(pad, number, rows, cols, da, 0, o)
            row = number(AT_ROW, o).astype(jnp.int32) - 1 + da * rows
            row = jnp.clip(row, -2, rows) + SUB
            col = number(AT_COL, o).astype(jnp.int32)
            for side, at in enumerate((0, cols)):
                for k in (side, side + 2):
                    weight = jnp.where(col == at, number(k, o), 0.0)
                    total = total + weight * sides[side, pl.ds(row + k // 2, 1), :]
            block[pl.ds(n * SUB + o, 1), :] = total
        if da == 0:
            own = pl.ds(n * SUB, SUB)
            block[own, :] = block[own, :] - own_shift(number)
    block[pl.ds(len(NEAR) * SUB, SUB), :] = mine[1]
    for slot in range(out_ref.shape[0]):
        out_ref[slot] = block[...]


def window_start(lat_count, my_lat):
    return 0 if lat_count <= WIN else jnp.clip(my_lat - REACH, 0, lat_count - WIN)


def tile_sum(shares, lat, lon, lat_count, lon_count):
    total = jnp.zeros((SUB, LANES), F32)
    for n, da in enumerate(NEAR):
        source = lat - da
        part = pl.ds(n * SUB, SUB)
        if isinstance(source, int):
            if 0 <= source < lat_count:
                total = total + shares[source * lon_count + lon, part, :]
        else:
            inside = (source >= 0) & (source < lat_count)
            source = jnp.clip(source, 0, lat_count - 1)
            total = total + jnp.where(inside, shares[source * lon_count + lon, part, :], 0.0)
    return total


def row_of(block, j):
    return jnp.broadcast_to(block[j:j + 1, :], (SUB, LANES))


def reciprocal(value):
    guess = pl.reciprocal(value, approx=True)
    return guess * (2.0 - value * guess)


def eliminate(blocks):
    count = len(blocks) - 1
    blocks = list(blocks)
    sub = lax.broadcasted_iota(jnp.int32, (SUB, LANES), 0)
    lane = lax.broadcasted_iota(jnp.int32, (SUB, LANES), 1)
    inverse = []
    for k in range(count):
        here = (lane >= k * SUB) & (lane < (k + 1) * SUB)
        column = [
            [jnp.broadcast_to(blocks[i][:, k * SUB + j:k * SUB + j + 1], (SUB, LANES)) for j in range(SUB)]
            for i in range(k, count + 1)
        ]
        diag = column[0]
        full = jnp.where(here, jnp.where(lane - k * SUB == sub, 1.0, 0.0), blocks[k])
        lower = full
        scale = jnp.zeros((SUB, LANES), F32)
        for j in range(0, SUB, 2):
            a, b, c = (row_of(diag[j], j), row_of(diag[j + 1], j), row_of(diag[j + 1], j + 1))
            det = a * c - b * b
            over_det = reciprocal(det)
            first = jnp.where(sub == j, -c, jnp.where(sub == j + 1, b, diag[j] * c - diag[j + 1] * b))
            second = jnp.where(sub == j, b, jnp.where(sub == j + 1, -a, diag[j + 1] * a - diag[j] * b))
            first, second = (first * over_det, second * over_det)
            other = (sub != j) & (sub != j + 1)
            for n in range(j + 2, SUB):
                diag[n] = jnp.where(other, diag[n], 0.0) - first * row_of(diag[n], j) - second * row_of(diag[n], j + 1)
            full = jnp.where(other, full, 0.0) - first * row_of(full, j) - second * row_of(full, j + 1)
            over_a = reciprocal(a)
            top, bottom = (row_of(lower, j), row_of(lower, j + 1))
            below = sub > j + 1
            lower = lower - jnp.where(sub == j + 1, b * over_a, jnp.where(below, first, 0.0)) * top
            lower = lower - jnp.where(below, second, 0.0) * bottom
            scale = jnp.where(sub == j, lax.rsqrt(a), jnp.where(sub == j + 1, lax.rsqrt(det * over_a), scale))
        inverse.append(jnp.where(lane < (k + 1) * SUB, lower * scale, 0.0))
        pivot = [row_of(full, j) for j in range(SUB)]
        for i in range(k + 1, count + 1):
            terms = [column[i - k][j] * pivot[j] for j in range(SUB)]
            while len(terms) > 1:
                terms = [terms[n] + terms[n + 1] for n in range(0, len(terms), 2)]
            blocks[i] = jnp.where(here, 0.0, blocks[i]) - terms[0]
    return inverse, blocks[count][:1]


def batch_map(batch, lat_count, lon_count, near_ref, pattern_ref):
    held = min(WIN, lat_count)
    my_lat = lax.axis_index("lat")
    start = window_start(lat_count, my_lat)
    marks, value = ([], [])
    for e in range(lon_count):
        for j in range(held):
            value.append(tile_sum(near_ref, start + j, e, lat_count, lon_count))
            offset = start + j - my_lat + REACH
            inside = (offset >= 0) & (offset < WIN)
            mark = jnp.where(inside, pattern_ref[batch, 0, 0, jnp.clip(offset, 0, WIN - 1), e], 0)
            marks.append(jnp.full((SUB, LANES), mark.astype(F32)))
    marks = jnp.concatenate(marks, axis=0)
    value = jnp.concatenate(value, axis=0)
    mean = jnp.mean(value, axis=-1, keepdims=True)
    scaled = (value - mean).astype(BF16)
    innov = (-mean).astype(BF16).astype(F32)
    weighted = scaled.astype(F32) * marks
    proj = jnp.sum((weighted * innov).reshape(-1, SUB, LANES), axis=0)
    proj = jnp.sum(proj, axis=0, keepdims=True)
    gram = lax.dot_general(
        weighted.astype(BF16), scaled, (((0,), (0,)), ((), ())), preferred_element_type=F32
    )
    sub = lax.broadcasted_iota(jnp.int32, (SUB, LANES), 0)
    lane = lax.broadcasted_iota(jnp.int32, (SUB, LANES), 1)
    members = LANES
    blocks = []
    for k in range(members // SUB):
        block = gram[k * SUB:(k + 1) * SUB, :]
        blocks.append(block + jnp.where(lane - k * SUB == sub, members - 1.0, 0.0))
    blocks.append(jnp.broadcast_to(proj, (SUB, LANES)))
    inverse, weights = eliminate(blocks)
    flipped = jnp.concatenate(inverse, axis=0) * (members - 1.0) ** 0.5 - weights
    return flipped - jnp.mean(flipped, axis=-1, keepdims=True) + 1.0 / members


def exact_dot(a, b, contract_b):
    return lax.dot_general(
        a, b, (((1,), (contract_b,)), ((), ())), precision=lax.Precision.HIGHEST, preferred_element_type=F32
    )


def first_kernel(
    batch, lat_count, lon_count, near_ref, pattern_ref, pad, left_ref, mid_ref, right_ref, map_ref,
    later, params, sems
):
    rows, cols = (pad.shape[0] - 4, pad.shape[1] - 2 * SUB)
    my_lat, my_lon = (lax.axis_index("lat"), lax.axis_index("lon"))
    copies = []
    for n, dc in enumerate(NEAR):
        lon = lax.rem(my_lon + dc + lon_count, lon_count)
        for m, da in enumerate(NEAR):
            lat = jnp.clip(my_lat + da, 0, lat_count - 1)
            block = near_ref.at[lat * lon_count + lon, pl.ds(len(NEAR) * SUB, SUB)]
            copies.append(pltpu.make_async_copy(block, params.at[n, m], sems.at[n, m]))
            copies[-1].start()
    for copy in copies:
        copy.wait()
    for n, dc in enumerate(NEAR):
        for m, da in enumerate(NEAR):
            number = lambda kind, o: params[n, m, kind, o]
            for o in range(SUB):
                at = (n * len(NEAR) + m) * SUB + o
                later[pl.ds(at, 1), :] = share(pad, number, rows, cols, da, dc, o)
    flipped = batch_map(batch, lat_count, lon_count, near_ref, pattern_ref)
    map_ref[...] = flipped
    moved = exact_dot(later[...], flipped, 1)
    size = len(NEAR) * SUB
    left_ref[...] = moved[:size]
    mid_ref[...] = moved[size:2 * size]
    right_ref[...] = moved[2 * size:]
    own = pl.ds(SUB, SUB)
    mid_ref[own, :] = mid_ref[own, :] - own_shift(lambda kind, o: params[1, 1, kind, o])


def meet_kernel(mid, from_left, from_right, out_ref):
    total = mid[...] + from_left[...] + from_right[...]
    out_ref[...] = jnp.broadcast_to(total, out_ref.shape)


def last_kernel(
    batch, lat_count, lon_count, near_ref, pattern_ref, map_ref, cells_ref, out_ref, cells, result, cell_sem, out_sem
):
    parts = out_sem.shape[0]
    rows = cells.shape[0] // parts
    copy = pltpu.make_async_copy(cells_ref, cells, cell_sem)
    copy.start()
    flipped = exact_dot(batch_map(batch, lat_count, lon_count, near_ref, pattern_ref), map_ref[...], 0)
    high = flipped.astype(BF16)
    low = (flipped - high.astype(F32)).astype(BF16)
    right = jnp.concatenate(
        [jnp.concatenate([high, high], axis=1), jnp.concatenate([low, jnp.zeros_like(low)], axis=1)], axis=0
    )
    copy.wait()
    copies = []
    for n in range(parts):
        part = pl.ds(n * rows, rows)
        value = cells[part, :]
        upper = value.astype(BF16)
        rest = (value - upper.astype(F32)).astype(BF16)
        both = lax.dot_general(
            jnp.concatenate([upper, rest], axis=1), right, (((1,), (1,)), ((), ())), preferred_element_type=F32
        )
        result[part, :] = both[:, :LANES] + both[:, LANES:]
        copies.append(pltpu.make_async_copy(result.at[part], out_ref.at[part], out_sem.at[n]))
        copies[-1].start()
    for out_copy in copies:
        out_copy.wait()


def local(ensemble, observed, precision, interp_weight, stencil, owned, pattern):
    rows, cols, members = ensemble.shape
    batches = observed.shape[0]
    lat_count, lon_count = (lax.axis_size("lat"), lax.axis_size("lon"))
    tiles = lat_count * lon_count
    column = len(NEAR) * SUB
    vmem = pl.BlockSpec(memory_space=pltpu.VMEM)
    smem = pl.BlockSpec(memory_space=pltpu.SMEM)
    anywhere = pl.BlockSpec(memory_space=pl.ANY)
    hbm = pl.BlockSpec(memory_space=pltpu.HBM)
    limit = pltpu.CompilerParams(vmem_limit_bytes=48 * 1024 * 1024)
    whole = pltpu.CompilerParams(vmem_limit_bytes=63 * 1024 * 1024)

    def shape(*dims):
        return jax.ShapeDtypeStruct(dims, F32)

    def exchange(slots):
        return lax.all_to_all(slots, ("lat", "lon"), split_axis=0, concat_axis=0, tiled=True)

    def to_next(array, axis, step, count, wraps):
        route = [(i, (i + step) % count) for i in range(count) if wraps or 0 <= i + step < count]
        return lax.ppermute(array, axis, route)

    small = (observed, precision, interp_weight, stencil, owned)
    mine, left, right = pl.pallas_call(
        functools.partial(start_kernel, cols + 2),
        out_shape=(shape(batches, SUB, LANES), shape(rows, members), shape(rows, members)),
        in_specs=[hbm] * 6,
        out_specs=(vmem,) * 3,
        scratch_shapes=[pltpu.VMEM(array.shape, array.dtype) for array in small]
        + [pltpu.VMEM((rows, SUB, members), F32)] * 2
        + [pltpu.SemaphoreType.DMA((7,))],
        compiler_params=whole,
        name="start",
    )(*small, ensemble)
    from_left = to_next(right, "lon", 1, lon_count, True)
    from_right = to_next(left, "lon", -1, lon_count, True)
    above = to_next(mine, "lat", 1, lat_count, False)
    below = to_next(mine, "lat", -1, lat_count, False)
    pad = pl.pallas_call(
        pad_kernel,
        out_shape=shape(rows + 4, cols + 2 * SUB, members),
        in_specs=[hbm],
        out_specs=vmem,
        scratch_shapes=[pltpu.SemaphoreType.DMA],
        compiler_params=limit,
        name="pad",
    )(ensemble)
    shares = pl.pallas_call(
        column_kernel,
        out_shape=shape(tiles, column + SUB, members),
        in_specs=[vmem] * 6,
        out_specs=vmem,
        scratch_shapes=[
            pltpu.VMEM((column + SUB, members), F32),
            pltpu.VMEM((2, rows + 2 * SUB, members), F32),
            pltpu.SMEM((3, SUB, LANES), F32),
            pltpu.SemaphoreType.DMA((3,)),
        ],
        compiler_params=limit,
        name="column_shares",
    )(mine, above, below, from_left, from_right, pad)
    near = exchange(shares)
    part = shape(column, members)
    left, mid, right, first_map = pl.pallas_call(
        functools.partial(first_kernel, 0, lat_count, lon_count),
        out_shape=(part, part, part, shape(members, members)),
        in_specs=[vmem, smem, vmem],
        out_specs=(vmem,) * 4,
        scratch_shapes=[
            pltpu.VMEM((len(NEAR) * column, members), F32),
            pltpu.SMEM((3, 3, SUB, LANES), F32),
            pltpu.SemaphoreType.DMA((3, 3)),
        ],
        compiler_params=limit,
        name="first_batch",
    )(near, pattern, pad)
    from_left = to_next(right, "lon", 1, lon_count, True)
    from_right = to_next(left, "lon", -1, lon_count, True)
    shares = pl.pallas_call(
        meet_kernel,
        out_shape=shape(tiles, column, members),
        in_specs=[vmem] * 3,
        out_specs=vmem,
        compiler_params=limit,
        name="meet",
    )(mid, from_left, from_right)
    near = exchange(shares)
    parts = 8
    result = pl.pallas_call(
        functools.partial(last_kernel, 1, lat_count, lon_count),
        out_shape=shape(rows * cols, members),
        in_specs=[vmem, smem, vmem, anywhere],
        out_specs=anywhere,
        scratch_shapes=[
            pltpu.VMEM((rows * cols, members), F32),
            pltpu.VMEM((rows * cols, members), F32),
            pltpu.SemaphoreType.DMA,
            pltpu.SemaphoreType.DMA((parts,)),
        ],
        compiler_params=limit,
        name="second_batch",
    )(near, pattern, first_map, ensemble.reshape(rows * cols, members))
    return result.reshape(rows, cols, members)


def solution(mesh):
    placed = (
        P("lat", "lon", None),
        P(None, "lat", "lon", None),
        P(None, "lat", "lon", None),
        P(None, "lat", "lon", None, None),
        P(None, "lat", "lon", None, None),
        P(None, "lat", "lon", None),
        P(None, "lat", "lon", None, None),
    )
    return jax.shard_map(
        local, mesh=mesh, in_specs=placed, out_specs=P("lat", "lon", None), check_vma=False
    )
```

```python
import functools
import jax
import jax.numpy as jnp
from jax import lax
from jax.experimental import pallas as pl
from jax.experimental.pallas import tpu as pltpu
from jax.sharding import PartitionSpec as P

REACH = 2
WIN = 2 * REACH + 1
SUB = 8
LANES = 128
NEAR = (-1, 0, 1)
AT_ROW, AT_COL, AT_OBS = (4, 5, 6)
F32 = jnp.float32
BF16 = jnp.bfloat16


def swap(block, axis, kind, count, wraps):
    route = []
    for place in range(count):
        partner = place + (1 if place % 2 == kind else -1)
        if wraps or 0 <= partner < count:
            route.append((place, partner % count))
    return lax.ppermute(block, axis, route)


def is_even(axis):
    return lax.rem(lax.axis_index(axis), 2) == 0


def start_kernel(
    width, observed, precision, weight, stencil, owned, cells, params_ref, sides_0, sides_1,
    observed_v, precision_v, weight_v, stencil_v, owned_v, left_v, right_v, sems
):
    batches, cols = (observed.shape[0], cells.shape[1])
    pairs = (
        (observed, observed_v),
        (precision, precision_v),
        (weight, weight_v),
        (stencil, stencil_v),
        (owned, owned_v),
        (cells.at[:, pl.ds(0, SUB)], left_v),
        (cells.at[:, pl.ds(cols - SUB, SUB)], right_v),
    )
    copies = [pltpu.make_async_copy(source, target, sems.at[n]) for n, (source, target) in enumerate(pairs)]
    for copy in copies:
        copy.start()
    for copy in copies:
        copy.wait()
    params_ref[...] = jnp.zeros_like(params_ref)
    for b in range(batches):
        root = jnp.sqrt(precision_v[b, 0]) * owned_v[b, 0].astype(F32)
        corner = stencil_v[b, 0, 0, pl.ds(0, 1)].astype(F32)
        row = jnp.floor((corner + 0.5) * (1.0 / width))
        params_ref[b, pl.ds(0, 4), pl.ds(0, SUB)] = weight_v[b, 0, 0] * root
        params_ref[b, pl.ds(AT_ROW, 1), pl.ds(0, SUB)] = row
        params_ref[b, pl.ds(AT_COL, 1), pl.ds(0, SUB)] = corner - row * width
        params_ref[b, pl.ds(AT_OBS, 1), pl.ds(0, SUB)] = observed_v[b, 0] * root
    rows = cells.shape[0]
    even = is_even("lon")
    left, right = (left_v[:, 0, :], right_v[:, SUB - 1, :])
    sides_0[pl.ds(0, rows), :] = jnp.where(even, right, left)
    sides_1[pl.ds(0, rows), :] = jnp.where(even, left, right)
    sides_0[pl.ds(rows, SUB), :] = params_ref[1]
    sides_1[pl.ds(rows, SUB), :] = params_ref[1]


def clear_rim(pad, rows, cols):
    edge = jnp.zeros((2, cols + 2 * SUB, LANES), F32)
    pad[pl.ds(0, 2)] = edge
    pad[pl.ds(rows + 2, 2)] = edge
    side = jnp.zeros((rows, SUB, LANES), F32)
    pad[pl.ds(2, rows), pl.ds(0, SUB)] = side
    pad[pl.ds(2, rows), pl.ds(SUB + cols, SUB)] = side


def share(pad, number, rows, cols, da, dc, o):
    row = number(AT_ROW, o).astype(jnp.int32) - 1 + da * rows
    col = number(AT_COL, o).astype(jnp.int32) - 1 + dc * cols
    row = jnp.clip(row, -2, rows) + 2
    col = jnp.clip(col, -2, cols) + SUB
    terms = [number(k, o) * pad[row + k // 2, pl.ds(col + k % 2, 1), :] for k in range(4)]
    return (terms[0] + terms[1]) + (terms[2] + terms[3])


def own_shift(number):
    sub = lax.broadcasted_iota(jnp.int32, (SUB, LANES), 0)
    shift = jnp.zeros((SUB, LANES), F32)
    for o in range(SUB):
        shift = jnp.where(sub == o, number(AT_OBS, o), shift)
    return shift


def pad_kernel(cells, pad, sem):
    rows, cols = (cells.shape[0], cells.shape[1])
    copy = pltpu.make_async_copy(cells, pad.at[pl.ds(2, rows), pl.ds(SUB, cols)], sem)
    copy.start()
    clear_rim(pad, rows, cols)
    copy.wait()


def column_kernel(mine, sides_0, sides_1, ends_0, ends_1, pad, own_ref, out_0, out_1, block, sides, params, sems):
    rows, cols = (pad.shape[0] - 4, pad.shape[1] - 2 * SUB)
    lon_even, lat_even = (is_even("lon"), is_even("lat"))
    copies = []
    for n, source in enumerate((ends_0, mine.at[0], ends_1)):
        copies.append(pltpu.make_async_copy(source, params.at[n], sems.at[n]))
        copies[-1].start()
    sides[...] = jnp.zeros_like(sides)
    left = jnp.where(lon_even, sides_1[...], sides_0[...])
    right = jnp.where(lon_even, sides_0[...], sides_1[...])
    sides[0, pl.ds(SUB, rows), :] = left[:rows]
    sides[1, pl.ds(SUB, rows), :] = right[:rows]
    lane = lax.broadcasted_iota(jnp.int32, (SUB, LANES), 1)
    packed = jnp.where(lane < SUB, left[rows:], pltpu.roll(mine[1], SUB, 1))
    packed = jnp.where(lane < 2 * SUB, packed, pltpu.roll(right[rows:], 2 * SUB, 1))
    out_0[pl.ds(SUB, SUB), :] = packed
    out_1[pl.ds(SUB, SUB), :] = packed
    for copy in copies:
        copy.wait()
    spots = (jnp.where(lat_even, 2, 0), 1, jnp.where(lat_even, 0, 2))
    for n, da in enumerate(NEAR):
        number = lambda kind, o: params[spots[n], kind, o]
        for o in range(SUB):
            total = share(pad, number, rows, cols, da, 0, o)
            row = number(AT_ROW, o).astype(jnp.int32) - 1 + da * rows
            row = jnp.clip(row, -2, rows) + SUB
            col = number(AT_COL, o).astype(jnp.int32)
            for side, at in enumerate((0, cols)):
                for k in (side, side + 2):
                    weight = jnp.where(col == at, number(k, o), 0.0)
                    total = total + weight * sides[side, pl.ds(row + k // 2, 1), :]
            block[n, pl.ds(o, 1), :] = total
    own_ref[...] = block[1] - own_shift(lambda kind, o: params[1, kind, o])
    out_0[pl.ds(0, SUB), :] = jnp.where(lat_even, block[2], block[0])
    out_1[pl.ds(0, SUB), :] = jnp.where(lat_even, block[0], block[2])


def block_kernel(own, ends_0, ends_1, out_ref):
    part = pl.ds(0, SUB)
    value = own[...] + ends_0[part, :] + ends_1[part, :]
    mean = jnp.mean(value, axis=-1, keepdims=True)
    innov = jnp.broadcast_to(-mean, value.shape)
    block = jnp.concatenate([value - mean, innov], axis=0).astype(BF16)
    out_ref[...] = jnp.broadcast_to(block, out_ref.shape)


def later_kernel(mine, sides_0, sides_1, ends_0, ends_1, pad, out_ref, params, sems):
    rows, cols = (pad.shape[0] - 4, pad.shape[1] - 2 * SUB)
    lon_even, lat_even = (is_even("lon"), is_even("lat"))
    side, end = (pl.ds(rows, SUB), pl.ds(SUB, SUB))
    sources = (sides_0.at[side], mine.at[1], sides_1.at[side], ends_0.at[end], ends_1.at[end])
    copies = []
    for n, source in enumerate(sources):
        copies.append(pltpu.make_async_copy(source, params.at[n], sems.at[n]))
        copies[-1].start()
    for copy in copies:
        copy.wait()
    beside = (jnp.where(lon_even, 2, 0), 1, jnp.where(lon_even, 0, 2))
    above = (jnp.where(lat_even, 4, 3), None, jnp.where(lat_even, 3, 4))
    for n, dc in enumerate(NEAR):
        for m, da in enumerate(NEAR):
            if da == 0:
                number = lambda kind, o: params[beside[n], kind, o]
            else:
                number = lambda kind, o: params[above[m], kind, n * SUB + o]
            for o in range(SUB):
                at = (n * len(NEAR) + m) * SUB + o
                out_ref[pl.ds(at, 1), :] = share(pad, number, rows, cols, da, dc, o)
    out_ref[pl.ds(len(NEAR) ** 2 * SUB, SUB), :] = own_shift(lambda kind, o: params[1, kind, o])


def window_start(lat_count, my_lat):
    return 0 if lat_count <= WIN else jnp.clip(my_lat - REACH, 0, lat_count - WIN)


def row_of(block, j):
    return jnp.broadcast_to(block[j:j + 1, :], (SUB, LANES))


def reciprocal(value):
    guess = pl.reciprocal(value, approx=True)
    return guess * (2.0 - value * guess)


def eliminate(blocks):
    count = len(blocks) - 1
    blocks = list(blocks)
    sub = lax.broadcasted_iota(jnp.int32, (SUB, LANES), 0)
    lane = lax.broadcasted_iota(jnp.int32, (SUB, LANES), 1)
    inverse = []
    for k in range(count):
        here = (lane >= k * SUB) & (lane < (k + 1) * SUB)
        column = [
            [jnp.broadcast_to(blocks[i][:, k * SUB + j:k * SUB + j + 1], (SUB, LANES)) for j in range(SUB)]
            for i in range(k, count + 1)
        ]
        diag = column[0]
        full = jnp.where(here, jnp.where(lane - k * SUB == sub, 1.0, 0.0), blocks[k])
        lower = full
        scale = jnp.zeros((SUB, LANES), F32)
        for j in range(0, SUB, 2):
            a, b, c = (row_of(diag[j], j), row_of(diag[j + 1], j), row_of(diag[j + 1], j + 1))
            det = a * c - b * b
            over_det = reciprocal(det)
            first = jnp.where(sub == j, -c, jnp.where(sub == j + 1, b, diag[j] * c - diag[j + 1] * b))
            second = jnp.where(sub == j, b, jnp.where(sub == j + 1, -a, diag[j + 1] * a - diag[j] * b))
            first, second = (first * over_det, second * over_det)
            other = (sub != j) & (sub != j + 1)
            for n in range(j + 2, SUB):
                diag[n] = jnp.where(other, diag[n], 0.0) - first * row_of(diag[n], j) - second * row_of(diag[n], j + 1)
            full = jnp.where(other, full, 0.0) - first * row_of(full, j) - second * row_of(full, j + 1)
            over_a = reciprocal(a)
            top, bottom = (row_of(lower, j), row_of(lower, j + 1))
            below = sub > j + 1
            lower = lower - jnp.where(sub == j + 1, b * over_a, jnp.where(below, first, 0.0)) * top
            lower = lower - jnp.where(below, second, 0.0) * bottom
            scale = jnp.where(sub == j, lax.rsqrt(a), jnp.where(sub == j + 1, lax.rsqrt(det * over_a), scale))
        inverse.append(jnp.where(lane < (k + 1) * SUB, lower * scale, 0.0))
        pivot = [row_of(full, j) for j in range(SUB)]
        for i in range(k + 1, count + 1):
            terms = [column[i - k][j] * pivot[j] for j in range(SUB)]
            while len(terms) > 1:
                terms = [terms[n] + terms[n + 1] for n in range(0, len(terms), 2)]
            blocks[i] = jnp.where(here, 0.0, blocks[i]) - terms[0]
    return inverse, blocks[count][:1]


def batch_map(batch, lat_count, near_ref, pattern_ref):
    lon_count = pattern_ref.shape[-1]
    held = min(WIN, lat_count)
    my_lat = lax.axis_index("lat")
    start = window_start(lat_count, my_lat)
    marks = []
    for j in range(held):
        offset = start + j - my_lat + REACH
        inside = (offset >= 0) & (offset < WIN)
        offset = jnp.clip(offset, 0, WIN - 1)
        for e in range(lon_count):
            mark = jnp.where(inside, pattern_ref[batch, 0, 0, offset, e], 0).astype(F32)
            marks.append(jnp.full((SUB, LANES), mark))
    marks = jnp.concatenate(marks, axis=0)
    near = near_ref[...].astype(F32)
    scaled = near[:, :SUB].reshape(-1, LANES)
    innov = near[:, SUB:].reshape(-1, LANES)
    weighted = scaled * marks
    scaled = scaled.astype(BF16)
    proj = jnp.sum((weighted * innov).reshape(-1, SUB, LANES), axis=0)
    proj = jnp.sum(proj, axis=0, keepdims=True)
    gram = lax.dot_general(
        weighted.astype(BF16), scaled, (((0,), (0,)), ((), ())), preferred_element_type=F32
    )
    sub = lax.broadcasted_iota(jnp.int32, (SUB, LANES), 0)
    lane = lax.broadcasted_iota(jnp.int32, (SUB, LANES), 1)
    members = LANES
    blocks = []
    for k in range(members // SUB):
        block = gram[k * SUB:(k + 1) * SUB, :]
        blocks.append(block + jnp.where(lane - k * SUB == sub, members - 1.0, 0.0))
    blocks.append(jnp.broadcast_to(proj, (SUB, LANES)))
    inverse, weights = eliminate(blocks)
    flipped = jnp.concatenate(inverse, axis=0) * (members - 1.0) ** 0.5 - weights
    return flipped - jnp.mean(flipped, axis=-1, keepdims=True) + 1.0 / members


def exact_dot(a, b, contract_b):
    return lax.dot_general(
        a, b, (((1,), (contract_b,)), ((), ())), precision=lax.Precision.HIGHEST, preferred_element_type=F32
    )


def first_kernel(batch, lat_count, near_ref, pattern_ref, later, mid_ref, out_0, out_1, map_ref):
    flipped = batch_map(batch, lat_count, near_ref, pattern_ref)
    map_ref[...] = flipped
    size = len(NEAR) * SUB
    moved = exact_dot(later[pl.ds(0, len(NEAR) * size), :], flipped, 1)
    left, right = (moved[:size], moved[2 * size:])
    even = is_even("lon")
    out_0[...] = jnp.where(even, right, left)
    out_1[...] = jnp.where(even, left, right)
    mid_ref[...] = moved[size:2 * size]
    own = pl.ds(SUB, SUB)
    mid_ref[own, :] = mid_ref[own, :] - later[pl.ds(len(NEAR) * size, SUB), :]


def meet_kernel(mid, sides_0, sides_1, own_ref, out_0, out_1):
    total = mid[...] + sides_0[...] + sides_1[...]
    above, own_ref[...], below = (total[:SUB], total[SUB:2 * SUB], total[2 * SUB:])
    even = is_even("lat")
    out_0[...] = jnp.where(even, below, above)
    out_1[...] = jnp.where(even, above, below)


def last_kernel(
    batch, lat_count, near_ref, pattern_ref, map_ref, cells_ref, out_ref, cells, result, cell_sem, out_sem
):
    parts = out_sem.shape[0]
    rows = cells.shape[0] // parts
    copy = pltpu.make_async_copy(cells_ref, cells, cell_sem)
    copy.start()
    flipped = exact_dot(batch_map(batch, lat_count, near_ref, pattern_ref), map_ref[...], 0)
    high = flipped.astype(BF16)
    low = (flipped - high.astype(F32)).astype(BF16)
    right = jnp.concatenate(
        [jnp.concatenate([high, high], axis=1), jnp.concatenate([low, jnp.zeros_like(low)], axis=1)], axis=0
    )
    copy.wait()
    copies = []
    for n in range(parts):
        part = pl.ds(n * rows, rows)
        value = cells[part, :]
        upper = value.astype(BF16)
        rest = (value - upper.astype(F32)).astype(BF16)
        both = lax.dot_general(
            jnp.concatenate([upper, rest], axis=1), right, (((1,), (1,)), ((), ())), preferred_element_type=F32
        )
        result[part, :] = both[:, :LANES] + both[:, LANES:]
        copies.append(pltpu.make_async_copy(result.at[part], out_ref.at[part], out_sem.at[n]))
        copies[-1].start()
    for out_copy in copies:
        out_copy.wait()


def window(tiles, lat_count, lon_count):
    held = min(WIN, lat_count)
    if held == lat_count:
        return tiles
    start = jnp.clip(lax.axis_index("lat") - REACH, 0, lat_count - held)
    return lax.dynamic_slice_in_dim(tiles, start * lon_count, held * lon_count, axis=0)


def local(ensemble, observed, precision, interp_weight, stencil, owned, pattern):
    rows, cols, members = ensemble.shape
    batches = observed.shape[0]
    lat_count, lon_count = (lax.axis_size("lat"), lax.axis_size("lon"))
    tiles = lat_count * lon_count
    column = len(NEAR) * SUB
    vmem = pl.BlockSpec(memory_space=pltpu.VMEM)
    smem = pl.BlockSpec(memory_space=pltpu.SMEM)
    anywhere = pl.BlockSpec(memory_space=pl.ANY)
    hbm = pl.BlockSpec(memory_space=pltpu.HBM)
    megabyte = 1024 * 1024

    def shape(*dims, dtype=F32):
        return jax.ShapeDtypeStruct(dims, dtype)

    def call(kernel, name, specs, out_shape, scratch, *operands, out_specs=None, limit=48):
        return pl.pallas_call(
            kernel,
            out_shape=out_shape,
            in_specs=specs,
            out_specs=out_specs or jax.tree.map(lambda _: vmem, out_shape),
            scratch_shapes=scratch,
            compiler_params=pltpu.CompilerParams(vmem_limit_bytes=limit * megabyte),
            name=name,
        )(*operands)

    def trade(blocks, axis):
        count, wraps = ((lon_count, True) if axis == "lon" else (lat_count, False))
        second = swap(blocks[1], axis, 1, count, wraps)
        first = swap(blocks[0], axis, 0, count, wraps)
        return (first, second)

    def gathered(own, ends):
        block = shape(tiles, 2 * SUB, members, dtype=BF16)
        blocks = call(block_kernel, "own_block", [vmem] * 3, block, [], own, *ends)
        blocks = lax.all_to_all(blocks, ("lat", "lon"), split_axis=0, concat_axis=0, tiled=True)
        return window(blocks, lat_count, lon_count)

    small = (observed, precision, interp_weight, stencil, owned)
    side = shape(rows + SUB, members)
    mine, *sides = call(
        functools.partial(start_kernel, cols + 2),
        "start",
        [hbm] * 6,
        (shape(batches, SUB, LANES), side, side),
        [pltpu.VMEM(array.shape, array.dtype) for array in small]
        + [pltpu.VMEM((rows, SUB, members), F32)] * 2
        + [pltpu.SemaphoreType.DMA((7,))],
        *small,
        ensemble,
        limit=63,
    )
    sides = trade(sides, "lon")
    ends = trade((mine[0], mine[0]), "lat")
    padded = shape(rows + 4, cols + 2 * SUB, members)
    pad = call(pad_kernel, "pad", [hbm], padded, [pltpu.SemaphoreType.DMA], ensemble)
    end = shape(2 * SUB, members)
    own, *ends = call(
        column_kernel,
        "column_shares",
        [vmem] * 6,
        (shape(SUB, members), end, end),
        [
            pltpu.VMEM((3, SUB, members), F32),
            pltpu.VMEM((2, rows + 2 * SUB, members), F32),
            pltpu.SMEM((3, SUB, LANES), F32),
            pltpu.SemaphoreType.DMA((3,)),
        ],
        mine,
        *sides,
        *ends,
        pad,
    )
    ends = trade(ends, "lat")
    near = gathered(own, ends)
    later = call(
        later_kernel,
        "later_shares",
        [vmem] * 6,
        shape(len(NEAR) * column + SUB, members),
        [pltpu.SMEM((5, SUB, LANES), F32), pltpu.SemaphoreType.DMA((5,))],
        mine,
        *sides,
        *ends,
        pad,
    )
    part = shape(column, members)
    mid, first, second, first_map = call(
        functools.partial(first_kernel, 0, lat_count),
        "first_batch",
        [vmem, smem, vmem],
        (part, part, part, shape(members, members)),
        [],
        near,
        pattern,
        later,
    )
    sides = trade((first, second), "lon")
    block = shape(SUB, members)
    own, *ends = call(meet_kernel, "meet", [vmem] * 3, (block, block, block), [], mid, *sides)
    near = gathered(own, trade(ends, "lat"))
    parts = 8
    result = call(
        functools.partial(last_kernel, 1, lat_count),
        "second_batch",
        [vmem, smem, vmem, anywhere],
        shape(rows * cols, members),
        [
            pltpu.VMEM((rows * cols, members), F32),
            pltpu.VMEM((rows * cols, members), F32),
            pltpu.SemaphoreType.DMA,
            pltpu.SemaphoreType.DMA((parts,)),
        ],
        near,
        pattern,
        first_map,
        ensemble.reshape(rows * cols, members),
        out_specs=anywhere,
    )
    return result.reshape(rows, cols, members)


def solution(mesh):
    placed = (
        P("lat", "lon", None),
        P(None, "lat", "lon", None),
        P(None, "lat", "lon", None),
        P(None, "lat", "lon", None, None),
        P(None, "lat", "lon", None, None),
        P(None, "lat", "lon", None),
        P(None, "lat", "lon", None, None),
    )
    return jax.shard_map(
        local, mesh=mesh, in_specs=placed, out_specs=P("lat", "lon", None), check_vma=False
    )
```

```python
import functools
import jax
import jax.numpy as jnp
from jax import lax
from jax.experimental import pallas as pl
from jax.experimental.pallas import tpu as pltpu
from jax.sharding import PartitionSpec as P

REACH = 2
WIN = 2 * REACH + 1
SUB = 8
LANES = 128
NEAR = (-1, 0, 1)
AT_ROW, AT_COL, AT_OBS = (4, 5, 6)
MEAN_LANES = 32
F32 = jnp.float32
BF16 = jnp.bfloat16


def swap(block, axis, kind, count, wraps):
    route = []
    for place in range(count):
        partner = place + (1 if place % 2 == kind else -1)
        if wraps or 0 <= partner < count:
            route.append((place, partner % count))
    return lax.ppermute(block, axis, route)


def is_even(axis):
    return lax.rem(lax.axis_index(axis), 2) == 0


def start_kernel(
    width, observed, precision, weight, stencil, owned, pattern, cells, params_ref, marks_ref, sides_0, sides_1,
    observed_v, precision_v, weight_v, stencil_v, owned_v, pattern_v, left_v, right_v, sems
):
    batches, cols = (observed.shape[0], cells.shape[1])
    pairs = (
        (observed, observed_v),
        (precision, precision_v),
        (weight, weight_v),
        (stencil, stencil_v),
        (owned, owned_v),
        (pattern, pattern_v),
        (cells.at[:, pl.ds(0, SUB)], left_v),
        (cells.at[:, pl.ds(cols - SUB, SUB)], right_v),
    )
    copies = [pltpu.make_async_copy(source, target, sems.at[n]) for n, (source, target) in enumerate(pairs)]
    for copy in copies:
        copy.start()
    for copy in copies:
        copy.wait()
    params_ref[...] = jnp.zeros_like(params_ref)
    marks_ref[...] = jnp.zeros_like(marks_ref)
    for b in range(batches):
        marks_ref[b, pl.ds(0, WIN), pl.ds(0, pattern.shape[-1])] = pattern_v[b, :, 0, :].astype(F32)
        root = jnp.sqrt(precision_v[b, 0]) * owned_v[b, 0].astype(F32)
        corner = stencil_v[b, 0, 0, pl.ds(0, 1)].astype(F32)
        row = jnp.floor((corner + 0.5) * (1.0 / width))
        params_ref[b, pl.ds(0, 4), pl.ds(0, SUB)] = weight_v[b, 0, 0] * root
        params_ref[b, pl.ds(AT_ROW, 1), pl.ds(0, SUB)] = row
        params_ref[b, pl.ds(AT_COL, 1), pl.ds(0, SUB)] = corner - row * width
        params_ref[b, pl.ds(AT_OBS, 1), pl.ds(0, SUB)] = observed_v[b, 0] * root
    rows = cells.shape[0]
    even = is_even("lon")
    left, right = (left_v[:, 0, :], right_v[:, SUB - 1, :])
    sides_0[pl.ds(0, rows), :] = jnp.where(even, right, left)
    sides_1[pl.ds(0, rows), :] = jnp.where(even, left, right)
    sides_0[pl.ds(rows, SUB), :] = marks_ref[0]
    sides_1[pl.ds(rows, SUB), :] = marks_ref[0]


def clear_rim(pad, rows, cols):
    edge = jnp.zeros((2, cols + 2 * SUB, LANES), F32)
    pad[pl.ds(0, 2)] = edge
    pad[pl.ds(rows + 2, 2)] = edge
    side = jnp.zeros((rows, SUB, LANES), F32)
    pad[pl.ds(2, rows), pl.ds(0, SUB)] = side
    pad[pl.ds(2, rows), pl.ds(SUB + cols, SUB)] = side


def share(pad, number, rows, cols, da, dc, o):
    row = number(AT_ROW, o).astype(jnp.int32) - 1 + da * rows
    col = number(AT_COL, o).astype(jnp.int32) - 1 + dc * cols
    row = jnp.clip(row, -2, rows) + 2
    col = jnp.clip(col, -2, cols) + SUB
    terms = [number(k, o) * pad[row + k // 2, pl.ds(col + k % 2, 1), :] for k in range(4)]
    return (terms[0] + terms[1]) + (terms[2] + terms[3])


def own_shift(number):
    sub = lax.broadcasted_iota(jnp.int32, (SUB, LANES), 0)
    shift = jnp.zeros((SUB, LANES), F32)
    for o in range(SUB):
        shift = jnp.where(sub == o, number(AT_OBS, o), shift)
    return shift


def pad_kernel(cells, pad, sem):
    rows, cols = (cells.shape[0], cells.shape[1])
    copy = pltpu.make_async_copy(cells, pad.at[pl.ds(2, rows), pl.ds(SUB, cols)], sem)
    copy.start()
    clear_rim(pad, rows, cols)
    copy.wait()


def fetch_params(batch, mine, ends_0, ends_1, params, sems):
    copies = []
    for n, source in enumerate((ends_0, mine, ends_1)):
        copies.append(pltpu.make_async_copy(source.at[batch], params.at[n], sems.at[n]))
        copies[-1].start()
    for copy in copies:
        copy.wait()
    even = is_even("lat")
    above, below = (jnp.where(even, 2, 0), jnp.where(even, 0, 2))
    return [lambda kind, o, spot=spot: params[spot, kind, o] for spot in (above, 1, below)]


def hold_sides(sides_0, sides_1, sides):
    rows = sides_0.shape[0] - SUB
    even = is_even("lon")
    first, second = (sides_0[pl.ds(0, rows), :], sides_1[pl.ds(0, rows), :])
    sides[...] = jnp.zeros_like(sides)
    sides[0, pl.ds(SUB, rows), :] = jnp.where(even, second, first)
    sides[1, pl.ds(SUB, rows), :] = jnp.where(even, first, second)


def side_share(sides, side, number, rows, cols, da, o):
    row = number(AT_ROW, o).astype(jnp.int32) - 1 + da * rows
    row = jnp.clip(row, -2, rows) + SUB
    used = number(AT_COL, o).astype(jnp.int32) == (0, cols)[side]
    terms = [jnp.where(used, number(side + 2 * k, o), 0.0) * sides[side, pl.ds(row + k, 1), :] for k in range(2)]
    return terms[0] + terms[1]


def send_shares(shares, out_ref):
    means = [jnp.mean(part, axis=-1, keepdims=True) for part in shares]
    lane = lax.broadcasted_iota(jnp.int32, (SUB, LANES), 1)
    packed = jnp.where(lane < MEAN_LANES, means[0], jnp.where(lane < 2 * MEAN_LANES, means[1], means[2]))
    rows = [part - mean for part, mean in zip(shares, means)]
    slot = jnp.concatenate(rows + [packed], axis=0).astype(BF16)
    out_ref[...] = jnp.broadcast_to(slot, out_ref.shape)


def column_kernel(mine, sides_0, sides_1, ends_0, ends_1, pad, out_ref, block, sides, params, sems):
    rows, cols = (pad.shape[0] - 4, pad.shape[1] - 2 * SUB)
    hold_sides(sides_0, sides_1, sides)
    numbers = fetch_params(0, mine, ends_0, ends_1, params, sems)
    for n, da in enumerate(NEAR):
        for o in range(SUB):
            total = share(pad, numbers[n], rows, cols, da, 0, o)
            for side in range(2):
                total = total + side_share(sides, side, numbers[n], rows, cols, da, o)
            block[n, pl.ds(o, 1), :] = total
    send_shares([block[0], block[1] - own_shift(numbers[1]), block[2]], out_ref)


def later_kernel(mine, sides_0, sides_1, ends_0, ends_1, pad, out_ref, sides, params, sems):
    rows, cols = (pad.shape[0] - 4, pad.shape[1] - 2 * SUB)
    hold_sides(sides_0, sides_1, sides)
    numbers = fetch_params(1, mine, ends_0, ends_1, params, sems)
    for n, da in enumerate(NEAR):
        for o in range(SUB):
            at = pl.ds(n * SUB + o, 1)
            out_ref[0, at, :] = side_share(sides, 0, numbers[n], rows, cols, da, o)
            out_ref[1, at, :] = share(pad, numbers[n], rows, cols, da, 0, o)
            out_ref[2, at, :] = side_share(sides, 1, numbers[n], rows, cols, da, o)
    out_ref[len(NEAR), pl.ds(0, SUB), :] = own_shift(numbers[1])


def window_start(lat_count, my_lat):
    return 0 if lat_count <= WIN else jnp.clip(my_lat - REACH, 0, lat_count - WIN)


def row_of(block, j):
    return jnp.broadcast_to(block[j:j + 1, :], (SUB, LANES))


def reciprocal(value):
    guess = pl.reciprocal(value, approx=True)
    return guess * (2.0 - value * guess)


def eliminate(systems):
    systems = [list(blocks) for blocks in systems]
    inverses = [[] for _ in systems]
    for k in range(len(systems[0]) - 1):
        for blocks, inverse in zip(systems, inverses):
            inverse.append(eliminate_block(blocks, k))
    return [(inverse, blocks[-1][:1]) for inverse, blocks in zip(inverses, systems)]


def eliminate_block(blocks, k):
    count = len(blocks) - 1
    sub = lax.broadcasted_iota(jnp.int32, (SUB, LANES), 0)
    lane = lax.broadcasted_iota(jnp.int32, (SUB, LANES), 1)
    here = (lane >= k * SUB) & (lane < (k + 1) * SUB)
    column = [
        [jnp.broadcast_to(blocks[i][:, k * SUB + j:k * SUB + j + 1], (SUB, LANES)) for j in range(SUB)]
        for i in range(k, count + 1)
    ]
    diag = list(column[0])
    full = jnp.where(here, jnp.where(lane - k * SUB == sub, 1.0, 0.0), blocks[k])
    lower = full
    scale = jnp.zeros((SUB, LANES), F32)
    for j in range(0, SUB, 2):
        a, b, c = (row_of(diag[j], j), row_of(diag[j + 1], j), row_of(diag[j + 1], j + 1))
        det = a * c - b * b
        over_det = reciprocal(det)
        first = jnp.where(sub == j, -c, jnp.where(sub == j + 1, b, diag[j] * c - diag[j + 1] * b))
        second = jnp.where(sub == j, b, jnp.where(sub == j + 1, -a, diag[j + 1] * a - diag[j] * b))
        first, second = (first * over_det, second * over_det)
        other = (sub != j) & (sub != j + 1)
        for n in range(j + 2, SUB):
            diag[n] = jnp.where(other, diag[n], 0.0) - first * row_of(diag[n], j) - second * row_of(diag[n], j + 1)
        full = jnp.where(other, full, 0.0) - first * row_of(full, j) - second * row_of(full, j + 1)
        over_a = reciprocal(a)
        top, bottom = (row_of(lower, j), row_of(lower, j + 1))
        below = sub > j + 1
        lower = lower - jnp.where(sub == j + 1, b * over_a, jnp.where(below, first, 0.0)) * top
        lower = lower - jnp.where(below, second, 0.0) * bottom
        scale = jnp.where(sub == j, lax.rsqrt(a), jnp.where(sub == j + 1, lax.rsqrt(det * over_a), scale))
    pivot = [row_of(full, j) for j in range(SUB)]
    for i in range(k + 1, count + 1):
        terms = [column[i - k][j] * pivot[j] for j in range(SUB)]
        while len(terms) > 1:
            terms = [terms[n] + terms[n + 1] for n in range(0, len(terms), 2)]
        blocks[i] = jnp.where(here, 0.0, blocks[i]) - terms[0]
    return jnp.where(lane < (k + 1) * SUB, lower * scale, 0.0)


def tile_block(near_ref, lat, lon, lat_count, lon_count):
    lane = lax.broadcasted_iota(jnp.int32, (SUB, LANES), 1)
    scaled, means = (jnp.zeros((SUB, LANES), F32), jnp.zeros((SUB, LANES), F32))
    for n, da in enumerate(NEAR):
        source = lat - da
        inside = True
        if isinstance(source, int):
            if not 0 <= source < lat_count:
                continue
        else:
            inside = (source >= 0) & (source < lat_count)
            source = jnp.clip(source, 0, lat_count - 1)
        slot = near_ref[source * lon_count + lon].astype(F32)
        values, mean = (slot[n * SUB:(n + 1) * SUB], slot[len(NEAR) * SUB:])
        if inside is not True:
            values, mean = (jnp.where(inside, values, 0.0), jnp.where(inside, mean, 0.0))
        scaled = scaled + values
        lanes = (lane >= n * MEAN_LANES) & (lane < (n + 1) * MEAN_LANES)
        means = jnp.where(lanes, mean, means)
    return scaled, jnp.sum(means, axis=-1, keepdims=True) * (-1.0 / MEAN_LANES)


def batch_maps(lat_count, lon_count, near_ref, marks):
    held = min(WIN, lat_count)
    my_lat = lax.axis_index("lat")
    start = window_start(lat_count, my_lat)
    scaled, innov, picked = ([], [], [[] for _ in marks])
    for j in range(held):
        offset = start + j - my_lat + REACH
        inside = (offset >= 0) & (offset < WIN)
        offset = jnp.clip(offset, 0, WIN - 1)
        for e in range(lon_count):
            values, value = tile_block(near_ref, start + j, e, lat_count, lon_count)
            scaled.append(values)
            innov.append(value)
            for pick, mark in zip(picked, marks):
                pick.append(jnp.full((SUB, LANES), jnp.where(inside, mark(offset, e), 0.0)))
    scaled = jnp.concatenate(scaled, axis=0).astype(BF16)
    innov = jnp.concatenate(innov, axis=0).astype(BF16).astype(F32)
    rounded = scaled.astype(F32)
    weighted = [rounded * jnp.concatenate(pick, axis=0) for pick in picked]
    grams = lax.dot_general(
        jnp.concatenate(weighted, axis=1).astype(BF16),
        scaled,
        (((0,), (0,)), ((), ())),
        preferred_element_type=F32,
    )
    sub = lax.broadcasted_iota(jnp.int32, (SUB, LANES), 0)
    lane = lax.broadcasted_iota(jnp.int32, (SUB, LANES), 1)
    members = LANES
    systems = []
    for n, part in enumerate(weighted):
        blocks = []
        for k in range(members // SUB):
            at = n * members + k * SUB
            blocks.append(grams[at:at + SUB, :] + jnp.where(lane - k * SUB == sub, members - 1.0, 0.0))
        proj = jnp.sum((part * innov).reshape(-1, SUB, LANES), axis=0)
        blocks.append(jnp.broadcast_to(jnp.sum(proj, axis=0, keepdims=True), (SUB, LANES)))
        systems.append(blocks)
    maps = []
    for inverse, weights in eliminate(systems):
        flipped = jnp.concatenate(inverse, axis=0) * (members - 1.0) ** 0.5 - weights
        maps.append(flipped - jnp.mean(flipped, axis=-1, keepdims=True) + 1.0 / members)
    return maps


def exact_dot(a, b, contract_b):
    return lax.dot_general(
        a, b, (((1,), (contract_b,)), ((), ())), precision=lax.Precision.HIGHEST, preferred_element_type=F32
    )


def first_kernel(lat_count, lon_count, near_ref, marks_ref, sides_0, sides_1, later, out_ref, map_ref, marks, sems):
    rows = sides_0.shape[0] - SUB
    side = pl.ds(rows, SUB)
    copies = []
    for n, source in enumerate((sides_0.at[side], marks_ref.at[0], sides_1.at[side])):
        copies.append(pltpu.make_async_copy(source, marks.at[n], sems.at[n]))
        copies[-1].start()
    for copy in copies:
        copy.wait()
    even = is_even("lon")
    left, right = (jnp.where(even, 2, 0), jnp.where(even, 0, 2))
    picks = [lambda offset, e, spot=spot: marks[spot, offset, e] for spot in (left, 1, right)]
    maps = batch_maps(lat_count, lon_count, near_ref, picks)
    map_ref[...] = maps[1]
    moved = [exact_dot(later[n], flipped, 1) for n, flipped in enumerate(maps)]
    moved = moved[0] + moved[1] + moved[2]
    shares = [moved[n * SUB:(n + 1) * SUB] for n in range(len(NEAR))]
    shares[1] = shares[1] - later[len(NEAR), pl.ds(0, SUB), :]
    send_shares(shares, out_ref)


def last_kernel(lat_count, lon_count, near_ref, marks_ref, map_ref, pad, out_ref, result, marks, mark_sem, out_sem):
    parts = out_sem.shape[0]
    rows, cols = (pad.shape[0] - 4, pad.shape[1] - 2 * SUB)
    copy = pltpu.make_async_copy(marks_ref.at[1], marks, mark_sem)
    copy.start()
    copy.wait()
    maps = batch_maps(lat_count, lon_count, near_ref, [lambda offset, e: marks[offset, e]])
    flipped = exact_dot(maps[0], map_ref[...], 0)
    high = flipped.astype(BF16)
    low = (flipped - high.astype(F32)).astype(BF16)
    right = jnp.concatenate(
        [jnp.concatenate([high, high], axis=1), jnp.concatenate([low, jnp.zeros_like(low)], axis=1)], axis=0
    )
    copies = []
    size = rows // parts
    for n in range(parts):
        part = pl.ds(n * size * cols, size * cols)
        value = pad[pl.ds(2 + n * size, size), pl.ds(SUB, cols), :].reshape(size * cols, LANES)
        upper = value.astype(BF16)
        rest = (value - upper.astype(F32)).astype(BF16)
        both = lax.dot_general(
            jnp.concatenate([upper, rest], axis=1), right, (((1,), (1,)), ((), ())), preferred_element_type=F32
        )
        result[part, :] = both[:, :LANES] + both[:, LANES:]
        copies.append(pltpu.make_async_copy(result.at[part], out_ref.at[part], out_sem.at[n]))
        copies[-1].start()
    for out_copy in copies:
        out_copy.wait()


def local(ensemble, observed, precision, interp_weight, stencil, owned, pattern):
    rows, cols, members = ensemble.shape
    batches = observed.shape[0]
    lat_count, lon_count = (lax.axis_size("lat"), lax.axis_size("lon"))
    tiles = lat_count * lon_count
    column = len(NEAR) * SUB
    slots = (tiles, column + SUB, members)
    vmem = pl.BlockSpec(memory_space=pltpu.VMEM)
    anywhere = pl.BlockSpec(memory_space=pl.ANY)
    hbm = pl.BlockSpec(memory_space=pltpu.HBM)
    megabyte = 1024 * 1024

    def shape(*dims, dtype=F32):
        return jax.ShapeDtypeStruct(dims, dtype)

    def call(kernel, name, specs, out_shape, scratch, *operands, out_specs=None, limit=48):
        return pl.pallas_call(
            kernel,
            out_shape=out_shape,
            in_specs=specs,
            out_specs=out_specs or jax.tree.map(lambda _: vmem, out_shape),
            scratch_shapes=scratch,
            compiler_params=pltpu.CompilerParams(vmem_limit_bytes=limit * megabyte),
            name=name,
        )(*operands)

    def trade(blocks, axis):
        count, wraps = ((lon_count, True) if axis == "lon" else (lat_count, False))
        second = swap(blocks[1], axis, 1, count, wraps)
        first = swap(blocks[0], axis, 0, count, wraps)
        return (first, second)

    def exchange(blocks):
        return lax.all_to_all(blocks, ("lat", "lon"), split_axis=0, concat_axis=0, tiled=True)

    by_row = pattern.reshape(batches, WIN, 1, lon_count)
    small = (observed, precision, interp_weight, stencil, owned, by_row)
    side = shape(rows + SUB, members)
    block = shape(batches, SUB, LANES)
    mine, marks, *sides = call(
        functools.partial(start_kernel, cols + 2),
        "start",
        [hbm] * 7,
        (block, block, side, side),
        [pltpu.VMEM(array.shape, array.dtype) for array in small]
        + [pltpu.VMEM((rows, SUB, members), F32)] * 2
        + [pltpu.SemaphoreType.DMA((8,))],
        *small,
        ensemble,
        limit=63,
    )
    sides = trade(sides, "lon")
    ends = trade((mine, mine), "lat")
    padded = shape(rows + 4, cols + 2 * SUB, members)
    pad = call(pad_kernel, "pad", [hbm], padded, [pltpu.SemaphoreType.DMA], ensemble)
    near_tiles = (mine, *sides, *ends, pad)
    held_sides = pltpu.VMEM((2, rows + 2 * SUB, members), F32)
    numbers = [pltpu.SMEM((3, SUB, LANES), F32), pltpu.SemaphoreType.DMA((3,))]
    shares = call(
        column_kernel,
        "column_shares",
        [vmem] * 6,
        shape(*slots, dtype=BF16),
        [pltpu.VMEM((3, SUB, members), F32), held_sides] + numbers,
        *near_tiles,
    )
    near = exchange(shares)
    later = call(
        later_kernel, "later_shares", [vmem] * 6, shape(4, column, members), [held_sides] + numbers, *near_tiles
    )
    shares, first_map = call(
        functools.partial(first_kernel, lat_count, lon_count),
        "first_batch",
        [vmem] * 5,
        (shape(*slots, dtype=BF16), shape(members, members)),
        numbers,
        near,
        marks,
        *sides,
        later,
    )
    near = exchange(shares)
    parts = 8
    result = call(
        functools.partial(last_kernel, lat_count, lon_count),
        "second_batch",
        [vmem] * 4,
        shape(rows * cols, members),
        [
            pltpu.VMEM((rows * cols, members), F32),
            pltpu.SMEM((SUB, LANES), F32),
            pltpu.SemaphoreType.DMA,
            pltpu.SemaphoreType.DMA((parts,)),
        ],
        near,
        marks,
        first_map,
        pad,
        out_specs=anywhere,
    )
    return result.reshape(rows, cols, members)


def solution(mesh):
    placed = (
        P("lat", "lon", None),
        P(None, "lat", "lon", None),
        P(None, "lat", "lon", None),
        P(None, "lat", "lon", None, None),
        P(None, "lat", "lon", None, None),
        P(None, "lat", "lon", None),
        P(None, "lat", "lon", None, None),
    )
    return jax.shard_map(
        local, mesh=mesh, in_specs=placed, out_specs=P("lat", "lon", None), check_vma=False
    )
```

```python
import functools
import jax
import jax.numpy as jnp
from jax import lax
from jax.experimental import pallas as pl
from jax.experimental.pallas import tpu as pltpu
from jax.sharding import PartitionSpec as P

REACH = 2
WIN = 2 * REACH + 1
SUB = 8
LANES = 128
NEAR = (-1, 0, 1)
AROUND = tuple((dc, da) for dc in NEAR for da in NEAR)
TRADES = ((0, None), (1, None), (None, 0), (None, 1), (0, 0), (0, 1), (1, 0), (1, 1))
AT_ROW, AT_COL, AT_OBS = (4, 5, 6)
F32 = jnp.float32
BF16 = jnp.bfloat16


def partner(place, kind):
    return place if kind is None else place + (1 if place % 2 == kind else -1)


def trade(blocks, lat_count, lon_count):
    results = []
    for (lat_kind, lon_kind), block in zip(TRADES, blocks):
        route = []
        for lat in range(lat_count):
            for lon in range(lon_count):
                other = partner(lat, lat_kind)
                if 0 <= other < lat_count:
                    target = other * lon_count + partner(lon, lon_kind) % lon_count
                    route.append((lat * lon_count + lon, target))
        results.append(lax.ppermute(block, ("lat", "lon"), route))
    return results


def is_even(axis):
    return lax.rem(lax.axis_index(axis), 2) == 0


def toward(axis, kind):
    if kind is None:
        return 0
    return jnp.where(is_even(axis), 1 - 2 * kind, 2 * kind - 1)


def kind_at(axis, step):
    return jnp.where(is_even(axis), (1 - step) // 2, (1 + step) // 2)


def start_kernel(width, observed, precision, weight, stencil, owned, cells, params_ref, *refs):
    outs, (observed_v, precision_v, weight_v, stencil_v, owned_v, cols_v, rows_v, sems) = (refs[:8], refs[8:])
    batches = observed.shape[0]
    rows, cols = (cells.shape[0], cells.shape[1])
    pairs = (
        (observed, observed_v),
        (precision, precision_v),
        (weight, weight_v),
        (stencil, stencil_v),
        (owned, owned_v),
        (cells.at[:, pl.ds(0, SUB)], cols_v.at[0]),
        (cells.at[:, pl.ds(cols - SUB, SUB)], cols_v.at[1]),
        (cells.at[0], rows_v.at[0]),
        (cells.at[rows - 1], rows_v.at[1]),
    )
    copies = [pltpu.make_async_copy(source, target, sems.at[n]) for n, (source, target) in enumerate(pairs)]
    for copy in copies:
        copy.start()
    for copy in copies:
        copy.wait()
    params_ref[...] = jnp.zeros_like(params_ref)
    for b in range(batches):
        root = jnp.sqrt(precision_v[b, 0]) * owned_v[b, 0].astype(F32)
        corner = stencil_v[b, 0, 0, pl.ds(0, 1)].astype(F32)
        row = jnp.floor((corner + 0.5) * (1.0 / width))
        params_ref[b, pl.ds(0, 4), pl.ds(0, SUB)] = weight_v[b, 0, 0] * root
        params_ref[b, pl.ds(AT_ROW, 1), pl.ds(0, SUB)] = row
        params_ref[b, pl.ds(AT_COL, 1), pl.ds(0, SUB)] = corner - row * width
        params_ref[b, pl.ds(AT_OBS, 1), pl.ds(0, SUB)] = observed_v[b, 0] * root
    lon_even, lat_even = (is_even("lon"), is_even("lat"))
    column = (cols_v[0, :, 0, :], cols_v[1, :, SUB - 1, :])
    edge = (rows_v[0], rows_v[1])
    sides = [jnp.where(lon_even, column[1 - kind], column[kind]) for kind in range(2)]
    ends = [jnp.where(lat_even, edge[1 - kind], edge[kind]) for kind in range(2)]
    for (lat_kind, lon_kind), out in zip(TRADES, outs):
        if lat_kind is None:
            block = sides[lon_kind]
        elif lon_kind is None:
            block = ends[lat_kind]
        else:
            last = jnp.where(lon_even, 1 - lon_kind, lon_kind) == 1
            block = jnp.where(last, ends[lat_kind][cols - 1:], ends[lat_kind][:1])
            block = jnp.broadcast_to(block, (SUB, LANES))
        size = block.shape[0]
        out[pl.ds(0, size), :] = block
        out[pl.ds(size, SUB), :] = params_ref[1]


def clear_rim(pad, rows, cols):
    edge = jnp.zeros((2, cols + 2 * SUB, LANES), F32)
    pad[pl.ds(0, 2)] = edge
    pad[pl.ds(rows + 2, 2)] = edge
    side = jnp.zeros((rows, SUB, LANES), F32)
    pad[pl.ds(2, rows), pl.ds(0, SUB)] = side
    pad[pl.ds(2, rows), pl.ds(SUB + cols, SUB)] = side


def share(pad, number, rows, cols, da, dc, o):
    row = number(AT_ROW, o).astype(jnp.int32) - 1 + da * rows
    col = number(AT_COL, o).astype(jnp.int32) - 1 + dc * cols
    row = jnp.clip(row, -2, rows) + 2
    col = jnp.clip(col, -2, cols) + SUB
    terms = [number(k, o) * pad[row + k // 2, pl.ds(col + k % 2, 1), :] for k in range(4)]
    return (terms[0] + terms[1]) + (terms[2] + terms[3])


def own_shift(number):
    sub = lax.broadcasted_iota(jnp.int32, (SUB, LANES), 0)
    shift = jnp.zeros((SUB, LANES), F32)
    for o in range(SUB):
        shift = jnp.where(sub == o, number(AT_OBS, o), shift)
    return shift


def pad_kernel(cells, pad, sem):
    rows, cols = (cells.shape[0], cells.shape[1])
    copy = pltpu.make_async_copy(cells, pad.at[pl.ds(2, rows), pl.ds(SUB, cols)], sem)
    copy.start()
    clear_rim(pad, rows, cols)
    copy.wait()


def send_block(value, out_ref):
    mean = jnp.mean(value, axis=-1, keepdims=True)
    innov = jnp.broadcast_to(-mean, value.shape)
    block = jnp.concatenate([value - mean, innov], axis=0).astype(BF16)
    out_ref[...] = jnp.broadcast_to(block, out_ref.shape)


def prior_kernel(mine, *refs):
    came, (pad, out_ref, ends, sides, corners, value, params, sem) = (refs[:8], refs[8:])
    rows, cols = (pad.shape[0] - 4, pad.shape[1] - 2 * SUB)
    copy = pltpu.make_async_copy(mine.at[0], params, sem)
    copy.start()
    lon_even, lat_even = (is_even("lon"), is_even("lat"))
    held = dict(zip(TRADES, came))
    first, second = (held[0, None][pl.ds(0, cols), :], held[1, None][pl.ds(0, cols), :])
    ends[0, pl.ds(SUB, cols), :] = jnp.where(lat_even, second, first)
    ends[1, pl.ds(SUB, cols), :] = jnp.where(lat_even, first, second)
    first, second = (held[None, 0][pl.ds(0, rows), :], held[None, 1][pl.ds(0, rows), :])
    sides[...] = jnp.zeros_like(sides)
    sides[0, pl.ds(SUB, rows), :] = jnp.where(lon_even, second, first)
    sides[1, pl.ds(SUB, rows), :] = jnp.where(lon_even, first, second)
    for lat_kind in range(2):
        for lon_kind in range(2):
            corners[2 * lat_kind + lon_kind] = held[lat_kind, lon_kind][pl.ds(0, SUB), :]
    for end, da in enumerate((-1, 1)):
        for side, dc in enumerate((-1, 1)):
            corner = corners[2 * kind_at("lat", da) + kind_at("lon", dc)]
            ends[end, pl.ds(side * (cols + SUB), SUB), :] = corner
    copy.wait()
    number = lambda kind, o: params[kind, o]
    for o in range(SUB):
        total = share(pad, number, rows, cols, 0, 0, o)
        row = number(AT_ROW, o).astype(jnp.int32)
        col = number(AT_COL, o).astype(jnp.int32)
        for n, at in enumerate((0, rows)):
            for k in range(2):
                weight = jnp.where(row == at, number(2 * n + k, o), 0.0)
                total = total + weight * ends[n, pl.ds(col + SUB - 1 + k, 1), :]
        for n, at in enumerate((0, cols)):
            for k in range(2):
                weight = jnp.where(col == at, number(n + 2 * k, o), 0.0)
                total = total + weight * sides[n, pl.ds(row + SUB - 1 + k, 1), :]
        value[pl.ds(o, 1), :] = total
    send_block(value[...] - own_shift(number), out_ref)


def meet_kernel(own, *refs):
    total = own[...]
    for share_ref in refs[:-1]:
        total = total + share_ref[...]
    send_block(total, refs[-1])


def later_kernel(mine, *refs):
    came, (pad, out_ref, params, sems) = (refs[:8], refs[8:])
    rows, cols = (pad.shape[0] - 4, pad.shape[1] - 2 * SUB)
    sources = [block.at[pl.ds(block.shape[0] - SUB, SUB)] for block in came] + [mine.at[1]]
    copies = []
    for n, source in enumerate(sources):
        copies.append(pltpu.make_async_copy(source, params.at[n], sems.at[n]))
        copies[-1].start()
    for copy in copies:
        copy.wait()
    for n, (dc, da) in enumerate(AROUND):
        if da == 0 and dc == 0:
            spot = len(TRADES)
        elif dc == 0:
            spot = TRADES.index((0, None)) + kind_at("lat", da)
        elif da == 0:
            spot = TRADES.index((None, 0)) + kind_at("lon", dc)
        else:
            spot = TRADES.index((0, 0)) + 2 * kind_at("lat", da) + kind_at("lon", dc)
        number = lambda kind, o: params[spot, kind, o]
        for o in range(SUB):
            out_ref[n, pl.ds(o, 1), :] = share(pad, number, rows, cols, da, dc, o)
    out_ref[len(AROUND)] = own_shift(lambda kind, o: params[len(TRADES), kind, o])


def window_start(lat_count, my_lat):
    return 0 if lat_count <= WIN else jnp.clip(my_lat - REACH, 0, lat_count - WIN)


def row_of(block, j):
    return jnp.broadcast_to(block[j:j + 1, :], (SUB, LANES))


def reciprocal(value):
    guess = pl.reciprocal(value, approx=True)
    return guess * (2.0 - value * guess)


def eliminate(blocks):
    count = len(blocks) - 1
    blocks = list(blocks)
    sub = lax.broadcasted_iota(jnp.int32, (SUB, LANES), 0)
    lane = lax.broadcasted_iota(jnp.int32, (SUB, LANES), 1)
    inverse = []
    for k in range(count):
        here = (lane >= k * SUB) & (lane < (k + 1) * SUB)
        column = [
            [jnp.broadcast_to(blocks[i][:, k * SUB + j:k * SUB + j + 1], (SUB, LANES)) for j in range(SUB)]
            for i in range(k, count + 1)
        ]
        diag = column[0]
        full = jnp.where(here, jnp.where(lane - k * SUB == sub, 1.0, 0.0), blocks[k])
        lower = full
        scale = jnp.zeros((SUB, LANES), F32)
        for j in range(0, SUB, 2):
            a, b, c = (row_of(diag[j], j), row_of(diag[j + 1], j), row_of(diag[j + 1], j + 1))
            det = a * c - b * b
            over_det = reciprocal(det)
            first = jnp.where(sub == j, -c, jnp.where(sub == j + 1, b, diag[j] * c - diag[j + 1] * b))
            second = jnp.where(sub == j, b, jnp.where(sub == j + 1, -a, diag[j + 1] * a - diag[j] * b))
            first, second = (first * over_det, second * over_det)
            other = (sub != j) & (sub != j + 1)
            for n in range(j + 2, SUB):
                diag[n] = jnp.where(other, diag[n], 0.0) - first * row_of(diag[n], j) - second * row_of(diag[n], j + 1)
            full = jnp.where(other, full, 0.0) - first * row_of(full, j) - second * row_of(full, j + 1)
            over_a = reciprocal(a)
            top, bottom = (row_of(lower, j), row_of(lower, j + 1))
            below = sub > j + 1
            lower = lower - jnp.where(sub == j + 1, b * over_a, jnp.where(below, first, 0.0)) * top
            lower = lower - jnp.where(below, second, 0.0) * bottom
            scale = jnp.where(sub == j, lax.rsqrt(a), jnp.where(sub == j + 1, lax.rsqrt(det * over_a), scale))
        inverse.append(jnp.where(lane < (k + 1) * SUB, lower * scale, 0.0))
        pivot = [row_of(full, j) for j in range(SUB)]
        for i in range(k + 1, count + 1):
            terms = [column[i - k][j] * pivot[j] for j in range(SUB)]
            while len(terms) > 1:
                terms = [terms[n] + terms[n + 1] for n in range(0, len(terms), 2)]
            blocks[i] = jnp.where(here, 0.0, blocks[i]) - terms[0]
    return inverse, blocks[count][:1]


def batch_map(batch, lat_count, near_ref, pattern_ref):
    lon_count = pattern_ref.shape[-1]
    held = min(WIN, lat_count)
    my_lat = lax.axis_index("lat")
    start = window_start(lat_count, my_lat)
    marks = []
    for j in range(held):
        offset = start + j - my_lat + REACH
        inside = (offset >= 0) & (offset < WIN)
        offset = jnp.clip(offset, 0, WIN - 1)
        for e in range(lon_count):
            mark = jnp.where(inside, pattern_ref[batch, 0, 0, offset, e], 0).astype(F32)
            marks.append(jnp.full((SUB, LANES), mark))
    marks = jnp.concatenate(marks, axis=0)
    near = near_ref[...].astype(F32)
    scaled = near[:, :SUB].reshape(-1, LANES)
    innov = near[:, SUB:].reshape(-1, LANES)
    weighted = scaled * marks
    scaled = scaled.astype(BF16)
    proj = jnp.sum((weighted * innov).reshape(-1, SUB, LANES), axis=0)
    proj = jnp.sum(proj, axis=0, keepdims=True)
    gram = lax.dot_general(
        weighted.astype(BF16), scaled, (((0,), (0,)), ((), ())), preferred_element_type=F32
    )
    sub = lax.broadcasted_iota(jnp.int32, (SUB, LANES), 0)
    lane = lax.broadcasted_iota(jnp.int32, (SUB, LANES), 1)
    members = LANES
    blocks = []
    for k in range(members // SUB):
        block = gram[k * SUB:(k + 1) * SUB, :]
        blocks.append(block + jnp.where(lane - k * SUB == sub, members - 1.0, 0.0))
    blocks.append(jnp.broadcast_to(proj, (SUB, LANES)))
    inverse, weights = eliminate(blocks)
    flipped = jnp.concatenate(inverse, axis=0) * (members - 1.0) ** 0.5 - weights
    return flipped - jnp.mean(flipped, axis=-1, keepdims=True) + 1.0 / members


def exact_dot(a, b, contract_b):
    return lax.dot_general(
        a, b, (((1,), (contract_b,)), ((), ())), precision=lax.Precision.HIGHEST, preferred_element_type=F32
    )


def first_kernel(batch, lat_count, near_ref, pattern_ref, later, map_ref, own_ref, *refs):
    outs, moved = (refs[:-1], refs[-1])
    flipped = batch_map(batch, lat_count, near_ref, pattern_ref)
    map_ref[...] = flipped
    count = len(AROUND)
    moved[...] = exact_dot(later[pl.ds(0, count)].reshape(-1, LANES), flipped, 1).reshape(moved.shape)
    own_ref[...] = moved[AROUND.index((0, 0))] - later[count]
    for (lat_kind, lon_kind), out in zip(TRADES, outs):
        out[...] = moved[(toward("lon", lon_kind) + 1) * len(NEAR) + toward("lat", lat_kind) + 1]


def last_kernel(batch, lat_count, near_ref, pattern_ref, map_ref, pad, out_ref, result, out_sem):
    parts = out_sem.shape[0]
    rows, cols = (pad.shape[0] - 4, pad.shape[1] - 2 * SUB)
    flipped = exact_dot(batch_map(batch, lat_count, near_ref, pattern_ref), map_ref[...], 0)
    high = flipped.astype(BF16)
    low = (flipped - high.astype(F32)).astype(BF16)
    right = jnp.concatenate(
        [jnp.concatenate([high, high], axis=1), jnp.concatenate([low, jnp.zeros_like(low)], axis=1)], axis=0
    )
    copies = []
    size = rows // parts
    for n in range(parts):
        part = pl.ds(n * size * cols, size * cols)
        value = pad[pl.ds(2 + n * size, size), pl.ds(SUB, cols), :].reshape(size * cols, LANES)
        upper = value.astype(BF16)
        rest = (value - upper.astype(F32)).astype(BF16)
        both = lax.dot_general(
            jnp.concatenate([upper, rest], axis=1), right, (((1,), (1,)), ((), ())), preferred_element_type=F32
        )
        result[part, :] = both[:, :LANES] + both[:, LANES:]
        copies.append(pltpu.make_async_copy(result.at[part], out_ref.at[part], out_sem.at[n]))
        copies[-1].start()
    for out_copy in copies:
        out_copy.wait()


def window(tiles, lat_count, lon_count):
    held = min(WIN, lat_count)
    if held == lat_count:
        return tiles
    start = jnp.clip(lax.axis_index("lat") - REACH, 0, lat_count - held)
    return lax.dynamic_slice_in_dim(tiles, start * lon_count, held * lon_count, axis=0)


def local(ensemble, observed, precision, interp_weight, stencil, owned, pattern):
    rows, cols, members = ensemble.shape
    batches = observed.shape[0]
    lat_count, lon_count = (lax.axis_size("lat"), lax.axis_size("lon"))
    tiles = lat_count * lon_count
    vmem = pl.BlockSpec(memory_space=pltpu.VMEM)
    smem = pl.BlockSpec(memory_space=pltpu.SMEM)
    anywhere = pl.BlockSpec(memory_space=pl.ANY)
    hbm = pl.BlockSpec(memory_space=pltpu.HBM)
    megabyte = 1024 * 1024

    def shape(*dims, dtype=F32):
        return jax.ShapeDtypeStruct(dims, dtype)

    def call(kernel, name, specs, out_shape, scratch, *operands, out_specs=None, limit=48):
        return pl.pallas_call(
            kernel,
            out_shape=out_shape,
            in_specs=specs,
            out_specs=out_specs or jax.tree.map(lambda _: vmem, out_shape),
            scratch_shapes=scratch,
            compiler_params=pltpu.CompilerParams(vmem_limit_bytes=limit * megabyte),
            name=name,
        )(*operands)

    def exchange(blocks):
        blocks = lax.all_to_all(blocks, ("lat", "lon"), split_axis=0, concat_axis=0, tiled=True)
        return window(blocks, lat_count, lon_count)

    small = (observed, precision, interp_weight, stencil, owned)
    sizes = [rows if lat is None else cols if lon is None else SUB for lat, lon in TRADES]
    mine, *edges = call(
        functools.partial(start_kernel, cols + 2),
        "start",
        [hbm] * 6,
        (shape(batches, SUB, LANES),) + tuple(shape(size + SUB, members) for size in sizes),
        [pltpu.VMEM(array.shape, array.dtype) for array in small]
        + [pltpu.VMEM((2, rows, SUB, members), F32), pltpu.VMEM((2, cols, members), F32)]
        + [pltpu.SemaphoreType.DMA((9,))],
        *small,
        ensemble,
        limit=63,
    )
    edges = trade(edges, lat_count, lon_count)
    padded = shape(rows + 4, cols + 2 * SUB, members)
    pad = call(pad_kernel, "pad", [hbm], padded, [pltpu.SemaphoreType.DMA], ensemble)
    slots = shape(tiles, 2 * SUB, members, dtype=BF16)
    blocks = call(
        prior_kernel,
        "prior",
        [vmem] * 10,
        slots,
        [
            pltpu.VMEM((2, cols + 2 * SUB, members), F32),
            pltpu.VMEM((2, rows + 2 * SUB, members), F32),
            pltpu.VMEM((4, SUB, members), F32),
            pltpu.VMEM((SUB, members), F32),
            pltpu.SMEM((SUB, LANES), F32),
            pltpu.SemaphoreType.DMA,
        ],
        mine,
        *edges,
        pad,
    )
    near = exchange(blocks)
    count = len(AROUND)
    later = call(
        later_kernel,
        "later_shares",
        [vmem] * 10,
        shape(count + 1, SUB, members),
        [pltpu.SMEM((count, SUB, LANES), F32), pltpu.SemaphoreType.DMA((count,))],
        mine,
        *edges,
        pad,
    )
    block = shape(SUB, members)
    first_map, own, *shares = call(
        functools.partial(first_kernel, 0, lat_count),
        "first_batch",
        [vmem, smem, vmem],
        (shape(members, members),) + (block,) * count,
        [pltpu.VMEM((count, SUB, members), F32)],
        near,
        pattern,
        later,
    )
    shares = trade(shares, lat_count, lon_count)
    blocks = call(meet_kernel, "own_block", [vmem] * count, slots, [], own, *shares)
    near = exchange(blocks)
    parts = 8
    result = call(
        functools.partial(last_kernel, 1, lat_count),
        "second_batch",
        [vmem, smem, vmem, vmem],
        shape(rows * cols, members),
        [pltpu.VMEM((rows * cols, members), F32), pltpu.SemaphoreType.DMA((parts,))],
        near,
        pattern,
        first_map,
        pad,
        out_specs=anywhere,
    )
    return result.reshape(rows, cols, members)


def solution(mesh):
    placed = (
        P("lat", "lon", None),
        P(None, "lat", "lon", None),
        P(None, "lat", "lon", None),
        P(None, "lat", "lon", None, None),
        P(None, "lat", "lon", None, None),
        P(None, "lat", "lon", None),
        P(None, "lat", "lon", None, None),
    )
    return jax.shard_map(
        local, mesh=mesh, in_specs=placed, out_specs=P("lat", "lon", None), check_vma=False
    )
```

```python
import functools
import jax
import jax.numpy as jnp
from jax import lax
from jax.experimental import pallas as pl
from jax.experimental.pallas import tpu as pltpu
from jax.sharding import PartitionSpec as P

REACH = 2
WIN = 2 * REACH + 1
SUB = 8
LANES = 128
NEAR = (-1, 0, 1)
AT_ROW, AT_COL, AT_OBS = (4, 5, 6)
AT_MARK = 64
F32 = jnp.float32
BF16 = jnp.bfloat16


def swap(block, axis, kind, count, wraps):
    route = []
    for place in range(count):
        partner = place + (1 if place % 2 == kind else -1)
        if wraps or 0 <= partner < count:
            route.append((place, partner % count))
    return lax.ppermute(block, axis, route)


def is_even(axis):
    return lax.rem(lax.axis_index(axis), 2) == 0


def start_kernel(
    width, observed, precision, weight, stencil, owned, cells, params_ref, sides_0, sides_1,
    observed_v, precision_v, weight_v, stencil_v, owned_v, left_v, right_v, sems
):
    batches, cols = (observed.shape[0], cells.shape[1])
    pairs = (
        (observed, observed_v),
        (precision, precision_v),
        (weight, weight_v),
        (stencil, stencil_v),
        (owned, owned_v),
        (cells.at[:, pl.ds(0, SUB)], left_v),
        (cells.at[:, pl.ds(cols - SUB, SUB)], right_v),
    )
    copies = [pltpu.make_async_copy(source, target, sems.at[n]) for n, (source, target) in enumerate(pairs)]
    for copy in copies:
        copy.start()
    for copy in copies:
        copy.wait()
    params_ref[...] = jnp.zeros_like(params_ref)
    for b in range(batches):
        root = jnp.sqrt(precision_v[b, 0]) * owned_v[b, 0].astype(F32)
        corner = stencil_v[b, 0, 0, pl.ds(0, 1)].astype(F32)
        row = jnp.floor((corner + 0.5) * (1.0 / width))
        params_ref[b, pl.ds(0, 4), pl.ds(0, SUB)] = weight_v[b, 0, 0] * root
        params_ref[b, pl.ds(AT_ROW, 1), pl.ds(0, SUB)] = row
        params_ref[b, pl.ds(AT_COL, 1), pl.ds(0, SUB)] = corner - row * width
        params_ref[b, pl.ds(AT_OBS, 1), pl.ds(0, SUB)] = observed_v[b, 0] * root
    even = is_even("lon")
    left, right = (left_v[:, 0, :], right_v[:, SUB - 1, :])
    sides_0[...] = jnp.where(even, right, left)
    sides_1[...] = jnp.where(even, left, right)


def clear_rim(pad, rows, cols):
    edge = jnp.zeros((2, cols + 2 * SUB, LANES), F32)
    pad[pl.ds(0, 2)] = edge
    pad[pl.ds(rows + 2, 2)] = edge
    side = jnp.zeros((rows, SUB, LANES), F32)
    pad[pl.ds(2, rows), pl.ds(0, SUB)] = side
    pad[pl.ds(2, rows), pl.ds(SUB + cols, SUB)] = side


def share(pad, number, rows, cols, da, dc, o):
    row = number(AT_ROW, o).astype(jnp.int32) - 1 + da * rows
    col = number(AT_COL, o).astype(jnp.int32) - 1 + dc * cols
    row = jnp.clip(row, -2, rows) + 2
    col = jnp.clip(col, -2, cols) + SUB
    terms = [number(k, o) * pad[row + k // 2, pl.ds(col + k % 2, 1), :] for k in range(4)]
    return (terms[0] + terms[1]) + (terms[2] + terms[3])


def own_shift(number):
    sub = lax.broadcasted_iota(jnp.int32, (SUB, LANES), 0)
    shift = jnp.zeros((SUB, LANES), F32)
    for o in range(SUB):
        shift = jnp.where(sub == o, number(AT_OBS, o), shift)
    return shift


def pad_kernel(cells, pad, sem):
    rows, cols = (cells.shape[0], cells.shape[1])
    copy = pltpu.make_async_copy(cells, pad.at[pl.ds(2, rows), pl.ds(SUB, cols)], sem)
    copy.start()
    clear_rim(pad, rows, cols)
    copy.wait()


def fetch_params(mine, ends_0, ends_1, params, sems):
    last = pl.ds(ends_0.shape[0] - SUB, SUB)
    copies = []
    for n, source in enumerate((ends_0.at[last], mine.at[1], ends_1.at[last])):
        copies.append(pltpu.make_async_copy(source, params.at[n], sems.at[n]))
        copies[-1].start()
    for copy in copies:
        copy.wait()
    even = is_even("lat")
    above, below = (jnp.where(even, 2, 0), jnp.where(even, 0, 2))
    return [lambda kind, o, spot=spot: params[spot, kind, o] for spot in (above, 1, below)]


def hold_sides(sides_0, sides_1, sides):
    rows = sides_0.shape[0]
    even = is_even("lon")
    first, second = (sides_0[...], sides_1[...])
    sides[...] = jnp.zeros_like(sides)
    sides[0, pl.ds(SUB, rows), :] = jnp.where(even, second, first)
    sides[1, pl.ds(SUB, rows), :] = jnp.where(even, first, second)


def side_share(sides, side, number, rows, cols, da, o):
    row = number(AT_ROW, o).astype(jnp.int32) - 1 + da * rows
    row = jnp.clip(row, -2, rows) + SUB
    used = number(AT_COL, o).astype(jnp.int32) == (0, cols)[side]
    terms = [jnp.where(used, number(side + 2 * k, o), 0.0) * sides[side, pl.ds(row + k, 1), :] for k in range(2)]
    return terms[0] + terms[1]


def send_block(value, marks, scratch, out_ref):
    mean = jnp.mean(value, axis=-1, keepdims=True)
    scratch[...] = jnp.zeros_like(scratch)
    scratch[pl.ds(0, marks.shape[0]), pl.ds(0, marks.shape[1])] = marks.astype(F32)
    lane = lax.broadcasted_iota(jnp.int32, (SUB, LANES), 1)
    innov = jnp.where(lane < AT_MARK, -mean, pltpu.roll(scratch[...], AT_MARK, 1))
    block = jnp.concatenate([value - mean, innov], axis=0).astype(BF16)
    out_ref[...] = jnp.broadcast_to(block, out_ref.shape)


def rows_kernel(mine, sides_0, sides_1, pad, out_0, out_1):
    rows, cols = (pad.shape[0] - 4, pad.shape[1] - 2 * SUB)
    lon_even, lat_even = (is_even("lon"), is_even("lat"))
    edges = []
    for row in (0, rows - 1):
        first, second = (sides_0[pl.ds(row, 1), :], sides_1[pl.ds(row, 1), :])
        left, right = (jnp.where(lon_even, second, first), jnp.where(lon_even, first, second))
        cells = pad[2 + row, pl.ds(SUB, cols), :]
        beside = [jnp.broadcast_to(cell, (SUB, LANES)) for cell in (left, right)]
        edges.append(jnp.concatenate([beside[0], cells, beside[1]], axis=0))
    for kind, out in enumerate((out_0, out_1)):
        out[pl.ds(0, cols + 2 * SUB), :] = jnp.where(lat_even, edges[1 - kind], edges[kind])
        out[pl.ds(cols + 2 * SUB, SUB), :] = mine[1]


def prior_kernel(mine, sides_0, sides_1, ends_0, ends_1, pad, pattern, out_ref, ends, sides, value, params, sem):
    rows, cols = (pad.shape[0] - 4, pad.shape[1] - 2 * SUB)
    copy = pltpu.make_async_copy(mine.at[0], params, sem)
    copy.start()
    even = is_even("lat")
    first, second = (ends_0[pl.ds(0, cols + 2 * SUB), :], ends_1[pl.ds(0, cols + 2 * SUB), :])
    ends[0] = jnp.where(even, second, first)
    ends[1] = jnp.where(even, first, second)
    hold_sides(sides_0, sides_1, sides)
    copy.wait()
    number = lambda kind, o: params[kind, o]
    for o in range(SUB):
        total = share(pad, number, rows, cols, 0, 0, o)
        row = number(AT_ROW, o).astype(jnp.int32)
        col = number(AT_COL, o).astype(jnp.int32)
        for n, at in enumerate((0, rows)):
            for k in range(2):
                weight = jnp.where(row == at, number(2 * n + k, o), 0.0)
                total = total + weight * ends[n, pl.ds(col + SUB - 1 + k, 1), :]
        for side in range(2):
            total = total + side_share(sides, side, number, rows, cols, 0, o)
        value[pl.ds(o, 1), :] = total
    send_block(value[...] - own_shift(number), pattern[0, 0, 0], value, out_ref)


def meet_kernel(own, ends_0, ends_1, pattern, out_ref, scratch):
    send_block(own[...] + ends_0[...] + ends_1[...], pattern[1, 0, 0], scratch, out_ref)


def later_kernel(mine, sides_0, sides_1, ends_0, ends_1, pad, out_ref, sides, params, sems):
    rows, cols = (pad.shape[0] - 4, pad.shape[1] - 2 * SUB)
    hold_sides(sides_0, sides_1, sides)
    numbers = fetch_params(mine, ends_0, ends_1, params, sems)
    for n, da in enumerate(NEAR):
        for o in range(SUB):
            at = pl.ds(n * SUB + o, 1)
            out_ref[0, at, :] = side_share(sides, 0, numbers[n], rows, cols, da, o)
            out_ref[1, at, :] = share(pad, numbers[n], rows, cols, da, 0, o)
            out_ref[2, at, :] = side_share(sides, 1, numbers[n], rows, cols, da, o)
    out_ref[len(NEAR), pl.ds(0, SUB), :] = own_shift(numbers[1])


def window_start(lat_count, my_lat):
    return 0 if lat_count <= WIN else jnp.clip(my_lat - REACH, 0, lat_count - WIN)


def row_of(block, j):
    return jnp.broadcast_to(block[:, j:j + 1, :], block.shape)


def column_of(block, j):
    return jnp.broadcast_to(block[:, :, j:j + 1], block.shape)


def reciprocal(value):
    guess = pl.reciprocal(value, approx=True)
    return guess * (2.0 - value * guess)


def eliminate(blocks):
    count = len(blocks) - 1
    blocks = list(blocks)
    shape = blocks[0].shape
    sub = lax.broadcasted_iota(jnp.int32, shape, 1)
    lane = lax.broadcasted_iota(jnp.int32, shape, 2)
    inverse, waiting = ([], [])

    def update(i, k, pivot):
        terms = [column_of(blocks[i], k * SUB + j) * pivot[j] for j in range(SUB)]
        while len(terms) > 1:
            terms = [terms[n] + terms[n + 1] for n in range(0, len(terms), 2)]
        here = (lane >= k * SUB) & (lane < (k + 1) * SUB)
        blocks[i] = jnp.where(here, 0.0, blocks[i]) - terms[0]

    for k in range(count):
        here = (lane >= k * SUB) & (lane < (k + 1) * SUB)
        diag = [column_of(blocks[k], k * SUB + j) for j in range(SUB)]
        full = jnp.where(here, jnp.where(lane - k * SUB == sub, 1.0, 0.0), blocks[k])
        lower = full
        scale = jnp.zeros(shape, F32)
        share_of = -(-len(waiting) // 4)
        for j in range(0, SUB, 2):
            a, b, c = (row_of(diag[j], j), row_of(diag[j + 1], j), row_of(diag[j + 1], j + 1))
            det = a * c - b * b
            over_det = reciprocal(det)
            first = jnp.where(sub == j, -c, jnp.where(sub == j + 1, b, diag[j] * c - diag[j + 1] * b))
            second = jnp.where(sub == j, b, jnp.where(sub == j + 1, -a, diag[j + 1] * a - diag[j] * b))
            first, second = (first * over_det, second * over_det)
            other = (sub != j) & (sub != j + 1)
            for n in range(j + 2, SUB):
                above = first * row_of(diag[n], j) + second * row_of(diag[n], j + 1)
                diag[n] = jnp.where(other, diag[n], 0.0) - above
            above = first * row_of(full, j) + second * row_of(full, j + 1)
            full = jnp.where(other, full, 0.0) - above
            over_a = reciprocal(a)
            below = sub > j + 1
            step = jnp.where(sub == j + 1, b * over_a, jnp.where(below, first, 0.0)) * row_of(lower, j)
            lower = lower - (step + jnp.where(below, second, 0.0) * row_of(lower, j + 1))
            scale = jnp.where(sub == j, lax.rsqrt(a), jnp.where(sub == j + 1, lax.rsqrt(det * over_a), scale))
            for task in waiting[:share_of]:
                update(*task)
            waiting = waiting[share_of:]
        pivot = [row_of(full, j) for j in range(SUB)]
        update(k + 1, k, pivot)
        waiting = [(i, k, pivot) for i in range(k + 2, count + 1)]
        inverse.append(jnp.where(lane < (k + 1) * SUB, lower * scale, 0.0))
    return inverse, blocks[count][:, :1]


def batch_maps(lat_count, near_ref, marks, steps):
    held = min(WIN, lat_count)
    lon_count = near_ref.shape[0] // held
    my_lat = lax.axis_index("lat")
    start = window_start(lat_count, my_lat)
    near = near_ref[...].astype(F32)
    rounded = near[:, :SUB].reshape(-1, LANES)
    innov = near[:, SUB:].reshape(-1, LANES)[:, :1]
    scaled = rounded.astype(BF16)
    weighted = []
    for n, step in enumerate(steps):
        lon = lax.rem(lax.axis_index("lon") + step + lon_count, lon_count)
        marks[n] = near_ref[(my_lat - start) * lon_count + lon, pl.ds(SUB, SUB), :].astype(F32)
        picked = []
        for j in range(held):
            offset = start + j - my_lat + REACH
            inside = (offset >= 0) & (offset < WIN)
            offset = jnp.clip(offset, 0, WIN - 1)
            row = jnp.where(inside, marks[n, pl.ds(offset, 1), :], 0.0)
            for e in range(lon_count):
                picked.append(jnp.broadcast_to(row[:, AT_MARK + e:AT_MARK + e + 1], (SUB, LANES)))
        weighted.append(rounded * jnp.concatenate(picked, axis=0))
    grams = lax.dot_general(
        jnp.concatenate(weighted, axis=1).astype(BF16),
        scaled,
        (((0,), (0,)), ((), ())),
        preferred_element_type=F32,
    )
    members = LANES
    grams = grams.reshape(len(steps), members, LANES)
    shape = (len(steps), SUB, LANES)
    sub = lax.broadcasted_iota(jnp.int32, shape, 1)
    lane = lax.broadcasted_iota(jnp.int32, shape, 2)
    blocks = []
    for k in range(members // SUB):
        block = grams[:, k * SUB:(k + 1) * SUB]
        blocks.append(block + jnp.where(lane - k * SUB == sub, members - 1.0, 0.0))
    projs = []
    for part in weighted:
        proj = jnp.sum((part * innov).reshape(-1, SUB, LANES), axis=0)
        projs.append(jnp.sum(proj, axis=0, keepdims=True)[None])
    blocks.append(jnp.broadcast_to(jnp.concatenate(projs, axis=0), shape))
    inverse, weights = eliminate(blocks)
    flipped = jnp.concatenate(inverse, axis=1) * (members - 1.0) ** 0.5 - weights
    flipped = flipped - jnp.mean(flipped, axis=-1, keepdims=True) + 1.0 / members
    return [flipped[n] for n in range(len(steps))]


def exact_dot(a, b, contract_b):
    return lax.dot_general(
        a, b, (((1,), (contract_b,)), ((), ())), precision=lax.Precision.HIGHEST, preferred_element_type=F32
    )


def first_kernel(lat_count, near_ref, later, map_ref, own_ref, out_0, out_1, marks):
    maps = batch_maps(lat_count, near_ref, marks, NEAR)
    map_ref[...] = maps[1]
    moved = [exact_dot(later[n], flipped, 1) for n, flipped in enumerate(maps)]
    moved = moved[0] + moved[1] + moved[2]
    above, own, below = [moved[n * SUB:(n + 1) * SUB] for n in range(len(NEAR))]
    own_ref[...] = own - later[len(NEAR), pl.ds(0, SUB), :]
    even = is_even("lat")
    out_0[...] = jnp.where(even, below, above)
    out_1[...] = jnp.where(even, above, below)


def last_kernel(lat_count, near_ref, map_ref, pad, out_ref, result, marks, out_sem):
    parts = out_sem.shape[0]
    rows, cols = (pad.shape[0] - 4, pad.shape[1] - 2 * SUB)
    maps = batch_maps(lat_count, near_ref, marks, (0,))
    flipped = exact_dot(maps[0], map_ref[...], 0)
    high = flipped.astype(BF16)
    low = (flipped - high.astype(F32)).astype(BF16)
    right = jnp.concatenate(
        [jnp.concatenate([high, high], axis=1), jnp.concatenate([low, jnp.zeros_like(low)], axis=1)], axis=0
    )
    copies = []
    size = rows // parts
    for n in range(parts):
        part = pl.ds(n * size * cols, size * cols)
        value = pad[pl.ds(2 + n * size, size), pl.ds(SUB, cols), :].reshape(size * cols, LANES)
        upper = value.astype(BF16)
        rest = (value - upper.astype(F32)).astype(BF16)
        both = lax.dot_general(
            jnp.concatenate([upper, rest], axis=1), right, (((1,), (1,)), ((), ())), preferred_element_type=F32
        )
        result[part, :] = both[:, :LANES] + both[:, LANES:]
        copies.append(pltpu.make_async_copy(result.at[part], out_ref.at[part], out_sem.at[n]))
        copies[-1].start()
    for out_copy in copies:
        out_copy.wait()


def window(tiles, lat_count, lon_count):
    held = min(WIN, lat_count)
    if held == lat_count:
        return tiles
    start = jnp.clip(lax.axis_index("lat") - REACH, 0, lat_count - held)
    return lax.dynamic_slice_in_dim(tiles, start * lon_count, held * lon_count, axis=0)


def local(ensemble, observed, precision, interp_weight, stencil, owned, pattern):
    rows, cols, members = ensemble.shape
    batches = observed.shape[0]
    lat_count, lon_count = (lax.axis_size("lat"), lax.axis_size("lon"))
    tiles = lat_count * lon_count
    column = len(NEAR) * SUB
    vmem = pl.BlockSpec(memory_space=pltpu.VMEM)
    anywhere = pl.BlockSpec(memory_space=pl.ANY)
    hbm = pl.BlockSpec(memory_space=pltpu.HBM)
    megabyte = 1024 * 1024

    def shape(*dims, dtype=F32):
        return jax.ShapeDtypeStruct(dims, dtype)

    def call(kernel, name, specs, out_shape, scratch, *operands, out_specs=None, limit=48):
        return pl.pallas_call(
            kernel,
            out_shape=out_shape,
            in_specs=specs,
            out_specs=out_specs or jax.tree.map(lambda _: vmem, out_shape),
            scratch_shapes=scratch,
            compiler_params=pltpu.CompilerParams(vmem_limit_bytes=limit * megabyte),
            name=name,
        )(*operands)

    def trade(blocks, axis):
        count, wraps = ((lon_count, True) if axis == "lon" else (lat_count, False))
        second = swap(blocks[1], axis, 1, count, wraps)
        first = swap(blocks[0], axis, 0, count, wraps)
        return (first, second)

    def exchange(blocks):
        blocks = lax.all_to_all(blocks, ("lat", "lon"), split_axis=0, concat_axis=0, tiled=True)
        return window(blocks, lat_count, lon_count)

    small = (observed, precision, interp_weight, stencil, owned)
    side = shape(rows, members)
    mine, *sides = call(
        functools.partial(start_kernel, cols + 2),
        "start",
        [hbm] * 6,
        (shape(batches, SUB, LANES), side, side),
        [pltpu.VMEM(array.shape, array.dtype) for array in small]
        + [pltpu.VMEM((rows, SUB, members), F32)] * 2
        + [pltpu.SemaphoreType.DMA((7,))],
        *small,
        ensemble,
        limit=63,
    )
    sides = trade(sides, "lon")
    padded = shape(rows + 4, cols + 2 * SUB, members)
    pad = call(pad_kernel, "pad", [hbm], padded, [pltpu.SemaphoreType.DMA], ensemble)
    end = shape(cols + 3 * SUB, members)
    ends = call(rows_kernel, "edge_rows", [vmem] * 4, (end, end), [], mine, *sides, pad)
    ends = trade(ends, "lat")
    around = (mine, *sides, *ends, pad)
    slots = shape(tiles, 2 * SUB, members, dtype=BF16)
    held_sides = pltpu.VMEM((2, rows + 2 * SUB, members), F32)
    numbers = [pltpu.SMEM((3, SUB, LANES), F32), pltpu.SemaphoreType.DMA((3,))]
    blocks = call(
        prior_kernel,
        "prior",
        [vmem] * 7,
        slots,
        [
            pltpu.VMEM((2, cols + 2 * SUB, members), F32),
            held_sides,
            pltpu.VMEM((SUB, members), F32),
            pltpu.SMEM((SUB, LANES), F32),
            pltpu.SemaphoreType.DMA,
        ],
        *around,
        pattern,
    )
    near = exchange(blocks)
    later = call(later_kernel, "later_shares", [vmem] * 6, shape(4, column, members), [held_sides] + numbers, *around)
    share_block = shape(SUB, members)
    first_map, own, *shares = call(
        functools.partial(first_kernel, lat_count),
        "first_batch",
        [vmem] * 2,
        (shape(members, members), share_block, share_block, share_block),
        [pltpu.VMEM((len(NEAR), SUB, LANES), F32)],
        near,
        later,
    )
    shares = trade(shares, "lat")
    scratch = [pltpu.VMEM((SUB, LANES), F32)]
    near = exchange(call(meet_kernel, "own_block", [vmem] * 4, slots, scratch, own, *shares, pattern))
    parts = 8
    result = call(
        functools.partial(last_kernel, lat_count),
        "second_batch",
        [vmem] * 3,
        shape(rows * cols, members),
        [
            pltpu.VMEM((rows * cols, members), F32),
            pltpu.VMEM((1, SUB, LANES), F32),
            pltpu.SemaphoreType.DMA((parts,)),
        ],
        near,
        first_map,
        pad,
        out_specs=anywhere,
    )
    return result.reshape(rows, cols, members)


def solution(mesh):
    placed = (
        P("lat", "lon", None),
        P(None, "lat", "lon", None),
        P(None, "lat", "lon", None),
        P(None, "lat", "lon", None, None),
        P(None, "lat", "lon", None, None),
        P(None, "lat", "lon", None),
        P(None, "lat", "lon", None, None),
    )
    return jax.shard_map(
        local, mesh=mesh, in_specs=placed, out_specs=P("lat", "lon", None), check_vma=False
    )
```

```python
import functools
import jax
import jax.numpy as jnp
from jax import lax
from jax.experimental import pallas as pl
from jax.experimental.pallas import tpu as pltpu
from jax.sharding import PartitionSpec as P

REACH = 2
WIN = 2 * REACH + 1
SUB = 8
LANES = 128
NEAR = (-1, 0, 1)
AT_ROW, AT_COL, AT_OBS = (4, 5, 6)
AT_MARK = 64
F32 = jnp.float32
BF16 = jnp.bfloat16


def swap(block, axis, kind, count, wraps):
    route = []
    for place in range(count):
        partner = place + (1 if place % 2 == kind else -1)
        if wraps or 0 <= partner < count:
            route.append((place, partner % count))
    return lax.ppermute(block, axis, route)


def is_even(axis):
    return lax.rem(lax.axis_index(axis), 2) == 0


def start_kernel(
    width, observed, precision, weight, stencil, owned, cells, params_ref, sides_0, sides_1,
    observed_v, precision_v, weight_v, stencil_v, owned_v, left_v, right_v, sems
):
    batches, cols = (observed.shape[0], cells.shape[1])
    pairs = (
        (observed, observed_v),
        (precision, precision_v),
        (weight, weight_v),
        (stencil, stencil_v),
        (owned, owned_v),
        (cells.at[:, pl.ds(0, SUB)], left_v),
        (cells.at[:, pl.ds(cols - SUB, SUB)], right_v),
    )
    copies = [pltpu.make_async_copy(source, target, sems.at[n]) for n, (source, target) in enumerate(pairs)]
    for copy in copies:
        copy.start()
    for copy in copies:
        copy.wait()
    params_ref[...] = jnp.zeros_like(params_ref)
    for b in range(batches):
        root = jnp.sqrt(precision_v[b, 0]) * owned_v[b, 0].astype(F32)
        corner = stencil_v[b, 0, 0, pl.ds(0, 1)].astype(F32)
        row = jnp.floor((corner + 0.5) * (1.0 / width))
        params_ref[b, pl.ds(0, 4), pl.ds(0, SUB)] = weight_v[b, 0, 0] * root
        params_ref[b, pl.ds(AT_ROW, 1), pl.ds(0, SUB)] = row
        params_ref[b, pl.ds(AT_COL, 1), pl.ds(0, SUB)] = corner - row * width
        params_ref[b, pl.ds(AT_OBS, 1), pl.ds(0, SUB)] = observed_v[b, 0] * root
    even = is_even("lon")
    left, right = (left_v[:, 0, :], right_v[:, SUB - 1, :])
    rows = cells.shape[0]
    sides_0[pl.ds(0, rows), :] = jnp.where(even, right, left)
    sides_1[pl.ds(0, rows), :] = jnp.where(even, left, right)
    sides_0[pl.ds(rows, SUB), :] = params_ref[1]
    sides_1[pl.ds(rows, SUB), :] = params_ref[1]


def clear_rim(pad, rows, cols):
    edge = jnp.zeros((2, cols + 2 * SUB, LANES), F32)
    pad[pl.ds(0, 2)] = edge
    pad[pl.ds(rows + 2, 2)] = edge
    side = jnp.zeros((rows, SUB, LANES), F32)
    pad[pl.ds(2, rows), pl.ds(0, SUB)] = side
    pad[pl.ds(2, rows), pl.ds(SUB + cols, SUB)] = side


def share(pad, number, rows, cols, da, dc, o):
    row = number(AT_ROW, o).astype(jnp.int32) - 1 + da * rows
    col = number(AT_COL, o).astype(jnp.int32) - 1 + dc * cols
    row = jnp.clip(row, -2, rows) + 2
    col = jnp.clip(col, -2, cols) + SUB
    terms = [number(k, o) * pad[row + k // 2, pl.ds(col + k % 2, 1), :] for k in range(4)]
    return (terms[0] + terms[1]) + (terms[2] + terms[3])


def own_shift(number):
    sub = lax.broadcasted_iota(jnp.int32, (SUB, LANES), 0)
    shift = jnp.zeros((SUB, LANES), F32)
    for o in range(SUB):
        shift = jnp.where(sub == o, number(AT_OBS, o), shift)
    return shift


def pad_kernel(cells, pad, sem):
    rows, cols = (cells.shape[0], cells.shape[1])
    copy = pltpu.make_async_copy(cells, pad.at[pl.ds(2, rows), pl.ds(SUB, cols)], sem)
    copy.start()
    clear_rim(pad, rows, cols)
    copy.wait()


def hold_sides(sides_0, sides_1, sides):
    rows = sides_0.shape[0] - SUB
    even = is_even("lon")
    first, second = (sides_0[pl.ds(0, rows), :], sides_1[pl.ds(0, rows), :])
    sides[...] = jnp.zeros_like(sides)
    sides[0, pl.ds(SUB, rows), :] = jnp.where(even, second, first)
    sides[1, pl.ds(SUB, rows), :] = jnp.where(even, first, second)


def side_share(sides, side, number, rows, cols, da, o):
    row = number(AT_ROW, o).astype(jnp.int32) - 1 + da * rows
    row = jnp.clip(row, -2, rows) + SUB
    used = number(AT_COL, o).astype(jnp.int32) == (0, cols)[side]
    terms = [jnp.where(used, number(side + 2 * k, o), 0.0) * sides[side, pl.ds(row + k, 1), :] for k in range(2)]
    return terms[0] + terms[1]


def send_block(value, marks, scratch, out_ref):
    mean = jnp.mean(value, axis=-1, keepdims=True)
    scratch[...] = jnp.zeros_like(scratch)
    scratch[pl.ds(0, marks.shape[0]), pl.ds(0, marks.shape[1])] = marks.astype(F32)
    lane = lax.broadcasted_iota(jnp.int32, (SUB, LANES), 1)
    innov = jnp.where(lane < AT_MARK, -mean, pltpu.roll(scratch[...], AT_MARK, 1))
    block = jnp.concatenate([value - mean, innov], axis=0).astype(BF16)
    out_ref[...] = jnp.broadcast_to(block, out_ref.shape)


def rows_kernel(mine, sides_0, sides_1, pad, out_0, out_1):
    rows, cols = (pad.shape[0] - 4, pad.shape[1] - 2 * SUB)
    lon_even, lat_even = (is_even("lon"), is_even("lat"))
    edges = []
    for row in (0, rows - 1):
        first, second = (sides_0[pl.ds(row, 1), :], sides_1[pl.ds(row, 1), :])
        left, right = (jnp.where(lon_even, second, first), jnp.where(lon_even, first, second))
        cells = pad[2 + row, pl.ds(SUB, cols), :]
        beside = [jnp.broadcast_to(cell, (SUB, LANES)) for cell in (left, right)]
        edges.append(jnp.concatenate([beside[0], cells, beside[1]], axis=0))
    first, second = (sides_0[pl.ds(rows, SUB), :], sides_1[pl.ds(rows, SUB), :])
    left, right = (jnp.where(lon_even, second, first), jnp.where(lon_even, first, second))
    lane = lax.broadcasted_iota(jnp.int32, (SUB, LANES), 1)
    packed = jnp.where(lane < SUB, left, pltpu.roll(mine[1], SUB, 1))
    packed = jnp.where(lane < 2 * SUB, packed, pltpu.roll(right, 2 * SUB, 1))
    for kind, out in enumerate((out_0, out_1)):
        out[pl.ds(0, cols + 2 * SUB), :] = jnp.where(lat_even, edges[1 - kind], edges[kind])
        out[pl.ds(cols + 2 * SUB, SUB), :] = packed


def prior_kernel(mine, sides_0, sides_1, ends_0, ends_1, pad, pattern, out_ref, ends, sides, value, params, sem):
    rows, cols = (pad.shape[0] - 4, pad.shape[1] - 2 * SUB)
    copy = pltpu.make_async_copy(mine.at[0], params, sem)
    copy.start()
    even = is_even("lat")
    first, second = (ends_0[pl.ds(0, cols + 2 * SUB), :], ends_1[pl.ds(0, cols + 2 * SUB), :])
    ends[0] = jnp.where(even, second, first)
    ends[1] = jnp.where(even, first, second)
    hold_sides(sides_0, sides_1, sides)
    copy.wait()
    number = lambda kind, o: params[kind, o]
    for o in range(SUB):
        total = share(pad, number, rows, cols, 0, 0, o)
        row = number(AT_ROW, o).astype(jnp.int32)
        col = number(AT_COL, o).astype(jnp.int32)
        for n, at in enumerate((0, rows)):
            for k in range(2):
                weight = jnp.where(row == at, number(2 * n + k, o), 0.0)
                total = total + weight * ends[n, pl.ds(col + SUB - 1 + k, 1), :]
        for side in range(2):
            total = total + side_share(sides, side, number, rows, cols, 0, o)
        value[pl.ds(o, 1), :] = total
    send_block(value[...] - own_shift(number), pattern[0, 0, 0], value, out_ref)


def meet_kernel(shares, pattern, out_ref, scratch):
    send_block(jnp.sum(shares[...], axis=0), pattern[1, 0, 0], scratch, out_ref)


def later_kernel(mine, sides_0, sides_1, ends_0, ends_1, pad, out_ref, params, sems):
    rows, cols = (pad.shape[0] - 4, pad.shape[1] - 2 * SUB)
    lon_even, lat_even = (is_even("lon"), is_even("lat"))
    side, end = (pl.ds(rows, SUB), pl.ds(cols + 2 * SUB, SUB))
    sources = (sides_0.at[side], mine.at[1], sides_1.at[side], ends_0.at[end], ends_1.at[end])
    copies = []
    for n, source in enumerate(sources):
        copies.append(pltpu.make_async_copy(source, params.at[n], sems.at[n]))
        copies[-1].start()
    for copy in copies:
        copy.wait()
    beside = (jnp.where(lon_even, 2, 0), 1, jnp.where(lon_even, 0, 2))
    above = (jnp.where(lat_even, 4, 3), None, jnp.where(lat_even, 3, 4))
    for n, dc in enumerate(NEAR):
        for m, da in enumerate(NEAR):
            if da == 0:
                number = lambda kind, o: params[beside[n], kind, o]
            else:
                number = lambda kind, o: params[above[m], kind, n * SUB + o]
            for o in range(SUB):
                out_ref[n * len(NEAR) + m, pl.ds(o, 1), :] = share(pad, number, rows, cols, da, dc, o)
    out_ref[len(NEAR) ** 2] = own_shift(lambda kind, o: params[1, kind, o])


def window_start(lat_count, my_lat):
    return 0 if lat_count <= WIN else jnp.clip(my_lat - REACH, 0, lat_count - WIN)


def row_of(block, j):
    return jnp.broadcast_to(block[j:j + 1, :], block.shape)


def column_of(block, j):
    return jnp.broadcast_to(block[:, j:j + 1], block.shape)


def reciprocal(value):
    guess = pl.reciprocal(value, approx=True)
    return guess * (2.0 - value * guess)


def pivot_rows(block, k, between):
    sub = lax.broadcasted_iota(jnp.int32, block.shape, 0)
    lane = lax.broadcasted_iota(jnp.int32, block.shape, 1) - k * SUB
    rows = [row_of(block, r) for r in range(SUB)]
    at = {(r, n): column_of(rows[r], k * SUB + n) for r in range(SUB) for n in range(r + 1)}
    here = (lane >= 0) & (lane < SUB)
    rows = [jnp.where(here, jnp.where(lane == r, 1.0, 0.0), row) for r, row in enumerate(rows)]
    inverse = jnp.zeros(block.shape, F32)
    for j in range(0, SUB, 2):
        a, b, c = (at[j, j], at[j + 1, j], at[j + 1, j + 1])
        det = a * c - b * b
        over_det = reciprocal(det)
        top, bottom = (rows[j], rows[j + 1])
        rest = range(j + 2, SUB)
        upper = {n: (at[n, j], at[n, j + 1]) for n in rest}
        for r in rest:
            first = (at[r, j] * c - at[r, j + 1] * b) * over_det
            second = (at[r, j + 1] * a - at[r, j] * b) * over_det
            for n in range(j + 2, r + 1):
                at[r, n] = at[r, n] - (first * upper[n][0] + second * upper[n][1])
            rows[r] = rows[r] - (first * top + second * bottom)
        a_part, b_part, c_part = (a * over_det, b * over_det, c * over_det)
        for r in range(j):
            first = at[r, j] * c_part - at[r, j + 1] * b_part
            second = at[r, j + 1] * a_part - at[r, j] * b_part
            for n in rest:
                at[r, n] = at[r, n] - (first * upper[n][0] + second * upper[n][1])
            rows[r] = rows[r] - (first * top + second * bottom)
        for n in rest:
            at[j, n] = c_part * upper[n][0] - b_part * upper[n][1]
            at[j + 1, n] = a_part * upper[n][1] - b_part * upper[n][0]
        rows[j] = c_part * top - b_part * bottom
        rows[j + 1] = a_part * bottom - b_part * top
        over_a = reciprocal(a)
        inverse = jnp.where(sub == j, lax.rsqrt(a) * top, inverse)
        inverse = jnp.where(sub == j + 1, lax.rsqrt(det * over_a) * (bottom - b * over_a * top), inverse)
        between()
    return rows, jnp.where(lane < SUB, inverse, 0.0)


def eliminate(blocks):
    count = len(blocks) - 1
    blocks = list(blocks)
    lane = lax.broadcasted_iota(jnp.int32, blocks[0].shape, 1)
    inverse, waiting = ([], [])

    def update(i, k, pivot):
        terms = [column_of(blocks[i], k * SUB + j) * pivot[j] for j in range(SUB)]
        while len(terms) > 1:
            terms = [terms[n] + terms[n + 1] for n in range(0, len(terms), 2)]
        here = (lane >= k * SUB) & (lane < (k + 1) * SUB)
        blocks[i] = jnp.where(here, 0.0, blocks[i]) - terms[0]

    for k in range(count):
        share_of = -(-len(waiting) // 4)

        def between():
            for task in waiting[:share_of]:
                update(*task)
            del waiting[:share_of]

        pivot, rows = pivot_rows(blocks[k], k, between)
        update(k + 1, k, pivot)
        waiting = [(i, k, pivot) for i in range(k + 2, count + 1)]
        inverse.append(rows)
    return inverse, blocks[count][:1]


def batch_map(lat_count, near_ref, marks):
    held = min(WIN, lat_count)
    lon_count = near_ref.shape[0] // held
    my_lat, my_lon = (lax.axis_index("lat"), lax.axis_index("lon"))
    start = window_start(lat_count, my_lat)
    near = near_ref[...].astype(F32)
    rounded = near[:, :SUB].reshape(-1, LANES)
    innov = near[:, SUB:].reshape(-1, LANES)[:, :1]
    scaled = rounded.astype(BF16)
    marks[...] = near_ref[(my_lat - start) * lon_count + my_lon, pl.ds(SUB, SUB), :].astype(F32)
    picked = []
    for j in range(held):
        offset = start + j - my_lat + REACH
        inside = (offset >= 0) & (offset < WIN)
        row = jnp.where(inside, marks[pl.ds(jnp.clip(offset, 0, WIN - 1), 1), :], 0.0)
        for e in range(lon_count):
            picked.append(jnp.broadcast_to(row[:, AT_MARK + e:AT_MARK + e + 1], (SUB, LANES)))
    weighted = rounded * jnp.concatenate(picked, axis=0)
    gram = lax.dot_general(
        weighted.astype(BF16), scaled, (((0,), (0,)), ((), ())), preferred_element_type=F32
    )
    sub = lax.broadcasted_iota(jnp.int32, (SUB, LANES), 0)
    lane = lax.broadcasted_iota(jnp.int32, (SUB, LANES), 1)
    members = LANES
    blocks = []
    for k in range(members // SUB):
        block = gram[k * SUB:(k + 1) * SUB, :]
        blocks.append(block + jnp.where(lane - k * SUB == sub, members - 1.0, 0.0))
    proj = jnp.sum((weighted * innov).reshape(-1, SUB, LANES), axis=0)
    blocks.append(jnp.broadcast_to(jnp.sum(proj, axis=0, keepdims=True), (SUB, LANES)))
    inverse, weights = eliminate(blocks)
    flipped = jnp.concatenate(inverse, axis=0) * (members - 1.0) ** 0.5 - weights
    return flipped - jnp.mean(flipped, axis=-1, keepdims=True) + 1.0 / members


def exact_dot(a, b, contract_b):
    return lax.dot_general(
        a, b, (((1,), (contract_b,)), ((), ())), precision=lax.Precision.HIGHEST, preferred_element_type=F32
    )


def first_kernel(lat_count, lon_count, near_ref, later, map_ref, out_ref, marks, moved):
    flipped = batch_map(lat_count, near_ref, marks)
    map_ref[...] = flipped
    count = len(NEAR) ** 2
    moved[...] = exact_dot(later[pl.ds(0, count)].reshape(-1, LANES), flipped, 1).reshape(moved.shape)
    moved[count // 2] = moved[count // 2] - later[count]
    out_ref[...] = jnp.zeros_like(out_ref)
    my_lat, my_lon = (lax.axis_index("lat"), lax.axis_index("lon"))
    for n, dc in enumerate(NEAR):
        lon = lax.rem(my_lon + dc + lon_count, lon_count)
        for m, da in enumerate(NEAR):
            lat = my_lat + da

            @pl.when((lat >= 0) & (lat < lat_count))
            def _():
                out_ref[lat * lon_count + lon] = moved[n * len(NEAR) + m]


def last_kernel(lat_count, near_ref, map_ref, pad, out_ref, result, marks, out_sem):
    parts = out_sem.shape[0]
    rows, cols = (pad.shape[0] - 4, pad.shape[1] - 2 * SUB)
    flipped = exact_dot(batch_map(lat_count, near_ref, marks), map_ref[...], 0)
    high = flipped.astype(BF16)
    low = (flipped - high.astype(F32)).astype(BF16)
    right = jnp.concatenate(
        [jnp.concatenate([high, high], axis=1), jnp.concatenate([low, jnp.zeros_like(low)], axis=1)], axis=0
    )
    copies = []
    size = rows // parts
    for n in range(parts):
        part = pl.ds(n * size * cols, size * cols)
        value = pad[pl.ds(2 + n * size, size), pl.ds(SUB, cols), :].reshape(size * cols, LANES)
        upper = value.astype(BF16)
        rest = (value - upper.astype(F32)).astype(BF16)
        both = lax.dot_general(
            jnp.concatenate([upper, rest], axis=1), right, (((1,), (1,)), ((), ())), preferred_element_type=F32
        )
        result[part, :] = both[:, :LANES] + both[:, LANES:]
        copies.append(pltpu.make_async_copy(result.at[part], out_ref.at[part], out_sem.at[n]))
        copies[-1].start()
    for out_copy in copies:
        out_copy.wait()


def window(tiles, lat_count, lon_count):
    held = min(WIN, lat_count)
    if held == lat_count:
        return tiles
    start = jnp.clip(lax.axis_index("lat") - REACH, 0, lat_count - held)
    return lax.dynamic_slice_in_dim(tiles, start * lon_count, held * lon_count, axis=0)


def local(ensemble, observed, precision, interp_weight, stencil, owned, pattern):
    rows, cols, members = ensemble.shape
    batches = observed.shape[0]
    lat_count, lon_count = (lax.axis_size("lat"), lax.axis_size("lon"))
    tiles = lat_count * lon_count
    vmem = pl.BlockSpec(memory_space=pltpu.VMEM)
    anywhere = pl.BlockSpec(memory_space=pl.ANY)
    hbm = pl.BlockSpec(memory_space=pltpu.HBM)
    megabyte = 1024 * 1024

    def shape(*dims, dtype=F32):
        return jax.ShapeDtypeStruct(dims, dtype)

    def call(kernel, name, specs, out_shape, scratch, *operands, out_specs=None, limit=48):
        return pl.pallas_call(
            kernel,
            out_shape=out_shape,
            in_specs=specs,
            out_specs=out_specs or jax.tree.map(lambda _: vmem, out_shape),
            scratch_shapes=scratch,
            compiler_params=pltpu.CompilerParams(vmem_limit_bytes=limit * megabyte),
            name=name,
        )(*operands)

    def trade(blocks, axis):
        count, wraps = ((lon_count, True) if axis == "lon" else (lat_count, False))
        second = swap(blocks[1], axis, 1, count, wraps)
        first = swap(blocks[0], axis, 0, count, wraps)
        return (first, second)

    def exchange(blocks):
        return lax.all_to_all(blocks, ("lat", "lon"), split_axis=0, concat_axis=0, tiled=True)

    small = (observed, precision, interp_weight, stencil, owned)
    side = shape(rows + SUB, members)
    mine, *sides = call(
        functools.partial(start_kernel, cols + 2),
        "start",
        [hbm] * 6,
        (shape(batches, SUB, LANES), side, side),
        [pltpu.VMEM(array.shape, array.dtype) for array in small]
        + [pltpu.VMEM((rows, SUB, members), F32)] * 2
        + [pltpu.SemaphoreType.DMA((7,))],
        *small,
        ensemble,
        limit=63,
    )
    sides = trade(sides, "lon")
    padded = shape(rows + 4, cols + 2 * SUB, members)
    pad = call(pad_kernel, "pad", [hbm], padded, [pltpu.SemaphoreType.DMA], ensemble)
    end = shape(cols + 3 * SUB, members)
    ends = call(rows_kernel, "edge_rows", [vmem] * 4, (end, end), [], mine, *sides, pad)
    ends = trade(ends, "lat")
    around = (mine, *sides, *ends, pad)
    slots = shape(tiles, 2 * SUB, members, dtype=BF16)
    held_sides = pltpu.VMEM((2, rows + 2 * SUB, members), F32)
    blocks = call(
        prior_kernel,
        "prior",
        [vmem] * 7,
        slots,
        [
            pltpu.VMEM((2, cols + 2 * SUB, members), F32),
            held_sides,
            pltpu.VMEM((SUB, members), F32),
            pltpu.SMEM((SUB, LANES), F32),
            pltpu.SemaphoreType.DMA,
        ],
        *around,
        pattern,
    )
    near = window(exchange(blocks), lat_count, lon_count)
    count = len(NEAR) ** 2
    later = call(
        later_kernel,
        "later_shares",
        [vmem] * 6,
        shape(count + 1, SUB, members),
        [pltpu.SMEM((5, SUB, LANES), F32), pltpu.SemaphoreType.DMA((5,))],
        *around,
    )
    block = pltpu.VMEM((SUB, members), F32)
    first_map, shares = call(
        functools.partial(first_kernel, lat_count, lon_count),
        "first_batch",
        [vmem] * 2,
        (shape(members, members), shape(tiles, SUB, members)),
        [block, pltpu.VMEM((count, SUB, members), F32)],
        near,
        later,
    )
    blocks = call(meet_kernel, "own_block", [vmem] * 2, slots, [block], exchange(shares), pattern)
    near = window(exchange(blocks), lat_count, lon_count)
    parts = 8
    result = call(
        functools.partial(last_kernel, lat_count),
        "second_batch",
        [vmem] * 3,
        shape(rows * cols, members),
        [
            pltpu.VMEM((rows * cols, members), F32),
            block,
            pltpu.SemaphoreType.DMA((parts,)),
        ],
        near,
        first_map,
        pad,
        out_specs=anywhere,
    )
    return result.reshape(rows, cols, members)


def solution(mesh):
    placed = (
        P("lat", "lon", None),
        P(None, "lat", "lon", None),
        P(None, "lat", "lon", None),
        P(None, "lat", "lon", None, None),
        P(None, "lat", "lon", None, None),
        P(None, "lat", "lon", None),
        P(None, "lat", "lon", None, None),
    )
    return jax.shard_map(
        local, mesh=mesh, in_specs=placed, out_specs=P("lat", "lon", None), check_vma=False
    )
```

```python
import functools
import jax
import jax.numpy as jnp
from jax import lax
from jax.experimental import pallas as pl
from jax.experimental.pallas import tpu as pltpu
from jax.sharding import PartitionSpec as P

REACH = 2
WIN = 2 * REACH + 1
SUB = 8
LANES = 128
NEAR = (-1, 0, 1)
AT_ROW, AT_COL, AT_OBS = (4, 5, 6)
PAIRS = SUB // 2 + 1
F32 = jnp.float32
BF16 = jnp.bfloat16


def shifted(block, axis, step, count, wraps):
    route = [(i, (i + step) % count) for i in range(count) if wraps or 0 <= i + step < count]
    return lax.ppermute(block, axis, route)


def start_kernel(
    width, observed, precision, weight, stencil, owned, cells, params_ref, left_ref, right_ref,
    observed_v, precision_v, weight_v, stencil_v, owned_v, left_v, right_v, sems
):
    batches, cols = (observed.shape[0], cells.shape[1])
    pairs = (
        (observed, observed_v),
        (precision, precision_v),
        (weight, weight_v),
        (stencil, stencil_v),
        (owned, owned_v),
        (cells.at[:, pl.ds(0, SUB)], left_v),
        (cells.at[:, pl.ds(cols - SUB, SUB)], right_v),
    )
    copies = [pltpu.make_async_copy(source, target, sems.at[n]) for n, (source, target) in enumerate(pairs)]
    for copy in copies:
        copy.start()
    for copy in copies:
        copy.wait()
    params_ref[...] = jnp.zeros_like(params_ref)
    for b in range(batches):
        root = jnp.sqrt(precision_v[b, 0]) * owned_v[b, 0].astype(F32)
        corner = stencil_v[b, 0, 0, pl.ds(0, 1)].astype(F32)
        row = jnp.floor((corner + 0.5) * (1.0 / width))
        params_ref[b, pl.ds(0, 4), pl.ds(0, SUB)] = weight_v[b, 0, 0] * root
        params_ref[b, pl.ds(AT_ROW, 1), pl.ds(0, SUB)] = row
        params_ref[b, pl.ds(AT_COL, 1), pl.ds(0, SUB)] = corner - row * width
        params_ref[b, pl.ds(AT_OBS, 1), pl.ds(0, SUB)] = observed_v[b, 0] * root
    rows = cells.shape[0]
    left_ref[pl.ds(0, rows), :] = left_v[:, 0, :]
    right_ref[pl.ds(0, rows), :] = right_v[:, SUB - 1, :]
    left_ref[pl.ds(rows, SUB), :] = params_ref[1]
    right_ref[pl.ds(rows, SUB), :] = params_ref[1]


def clear_rim(pad, rows, cols):
    edge = jnp.zeros((2, cols + 2 * SUB, LANES), F32)
    pad[pl.ds(0, 2)] = edge
    pad[pl.ds(rows + 2, 2)] = edge
    side = jnp.zeros((rows, SUB, LANES), F32)
    pad[pl.ds(2, rows), pl.ds(0, SUB)] = side
    pad[pl.ds(2, rows), pl.ds(SUB + cols, SUB)] = side


def share(pad, number, rows, cols, da, dc, o):
    row = number(AT_ROW, o).astype(jnp.int32) - 1 + da * rows
    col = number(AT_COL, o).astype(jnp.int32) - 1 + dc * cols
    row = jnp.clip(row, -2, rows) + 2
    col = jnp.clip(col, -2, cols) + SUB
    terms = [number(k, o) * pad[row + k // 2, pl.ds(col + k % 2, 1), :] for k in range(4)]
    return (terms[0] + terms[1]) + (terms[2] + terms[3])


def own_shift(number):
    sub = lax.broadcasted_iota(jnp.int32, (SUB, LANES), 0)
    shift = jnp.zeros((SUB, LANES), F32)
    for o in range(SUB):
        shift = jnp.where(sub == o, number(AT_OBS, o), shift)
    return shift


def pad_kernel(cells, pad, sem):
    rows, cols = (cells.shape[0], cells.shape[1])
    copy = pltpu.make_async_copy(cells, pad.at[pl.ds(2, rows), pl.ds(SUB, cols)], sem)
    copy.start()
    clear_rim(pad, rows, cols)
    copy.wait()


def hold_sides(left, right, sides):
    rows = left.shape[0] - SUB
    sides[...] = jnp.zeros_like(sides)
    sides[0, pl.ds(SUB, rows), :] = left[pl.ds(0, rows), :]
    sides[1, pl.ds(SUB, rows), :] = right[pl.ds(0, rows), :]


def side_share(sides, side, number, rows, cols, da, o):
    row = number(AT_ROW, o).astype(jnp.int32) - 1 + da * rows
    row = jnp.clip(row, -2, rows) + SUB
    used = number(AT_COL, o).astype(jnp.int32) == (0, cols)[side]
    terms = [jnp.where(used, number(side + 2 * k, o), 0.0) * sides[side, pl.ds(row + k, 1), :] for k in range(2)]
    return terms[0] + terms[1]


def send_block(value, out_ref):
    mean = jnp.mean(value, axis=-1, keepdims=True)
    sub = lax.broadcasted_iota(jnp.int32, (SUB, LANES), 0)
    lane = lax.broadcasted_iota(jnp.int32, (SUB, LANES), 1)
    innov = jnp.sum(jnp.where(lane == sub, -mean, 0.0), axis=0, keepdims=True)
    rows = jnp.concatenate([value - mean, jnp.broadcast_to(innov, (2, LANES))], axis=0).astype(BF16)
    for n in range(PAIRS):
        pair = rows[2 * n:2 * n + 2]
        out_ref[:, n] = jnp.broadcast_to(pair, (out_ref.shape[0],) + pair.shape)


def rows_kernel(mine, left, right, pad, first_ref, last_ref):
    rows, cols = (pad.shape[0] - 4, pad.shape[1] - 2 * SUB)
    lane = lax.broadcasted_iota(jnp.int32, (SUB, LANES), 1)
    block = pl.ds(rows, SUB)
    packed = jnp.where(lane < SUB, left[block, :], pltpu.roll(mine[1], SUB, 1))
    packed = jnp.where(lane < 2 * SUB, packed, pltpu.roll(right[block, :], 2 * SUB, 1))
    for row, out in ((0, first_ref), (rows - 1, last_ref)):
        out[pl.ds(0, SUB), :] = jnp.broadcast_to(left[pl.ds(row, 1), :], (SUB, LANES))
        out[pl.ds(SUB, cols), :] = pad[2 + row, pl.ds(SUB, cols), :]
        out[pl.ds(SUB + cols, SUB), :] = jnp.broadcast_to(right[pl.ds(row, 1), :], (SUB, LANES))
        out[pl.ds(2 * SUB + cols, SUB), :] = packed


def row_kernel(mine, left, right, pad, out_ref, sides, params, sem):
    rows, cols = (pad.shape[0] - 4, pad.shape[1] - 2 * SUB)
    copy = pltpu.make_async_copy(mine.at[0], params, sem)
    copy.start()
    hold_sides(left, right, sides)
    copy.wait()
    number = lambda kind, o: params[kind, o]
    for o in range(SUB):
        total = share(pad, number, rows, cols, 0, 0, o)
        for side in range(2):
            total = total + side_share(sides, side, number, rows, cols, 0, o)
        out_ref[pl.ds(o, 1), :] = total
    out_ref[...] = out_ref[...] - own_shift(number)


def prior_kernel(rows, mine, own, above, below, out_ref, value, params, sem):
    copy = pltpu.make_async_copy(mine.at[0], params, sem)
    copy.start()
    copy.wait()
    for o in range(SUB):
        row, col = (params[AT_ROW, o].astype(jnp.int32), params[AT_COL, o].astype(jnp.int32))
        total = own[pl.ds(o, 1), :]
        for n, (end, at) in enumerate(((above, 0), (below, rows))):
            for k in range(2):
                weight = jnp.where(row == at, params[2 * n + k, o], 0.0)
                total = total + weight * end[pl.ds(col + SUB - 1 + k, 1), :]
        value[pl.ds(o, 1), :] = total
    send_block(value[...], out_ref)


def meet_kernel(shares, out_ref):
    send_block(jnp.sum(shares[...], axis=0), out_ref)


def later_kernel(mine, left, right, above, below, pad, out_ref, params, sems):
    rows, cols = (pad.shape[0] - 4, pad.shape[1] - 2 * SUB)
    side, end = (pl.ds(rows, SUB), pl.ds(cols + 2 * SUB, SUB))
    sources = (left.at[side], mine.at[1], right.at[side], above.at[end], below.at[end])
    copies = []
    for n, source in enumerate(sources):
        copies.append(pltpu.make_async_copy(source, params.at[n], sems.at[n]))
        copies[-1].start()
    for copy in copies:
        copy.wait()
    for n, dc in enumerate(NEAR):
        for m, da in enumerate(NEAR):
            spot, lane = (n, 0) if da == 0 else (len(NEAR) + m // 2, n * SUB)
            number = lambda kind, o: params[spot, kind, lane + o]
            for o in range(SUB):
                out_ref[n * len(NEAR) + m, pl.ds(o, 1), :] = share(pad, number, rows, cols, da, dc, o)
    out_ref[len(NEAR) ** 2] = own_shift(lambda kind, o: params[1, kind, o])


def window_start(lat_count, my_lat):
    return 0 if lat_count <= WIN else jnp.clip(my_lat - REACH, 0, lat_count - WIN)


def row_of(block, j):
    return jnp.broadcast_to(block[j:j + 1, :], block.shape)


def column_of(block, j):
    return jnp.broadcast_to(block[:, j:j + 1], block.shape)


def reciprocal(value):
    guess = pl.reciprocal(value, approx=True)
    return guess * (2.0 - value * guess)


def pivot_rows(block, k, between):
    sub = lax.broadcasted_iota(jnp.int32, block.shape, 0)
    lane = lax.broadcasted_iota(jnp.int32, block.shape, 1) - k * SUB
    rows = [row_of(block, r) for r in range(SUB)]
    at = {(r, n): column_of(rows[r], k * SUB + n) for r in range(SUB) for n in range(r + 1)}
    here = (lane >= 0) & (lane < SUB)
    rows = [jnp.where(here, jnp.where(lane == r, 1.0, 0.0), row) for r, row in enumerate(rows)]
    inverse = jnp.zeros(block.shape, F32)
    for j in range(0, SUB, 2):
        a, b, c = (at[j, j], at[j + 1, j], at[j + 1, j + 1])
        det = a * c - b * b
        over_det = reciprocal(det)
        top, bottom = (rows[j], rows[j + 1])
        rest = range(j + 2, SUB)
        upper = {n: (at[n, j], at[n, j + 1]) for n in rest}
        for r in rest:
            first = (at[r, j] * c - at[r, j + 1] * b) * over_det
            second = (at[r, j + 1] * a - at[r, j] * b) * over_det
            for n in range(j + 2, r + 1):
                at[r, n] = at[r, n] - (first * upper[n][0] + second * upper[n][1])
            rows[r] = rows[r] - (first * top + second * bottom)
        a_part, b_part, c_part = (a * over_det, b * over_det, c * over_det)
        for r in range(j):
            first = at[r, j] * c_part - at[r, j + 1] * b_part
            second = at[r, j + 1] * a_part - at[r, j] * b_part
            for n in rest:
                at[r, n] = at[r, n] - (first * upper[n][0] + second * upper[n][1])
            rows[r] = rows[r] - (first * top + second * bottom)
        for n in rest:
            at[j, n] = c_part * upper[n][0] - b_part * upper[n][1]
            at[j + 1, n] = a_part * upper[n][1] - b_part * upper[n][0]
        rows[j] = c_part * top - b_part * bottom
        rows[j + 1] = a_part * bottom - b_part * top
        over_a = reciprocal(a)
        inverse = jnp.where(sub == j, lax.rsqrt(a) * top, inverse)
        inverse = jnp.where(sub == j + 1, lax.rsqrt(det * over_a) * (bottom - b * over_a * top), inverse)
        between()
    return rows, jnp.where(lane < SUB, inverse, 0.0)


def eliminate(blocks):
    count = len(blocks) - 1
    blocks = list(blocks)
    lane = lax.broadcasted_iota(jnp.int32, blocks[0].shape, 1)
    inverse, waiting = ([], [])

    def update(i, k, pivot):
        terms = [column_of(blocks[i], k * SUB + j) * pivot[j] for j in range(SUB)]
        while len(terms) > 1:
            terms = [terms[n] + terms[n + 1] for n in range(0, len(terms), 2)]
        here = (lane >= k * SUB) & (lane < (k + 1) * SUB)
        blocks[i] = jnp.where(here, 0.0, blocks[i]) - terms[0]

    for k in range(count):
        share_of = -(-len(waiting) // 4)

        def between():
            for task in waiting[:share_of]:
                update(*task)
            del waiting[:share_of]

        pivot, rows = pivot_rows(blocks[k], k, between)
        update(k + 1, k, pivot)
        waiting = [(i, k, pivot) for i in range(k + 2, count + 1)]
        inverse.append(rows)
    return inverse, blocks[count][:1]


def batch_map(batch, lat_count, near_ref, pattern):
    held = min(WIN, lat_count)
    count = near_ref.shape[0]
    my_lat = lax.axis_index("lat")
    start = window_start(lat_count, my_lat)
    scaled = jnp.concatenate([near_ref[:, n].astype(F32) for n in range(PAIRS - 1)], axis=1)
    innov = near_ref[:, PAIRS - 1].astype(F32)[:, :1]
    sub = lax.broadcasted_iota(jnp.int32, scaled.shape, 1)
    lane = lax.broadcasted_iota(jnp.int32, scaled.shape, 2)
    innov = jnp.where(lane == sub, jnp.broadcast_to(innov, scaled.shape), 0.0)
    picked = []
    for j in range(held):
        offset = start + j - my_lat + REACH
        inside = (offset >= 0) & (offset < WIN)
        row = pattern[batch, 0, 0, pl.ds(jnp.clip(offset, 0, WIN - 1), 1), :].astype(F32)
        row = jnp.where(inside, row, 0.0)
        for e in range(count // held):
            picked.append(jnp.broadcast_to(row[:, e:e + 1], (1, SUB, LANES)))
    weighted = scaled * jnp.concatenate(picked, axis=0)
    both = jnp.concatenate([scaled, innov], axis=2).reshape(count * SUB, 2 * LANES).astype(BF16)
    product = lax.dot_general(
        both,
        weighted.reshape(count * SUB, LANES).astype(BF16),
        (((0,), (0,)), ((), ())),
        preferred_element_type=F32,
    )
    sub = lax.broadcasted_iota(jnp.int32, (SUB, LANES), 0)
    lane = lax.broadcasted_iota(jnp.int32, (SUB, LANES), 1)
    members = LANES
    blocks = []
    for k in range(members // SUB):
        block = product[k * SUB:(k + 1) * SUB, :]
        blocks.append(block + jnp.where(lane - k * SUB == sub, members - 1.0, 0.0))
    proj = jnp.sum(product[members:members + SUB, :], axis=0, keepdims=True)
    blocks.append(jnp.broadcast_to(proj, (SUB, LANES)))
    inverse, weights = eliminate(blocks)
    flipped = jnp.concatenate(inverse, axis=0) * (members - 1.0) ** 0.5 - weights
    return flipped - jnp.mean(flipped, axis=-1, keepdims=True) + 1.0 / members


def exact_dot(a, b, contract_b):
    return lax.dot_general(
        a, b, (((1,), (contract_b,)), ((), ())), precision=lax.Precision.HIGHEST, preferred_element_type=F32
    )


def first_kernel(lat_count, lon_count, near_ref, pattern, later, map_ref, out_ref, moved):
    flipped = batch_map(0, lat_count, near_ref, pattern)
    map_ref[...] = flipped
    count = len(NEAR) ** 2
    moved[...] = exact_dot(later[pl.ds(0, count)].reshape(-1, LANES), flipped, 1).reshape(moved.shape)
    moved[count // 2] = moved[count // 2] - later[count]
    out_ref[...] = jnp.zeros_like(out_ref)
    my_lat, my_lon = (lax.axis_index("lat"), lax.axis_index("lon"))
    for n, dc in enumerate(NEAR):
        lon = lax.rem(my_lon + dc + lon_count, lon_count)
        for m, da in enumerate(NEAR):
            lat = my_lat + da

            @pl.when((lat >= 0) & (lat < lat_count))
            def _():
                out_ref[lat * lon_count + lon] = moved[n * len(NEAR) + m]


def last_kernel(lat_count, near_ref, pattern, map_ref, pad, out_ref, result, out_sem):
    parts = out_sem.shape[0]
    rows, cols = (pad.shape[0] - 4, pad.shape[1] - 2 * SUB)
    flipped = exact_dot(batch_map(1, lat_count, near_ref, pattern), map_ref[...], 0)
    high = flipped.astype(BF16)
    low = (flipped - high.astype(F32)).astype(BF16)
    right = jnp.concatenate(
        [jnp.concatenate([high, high], axis=1), jnp.concatenate([low, jnp.zeros_like(low)], axis=1)], axis=0
    )
    copies = []
    size = rows // parts
    for n in range(parts):
        part = pl.ds(n * size * cols, size * cols)
        value = pad[pl.ds(2 + n * size, size), pl.ds(SUB, cols), :].reshape(size * cols, LANES)
        upper = value.astype(BF16)
        rest = (value - upper.astype(F32)).astype(BF16)
        both = lax.dot_general(
            jnp.concatenate([upper, rest], axis=1), right, (((1,), (1,)), ((), ())), preferred_element_type=F32
        )
        result[part, :] = both[:, :LANES] + both[:, LANES:]
        copies.append(pltpu.make_async_copy(result.at[part], out_ref.at[part], out_sem.at[n]))
        copies[-1].start()
    for out_copy in copies:
        out_copy.wait()


def window(tiles, lat_count, lon_count):
    held = min(WIN, lat_count)
    if held == lat_count:
        return tiles
    start = jnp.clip(lax.axis_index("lat") - REACH, 0, lat_count - held)
    return lax.dynamic_slice_in_dim(tiles, start * lon_count, held * lon_count, axis=0)


def local(ensemble, observed, precision, interp_weight, stencil, owned, pattern):
    rows, cols, members = ensemble.shape
    batches = observed.shape[0]
    lat_count, lon_count = (lax.axis_size("lat"), lax.axis_size("lon"))
    tiles = lat_count * lon_count
    vmem = pl.BlockSpec(memory_space=pltpu.VMEM)
    anywhere = pl.BlockSpec(memory_space=pl.ANY)
    hbm = pl.BlockSpec(memory_space=pltpu.HBM)
    megabyte = 1024 * 1024

    def shape(*dims, dtype=F32):
        return jax.ShapeDtypeStruct(dims, dtype)

    def call(kernel, name, specs, out_shape, scratch, *operands, out_specs=None, limit=48):
        return pl.pallas_call(
            kernel,
            out_shape=out_shape,
            in_specs=specs,
            out_specs=out_specs or jax.tree.map(lambda _: vmem, out_shape),
            scratch_shapes=scratch,
            compiler_params=pltpu.CompilerParams(vmem_limit_bytes=limit * megabyte),
            name=name,
        )(*operands)

    def exchange(blocks):
        return lax.all_to_all(blocks, ("lat", "lon"), split_axis=0, concat_axis=0, tiled=True)

    small = (observed, precision, interp_weight, stencil, owned)
    side = shape(rows + SUB, members)
    mine, left, right = call(
        functools.partial(start_kernel, cols + 2),
        "start",
        [hbm] * 6,
        (shape(batches, SUB, LANES), side, side),
        [pltpu.VMEM(array.shape, array.dtype) for array in small]
        + [pltpu.VMEM((rows, SUB, members), F32)] * 2
        + [pltpu.SemaphoreType.DMA((7,))],
        *small,
        ensemble,
        limit=63,
    )
    sides = (shifted(right, "lon", 1, lon_count, True), shifted(left, "lon", -1, lon_count, True))
    padded = shape(rows + 4, cols + 2 * SUB, members)
    pad = call(pad_kernel, "pad", [hbm], padded, [pltpu.SemaphoreType.DMA], ensemble)
    end = shape(cols + 3 * SUB, members)
    first, last = call(rows_kernel, "edge_rows", [vmem] * 4, (end, end), [], mine, *sides, pad)
    ends = (shifted(last, "lat", 1, lat_count, False), shifted(first, "lat", -1, lat_count, False))
    slots = shape(tiles, PAIRS, 2, members, dtype=BF16)
    numbers = [pltpu.SMEM((SUB, LANES), F32), pltpu.SemaphoreType.DMA]
    block = shape(SUB, members)
    held_sides = pltpu.VMEM((2, rows + 2 * SUB, members), F32)
    own = call(row_kernel, "row_shares", [vmem] * 4, block, [held_sides] + numbers, mine, *sides, pad)
    blocks = call(
        functools.partial(prior_kernel, rows),
        "prior",
        [vmem] * 4,
        slots,
        [pltpu.VMEM((SUB, members), F32)] + numbers,
        mine,
        own,
        *ends,
    )
    near = window(exchange(blocks), lat_count, lon_count)
    count = len(NEAR) ** 2
    later = call(
        later_kernel,
        "later_shares",
        [vmem] * 6,
        shape(count + 1, SUB, members),
        [pltpu.SMEM((5, SUB, LANES), F32), pltpu.SemaphoreType.DMA((5,))],
        mine,
        *sides,
        *ends,
        pad,
    )
    first_map, shares = call(
        functools.partial(first_kernel, lat_count, lon_count),
        "first_batch",
        [vmem] * 3,
        (shape(members, members), shape(tiles, SUB, members)),
        [pltpu.VMEM((count, SUB, members), F32)],
        near,
        pattern,
        later,
    )
    blocks = call(meet_kernel, "own_block", [vmem], slots, [], exchange(shares))
    near = window(exchange(blocks), lat_count, lon_count)
    parts = 8
    result = call(
        functools.partial(last_kernel, lat_count),
        "second_batch",
        [vmem] * 4,
        shape(rows * cols, members),
        [
            pltpu.VMEM((rows * cols, members), F32),
            pltpu.SemaphoreType.DMA((parts,)),
        ],
        near,
        pattern,
        first_map,
        pad,
        out_specs=anywhere,
    )
    return result.reshape(rows, cols, members)


def solution(mesh):
    placed = (
        P("lat", "lon", None),
        P(None, "lat", "lon", None),
        P(None, "lat", "lon", None),
        P(None, "lat", "lon", None, None),
        P(None, "lat", "lon", None, None),
        P(None, "lat", "lon", None),
        P(None, "lat", "lon", None, None),
    )
    return jax.shard_map(
        local, mesh=mesh, in_specs=placed, out_specs=P("lat", "lon", None), check_vma=False
    )
```

```python
import functools
import jax
import jax.numpy as jnp
from jax import lax
from jax.experimental import pallas as pl
from jax.experimental.pallas import tpu as pltpu
from jax.sharding import PartitionSpec as P

REACH = 2
WIN = 2 * REACH + 1
SUB = 8
LANES = 128
NEAR = (-1, 0, 1)
AT_ROW, AT_COL, AT_OBS = (4, 5, 6)
PAIRS = SUB // 2 + 1
F32 = jnp.float32
BF16 = jnp.bfloat16


def swap(block, axis, kind, count, wraps):
    route = []
    for place in range(count):
        partner = place + (1 if place % 2 == kind else -1)
        if wraps or 0 <= partner < count:
            route.append((place, partner % count))
    return lax.ppermute(block, axis, route)


def is_even(axis):
    return lax.rem(lax.axis_index(axis), 2) == 0


def start_kernel(
    width, observed, precision, weight, stencil, owned, cells, params_ref, sides_1, sides_0,
    observed_v, precision_v, weight_v, stencil_v, owned_v, left_v, right_v, sems
):
    batches, cols = (observed.shape[0], cells.shape[1])
    pairs = (
        (observed, observed_v),
        (precision, precision_v),
        (weight, weight_v),
        (stencil, stencil_v),
        (owned, owned_v),
        (cells.at[:, pl.ds(0, SUB)], left_v),
        (cells.at[:, pl.ds(cols - SUB, SUB)], right_v),
    )
    copies = [pltpu.make_async_copy(source, target, sems.at[n]) for n, (source, target) in enumerate(pairs)]
    for copy in copies:
        copy.start()
    for copy in copies:
        copy.wait()
    params_ref[...] = jnp.zeros_like(params_ref)
    for b in range(batches):
        root = jnp.sqrt(precision_v[b, 0]) * owned_v[b, 0].astype(F32)
        corner = stencil_v[b, 0, 0, pl.ds(0, 1)].astype(F32)
        row = jnp.floor((corner + 0.5) * (1.0 / width))
        params_ref[b, pl.ds(0, 4), pl.ds(0, SUB)] = weight_v[b, 0, 0] * root
        params_ref[b, pl.ds(AT_ROW, 1), pl.ds(0, SUB)] = row
        params_ref[b, pl.ds(AT_COL, 1), pl.ds(0, SUB)] = corner - row * width
        params_ref[b, pl.ds(AT_OBS, 1), pl.ds(0, SUB)] = observed_v[b, 0] * root
    rows = cells.shape[0]
    even = is_even("lon")
    left, right = (left_v[:, 0, :], right_v[:, SUB - 1, :])
    sides_0[pl.ds(0, rows), :] = jnp.where(even, right, left)
    sides_1[pl.ds(0, rows), :] = jnp.where(even, left, right)
    sides_0[pl.ds(rows, SUB), :] = params_ref[1]
    sides_1[pl.ds(rows, SUB), :] = params_ref[1]


def hold_kernel(block, out_ref):
    out_ref[...] = block[...]


def clear_rim(pad, rows, cols):
    edge = jnp.zeros((2, cols + 2 * SUB, LANES), F32)
    pad[pl.ds(0, 2)] = edge
    pad[pl.ds(rows + 2, 2)] = edge
    side = jnp.zeros((rows, SUB, LANES), F32)
    pad[pl.ds(2, rows), pl.ds(0, SUB)] = side
    pad[pl.ds(2, rows), pl.ds(SUB + cols, SUB)] = side


def share(pad, number, rows, cols, da, dc, o):
    row = number(AT_ROW, o).astype(jnp.int32) - 1 + da * rows
    col = number(AT_COL, o).astype(jnp.int32) - 1 + dc * cols
    row = jnp.clip(row, -2, rows) + 2
    col = jnp.clip(col, -2, cols) + SUB
    terms = [number(k, o) * pad[row + k // 2, pl.ds(col + k % 2, 1), :] for k in range(4)]
    return (terms[0] + terms[1]) + (terms[2] + terms[3])


def own_shift(number):
    sub = lax.broadcasted_iota(jnp.int32, (SUB, LANES), 0)
    shift = jnp.zeros((SUB, LANES), F32)
    for o in range(SUB):
        shift = jnp.where(sub == o, number(AT_OBS, o), shift)
    return shift


def pad_kernel(cells, pad, sem):
    rows, cols = (cells.shape[0], cells.shape[1])
    copy = pltpu.make_async_copy(cells, pad.at[pl.ds(2, rows), pl.ds(SUB, cols)], sem)
    copy.start()
    clear_rim(pad, rows, cols)
    copy.wait()


def hold_sides(left, right, sides):
    rows = left.shape[0] - SUB
    sides[...] = jnp.zeros_like(sides)
    sides[0, pl.ds(SUB, rows), :] = left[pl.ds(0, rows), :]
    sides[1, pl.ds(SUB, rows), :] = right[pl.ds(0, rows), :]


def side_share(sides, side, number, rows, cols, da, o):
    row = number(AT_ROW, o).astype(jnp.int32) - 1 + da * rows
    row = jnp.clip(row, -2, rows) + SUB
    used = number(AT_COL, o).astype(jnp.int32) == (0, cols)[side]
    terms = [jnp.where(used, number(side + 2 * k, o), 0.0) * sides[side, pl.ds(row + k, 1), :] for k in range(2)]
    return terms[0] + terms[1]


def send_block(value, out_ref):
    mean = jnp.mean(value, axis=-1, keepdims=True)
    sub = lax.broadcasted_iota(jnp.int32, (SUB, LANES), 0)
    lane = lax.broadcasted_iota(jnp.int32, (SUB, LANES), 1)
    innov = jnp.sum(jnp.where(lane == sub, -mean, 0.0), axis=0, keepdims=True)
    rows = jnp.concatenate([value - mean, jnp.broadcast_to(innov, (2, LANES))], axis=0).astype(BF16)
    for n in range(PAIRS):
        pair = rows[2 * n:2 * n + 2]
        out_ref[:, n] = jnp.broadcast_to(pair, (out_ref.shape[0],) + pair.shape)


def rows_kernel(mine, sides_0, sides_1, pad, left_ref, right_ref, out_0, out_1):
    rows, cols = (pad.shape[0] - 4, pad.shape[1] - 2 * SUB)
    even = is_even("lon")
    left_ref[...] = jnp.where(even, sides_1[...], sides_0[...])
    right_ref[...] = jnp.where(even, sides_0[...], sides_1[...])
    lane = lax.broadcasted_iota(jnp.int32, (SUB, LANES), 1)
    block = pl.ds(rows, SUB)
    packed = jnp.where(lane < SUB, left_ref[block, :], pltpu.roll(mine[1], SUB, 1))
    packed = jnp.where(lane < 2 * SUB, packed, pltpu.roll(right_ref[block, :], 2 * SUB, 1))
    even = is_even("lat")
    for kind, out in enumerate((out_0, out_1)):
        row = jnp.where(even, (1 - kind) * (rows - 1), kind * (rows - 1))
        out[pl.ds(0, SUB), :] = jnp.broadcast_to(left_ref[pl.ds(row, 1), :], (SUB, LANES))
        out[pl.ds(SUB, cols), :] = pad[2 + row, pl.ds(SUB, cols), :]
        out[pl.ds(SUB + cols, SUB), :] = jnp.broadcast_to(right_ref[pl.ds(row, 1), :], (SUB, LANES))
        out[pl.ds(2 * SUB + cols, SUB), :] = packed


def row_kernel(mine, left, right, pad, out_ref, sides, params, sem):
    rows, cols = (pad.shape[0] - 4, pad.shape[1] - 2 * SUB)
    copy = pltpu.make_async_copy(mine.at[0], params, sem)
    copy.start()
    hold_sides(left, right, sides)
    copy.wait()
    number = lambda kind, o: params[kind, o]
    for o in range(SUB):
        total = share(pad, number, rows, cols, 0, 0, o)
        for side in range(2):
            total = total + side_share(sides, side, number, rows, cols, 0, o)
        out_ref[pl.ds(o, 1), :] = total
    out_ref[...] = out_ref[...] - own_shift(number)


def prior_kernel(rows, mine, own, ends_0, ends_1, out_ref, ends, value, params, sem):
    copy = pltpu.make_async_copy(mine.at[0], params, sem)
    copy.start()
    even = is_even("lat")
    ends[0] = jnp.where(even, ends_1[...], ends_0[...])
    ends[1] = jnp.where(even, ends_0[...], ends_1[...])
    copy.wait()
    for o in range(SUB):
        row, col = (params[AT_ROW, o].astype(jnp.int32), params[AT_COL, o].astype(jnp.int32))
        total = own[pl.ds(o, 1), :]
        for n, at in enumerate((0, rows)):
            for k in range(2):
                weight = jnp.where(row == at, params[2 * n + k, o], 0.0)
                total = total + weight * ends[n, pl.ds(col + SUB - 1 + k, 1), :]
        value[pl.ds(o, 1), :] = total
    send_block(value[...], out_ref)


def meet_kernel(shares, out_ref):
    send_block(jnp.sum(shares[...], axis=0), out_ref)


def later_kernel(mine, left, right, ends_0, ends_1, pad, out_ref, params, sems):
    rows, cols = (pad.shape[0] - 4, pad.shape[1] - 2 * SUB)
    side, end = (pl.ds(rows, SUB), pl.ds(cols + 2 * SUB, SUB))
    sources = (left.at[side], mine.at[1], right.at[side], ends_0.at[end], ends_1.at[end])
    copies = []
    for n, source in enumerate(sources):
        copies.append(pltpu.make_async_copy(source, params.at[n], sems.at[n]))
        copies[-1].start()
    for copy in copies:
        copy.wait()
    even = is_even("lat")
    ends = {-1: jnp.where(even, 4, 3), 1: jnp.where(even, 3, 4)}
    for n, dc in enumerate(NEAR):
        for m, da in enumerate(NEAR):
            spot, lane = (n, 0) if da == 0 else (ends[da], n * SUB)
            number = lambda kind, o: params[spot, kind, lane + o]
            for o in range(SUB):
                out_ref[n * len(NEAR) + m, pl.ds(o, 1), :] = share(pad, number, rows, cols, da, dc, o)
    out_ref[len(NEAR) ** 2] = own_shift(lambda kind, o: params[1, kind, o])


def window_start(lat_count, my_lat):
    return 0 if lat_count <= WIN else jnp.clip(my_lat - REACH, 0, lat_count - WIN)


def row_of(block, j):
    return jnp.broadcast_to(block[j:j + 1, :], block.shape)


def column_of(block, j):
    return jnp.broadcast_to(block[:, j:j + 1], block.shape)


def reciprocal(value):
    guess = pl.reciprocal(value, approx=True)
    return guess * (2.0 - value * guess)


def pivot_rows(block, k, between):
    sub = lax.broadcasted_iota(jnp.int32, block.shape, 0)
    lane = lax.broadcasted_iota(jnp.int32, block.shape, 1) - k * SUB
    rows = [row_of(block, r) for r in range(SUB)]
    at = {(r, n): column_of(rows[r], k * SUB + n) for r in range(SUB) for n in range(r + 1)}
    here = (lane >= 0) & (lane < SUB)
    rows = [jnp.where(here, jnp.where(lane == r, 1.0, 0.0), row) for r, row in enumerate(rows)]
    inverse, scale = (jnp.zeros(block.shape, F32), jnp.ones(block.shape, F32))
    for j in range(0, SUB, 2):
        a, b, c = (at[j, j], at[j + 1, j], at[j + 1, j + 1])
        det = a * c - b * b
        over_det = reciprocal(det)
        top, bottom = (rows[j], rows[j + 1])
        rest = range(j + 2, SUB)
        upper = {n: (at[n, j], at[n, j + 1]) for n in rest}
        for r in rest:
            first = (at[r, j] * c - at[r, j + 1] * b) * over_det
            second = (at[r, j + 1] * a - at[r, j] * b) * over_det
            for n in range(j + 2, r + 1):
                at[r, n] = at[r, n] - (first * upper[n][0] + second * upper[n][1])
            rows[r] = rows[r] - (first * top + second * bottom)
        a_part, b_part, c_part = (a * over_det, b * over_det, c * over_det)
        for r in range(j):
            first = at[r, j] * c_part - at[r, j + 1] * b_part
            second = at[r, j + 1] * a_part - at[r, j] * b_part
            for n in rest:
                at[r, n] = at[r, n] - (first * upper[n][0] + second * upper[n][1])
            rows[r] = rows[r] - (first * top + second * bottom)
        for n in rest:
            at[j, n] = c_part * upper[n][0] - b_part * upper[n][1]
            at[j + 1, n] = a_part * upper[n][1] - b_part * upper[n][0]
        rows[j] = c_part * top - b_part * bottom
        rows[j + 1] = a_part * bottom - b_part * top
        inverse = jnp.where(sub == j, top, jnp.where(sub == j + 1, a * bottom - b * top, inverse))
        scale = jnp.where(sub == j, a, jnp.where(sub == j + 1, a * det, scale))
        between()
    return rows, jnp.where(lane < SUB, inverse * lax.rsqrt(scale), 0.0)


def eliminate(blocks):
    count = len(blocks) - 1
    blocks = list(blocks)
    lane = lax.broadcasted_iota(jnp.int32, blocks[0].shape, 1)
    inverse, waiting = ([], [])

    def update(i, k, pivot):
        terms = [column_of(blocks[i], k * SUB + j) * pivot[j] for j in range(SUB)]
        while len(terms) > 1:
            terms = [terms[n] + terms[n + 1] for n in range(0, len(terms), 2)]
        here = (lane >= k * SUB) & (lane < (k + 1) * SUB)
        blocks[i] = jnp.where(here, 0.0, blocks[i]) - terms[0]

    for k in range(count):
        share_of = -(-len(waiting) // 4)

        def between():
            for task in waiting[:share_of]:
                update(*task)
            del waiting[:share_of]

        pivot, rows = pivot_rows(blocks[k], k, between)
        update(k + 1, k, pivot)
        waiting = [(i, k, pivot) for i in range(k + 2, count + 1)]
        inverse.append(rows)
    return inverse, blocks[count][:1]


def batch_map(batch, lat_count, near_ref, pattern):
    held = min(WIN, lat_count)
    count = near_ref.shape[0]
    my_lat = lax.axis_index("lat")
    start = window_start(lat_count, my_lat)
    scaled = jnp.concatenate([near_ref[:, n].astype(F32) for n in range(PAIRS - 1)], axis=1)
    innov = near_ref[:, PAIRS - 1].astype(F32)[:, :1]
    sub = lax.broadcasted_iota(jnp.int32, scaled.shape, 1)
    lane = lax.broadcasted_iota(jnp.int32, scaled.shape, 2)
    innov = jnp.where(lane == sub, jnp.broadcast_to(innov, scaled.shape), 0.0)
    picked = []
    for j in range(held):
        offset = start + j - my_lat + REACH
        inside = (offset >= 0) & (offset < WIN)
        row = pattern[batch, 0, 0, pl.ds(jnp.clip(offset, 0, WIN - 1), 1), :].astype(F32)
        row = jnp.where(inside, row, 0.0)
        for e in range(count // held):
            picked.append(jnp.broadcast_to(row[:, e:e + 1], (1, SUB, LANES)))
    weighted = scaled * jnp.concatenate(picked, axis=0)
    both = jnp.concatenate([scaled, innov], axis=2).reshape(count * SUB, 2 * LANES).astype(BF16)
    product = lax.dot_general(
        both,
        weighted.reshape(count * SUB, LANES).astype(BF16),
        (((0,), (0,)), ((), ())),
        preferred_element_type=F32,
    )
    sub = lax.broadcasted_iota(jnp.int32, (SUB, LANES), 0)
    lane = lax.broadcasted_iota(jnp.int32, (SUB, LANES), 1)
    members = LANES
    blocks = []
    for k in range(members // SUB):
        block = product[k * SUB:(k + 1) * SUB, :]
        blocks.append(block + jnp.where(lane - k * SUB == sub, members - 1.0, 0.0))
    proj = jnp.sum(product[members:members + SUB, :], axis=0, keepdims=True)
    blocks.append(jnp.broadcast_to(proj, (SUB, LANES)))
    inverse, weights = eliminate(blocks)
    flipped = jnp.concatenate(inverse, axis=0) * (members - 1.0) ** 0.5 - weights
    return flipped - jnp.mean(flipped, axis=-1, keepdims=True) + 1.0 / members


def exact_dot(a, b, contract_b):
    return lax.dot_general(
        a, b, (((1,), (contract_b,)), ((), ())), precision=lax.Precision.HIGHEST, preferred_element_type=F32
    )


def first_kernel(lat_count, lon_count, near_ref, pattern, later, map_ref, out_ref, moved):
    flipped = batch_map(0, lat_count, near_ref, pattern)
    map_ref[...] = flipped
    count = len(NEAR) ** 2
    moved[...] = exact_dot(later[pl.ds(0, count)].reshape(-1, LANES), flipped, 1).reshape(moved.shape)
    moved[count // 2] = moved[count // 2] - later[count]
    out_ref[...] = jnp.zeros_like(out_ref)
    my_lat, my_lon = (lax.axis_index("lat"), lax.axis_index("lon"))
    for n, dc in enumerate(NEAR):
        lon = lax.rem(my_lon + dc + lon_count, lon_count)
        for m, da in enumerate(NEAR):
            lat = my_lat + da

            @pl.when((lat >= 0) & (lat < lat_count))
            def _():
                out_ref[lat * lon_count + lon] = moved[n * len(NEAR) + m]


def halves_kernel(pad, out_ref):
    rows, cols = (pad.shape[0] - 4, pad.shape[1] - 2 * SUB)
    for row in range(rows):
        value = pad[2 + row, pl.ds(SUB, cols), :]
        upper = value.astype(BF16)
        lower = (value - upper.astype(F32)).astype(BF16)
        out_ref[pl.ds(row * cols, cols), :] = jnp.concatenate([upper, lower], axis=1)


def last_kernel(lat_count, near_ref, pattern, map_ref, halves, out_ref, result, out_sem):
    parts = out_sem.shape[0]
    rows = result.shape[0] // parts
    flipped = exact_dot(batch_map(1, lat_count, near_ref, pattern), map_ref[...], 0)
    high = flipped.astype(BF16)
    low = (flipped - high.astype(F32)).astype(BF16)
    right = jnp.concatenate(
        [jnp.concatenate([high, high], axis=1), jnp.concatenate([low, jnp.zeros_like(low)], axis=1)], axis=0
    )
    copies = []
    for n in range(parts):
        part = pl.ds(n * rows, rows)
        both = lax.dot_general(halves[part, :], right, (((1,), (1,)), ((), ())), preferred_element_type=F32)
        result[part, :] = both[:, :LANES] + both[:, LANES:]
        copies.append(pltpu.make_async_copy(result.at[part], out_ref.at[part], out_sem.at[n]))
        copies[-1].start()
    for out_copy in copies:
        out_copy.wait()


def window(tiles, lat_count, lon_count):
    held = min(WIN, lat_count)
    if held == lat_count:
        return tiles
    start = jnp.clip(lax.axis_index("lat") - REACH, 0, lat_count - held)
    return lax.dynamic_slice_in_dim(tiles, start * lon_count, held * lon_count, axis=0)


def local(ensemble, observed, precision, interp_weight, stencil, owned, pattern):
    rows, cols, members = ensemble.shape
    batches = observed.shape[0]
    lat_count, lon_count = (lax.axis_size("lat"), lax.axis_size("lon"))
    tiles = lat_count * lon_count
    vmem = pl.BlockSpec(memory_space=pltpu.VMEM)
    anywhere = pl.BlockSpec(memory_space=pl.ANY)
    hbm = pl.BlockSpec(memory_space=pltpu.HBM)
    megabyte = 1024 * 1024

    def shape(*dims, dtype=F32):
        return jax.ShapeDtypeStruct(dims, dtype)

    def call(kernel, name, specs, out_shape, scratch, *operands, out_specs=None, limit=48):
        return pl.pallas_call(
            kernel,
            out_shape=out_shape,
            in_specs=specs,
            out_specs=out_specs or jax.tree.map(lambda _: vmem, out_shape),
            scratch_shapes=scratch,
            compiler_params=pltpu.CompilerParams(vmem_limit_bytes=limit * megabyte),
            name=name,
        )(*operands)

    def trade(blocks, axis):
        count, wraps = ((lon_count, True) if axis == "lon" else (lat_count, False))
        first, second = blocks
        second = swap(second, axis, 1, count, wraps)
        return [swap(first, axis, 0, count, wraps), second]

    def exchange(blocks):
        return lax.all_to_all(blocks, ("lat", "lon"), split_axis=0, concat_axis=0, tiled=True)

    small = (observed, precision, interp_weight, stencil, owned)
    side = shape(rows + SUB, members)
    mine, side_1, side_0 = call(
        functools.partial(start_kernel, cols + 2),
        "start",
        [hbm] * 6,
        (shape(batches, SUB, LANES), side, side),
        [pltpu.VMEM(array.shape, array.dtype) for array in small]
        + [pltpu.VMEM((rows, SUB, members), F32)] * 2
        + [pltpu.SemaphoreType.DMA((7,))],
        *small,
        ensemble,
        limit=63,
    )
    side_0 = call(hold_kernel, "hold", [vmem], side, [], side_0)
    sides = trade((side_0, side_1), "lon")
    padded = shape(rows + 4, cols + 2 * SUB, members)
    pad = call(pad_kernel, "pad", [hbm], padded, [pltpu.SemaphoreType.DMA], ensemble)
    end = shape(cols + 3 * SUB, members)
    left, right, *ends = call(rows_kernel, "edge_rows", [vmem] * 4, (side, side, end, end), [], mine, *sides, pad)
    ends = trade(ends, "lat")
    slots = shape(tiles, PAIRS, 2, members, dtype=BF16)
    numbers = [pltpu.SMEM((SUB, LANES), F32), pltpu.SemaphoreType.DMA]
    block = shape(SUB, members)
    held_sides = pltpu.VMEM((2, rows + 2 * SUB, members), F32)
    own = call(row_kernel, "row_shares", [vmem] * 4, block, [held_sides] + numbers, mine, left, right, pad)
    blocks = call(
        functools.partial(prior_kernel, rows),
        "prior",
        [vmem] * 4,
        slots,
        [pltpu.VMEM((2,) + end.shape, F32), pltpu.VMEM((SUB, members), F32)] + numbers,
        mine,
        own,
        *ends,
    )
    near = window(exchange(blocks), lat_count, lon_count)
    count = len(NEAR) ** 2
    later = call(
        later_kernel,
        "later_shares",
        [vmem] * 6,
        shape(count + 1, SUB, members),
        [pltpu.SMEM((5, SUB, LANES), F32), pltpu.SemaphoreType.DMA((5,))],
        mine,
        left,
        right,
        *ends,
        pad,
    )
    halves = call(halves_kernel, "halves", [vmem], shape(rows * cols, 2 * members, dtype=BF16), [], pad)
    first_map, shares = call(
        functools.partial(first_kernel, lat_count, lon_count),
        "first_batch",
        [vmem] * 3,
        (shape(members, members), shape(tiles, SUB, members)),
        [pltpu.VMEM((count, SUB, members), F32)],
        near,
        pattern,
        later,
    )
    blocks = call(meet_kernel, "own_block", [vmem], slots, [], exchange(shares))
    near = window(exchange(blocks), lat_count, lon_count)
    parts = 8
    result = call(
        functools.partial(last_kernel, lat_count),
        "second_batch",
        [vmem] * 4,
        shape(rows * cols, members),
        [
            pltpu.VMEM((rows * cols, members), F32),
            pltpu.SemaphoreType.DMA((parts,)),
        ],
        near,
        pattern,
        first_map,
        halves,
        out_specs=anywhere,
    )
    return result.reshape(rows, cols, members)


def solution(mesh):
    placed = (
        P("lat", "lon", None),
        P(None, "lat", "lon", None),
        P(None, "lat", "lon", None),
        P(None, "lat", "lon", None, None),
        P(None, "lat", "lon", None, None),
        P(None, "lat", "lon", None),
        P(None, "lat", "lon", None, None),
    )
    return jax.shard_map(
        local, mesh=mesh, in_specs=placed, out_specs=P("lat", "lon", None), check_vma=False
    )
```

```python
import functools
import jax
import jax.numpy as jnp
from jax import lax
from jax.experimental import pallas as pl
from jax.experimental.pallas import tpu as pltpu
from jax.sharding import PartitionSpec as P

REACH = 2
WIN = 2 * REACH + 1
SUB = 8
LANES = 128
NEAR = (-1, 0, 1)
AT_ROW, AT_COL, AT_OBS = (4, 5, 6)
PAIRS = SUB // 2 + 1
F32 = jnp.float32
BF16 = jnp.bfloat16


def swap(block, axis, kind, count, wraps):
    route = []
    for place in range(count):
        partner = place + (1 if place % 2 == kind else -1)
        if wraps or 0 <= partner < count:
            route.append((place, partner % count))
    return lax.ppermute(block, axis, route)


def is_even(axis):
    return lax.rem(lax.axis_index(axis), 2) == 0


def start_kernel(
    width, observed, precision, weight, stencil, owned, cells, params_ref, sides_1, sides_0,
    observed_v, precision_v, weight_v, stencil_v, owned_v, left_v, right_v, sems
):
    batches, cols = (observed.shape[0], cells.shape[1])
    pairs = (
        (observed, observed_v),
        (precision, precision_v),
        (weight, weight_v),
        (stencil, stencil_v),
        (owned, owned_v),
        (cells.at[:, pl.ds(0, SUB)], left_v),
        (cells.at[:, pl.ds(cols - SUB, SUB)], right_v),
    )
    copies = [pltpu.make_async_copy(source, target, sems.at[n]) for n, (source, target) in enumerate(pairs)]
    for copy in copies:
        copy.start()
    for copy in copies:
        copy.wait()
    params_ref[...] = jnp.zeros_like(params_ref)
    for b in range(batches):
        root = jnp.sqrt(precision_v[b, 0]) * owned_v[b, 0].astype(F32)
        corner = stencil_v[b, 0, 0, pl.ds(0, 1)].astype(F32)
        row = jnp.floor((corner + 0.5) * (1.0 / width))
        params_ref[b, pl.ds(0, 4), pl.ds(0, SUB)] = weight_v[b, 0, 0] * root
        params_ref[b, pl.ds(AT_ROW, 1), pl.ds(0, SUB)] = row
        params_ref[b, pl.ds(AT_COL, 1), pl.ds(0, SUB)] = corner - row * width
        params_ref[b, pl.ds(AT_OBS, 1), pl.ds(0, SUB)] = observed_v[b, 0] * root
    rows = cells.shape[0]
    even = is_even("lon")
    left, right = (left_v[:, 0, :], right_v[:, SUB - 1, :])
    sides_0[pl.ds(0, rows), :] = jnp.where(even, right, left)
    sides_1[pl.ds(0, rows), :] = jnp.where(even, left, right)
    sides_0[pl.ds(rows, SUB), :] = params_ref[1]
    sides_1[pl.ds(rows, SUB), :] = params_ref[1]


def clear_rim(pad, rows, cols):
    edge = jnp.zeros((2, cols + 2 * SUB, LANES), F32)
    pad[pl.ds(0, 2)] = edge
    pad[pl.ds(rows + 2, 2)] = edge
    side = jnp.zeros((rows, SUB, LANES), F32)
    pad[pl.ds(2, rows), pl.ds(0, SUB)] = side
    pad[pl.ds(2, rows), pl.ds(SUB + cols, SUB)] = side


def share(pad, number, rows, cols, da, dc, o):
    row = number(AT_ROW, o).astype(jnp.int32) - 1 + da * rows
    col = number(AT_COL, o).astype(jnp.int32) - 1 + dc * cols
    row = jnp.clip(row, -2, rows) + 2
    col = jnp.clip(col, -2, cols) + SUB
    terms = [number(k, o) * pad[row + k // 2, pl.ds(col + k % 2, 1), :] for k in range(4)]
    return (terms[0] + terms[1]) + (terms[2] + terms[3])


def own_shift(number):
    sub = lax.broadcasted_iota(jnp.int32, (SUB, LANES), 0)
    shift = jnp.zeros((SUB, LANES), F32)
    for o in range(SUB):
        shift = jnp.where(sub == o, number(AT_OBS, o), shift)
    return shift


def pad_kernel(cells, pad, sem):
    rows, cols = (cells.shape[0], cells.shape[1])
    copy = pltpu.make_async_copy(cells, pad.at[pl.ds(2, rows), pl.ds(SUB, cols)], sem)
    copy.start()
    clear_rim(pad, rows, cols)
    copy.wait()


def hold_sides(left, right, sides):
    rows = left.shape[0] - SUB
    sides[...] = jnp.zeros_like(sides)
    sides[0, pl.ds(SUB, rows), :] = left[pl.ds(0, rows), :]
    sides[1, pl.ds(SUB, rows), :] = right[pl.ds(0, rows), :]


def side_share(sides, side, number, rows, cols, da, o):
    row = number(AT_ROW, o).astype(jnp.int32) - 1 + da * rows
    row = jnp.clip(row, -2, rows) + SUB
    used = number(AT_COL, o).astype(jnp.int32) == (0, cols)[side]
    terms = [jnp.where(used, number(side + 2 * k, o), 0.0) * sides[side, pl.ds(row + k, 1), :] for k in range(2)]
    return terms[0] + terms[1]


def send_block(value, out_ref):
    mean = jnp.mean(value, axis=-1, keepdims=True)
    sub = lax.broadcasted_iota(jnp.int32, (SUB, LANES), 0)
    lane = lax.broadcasted_iota(jnp.int32, (SUB, LANES), 1)
    innov = jnp.sum(jnp.where(lane == sub, -mean, 0.0), axis=0, keepdims=True)
    rows = jnp.concatenate([value - mean, jnp.broadcast_to(innov, (2, LANES))], axis=0).astype(BF16)
    for n in range(PAIRS):
        pair = rows[2 * n:2 * n + 2]
        out_ref[:, n] = jnp.broadcast_to(pair, (out_ref.shape[0],) + pair.shape)


def rows_kernel(mine, sides_0, sides_1, pad, left_ref, right_ref, out_0, out_1):
    rows, cols = (pad.shape[0] - 4, pad.shape[1] - 2 * SUB)
    even = is_even("lon")
    left_ref[...] = jnp.where(even, sides_1[...], sides_0[...])
    right_ref[...] = jnp.where(even, sides_0[...], sides_1[...])
    lane = lax.broadcasted_iota(jnp.int32, (SUB, LANES), 1)
    block = pl.ds(rows, SUB)
    packed = jnp.where(lane < SUB, left_ref[block, :], pltpu.roll(mine[1], SUB, 1))
    packed = jnp.where(lane < 2 * SUB, packed, pltpu.roll(right_ref[block, :], 2 * SUB, 1))
    even = is_even("lat")
    for kind, out in enumerate((out_0, out_1)):
        row = jnp.where(even, (1 - kind) * (rows - 1), kind * (rows - 1))
        out[pl.ds(0, SUB), :] = jnp.broadcast_to(left_ref[pl.ds(row, 1), :], (SUB, LANES))
        out[pl.ds(SUB, cols), :] = pad[2 + row, pl.ds(SUB, cols), :]
        out[pl.ds(SUB + cols, SUB), :] = jnp.broadcast_to(right_ref[pl.ds(row, 1), :], (SUB, LANES))
        out[pl.ds(2 * SUB + cols, SUB), :] = packed


def row_kernel(mine, left, right, pad, out_ref, sides, params, sem):
    rows, cols = (pad.shape[0] - 4, pad.shape[1] - 2 * SUB)
    copy = pltpu.make_async_copy(mine.at[0], params, sem)
    copy.start()
    hold_sides(left, right, sides)
    copy.wait()
    number = lambda kind, o: params[kind, o]
    for o in range(SUB):
        total = share(pad, number, rows, cols, 0, 0, o)
        for side in range(2):
            total = total + side_share(sides, side, number, rows, cols, 0, o)
        out_ref[pl.ds(o, 1), :] = total
    out_ref[...] = out_ref[...] - own_shift(number)


def prior_kernel(rows, mine, own, ends_0, ends_1, out_ref, ends, value, params, sem):
    copy = pltpu.make_async_copy(mine.at[0], params, sem)
    copy.start()
    even = is_even("lat")
    ends[0] = jnp.where(even, ends_1[...], ends_0[...])
    ends[1] = jnp.where(even, ends_0[...], ends_1[...])
    copy.wait()
    for o in range(SUB):
        row, col = (params[AT_ROW, o].astype(jnp.int32), params[AT_COL, o].astype(jnp.int32))
        total = own[pl.ds(o, 1), :]
        for n, at in enumerate((0, rows)):
            for k in range(2):
                weight = jnp.where(row == at, params[2 * n + k, o], 0.0)
                total = total + weight * ends[n, pl.ds(col + SUB - 1 + k, 1), :]
        value[pl.ds(o, 1), :] = total
    send_block(value[...], out_ref)


def meet_kernel(shares, out_ref):
    send_block(jnp.sum(shares[...], axis=0), out_ref)


def later_kernel(mine, left, right, ends_0, ends_1, pad, out_ref, params, sems):
    rows, cols = (pad.shape[0] - 4, pad.shape[1] - 2 * SUB)
    side, end = (pl.ds(rows, SUB), pl.ds(cols + 2 * SUB, SUB))
    sources = (left.at[side], mine.at[1], right.at[side], ends_0.at[end], ends_1.at[end])
    copies = []
    for n, source in enumerate(sources):
        copies.append(pltpu.make_async_copy(source, params.at[n], sems.at[n]))
        copies[-1].start()
    for copy in copies:
        copy.wait()
    even = is_even("lat")
    ends = {-1: jnp.where(even, 4, 3), 1: jnp.where(even, 3, 4)}
    for n, dc in enumerate(NEAR):
        for m, da in enumerate(NEAR):
            spot, lane = (n, 0) if da == 0 else (ends[da], n * SUB)
            number = lambda kind, o: params[spot, kind, lane + o]
            for o in range(SUB):
                out_ref[n * len(NEAR) + m, pl.ds(o, 1), :] = share(pad, number, rows, cols, da, dc, o)
    out_ref[len(NEAR) ** 2] = own_shift(lambda kind, o: params[1, kind, o])


def window_start(lat_count, my_lat):
    return 0 if lat_count <= WIN else jnp.clip(my_lat - REACH, 0, lat_count - WIN)


def row_of(block, j):
    return jnp.broadcast_to(block[j:j + 1, :], block.shape)


def column_of(block, j):
    return jnp.broadcast_to(block[:, j:j + 1], block.shape)


def reciprocal(value):
    guess = pl.reciprocal(value, approx=True)
    return guess * (2.0 - value * guess)


def pivot_rows(block, k, between):
    sub = lax.broadcasted_iota(jnp.int32, block.shape, 0)
    lane = lax.broadcasted_iota(jnp.int32, block.shape, 1) - k * SUB
    rows = [row_of(block, r) for r in range(SUB)]
    at = {(r, n): column_of(rows[r], k * SUB + n) for r in range(SUB) for n in range(r + 1)}
    here = (lane >= 0) & (lane < SUB)
    rows = [jnp.where(here, jnp.where(lane == r, 1.0, 0.0), row) for r, row in enumerate(rows)]
    inverse, scale = (jnp.zeros(block.shape, F32), jnp.ones(block.shape, F32))
    for j in range(0, SUB, 2):
        a, b, c = (at[j, j], at[j + 1, j], at[j + 1, j + 1])
        det = a * c - b * b
        over_det = reciprocal(det)
        top, bottom = (rows[j], rows[j + 1])
        rest = range(j + 2, SUB)
        upper = {n: (at[n, j], at[n, j + 1]) for n in rest}
        for r in rest:
            first = (at[r, j] * c - at[r, j + 1] * b) * over_det
            second = (at[r, j + 1] * a - at[r, j] * b) * over_det
            for n in range(j + 2, r + 1):
                at[r, n] = at[r, n] - (first * upper[n][0] + second * upper[n][1])
            rows[r] = rows[r] - (first * top + second * bottom)
        a_part, b_part, c_part = (a * over_det, b * over_det, c * over_det)
        for r in range(j):
            first = at[r, j] * c_part - at[r, j + 1] * b_part
            second = at[r, j + 1] * a_part - at[r, j] * b_part
            for n in rest:
                at[r, n] = at[r, n] - (first * upper[n][0] + second * upper[n][1])
            rows[r] = rows[r] - (first * top + second * bottom)
        for n in rest:
            at[j, n] = c_part * upper[n][0] - b_part * upper[n][1]
            at[j + 1, n] = a_part * upper[n][1] - b_part * upper[n][0]
        rows[j] = c_part * top - b_part * bottom
        rows[j + 1] = a_part * bottom - b_part * top
        inverse = jnp.where(sub == j, top, jnp.where(sub == j + 1, a * bottom - b * top, inverse))
        scale = jnp.where(sub == j, a, jnp.where(sub == j + 1, a * det, scale))
        between()
    return rows, jnp.where(lane < SUB, inverse * lax.rsqrt(scale), 0.0)


def eliminate(blocks):
    count = len(blocks) - 1
    blocks = list(blocks)
    lane = lax.broadcasted_iota(jnp.int32, blocks[0].shape, 1)
    inverse, waiting = ([], [])

    def update(i, k, pivot):
        terms = [column_of(blocks[i], k * SUB + j) * pivot[j] for j in range(SUB)]
        while len(terms) > 1:
            terms = [terms[n] + terms[n + 1] for n in range(0, len(terms), 2)]
        here = (lane >= k * SUB) & (lane < (k + 1) * SUB)
        blocks[i] = jnp.where(here, 0.0, blocks[i]) - terms[0]

    for k in range(count):
        share_of = -(-len(waiting) // 4)

        def between():
            for task in waiting[:share_of]:
                update(*task)
            del waiting[:share_of]

        pivot, rows = pivot_rows(blocks[k], k, between)
        update(k + 1, k, pivot)
        waiting = [(i, k, pivot) for i in range(k + 2, count + 1)]
        inverse.append(rows)
    return inverse, blocks[count][:1]


def batch_map(batch, lat_count, near_ref, pattern):
    held = min(WIN, lat_count)
    count = near_ref.shape[0]
    my_lat = lax.axis_index("lat")
    start = window_start(lat_count, my_lat)
    scaled = jnp.concatenate([near_ref[:, n].astype(F32) for n in range(PAIRS - 1)], axis=1)
    innov = near_ref[:, PAIRS - 1].astype(F32)[:, :1]
    sub = lax.broadcasted_iota(jnp.int32, scaled.shape, 1)
    lane = lax.broadcasted_iota(jnp.int32, scaled.shape, 2)
    innov = jnp.where(lane == sub, jnp.broadcast_to(innov, scaled.shape), 0.0)
    picked = []
    for j in range(held):
        offset = start + j - my_lat + REACH
        inside = (offset >= 0) & (offset < WIN)
        row = pattern[batch, 0, 0, pl.ds(jnp.clip(offset, 0, WIN - 1), 1), :].astype(F32)
        row = jnp.where(inside, row, 0.0)
        for e in range(count // held):
            picked.append(jnp.broadcast_to(row[:, e:e + 1], (1, SUB, LANES)))
    weighted = scaled * jnp.concatenate(picked, axis=0)
    both = jnp.concatenate([scaled, innov], axis=2).reshape(count * SUB, 2 * LANES).astype(BF16)
    product = lax.dot_general(
        both,
        weighted.reshape(count * SUB, LANES).astype(BF16),
        (((0,), (0,)), ((), ())),
        preferred_element_type=F32,
    )
    sub = lax.broadcasted_iota(jnp.int32, (SUB, LANES), 0)
    lane = lax.broadcasted_iota(jnp.int32, (SUB, LANES), 1)
    members = LANES
    blocks = []
    for k in range(members // SUB):
        block = product[k * SUB:(k + 1) * SUB, :]
        blocks.append(block + jnp.where(lane - k * SUB == sub, members - 1.0, 0.0))
    proj = jnp.sum(product[members:members + SUB, :], axis=0, keepdims=True)
    blocks.append(jnp.broadcast_to(proj, (SUB, LANES)))
    inverse, weights = eliminate(blocks)
    flipped = jnp.concatenate(inverse, axis=0) * (members - 1.0) ** 0.5 - weights
    return flipped - jnp.mean(flipped, axis=-1, keepdims=True) + 1.0 / members


def exact_dot(a, b, contract_b):
    return lax.dot_general(
        a, b, (((1,), (contract_b,)), ((), ())), precision=lax.Precision.HIGHEST, preferred_element_type=F32
    )


def first_kernel(lat_count, lon_count, near_ref, pattern, later, map_ref, out_ref, moved):
    flipped = batch_map(0, lat_count, near_ref, pattern)
    map_ref[...] = flipped
    count = len(NEAR) ** 2
    moved[...] = exact_dot(later[pl.ds(0, count)].reshape(-1, LANES), flipped, 1).reshape(moved.shape)
    moved[count // 2] = moved[count // 2] - later[count]
    out_ref[...] = jnp.zeros_like(out_ref)
    my_lat, my_lon = (lax.axis_index("lat"), lax.axis_index("lon"))
    for n, dc in enumerate(NEAR):
        lon = lax.rem(my_lon + dc + lon_count, lon_count)
        for m, da in enumerate(NEAR):
            lat = my_lat + da

            @pl.when((lat >= 0) & (lat < lat_count))
            def _():
                out_ref[lat * lon_count + lon] = moved[n * len(NEAR) + m]


def last_kernel(lat_count, near_ref, pattern, map_ref, pad, out_ref, result, out_sem):
    parts = out_sem.shape[0]
    rows, cols = (pad.shape[0] - 4, pad.shape[1] - 2 * SUB)
    flipped = exact_dot(batch_map(1, lat_count, near_ref, pattern), map_ref[...], 0)
    high = flipped.astype(BF16)
    low = (flipped - high.astype(F32)).astype(BF16)
    right = jnp.concatenate(
        [jnp.concatenate([high, high], axis=1), jnp.concatenate([low, jnp.zeros_like(low)], axis=1)], axis=0
    )
    copies = []
    size = rows // parts
    for n in range(parts):
        part = pl.ds(n * size * cols, size * cols)
        value = pad[pl.ds(2 + n * size, size), pl.ds(SUB, cols), :].reshape(size * cols, LANES)
        upper = value.astype(BF16)
        rest = (value - upper.astype(F32)).astype(BF16)
        both = lax.dot_general(
            jnp.concatenate([upper, rest], axis=1), right, (((1,), (1,)), ((), ())), preferred_element_type=F32
        )
        result[part, :] = both[:, :LANES] + both[:, LANES:]
        copies.append(pltpu.make_async_copy(result.at[part], out_ref.at[part], out_sem.at[n]))
        copies[-1].start()
    for out_copy in copies:
        out_copy.wait()


def window(tiles, lat_count, lon_count):
    held = min(WIN, lat_count)
    if held == lat_count:
        return tiles
    start = jnp.clip(lax.axis_index("lat") - REACH, 0, lat_count - held)
    return lax.dynamic_slice_in_dim(tiles, start * lon_count, held * lon_count, axis=0)


def local(ensemble, observed, precision, interp_weight, stencil, owned, pattern):
    rows, cols, members = ensemble.shape
    batches = observed.shape[0]
    lat_count, lon_count = (lax.axis_size("lat"), lax.axis_size("lon"))
    tiles = lat_count * lon_count
    vmem = pl.BlockSpec(memory_space=pltpu.VMEM)
    anywhere = pl.BlockSpec(memory_space=pl.ANY)
    hbm = pl.BlockSpec(memory_space=pltpu.HBM)
    megabyte = 1024 * 1024

    def shape(*dims, dtype=F32):
        return jax.ShapeDtypeStruct(dims, dtype)

    def call(kernel, name, specs, out_shape, scratch, *operands, out_specs=None, limit=48):
        return pl.pallas_call(
            kernel,
            out_shape=out_shape,
            in_specs=specs,
            out_specs=out_specs or jax.tree.map(lambda _: vmem, out_shape),
            scratch_shapes=scratch,
            compiler_params=pltpu.CompilerParams(vmem_limit_bytes=limit * megabyte),
            name=name,
        )(*operands)

    def trade(blocks, axis):
        count, wraps = ((lon_count, True) if axis == "lon" else (lat_count, False))
        first, second = blocks
        second = swap(second, axis, 1, count, wraps)
        return [swap(first, axis, 0, count, wraps), second]

    def exchange(blocks):
        return lax.all_to_all(blocks, ("lat", "lon"), split_axis=0, concat_axis=0, tiled=True)

    small = (observed, precision, interp_weight, stencil, owned)
    side = shape(rows + SUB, members)
    mine, side_1, side_0 = call(
        functools.partial(start_kernel, cols + 2),
        "start",
        [hbm] * 6,
        (shape(batches, SUB, LANES), side, side),
        [pltpu.VMEM(array.shape, array.dtype) for array in small]
        + [pltpu.VMEM((rows, SUB, members), F32)] * 2
        + [pltpu.SemaphoreType.DMA((7,))],
        *small,
        ensemble,
        limit=63,
    )
    sides = trade((side_0, side_1), "lon")
    padded = shape(rows + 4, cols + 2 * SUB, members)
    pad = call(pad_kernel, "pad", [hbm], padded, [pltpu.SemaphoreType.DMA], ensemble)
    end = shape(cols + 3 * SUB, members)
    left, right, *ends = call(rows_kernel, "edge_rows", [vmem] * 4, (side, side, end, end), [], mine, *sides, pad)
    ends = trade(ends, "lat")
    slots = shape(tiles, PAIRS, 2, members, dtype=BF16)
    numbers = [pltpu.SMEM((SUB, LANES), F32), pltpu.SemaphoreType.DMA]
    block = shape(SUB, members)
    held_sides = pltpu.VMEM((2, rows + 2 * SUB, members), F32)
    own = call(row_kernel, "row_shares", [vmem] * 4, block, [held_sides] + numbers, mine, left, right, pad)
    blocks = call(
        functools.partial(prior_kernel, rows),
        "prior",
        [vmem] * 4,
        slots,
        [pltpu.VMEM((2,) + end.shape, F32), pltpu.VMEM((SUB, members), F32)] + numbers,
        mine,
        own,
        *ends,
    )
    near = window(exchange(blocks), lat_count, lon_count)
    count = len(NEAR) ** 2
    later = call(
        later_kernel,
        "later_shares",
        [vmem] * 6,
        shape(count + 1, SUB, members),
        [pltpu.SMEM((5, SUB, LANES), F32), pltpu.SemaphoreType.DMA((5,))],
        mine,
        left,
        right,
        *ends,
        pad,
    )
    first_map, shares = call(
        functools.partial(first_kernel, lat_count, lon_count),
        "first_batch",
        [vmem] * 3,
        (shape(members, members), shape(tiles, SUB, members)),
        [pltpu.VMEM((count, SUB, members), F32)],
        near,
        pattern,
        later,
    )
    blocks = call(meet_kernel, "own_block", [vmem], slots, [], exchange(shares))
    near = window(exchange(blocks), lat_count, lon_count)
    parts = 8
    result = call(
        functools.partial(last_kernel, lat_count),
        "second_batch",
        [vmem] * 4,
        shape(rows * cols, members),
        [
            pltpu.VMEM((rows * cols, members), F32),
            pltpu.SemaphoreType.DMA((parts,)),
        ],
        near,
        pattern,
        first_map,
        pad,
        out_specs=anywhere,
    )
    return result.reshape(rows, cols, members)


def solution(mesh):
    placed = (
        P("lat", "lon", None),
        P(None, "lat", "lon", None),
        P(None, "lat", "lon", None),
        P(None, "lat", "lon", None, None),
        P(None, "lat", "lon", None, None),
        P(None, "lat", "lon", None),
        P(None, "lat", "lon", None, None),
    )
    return jax.shard_map(
        local, mesh=mesh, in_specs=placed, out_specs=P("lat", "lon", None), check_vma=False
    )
```

```python
import functools
import jax
import jax.numpy as jnp
from jax import lax
from jax.experimental import pallas as pl
from jax.experimental.pallas import tpu as pltpu
from jax.sharding import PartitionSpec as P

REACH = 2
WIN = 2 * REACH + 1
SUB = 8
LANES = 128
NEAR = (-1, 0, 1)
AT_ROW, AT_COL, AT_OBS = (4, 5, 6)
PAIRS = SUB // 2 + 1
F32 = jnp.float32
BF16 = jnp.bfloat16


def partner(place, kind):
    return place + (1 if place % 2 == kind else -1)


def trade(blocks, axis):
    lat_count, lon_count = (lax.axis_size("lat"), lax.axis_size("lon"))
    results = []
    for turn, block in enumerate(blocks):
        route = []
        for lat in range(lat_count):
            for lon in range(lon_count):
                if axis == "lon":
                    to_lat, to_lon = (lat, partner(lon, turn) % lon_count)
                else:
                    to_lat, to_lon = (partner(lat, (turn + lon) % 2), lon)
                if 0 <= to_lat < lat_count:
                    route.append((lat * lon_count + lon, to_lat * lon_count + to_lon))
        results.append(lax.ppermute(block, ("lat", "lon"), route))
    return results


def is_even(axis):
    place = lax.axis_index("lon")
    if axis == "lat":
        place = place + lax.axis_index("lat")
    return lax.rem(place, 2) == 0


def start_kernel(
    width, observed, precision, weight, stencil, owned, cells, params_ref, sides_1, sides_0,
    observed_v, precision_v, weight_v, stencil_v, owned_v, left_v, right_v, sems
):
    batches, cols = (observed.shape[0], cells.shape[1])
    pairs = (
        (observed, observed_v),
        (precision, precision_v),
        (weight, weight_v),
        (stencil, stencil_v),
        (owned, owned_v),
        (cells.at[:, pl.ds(0, SUB)], left_v),
        (cells.at[:, pl.ds(cols - SUB, SUB)], right_v),
    )
    copies = [pltpu.make_async_copy(source, target, sems.at[n]) for n, (source, target) in enumerate(pairs)]
    for copy in copies:
        copy.start()
    for copy in copies:
        copy.wait()
    params_ref[...] = jnp.zeros_like(params_ref)
    for b in range(batches):
        root = jnp.sqrt(precision_v[b, 0]) * owned_v[b, 0].astype(F32)
        corner = stencil_v[b, 0, 0, pl.ds(0, 1)].astype(F32)
        row = jnp.floor((corner + 0.5) * (1.0 / width))
        params_ref[b, pl.ds(0, 4), pl.ds(0, SUB)] = weight_v[b, 0, 0] * root
        params_ref[b, pl.ds(AT_ROW, 1), pl.ds(0, SUB)] = row
        params_ref[b, pl.ds(AT_COL, 1), pl.ds(0, SUB)] = corner - row * width
        params_ref[b, pl.ds(AT_OBS, 1), pl.ds(0, SUB)] = observed_v[b, 0] * root
    rows = cells.shape[0]
    even = is_even("lon")
    left, right = (left_v[:, 0, :], right_v[:, SUB - 1, :])
    sides_0[pl.ds(0, rows), :] = jnp.where(even, right, left)
    sides_1[pl.ds(0, rows), :] = jnp.where(even, left, right)
    sides_0[pl.ds(rows, SUB), :] = params_ref[1]
    sides_1[pl.ds(rows, SUB), :] = params_ref[1]


def clear_rim(pad, rows, cols):
    edge = jnp.zeros((2, cols + 2 * SUB, LANES), F32)
    pad[pl.ds(0, 2)] = edge
    pad[pl.ds(rows + 2, 2)] = edge
    side = jnp.zeros((rows, SUB, LANES), F32)
    pad[pl.ds(2, rows), pl.ds(0, SUB)] = side
    pad[pl.ds(2, rows), pl.ds(SUB + cols, SUB)] = side


def share(pad, number, rows, cols, da, dc, o):
    row = number(AT_ROW, o).astype(jnp.int32) - 1 + da * rows
    col = number(AT_COL, o).astype(jnp.int32) - 1 + dc * cols
    row = jnp.clip(row, -2, rows) + 2
    col = jnp.clip(col, -2, cols) + SUB
    terms = [number(k, o) * pad[row + k // 2, pl.ds(col + k % 2, 1), :] for k in range(4)]
    return (terms[0] + terms[1]) + (terms[2] + terms[3])


def own_shift(number):
    sub = lax.broadcasted_iota(jnp.int32, (SUB, LANES), 0)
    shift = jnp.zeros((SUB, LANES), F32)
    for o in range(SUB):
        shift = jnp.where(sub == o, number(AT_OBS, o), shift)
    return shift


def pad_kernel(cells, pad, sem):
    rows, cols = (cells.shape[0], cells.shape[1])
    copy = pltpu.make_async_copy(cells, pad.at[pl.ds(2, rows), pl.ds(SUB, cols)], sem)
    copy.start()
    clear_rim(pad, rows, cols)
    copy.wait()


def hold_sides(left, right, sides):
    rows = left.shape[0] - SUB
    sides[...] = jnp.zeros_like(sides)
    sides[0, pl.ds(SUB, rows), :] = left[pl.ds(0, rows), :]
    sides[1, pl.ds(SUB, rows), :] = right[pl.ds(0, rows), :]


def side_share(sides, side, number, rows, cols, da, o):
    row = number(AT_ROW, o).astype(jnp.int32) - 1 + da * rows
    row = jnp.clip(row, -2, rows) + SUB
    used = number(AT_COL, o).astype(jnp.int32) == (0, cols)[side]
    terms = [jnp.where(used, number(side + 2 * k, o), 0.0) * sides[side, pl.ds(row + k, 1), :] for k in range(2)]
    return terms[0] + terms[1]


def send_block(value, out_ref):
    mean = jnp.mean(value, axis=-1, keepdims=True)
    sub = lax.broadcasted_iota(jnp.int32, (SUB, LANES), 0)
    lane = lax.broadcasted_iota(jnp.int32, (SUB, LANES), 1)
    innov = jnp.sum(jnp.where(lane == sub, -mean, 0.0), axis=0, keepdims=True)
    rows = jnp.concatenate([value - mean, jnp.broadcast_to(innov, (2, LANES))], axis=0).astype(BF16)
    for n in range(PAIRS):
        pair = rows[2 * n:2 * n + 2]
        out_ref[:, n] = jnp.broadcast_to(pair, (out_ref.shape[0],) + pair.shape)


def rows_kernel(mine, sides_0, sides_1, pad, left_ref, right_ref, out_0, out_1):
    rows, cols = (pad.shape[0] - 4, pad.shape[1] - 2 * SUB)
    even = is_even("lon")
    left_ref[...] = jnp.where(even, sides_1[...], sides_0[...])
    right_ref[...] = jnp.where(even, sides_0[...], sides_1[...])
    lane = lax.broadcasted_iota(jnp.int32, (SUB, LANES), 1)
    block = pl.ds(rows, SUB)
    packed = jnp.where(lane < SUB, left_ref[block, :], pltpu.roll(mine[1], SUB, 1))
    packed = jnp.where(lane < 2 * SUB, packed, pltpu.roll(right_ref[block, :], 2 * SUB, 1))
    even = is_even("lat")
    for kind, out in enumerate((out_0, out_1)):
        row = jnp.where(even, (1 - kind) * (rows - 1), kind * (rows - 1))
        out[pl.ds(0, SUB), :] = jnp.broadcast_to(left_ref[pl.ds(row, 1), :], (SUB, LANES))
        out[pl.ds(SUB, cols), :] = pad[2 + row, pl.ds(SUB, cols), :]
        out[pl.ds(SUB + cols, SUB), :] = jnp.broadcast_to(right_ref[pl.ds(row, 1), :], (SUB, LANES))
        out[pl.ds(2 * SUB + cols, SUB), :] = packed


def row_kernel(mine, left, right, pad, out_ref, sides, params, sem):
    rows, cols = (pad.shape[0] - 4, pad.shape[1] - 2 * SUB)
    copy = pltpu.make_async_copy(mine.at[0], params, sem)
    copy.start()
    hold_sides(left, right, sides)
    copy.wait()
    number = lambda kind, o: params[kind, o]
    for o in range(SUB):
        total = share(pad, number, rows, cols, 0, 0, o)
        for side in range(2):
            total = total + side_share(sides, side, number, rows, cols, 0, o)
        out_ref[pl.ds(o, 1), :] = total
    out_ref[...] = out_ref[...] - own_shift(number)


def prior_kernel(rows, mine, own, ends_0, ends_1, out_ref, ends, value, params, sem):
    copy = pltpu.make_async_copy(mine.at[0], params, sem)
    copy.start()
    even = is_even("lat")
    ends[0] = jnp.where(even, ends_1[...], ends_0[...])
    ends[1] = jnp.where(even, ends_0[...], ends_1[...])
    copy.wait()
    for o in range(SUB):
        row, col = (params[AT_ROW, o].astype(jnp.int32), params[AT_COL, o].astype(jnp.int32))
        total = own[pl.ds(o, 1), :]
        for n, at in enumerate((0, rows)):
            for k in range(2):
                weight = jnp.where(row == at, params[2 * n + k, o], 0.0)
                total = total + weight * ends[n, pl.ds(col + SUB - 1 + k, 1), :]
        value[pl.ds(o, 1), :] = total
    send_block(value[...], out_ref)


def meet_kernel(shares, out_ref):
    send_block(jnp.sum(shares[...], axis=0), out_ref)


def later_kernel(mine, left, right, ends_0, ends_1, pad, out_ref, params, sems):
    rows, cols = (pad.shape[0] - 4, pad.shape[1] - 2 * SUB)
    side, end = (pl.ds(rows, SUB), pl.ds(cols + 2 * SUB, SUB))
    sources = (left.at[side], mine.at[1], right.at[side], ends_0.at[end], ends_1.at[end])
    copies = []
    for n, source in enumerate(sources):
        copies.append(pltpu.make_async_copy(source, params.at[n], sems.at[n]))
        copies[-1].start()
    for copy in copies:
        copy.wait()
    even = is_even("lat")
    ends = {-1: jnp.where(even, 4, 3), 1: jnp.where(even, 3, 4)}
    for n, dc in enumerate(NEAR):
        for m, da in enumerate(NEAR):
            spot, lane = (n, 0) if da == 0 else (ends[da], n * SUB)
            number = lambda kind, o: params[spot, kind, lane + o]
            for o in range(SUB):
                out_ref[n * len(NEAR) + m, pl.ds(o, 1), :] = share(pad, number, rows, cols, da, dc, o)
    out_ref[len(NEAR) ** 2] = own_shift(lambda kind, o: params[1, kind, o])


def window_start(lat_count, my_lat):
    return 0 if lat_count <= WIN else jnp.clip(my_lat - REACH, 0, lat_count - WIN)


def row_of(block, j):
    return jnp.broadcast_to(block[j:j + 1, :], block.shape)


def column_of(block, j):
    return jnp.broadcast_to(block[:, j:j + 1], block.shape)


def reciprocal(value):
    guess = pl.reciprocal(value, approx=True)
    return guess * (2.0 - value * guess)


def pivot_rows(block, k, between):
    sub = lax.broadcasted_iota(jnp.int32, block.shape, 0)
    lane = lax.broadcasted_iota(jnp.int32, block.shape, 1) - k * SUB
    rows = [row_of(block, r) for r in range(SUB)]
    at = {(r, n): column_of(rows[r], k * SUB + n) for r in range(SUB) for n in range(r + 1)}
    here = (lane >= 0) & (lane < SUB)
    rows = [jnp.where(here, jnp.where(lane == r, 1.0, 0.0), row) for r, row in enumerate(rows)]
    inverse, scale = (jnp.zeros(block.shape, F32), jnp.ones(block.shape, F32))
    for j in range(0, SUB, 2):
        a, b, c = (at[j, j], at[j + 1, j], at[j + 1, j + 1])
        det = a * c - b * b
        over_det = reciprocal(det)
        top, bottom = (rows[j], rows[j + 1])
        rest = range(j + 2, SUB)
        upper = {n: (at[n, j], at[n, j + 1]) for n in rest}
        for r in rest:
            first = (at[r, j] * c - at[r, j + 1] * b) * over_det
            second = (at[r, j + 1] * a - at[r, j] * b) * over_det
            for n in range(j + 2, r + 1):
                at[r, n] = at[r, n] - (first * upper[n][0] + second * upper[n][1])
            rows[r] = rows[r] - (first * top + second * bottom)
        a_part, b_part, c_part = (a * over_det, b * over_det, c * over_det)
        for r in range(j):
            first = at[r, j] * c_part - at[r, j + 1] * b_part
            second = at[r, j + 1] * a_part - at[r, j] * b_part
            for n in rest:
                at[r, n] = at[r, n] - (first * upper[n][0] + second * upper[n][1])
            rows[r] = rows[r] - (first * top + second * bottom)
        for n in rest:
            at[j, n] = c_part * upper[n][0] - b_part * upper[n][1]
            at[j + 1, n] = a_part * upper[n][1] - b_part * upper[n][0]
        rows[j] = c_part * top - b_part * bottom
        rows[j + 1] = a_part * bottom - b_part * top
        inverse = jnp.where(sub == j, top, jnp.where(sub == j + 1, a * bottom - b * top, inverse))
        scale = jnp.where(sub == j, a, jnp.where(sub == j + 1, a * det, scale))
        between()
    return rows, jnp.where(lane < SUB, inverse * lax.rsqrt(scale), 0.0)


def eliminate(blocks):
    count = len(blocks) - 1
    blocks = list(blocks)
    lane = lax.broadcasted_iota(jnp.int32, blocks[0].shape, 1)
    inverse, waiting = ([], [])

    def update(i, k, pivot):
        terms = [column_of(blocks[i], k * SUB + j) * pivot[j] for j in range(SUB)]
        while len(terms) > 1:
            terms = [terms[n] + terms[n + 1] for n in range(0, len(terms), 2)]
        here = (lane >= k * SUB) & (lane < (k + 1) * SUB)
        blocks[i] = jnp.where(here, 0.0, blocks[i]) - terms[0]

    for k in range(count):
        share_of = -(-len(waiting) // 4)

        def between():
            for task in waiting[:share_of]:
                update(*task)
            del waiting[:share_of]

        pivot, rows = pivot_rows(blocks[k], k, between)
        update(k + 1, k, pivot)
        waiting = [(i, k, pivot) for i in range(k + 2, count + 1)]
        inverse.append(rows)
    return inverse, blocks[count][:1]


def batch_map(batch, lat_count, near_ref, pattern):
    held = min(WIN, lat_count)
    count = near_ref.shape[0]
    my_lat = lax.axis_index("lat")
    start = window_start(lat_count, my_lat)
    scaled = jnp.concatenate([near_ref[:, n].astype(F32) for n in range(PAIRS - 1)], axis=1)
    innov = near_ref[:, PAIRS - 1].astype(F32)[:, :1]
    sub = lax.broadcasted_iota(jnp.int32, scaled.shape, 1)
    lane = lax.broadcasted_iota(jnp.int32, scaled.shape, 2)
    innov = jnp.where(lane == sub, jnp.broadcast_to(innov, scaled.shape), 0.0)
    picked = []
    for j in range(held):
        offset = start + j - my_lat + REACH
        inside = (offset >= 0) & (offset < WIN)
        row = pattern[batch, 0, 0, pl.ds(jnp.clip(offset, 0, WIN - 1), 1), :].astype(F32)
        row = jnp.where(inside, row, 0.0)
        for e in range(count // held):
            picked.append(jnp.broadcast_to(row[:, e:e + 1], (1, SUB, LANES)))
    weighted = scaled * jnp.concatenate(picked, axis=0)
    both = jnp.concatenate([scaled, innov], axis=2).reshape(count * SUB, 2 * LANES).astype(BF16)
    product = lax.dot_general(
        both,
        weighted.reshape(count * SUB, LANES).astype(BF16),
        (((0,), (0,)), ((), ())),
        preferred_element_type=F32,
    )
    sub = lax.broadcasted_iota(jnp.int32, (SUB, LANES), 0)
    lane = lax.broadcasted_iota(jnp.int32, (SUB, LANES), 1)
    members = LANES
    blocks = []
    for k in range(members // SUB):
        block = product[k * SUB:(k + 1) * SUB, :]
        blocks.append(block + jnp.where(lane - k * SUB == sub, members - 1.0, 0.0))
    proj = jnp.sum(product[members:members + SUB, :], axis=0, keepdims=True)
    blocks.append(jnp.broadcast_to(proj, (SUB, LANES)))
    inverse, weights = eliminate(blocks)
    flipped = jnp.concatenate(inverse, axis=0) * (members - 1.0) ** 0.5 - weights
    return flipped - jnp.mean(flipped, axis=-1, keepdims=True) + 1.0 / members


def exact_dot(a, b, contract_b):
    return lax.dot_general(
        a, b, (((1,), (contract_b,)), ((), ())), precision=lax.Precision.HIGHEST, preferred_element_type=F32
    )


def first_kernel(lat_count, lon_count, near_ref, pattern, later, map_ref, out_ref, moved):
    flipped = batch_map(0, lat_count, near_ref, pattern)
    map_ref[...] = flipped
    count = len(NEAR) ** 2
    moved[...] = exact_dot(later[pl.ds(0, count)].reshape(-1, LANES), flipped, 1).reshape(moved.shape)
    moved[count // 2] = moved[count // 2] - later[count]
    out_ref[...] = jnp.zeros_like(out_ref)
    my_lat, my_lon = (lax.axis_index("lat"), lax.axis_index("lon"))
    for n, dc in enumerate(NEAR):
        lon = lax.rem(my_lon + dc + lon_count, lon_count)
        for m, da in enumerate(NEAR):
            lat = my_lat + da

            @pl.when((lat >= 0) & (lat < lat_count))
            def _():
                out_ref[lat * lon_count + lon] = moved[n * len(NEAR) + m]


def last_kernel(lat_count, near_ref, pattern, map_ref, pad, out_ref, result, out_sem):
    parts = out_sem.shape[0]
    rows, cols = (pad.shape[0] - 4, pad.shape[1] - 2 * SUB)
    flipped = exact_dot(batch_map(1, lat_count, near_ref, pattern), map_ref[...], 0)
    high = flipped.astype(BF16)
    low = (flipped - high.astype(F32)).astype(BF16)
    right = jnp.concatenate(
        [jnp.concatenate([high, high], axis=1), jnp.concatenate([low, jnp.zeros_like(low)], axis=1)], axis=0
    )
    copies = []
    size = rows // parts
    for n in range(parts):
        part = pl.ds(n * size * cols, size * cols)
        value = pad[pl.ds(2 + n * size, size), pl.ds(SUB, cols), :].reshape(size * cols, LANES)
        upper = value.astype(BF16)
        rest = (value - upper.astype(F32)).astype(BF16)
        both = lax.dot_general(
            jnp.concatenate([upper, rest], axis=1), right, (((1,), (1,)), ((), ())), preferred_element_type=F32
        )
        result[part, :] = both[:, :LANES] + both[:, LANES:]
        copies.append(pltpu.make_async_copy(result.at[part], out_ref.at[part], out_sem.at[n]))
        copies[-1].start()
    for out_copy in copies:
        out_copy.wait()


def window(tiles, lat_count, lon_count):
    held = min(WIN, lat_count)
    if held == lat_count:
        return tiles
    start = jnp.clip(lax.axis_index("lat") - REACH, 0, lat_count - held)
    return lax.dynamic_slice_in_dim(tiles, start * lon_count, held * lon_count, axis=0)


def local(ensemble, observed, precision, interp_weight, stencil, owned, pattern):
    rows, cols, members = ensemble.shape
    batches = observed.shape[0]
    lat_count, lon_count = (lax.axis_size("lat"), lax.axis_size("lon"))
    tiles = lat_count * lon_count
    vmem = pl.BlockSpec(memory_space=pltpu.VMEM)
    anywhere = pl.BlockSpec(memory_space=pl.ANY)
    hbm = pl.BlockSpec(memory_space=pltpu.HBM)
    megabyte = 1024 * 1024

    def shape(*dims, dtype=F32):
        return jax.ShapeDtypeStruct(dims, dtype)

    def call(kernel, name, specs, out_shape, scratch, *operands, out_specs=None, limit=48):
        return pl.pallas_call(
            kernel,
            out_shape=out_shape,
            in_specs=specs,
            out_specs=out_specs or jax.tree.map(lambda _: vmem, out_shape),
            scratch_shapes=scratch,
            compiler_params=pltpu.CompilerParams(vmem_limit_bytes=limit * megabyte),
            name=name,
        )(*operands)

    def exchange(blocks):
        return lax.all_to_all(blocks, ("lat", "lon"), split_axis=0, concat_axis=0, tiled=True)

    small = (observed, precision, interp_weight, stencil, owned)
    side = shape(rows + SUB, members)
    mine, side_1, side_0 = call(
        functools.partial(start_kernel, cols + 2),
        "start",
        [hbm] * 6,
        (shape(batches, SUB, LANES), side, side),
        [pltpu.VMEM(array.shape, array.dtype) for array in small]
        + [pltpu.VMEM((rows, SUB, members), F32)] * 2
        + [pltpu.SemaphoreType.DMA((7,))],
        *small,
        ensemble,
        limit=63,
    )
    sides = trade((side_0, side_1), "lon")
    padded = shape(rows + 4, cols + 2 * SUB, members)
    pad = call(pad_kernel, "pad", [hbm], padded, [pltpu.SemaphoreType.DMA], ensemble)
    end = shape(cols + 3 * SUB, members)
    left, right, *ends = call(rows_kernel, "edge_rows", [vmem] * 4, (side, side, end, end), [], mine, *sides, pad)
    ends = trade(ends, "lat")
    slots = shape(tiles, PAIRS, 2, members, dtype=BF16)
    numbers = [pltpu.SMEM((SUB, LANES), F32), pltpu.SemaphoreType.DMA]
    block = shape(SUB, members)
    held_sides = pltpu.VMEM((2, rows + 2 * SUB, members), F32)
    own = call(row_kernel, "row_shares", [vmem] * 4, block, [held_sides] + numbers, mine, left, right, pad)
    blocks = call(
        functools.partial(prior_kernel, rows),
        "prior",
        [vmem] * 4,
        slots,
        [pltpu.VMEM((2,) + end.shape, F32), pltpu.VMEM((SUB, members), F32)] + numbers,
        mine,
        own,
        *ends,
    )
    near = window(exchange(blocks), lat_count, lon_count)
    count = len(NEAR) ** 2
    later = call(
        later_kernel,
        "later_shares",
        [vmem] * 6,
        shape(count + 1, SUB, members),
        [pltpu.SMEM((5, SUB, LANES), F32), pltpu.SemaphoreType.DMA((5,))],
        mine,
        left,
        right,
        *ends,
        pad,
    )
    first_map, shares = call(
        functools.partial(first_kernel, lat_count, lon_count),
        "first_batch",
        [vmem] * 3,
        (shape(members, members), shape(tiles, SUB, members)),
        [pltpu.VMEM((count, SUB, members), F32)],
        near,
        pattern,
        later,
    )
    blocks = call(meet_kernel, "own_block", [vmem], slots, [], exchange(shares))
    near = window(exchange(blocks), lat_count, lon_count)
    parts = 8
    result = call(
        functools.partial(last_kernel, lat_count),
        "second_batch",
        [vmem] * 4,
        shape(rows * cols, members),
        [
            pltpu.VMEM((rows * cols, members), F32),
            pltpu.SemaphoreType.DMA((parts,)),
        ],
        near,
        pattern,
        first_map,
        pad,
        out_specs=anywhere,
    )
    return result.reshape(rows, cols, members)


def solution(mesh):
    placed = (
        P("lat", "lon", None),
        P(None, "lat", "lon", None),
        P(None, "lat", "lon", None),
        P(None, "lat", "lon", None, None),
        P(None, "lat", "lon", None, None),
        P(None, "lat", "lon", None),
        P(None, "lat", "lon", None, None),
    )
    return jax.shard_map(
        local, mesh=mesh, in_specs=placed, out_specs=P("lat", "lon", None), check_vma=False
    )
```

```python
import functools
import jax
import jax.numpy as jnp
from jax import lax
from jax.experimental import pallas as pl
from jax.experimental.pallas import tpu as pltpu
from jax.sharding import PartitionSpec as P

REACH = 2
WIN = 2 * REACH + 1
SUB = 8
LANES = 128
NEAR = (-1, 0, 1)
AT_ROW, AT_COL, AT_OBS = (4, 5, 6)
PAIRS = SUB // 2 + 1
F32 = jnp.float32
BF16 = jnp.bfloat16


def partner(place, turn):
    return place + (-1 if place % 2 == turn else 1)


def trade(blocks, axis, wraps):
    count = lax.axis_size(axis)
    results = []
    for turn, block in enumerate(blocks):
        route = [(place, partner(place, turn)) for place in range(count)]
        route = [(source, target % count) for source, target in route if wraps or 0 <= target < count]
        results.append(lax.ppermute(block, axis, route))
    return results


def next_first(axis):
    return lax.rem(lax.axis_index(axis), 2) == 1


def start_kernel(
    width, observed, precision, weight, stencil, owned, cells, params_ref, sides_1, sides_0,
    observed_v, precision_v, weight_v, stencil_v, owned_v, left_v, right_v, sems
):
    batches, cols = (observed.shape[0], cells.shape[1])
    pairs = (
        (observed, observed_v),
        (precision, precision_v),
        (weight, weight_v),
        (stencil, stencil_v),
        (owned, owned_v),
        (cells.at[:, pl.ds(0, SUB)], left_v),
        (cells.at[:, pl.ds(cols - SUB, SUB)], right_v),
    )
    copies = [pltpu.make_async_copy(source, target, sems.at[n]) for n, (source, target) in enumerate(pairs)]
    for copy in copies:
        copy.start()
    for copy in copies:
        copy.wait()
    params_ref[...] = jnp.zeros_like(params_ref)
    for b in range(batches):
        root = jnp.sqrt(precision_v[b, 0]) * owned_v[b, 0].astype(F32)
        corner = stencil_v[b, 0, 0, pl.ds(0, 1)].astype(F32)
        row = jnp.floor((corner + 0.5) * (1.0 / width))
        params_ref[b, pl.ds(0, 4), pl.ds(0, SUB)] = weight_v[b, 0, 0] * root
        params_ref[b, pl.ds(AT_ROW, 1), pl.ds(0, SUB)] = row
        params_ref[b, pl.ds(AT_COL, 1), pl.ds(0, SUB)] = corner - row * width
        params_ref[b, pl.ds(AT_OBS, 1), pl.ds(0, SUB)] = observed_v[b, 0] * root
    rows = cells.shape[0]
    forward = next_first("lon")
    left, right = (left_v[:, 0, :], right_v[:, SUB - 1, :])
    sides_0[pl.ds(0, rows), :] = jnp.where(forward, right, left)
    sides_1[pl.ds(0, rows), :] = jnp.where(forward, left, right)
    sides_0[pl.ds(rows, SUB), :] = params_ref[1]
    sides_1[pl.ds(rows, SUB), :] = params_ref[1]


def clear_rim(pad, rows, cols):
    edge = jnp.zeros((2, cols + 2 * SUB, LANES), F32)
    pad[pl.ds(0, 2)] = edge
    pad[pl.ds(rows + 2, 2)] = edge
    side = jnp.zeros((rows, SUB, LANES), F32)
    pad[pl.ds(2, rows), pl.ds(0, SUB)] = side
    pad[pl.ds(2, rows), pl.ds(SUB + cols, SUB)] = side


def share(pad, number, rows, cols, da, dc, o):
    row = number(AT_ROW, o).astype(jnp.int32) - 1 + da * rows
    col = number(AT_COL, o).astype(jnp.int32) - 1 + dc * cols
    row = jnp.clip(row, -2, rows) + 2
    col = jnp.clip(col, -2, cols) + SUB
    terms = [number(k, o) * pad[row + k // 2, pl.ds(col + k % 2, 1), :] for k in range(4)]
    return (terms[0] + terms[1]) + (terms[2] + terms[3])


def own_shift(number):
    sub = lax.broadcasted_iota(jnp.int32, (SUB, LANES), 0)
    shift = jnp.zeros((SUB, LANES), F32)
    for o in range(SUB):
        shift = jnp.where(sub == o, number(AT_OBS, o), shift)
    return shift


def pad_kernel(cells, pad, sem):
    rows, cols = (cells.shape[0], cells.shape[1])
    copy = pltpu.make_async_copy(cells, pad.at[pl.ds(2, rows), pl.ds(SUB, cols)], sem)
    copy.start()
    clear_rim(pad, rows, cols)
    copy.wait()


def hold_sides(left, right, sides):
    rows = left.shape[0] - SUB
    sides[...] = jnp.zeros_like(sides)
    sides[0, pl.ds(SUB, rows), :] = left[pl.ds(0, rows), :]
    sides[1, pl.ds(SUB, rows), :] = right[pl.ds(0, rows), :]


def side_share(sides, side, number, rows, cols, da, o):
    row = number(AT_ROW, o).astype(jnp.int32) - 1 + da * rows
    row = jnp.clip(row, -2, rows) + SUB
    used = number(AT_COL, o).astype(jnp.int32) == (0, cols)[side]
    terms = [jnp.where(used, number(side + 2 * k, o), 0.0) * sides[side, pl.ds(row + k, 1), :] for k in range(2)]
    return terms[0] + terms[1]


def send_block(value, out_ref):
    mean = jnp.mean(value, axis=-1, keepdims=True)
    sub = lax.broadcasted_iota(jnp.int32, (SUB, LANES), 0)
    lane = lax.broadcasted_iota(jnp.int32, (SUB, LANES), 1)
    innov = jnp.sum(jnp.where(lane == sub, -mean, 0.0), axis=0, keepdims=True)
    rows = jnp.concatenate([value - mean, jnp.broadcast_to(innov, (2, LANES))], axis=0).astype(BF16)
    for n in range(PAIRS):
        pair = rows[2 * n:2 * n + 2]
        out_ref[:, n] = jnp.broadcast_to(pair, (out_ref.shape[0],) + pair.shape)


def rows_kernel(mine, sides_0, sides_1, pad, left_ref, right_ref, out_0, out_1):
    rows, cols = (pad.shape[0] - 4, pad.shape[1] - 2 * SUB)
    forward = next_first("lon")
    left_ref[...] = jnp.where(forward, sides_1[...], sides_0[...])
    right_ref[...] = jnp.where(forward, sides_0[...], sides_1[...])
    lane = lax.broadcasted_iota(jnp.int32, (SUB, LANES), 1)
    block = pl.ds(rows, SUB)
    packed = jnp.where(lane < SUB, left_ref[block, :], pltpu.roll(mine[1], SUB, 1))
    packed = jnp.where(lane < 2 * SUB, packed, pltpu.roll(right_ref[block, :], 2 * SUB, 1))
    forward = next_first("lat")
    for turn, out in enumerate((out_0, out_1)):
        row = jnp.where(forward, (1 - turn) * (rows - 1), turn * (rows - 1))
        out[pl.ds(0, SUB), :] = jnp.broadcast_to(left_ref[pl.ds(row, 1), :], (SUB, LANES))
        out[pl.ds(SUB, cols), :] = pad[2 + row, pl.ds(SUB, cols), :]
        out[pl.ds(SUB + cols, SUB), :] = jnp.broadcast_to(right_ref[pl.ds(row, 1), :], (SUB, LANES))
        out[pl.ds(2 * SUB + cols, SUB), :] = packed


def row_kernel(mine, left, right, pad, out_ref, sides, params, sem):
    rows, cols = (pad.shape[0] - 4, pad.shape[1] - 2 * SUB)
    copy = pltpu.make_async_copy(mine.at[0], params, sem)
    copy.start()
    hold_sides(left, right, sides)
    copy.wait()
    number = lambda kind, o: params[kind, o]
    for o in range(SUB):
        total = share(pad, number, rows, cols, 0, 0, o)
        for side in range(2):
            total = total + side_share(sides, side, number, rows, cols, 0, o)
        out_ref[pl.ds(o, 1), :] = total
    out_ref[...] = out_ref[...] - own_shift(number)


def prior_kernel(rows, mine, own, ends_0, ends_1, out_ref, ends, value, params, sem):
    copy = pltpu.make_async_copy(mine.at[0], params, sem)
    copy.start()
    forward = next_first("lat")
    ends[0] = jnp.where(forward, ends_1[...], ends_0[...])
    ends[1] = jnp.where(forward, ends_0[...], ends_1[...])
    copy.wait()
    for o in range(SUB):
        row, col = (params[AT_ROW, o].astype(jnp.int32), params[AT_COL, o].astype(jnp.int32))
        total = own[pl.ds(o, 1), :]
        for n, at in enumerate((0, rows)):
            for k in range(2):
                weight = jnp.where(row == at, params[2 * n + k, o], 0.0)
                total = total + weight * ends[n, pl.ds(col + SUB - 1 + k, 1), :]
        value[pl.ds(o, 1), :] = total
    send_block(value[...], out_ref)


def meet_kernel(shares, out_ref):
    send_block(jnp.sum(shares[...], axis=0), out_ref)


def later_kernel(mine, left, right, ends_0, ends_1, pad, out_ref, params, sems):
    rows, cols = (pad.shape[0] - 4, pad.shape[1] - 2 * SUB)
    side, end = (pl.ds(rows, SUB), pl.ds(cols + 2 * SUB, SUB))
    sources = (left.at[side], mine.at[1], right.at[side], ends_0.at[end], ends_1.at[end])
    copies = []
    for n, source in enumerate(sources):
        copies.append(pltpu.make_async_copy(source, params.at[n], sems.at[n]))
        copies[-1].start()
    for copy in copies:
        copy.wait()
    forward = next_first("lat")
    ends = {-1: jnp.where(forward, 4, 3), 1: jnp.where(forward, 3, 4)}
    for n, dc in enumerate(NEAR):
        for m, da in enumerate(NEAR):
            spot, lane = (n, 0) if da == 0 else (ends[da], n * SUB)
            number = lambda kind, o: params[spot, kind, lane + o]
            for o in range(SUB):
                out_ref[n * len(NEAR) + m, pl.ds(o, 1), :] = share(pad, number, rows, cols, da, dc, o)
    out_ref[len(NEAR) ** 2] = own_shift(lambda kind, o: params[1, kind, o])


def window_start(lat_count, my_lat):
    return 0 if lat_count <= WIN else jnp.clip(my_lat - REACH, 0, lat_count - WIN)


def row_of(block, j):
    return jnp.broadcast_to(block[j:j + 1, :], block.shape)


def column_of(block, j):
    return jnp.broadcast_to(block[:, j:j + 1], block.shape)


def reciprocal(value):
    guess = pl.reciprocal(value, approx=True)
    return guess * (2.0 - value * guess)


def pivot_rows(block, k, between):
    sub = lax.broadcasted_iota(jnp.int32, block.shape, 0)
    lane = lax.broadcasted_iota(jnp.int32, block.shape, 1) - k * SUB
    rows = [row_of(block, r) for r in range(SUB)]
    at = {(r, n): column_of(rows[r], k * SUB + n) for r in range(SUB) for n in range(r + 1)}
    here = (lane >= 0) & (lane < SUB)
    rows = [jnp.where(here, jnp.where(lane == r, 1.0, 0.0), row) for r, row in enumerate(rows)]
    inverse, scale = (jnp.zeros(block.shape, F32), jnp.ones(block.shape, F32))
    for j in range(0, SUB, 2):
        a, b, c = (at[j, j], at[j + 1, j], at[j + 1, j + 1])
        det = a * c - b * b
        over_det = reciprocal(det)
        top, bottom = (rows[j], rows[j + 1])
        rest = range(j + 2, SUB)
        upper = {n: (at[n, j], at[n, j + 1]) for n in rest}
        for r in rest:
            first = (at[r, j] * c - at[r, j + 1] * b) * over_det
            second = (at[r, j + 1] * a - at[r, j] * b) * over_det
            for n in range(j + 2, r + 1):
                at[r, n] = at[r, n] - (first * upper[n][0] + second * upper[n][1])
            rows[r] = rows[r] - (first * top + second * bottom)
        a_part, b_part, c_part = (a * over_det, b * over_det, c * over_det)
        for r in range(j):
            first = at[r, j] * c_part - at[r, j + 1] * b_part
            second = at[r, j + 1] * a_part - at[r, j] * b_part
            for n in rest:
                at[r, n] = at[r, n] - (first * upper[n][0] + second * upper[n][1])
            rows[r] = rows[r] - (first * top + second * bottom)
        for n in rest:
            at[j, n] = c_part * upper[n][0] - b_part * upper[n][1]
            at[j + 1, n] = a_part * upper[n][1] - b_part * upper[n][0]
        rows[j] = c_part * top - b_part * bottom
        rows[j + 1] = a_part * bottom - b_part * top
        inverse = jnp.where(sub == j, top, jnp.where(sub == j + 1, a * bottom - b * top, inverse))
        scale = jnp.where(sub == j, a, jnp.where(sub == j + 1, a * det, scale))
        between()
    return rows, jnp.where(lane < SUB, inverse * lax.rsqrt(scale), 0.0)


def eliminate(blocks):
    count = len(blocks) - 1
    blocks = list(blocks)
    lane = lax.broadcasted_iota(jnp.int32, blocks[0].shape, 1)
    inverse, waiting = ([], [])

    def update(i, k, pivot):
        terms = [column_of(blocks[i], k * SUB + j) * pivot[j] for j in range(SUB)]
        while len(terms) > 1:
            terms = [terms[n] + terms[n + 1] for n in range(0, len(terms), 2)]
        here = (lane >= k * SUB) & (lane < (k + 1) * SUB)
        blocks[i] = jnp.where(here, 0.0, blocks[i]) - terms[0]

    for k in range(count):
        share_of = -(-len(waiting) // 4)

        def between():
            for task in waiting[:share_of]:
                update(*task)
            del waiting[:share_of]

        pivot, rows = pivot_rows(blocks[k], k, between)
        update(k + 1, k, pivot)
        waiting = [(i, k, pivot) for i in range(k + 2, count + 1)]
        inverse.append(rows)
    return inverse, blocks[count][:1]


def batch_map(batch, lat_count, near_ref, pattern):
    held = min(WIN, lat_count)
    count = near_ref.shape[0]
    my_lat = lax.axis_index("lat")
    start = window_start(lat_count, my_lat)
    scaled = jnp.concatenate([near_ref[:, n].astype(F32) for n in range(PAIRS - 1)], axis=1)
    innov = near_ref[:, PAIRS - 1].astype(F32)[:, :1]
    sub = lax.broadcasted_iota(jnp.int32, scaled.shape, 1)
    lane = lax.broadcasted_iota(jnp.int32, scaled.shape, 2)
    innov = jnp.where(lane == sub, jnp.broadcast_to(innov, scaled.shape), 0.0)
    picked = []
    for j in range(held):
        offset = start + j - my_lat + REACH
        inside = (offset >= 0) & (offset < WIN)
        row = pattern[batch, 0, 0, pl.ds(jnp.clip(offset, 0, WIN - 1), 1), :].astype(F32)
        row = jnp.where(inside, row, 0.0)
        for e in range(count // held):
            picked.append(jnp.broadcast_to(row[:, e:e + 1], (1, SUB, LANES)))
    weighted = scaled * jnp.concatenate(picked, axis=0)
    both = jnp.concatenate([scaled, innov], axis=2).reshape(count * SUB, 2 * LANES).astype(BF16)
    product = lax.dot_general(
        both,
        weighted.reshape(count * SUB, LANES).astype(BF16),
        (((0,), (0,)), ((), ())),
        preferred_element_type=F32,
    )
    sub = lax.broadcasted_iota(jnp.int32, (SUB, LANES), 0)
    lane = lax.broadcasted_iota(jnp.int32, (SUB, LANES), 1)
    members = LANES
    blocks = []
    for k in range(members // SUB):
        block = product[k * SUB:(k + 1) * SUB, :]
        blocks.append(block + jnp.where(lane - k * SUB == sub, members - 1.0, 0.0))
    proj = jnp.sum(product[members:members + SUB, :], axis=0, keepdims=True)
    blocks.append(jnp.broadcast_to(proj, (SUB, LANES)))
    inverse, weights = eliminate(blocks)
    flipped = jnp.concatenate(inverse, axis=0) * (members - 1.0) ** 0.5 - weights
    return flipped - jnp.mean(flipped, axis=-1, keepdims=True) + 1.0 / members


def exact_dot(a, b, contract_b):
    return lax.dot_general(
        a, b, (((1,), (contract_b,)), ((), ())), precision=lax.Precision.HIGHEST, preferred_element_type=F32
    )


def first_kernel(lat_count, lon_count, near_ref, pattern, later, map_ref, out_ref, moved):
    flipped = batch_map(0, lat_count, near_ref, pattern)
    map_ref[...] = flipped
    count = len(NEAR) ** 2
    moved[...] = exact_dot(later[pl.ds(0, count)].reshape(-1, LANES), flipped, 1).reshape(moved.shape)
    moved[count // 2] = moved[count // 2] - later[count]
    out_ref[...] = jnp.zeros_like(out_ref)
    my_lat, my_lon = (lax.axis_index("lat"), lax.axis_index("lon"))
    for n, dc in enumerate(NEAR):
        lon = lax.rem(my_lon + dc + lon_count, lon_count)
        for m, da in enumerate(NEAR):
            lat = my_lat + da

            @pl.when((lat >= 0) & (lat < lat_count))
            def _():
                out_ref[lat * lon_count + lon] = moved[n * len(NEAR) + m]


def last_kernel(lat_count, near_ref, pattern, map_ref, pad, out_ref, result, out_sem):
    parts = out_sem.shape[0]
    rows, cols = (pad.shape[0] - 4, pad.shape[1] - 2 * SUB)
    flipped = exact_dot(batch_map(1, lat_count, near_ref, pattern), map_ref[...], 0)
    high = flipped.astype(BF16)
    low = (flipped - high.astype(F32)).astype(BF16)
    right = jnp.concatenate(
        [jnp.concatenate([high, high], axis=1), jnp.concatenate([low, jnp.zeros_like(low)], axis=1)], axis=0
    )
    copies = []
    size = rows // parts
    for n in range(parts):
        part = pl.ds(n * size * cols, size * cols)
        value = pad[pl.ds(2 + n * size, size), pl.ds(SUB, cols), :].reshape(size * cols, LANES)
        upper = value.astype(BF16)
        rest = (value - upper.astype(F32)).astype(BF16)
        both = lax.dot_general(
            jnp.concatenate([upper, rest], axis=1), right, (((1,), (1,)), ((), ())), preferred_element_type=F32
        )
        result[part, :] = both[:, :LANES] + both[:, LANES:]
        copies.append(pltpu.make_async_copy(result.at[part], out_ref.at[part], out_sem.at[n]))
        copies[-1].start()
    for out_copy in copies:
        out_copy.wait()


def window(tiles, lat_count, lon_count):
    held = min(WIN, lat_count)
    if held == lat_count:
        return tiles
    start = jnp.clip(lax.axis_index("lat") - REACH, 0, lat_count - held)
    return lax.dynamic_slice_in_dim(tiles, start * lon_count, held * lon_count, axis=0)


def local(ensemble, observed, precision, interp_weight, stencil, owned, pattern):
    rows, cols, members = ensemble.shape
    batches = observed.shape[0]
    lat_count, lon_count = (lax.axis_size("lat"), lax.axis_size("lon"))
    tiles = lat_count * lon_count
    vmem = pl.BlockSpec(memory_space=pltpu.VMEM)
    anywhere = pl.BlockSpec(memory_space=pl.ANY)
    hbm = pl.BlockSpec(memory_space=pltpu.HBM)
    megabyte = 1024 * 1024

    def shape(*dims, dtype=F32):
        return jax.ShapeDtypeStruct(dims, dtype)

    def call(kernel, name, specs, out_shape, scratch, *operands, out_specs=None, limit=48):
        return pl.pallas_call(
            kernel,
            out_shape=out_shape,
            in_specs=specs,
            out_specs=out_specs or jax.tree.map(lambda _: vmem, out_shape),
            scratch_shapes=scratch,
            compiler_params=pltpu.CompilerParams(vmem_limit_bytes=limit * megabyte),
            name=name,
        )(*operands)

    def exchange(blocks):
        return lax.all_to_all(blocks, ("lat", "lon"), split_axis=0, concat_axis=0, tiled=True)

    small = (observed, precision, interp_weight, stencil, owned)
    side = shape(rows + SUB, members)
    mine, side_1, side_0 = call(
        functools.partial(start_kernel, cols + 2),
        "start",
        [hbm] * 6,
        (shape(batches, SUB, LANES), side, side),
        [pltpu.VMEM(array.shape, array.dtype) for array in small]
        + [pltpu.VMEM((rows, SUB, members), F32)] * 2
        + [pltpu.SemaphoreType.DMA((7,))],
        *small,
        ensemble,
        limit=63,
    )
    sides = trade((side_0, side_1), "lon", True)
    padded = shape(rows + 4, cols + 2 * SUB, members)
    pad = call(pad_kernel, "pad", [hbm], padded, [pltpu.SemaphoreType.DMA], ensemble)
    end = shape(cols + 3 * SUB, members)
    left, right, *ends = call(rows_kernel, "edge_rows", [vmem] * 4, (side, side, end, end), [], mine, *sides, pad)
    ends = trade(ends, "lat", False)
    slots = shape(tiles, PAIRS, 2, members, dtype=BF16)
    numbers = [pltpu.SMEM((SUB, LANES), F32), pltpu.SemaphoreType.DMA]
    block = shape(SUB, members)
    held_sides = pltpu.VMEM((2, rows + 2 * SUB, members), F32)
    own = call(row_kernel, "row_shares", [vmem] * 4, block, [held_sides] + numbers, mine, left, right, pad)
    blocks = call(
        functools.partial(prior_kernel, rows),
        "prior",
        [vmem] * 4,
        slots,
        [pltpu.VMEM((2,) + end.shape, F32), pltpu.VMEM((SUB, members), F32)] + numbers,
        mine,
        own,
        *ends,
    )
    near = window(exchange(blocks), lat_count, lon_count)
    count = len(NEAR) ** 2
    later = call(
        later_kernel,
        "later_shares",
        [vmem] * 6,
        shape(count + 1, SUB, members),
        [pltpu.SMEM((5, SUB, LANES), F32), pltpu.SemaphoreType.DMA((5,))],
        mine,
        left,
        right,
        *ends,
        pad,
    )
    first_map, shares = call(
        functools.partial(first_kernel, lat_count, lon_count),
        "first_batch",
        [vmem] * 3,
        (shape(members, members), shape(tiles, SUB, members)),
        [pltpu.VMEM((count, SUB, members), F32)],
        near,
        pattern,
        later,
    )
    blocks = call(meet_kernel, "own_block", [vmem], slots, [], exchange(shares))
    near = window(exchange(blocks), lat_count, lon_count)
    parts = 8
    result = call(
        functools.partial(last_kernel, lat_count),
        "second_batch",
        [vmem] * 4,
        shape(rows * cols, members),
        [
            pltpu.VMEM((rows * cols, members), F32),
            pltpu.SemaphoreType.DMA((parts,)),
        ],
        near,
        pattern,
        first_map,
        pad,
        out_specs=anywhere,
    )
    return result.reshape(rows, cols, members)


def solution(mesh):
    placed = (
        P("lat", "lon", None),
        P(None, "lat", "lon", None),
        P(None, "lat", "lon", None),
        P(None, "lat", "lon", None, None),
        P(None, "lat", "lon", None, None),
        P(None, "lat", "lon", None),
        P(None, "lat", "lon", None, None),
    )
    return jax.shard_map(
        local, mesh=mesh, in_specs=placed, out_specs=P("lat", "lon", None), check_vma=False
    )
```

```python
import functools
import jax
import jax.numpy as jnp
from jax import lax
from jax.experimental import pallas as pl
from jax.experimental.pallas import tpu as pltpu
from jax.sharding import PartitionSpec as P

REACH = 2
WIN = 2 * REACH + 1
SUB = 8
LANES = 128
NEAR = (-1, 0, 1)
AT_ROW, AT_COL, AT_OBS = (4, 5, 6)
PAIRS = SUB // 2 + 1
F32 = jnp.float32
BF16 = jnp.bfloat16
LON = ("far", "core")


def partner(place, turn):
    return place + (-1 if place % 2 == turn else 1)


def trade(blocks, axis, wraps):
    count = lax.axis_size(axis)
    results = []
    for turn, block in enumerate(blocks):
        route = [(place, partner(place, turn)) for place in range(count)]
        route = [(source, target % count) for source, target in route if wraps or 0 <= target < count]
        results.append(lax.ppermute(block, axis, route))
    return results


def next_first(axis):
    return lax.rem(lax.axis_index(axis), 2) == 1


def start_kernel(
    width, observed, precision, weight, stencil, owned, cells, params_ref, sides_1, sides_0,
    observed_v, precision_v, weight_v, stencil_v, owned_v, left_v, right_v, sems
):
    batches, cols = (observed.shape[0], cells.shape[1])
    pairs = (
        (observed, observed_v),
        (precision, precision_v),
        (weight, weight_v),
        (stencil, stencil_v),
        (owned, owned_v),
        (cells.at[:, pl.ds(0, SUB)], left_v),
        (cells.at[:, pl.ds(cols - SUB, SUB)], right_v),
    )
    copies = [pltpu.make_async_copy(source, target, sems.at[n]) for n, (source, target) in enumerate(pairs)]
    for copy in copies:
        copy.start()
    for copy in copies:
        copy.wait()
    params_ref[...] = jnp.zeros_like(params_ref)
    for b in range(batches):
        root = jnp.sqrt(precision_v[b, 0]) * owned_v[b, 0].astype(F32)
        corner = stencil_v[b, 0, 0, pl.ds(0, 1)].astype(F32)
        row = jnp.floor((corner + 0.5) * (1.0 / width))
        params_ref[b, pl.ds(0, 4), pl.ds(0, SUB)] = weight_v[b, 0, 0] * root
        params_ref[b, pl.ds(AT_ROW, 1), pl.ds(0, SUB)] = row
        params_ref[b, pl.ds(AT_COL, 1), pl.ds(0, SUB)] = corner - row * width
        params_ref[b, pl.ds(AT_OBS, 1), pl.ds(0, SUB)] = observed_v[b, 0] * root
    rows = cells.shape[0]
    forward = next_first("core")
    left, right = (left_v[:, 0, :], right_v[:, SUB - 1, :])
    sides_0[pl.ds(0, rows), :] = jnp.where(forward, right, left)
    sides_1[pl.ds(0, rows), :] = jnp.where(forward, left, right)
    sides_0[pl.ds(rows, SUB), :] = params_ref[1]
    sides_1[pl.ds(rows, SUB), :] = params_ref[1]


def clear_rim(pad, rows, cols):
    edge = jnp.zeros((2, cols + 2 * SUB, LANES), F32)
    pad[pl.ds(0, 2)] = edge
    pad[pl.ds(rows + 2, 2)] = edge
    side = jnp.zeros((rows, SUB, LANES), F32)
    pad[pl.ds(2, rows), pl.ds(0, SUB)] = side
    pad[pl.ds(2, rows), pl.ds(SUB + cols, SUB)] = side


def share(pad, number, rows, cols, da, dc, o):
    row = number(AT_ROW, o).astype(jnp.int32) - 1 + da * rows
    col = number(AT_COL, o).astype(jnp.int32) - 1 + dc * cols
    row = jnp.clip(row, -2, rows) + 2
    col = jnp.clip(col, -2, cols) + SUB
    terms = [number(k, o) * pad[row + k // 2, pl.ds(col + k % 2, 1), :] for k in range(4)]
    return (terms[0] + terms[1]) + (terms[2] + terms[3])


def own_shift(number):
    sub = lax.broadcasted_iota(jnp.int32, (SUB, LANES), 0)
    shift = jnp.zeros((SUB, LANES), F32)
    for o in range(SUB):
        shift = jnp.where(sub == o, number(AT_OBS, o), shift)
    return shift


def pad_kernel(cells, pad, sem):
    rows, cols = (cells.shape[0], cells.shape[1])
    copy = pltpu.make_async_copy(cells, pad.at[pl.ds(2, rows), pl.ds(SUB, cols)], sem)
    copy.start()
    clear_rim(pad, rows, cols)
    copy.wait()


def hold_sides(left, right, sides):
    rows = left.shape[0] - SUB
    sides[...] = jnp.zeros_like(sides)
    sides[0, pl.ds(SUB, rows), :] = left[pl.ds(0, rows), :]
    sides[1, pl.ds(SUB, rows), :] = right[pl.ds(0, rows), :]


def side_share(sides, side, number, rows, cols, da, o):
    row = number(AT_ROW, o).astype(jnp.int32) - 1 + da * rows
    row = jnp.clip(row, -2, rows) + SUB
    used = number(AT_COL, o).astype(jnp.int32) == (0, cols)[side]
    terms = [jnp.where(used, number(side + 2 * k, o), 0.0) * sides[side, pl.ds(row + k, 1), :] for k in range(2)]
    return terms[0] + terms[1]


def send_block(value, out_ref):
    mean = jnp.mean(value, axis=-1, keepdims=True)
    sub = lax.broadcasted_iota(jnp.int32, (SUB, LANES), 0)
    lane = lax.broadcasted_iota(jnp.int32, (SUB, LANES), 1)
    innov = jnp.sum(jnp.where(lane == sub, -mean, 0.0), axis=0, keepdims=True)
    rows = jnp.concatenate([value - mean, jnp.broadcast_to(innov, (2, LANES))], axis=0).astype(BF16)
    for n in range(PAIRS):
        pair = rows[2 * n:2 * n + 2]
        out_ref[:, n] = jnp.broadcast_to(pair, (out_ref.shape[0],) + pair.shape)


def rows_kernel(mine, sides_0, sides_1, pad, left_ref, right_ref, out_0, out_1):
    rows, cols = (pad.shape[0] - 4, pad.shape[1] - 2 * SUB)
    forward = next_first("core")
    left_ref[...] = jnp.where(forward, sides_1[...], sides_0[...])
    right_ref[...] = jnp.where(forward, sides_0[...], sides_1[...])
    lane = lax.broadcasted_iota(jnp.int32, (SUB, LANES), 1)
    block = pl.ds(rows, SUB)
    packed = jnp.where(lane < SUB, left_ref[block, :], pltpu.roll(mine[1], SUB, 1))
    packed = jnp.where(lane < 2 * SUB, packed, pltpu.roll(right_ref[block, :], 2 * SUB, 1))
    forward = next_first("lat")
    for turn, out in enumerate((out_0, out_1)):
        row = jnp.where(forward, (1 - turn) * (rows - 1), turn * (rows - 1))
        out[pl.ds(0, SUB), :] = jnp.broadcast_to(left_ref[pl.ds(row, 1), :], (SUB, LANES))
        out[pl.ds(SUB, cols), :] = pad[2 + row, pl.ds(SUB, cols), :]
        out[pl.ds(SUB + cols, SUB), :] = jnp.broadcast_to(right_ref[pl.ds(row, 1), :], (SUB, LANES))
        out[pl.ds(2 * SUB + cols, SUB), :] = packed


def row_kernel(mine, left, right, pad, out_ref, sides, params, sem):
    rows, cols = (pad.shape[0] - 4, pad.shape[1] - 2 * SUB)
    copy = pltpu.make_async_copy(mine.at[0], params, sem)
    copy.start()
    hold_sides(left, right, sides)
    copy.wait()
    number = lambda kind, o: params[kind, o]
    for o in range(SUB):
        total = share(pad, number, rows, cols, 0, 0, o)
        for side in range(2):
            total = total + side_share(sides, side, number, rows, cols, 0, o)
        out_ref[pl.ds(o, 1), :] = total
    out_ref[...] = out_ref[...] - own_shift(number)


def prior_kernel(rows, mine, own, ends_0, ends_1, out_ref, ends, value, params, sem):
    copy = pltpu.make_async_copy(mine.at[0], params, sem)
    copy.start()
    forward = next_first("lat")
    ends[0] = jnp.where(forward, ends_1[...], ends_0[...])
    ends[1] = jnp.where(forward, ends_0[...], ends_1[...])
    copy.wait()
    for o in range(SUB):
        row, col = (params[AT_ROW, o].astype(jnp.int32), params[AT_COL, o].astype(jnp.int32))
        total = own[pl.ds(o, 1), :]
        for n, at in enumerate((0, rows)):
            for k in range(2):
                weight = jnp.where(row == at, params[2 * n + k, o], 0.0)
                total = total + weight * ends[n, pl.ds(col + SUB - 1 + k, 1), :]
        value[pl.ds(o, 1), :] = total
    send_block(value[...], out_ref)


def meet_kernel(mid, sides_0, sides_1, out_ref):
    out_ref[...] = jnp.broadcast_to(mid[...] + sides_0[...] + sides_1[...], out_ref.shape)


def later_kernel(mine, left, right, ends_0, ends_1, pad, out_ref, params, sems):
    rows, cols = (pad.shape[0] - 4, pad.shape[1] - 2 * SUB)
    side, end = (pl.ds(rows, SUB), pl.ds(cols + 2 * SUB, SUB))
    sources = (left.at[side], mine.at[1], right.at[side], ends_0.at[end], ends_1.at[end])
    copies = []
    for n, source in enumerate(sources):
        copies.append(pltpu.make_async_copy(source, params.at[n], sems.at[n]))
        copies[-1].start()
    for copy in copies:
        copy.wait()
    forward = next_first("lat")
    ends = {-1: jnp.where(forward, 4, 3), 1: jnp.where(forward, 3, 4)}
    for n, dc in enumerate(NEAR):
        for m, da in enumerate(NEAR):
            spot, lane = (n, 0) if da == 0 else (ends[da], n * SUB)
            number = lambda kind, o: params[spot, kind, lane + o]
            for o in range(SUB):
                out_ref[n * len(NEAR) + m, pl.ds(o, 1), :] = share(pad, number, rows, cols, da, dc, o)
    out_ref[len(NEAR) ** 2] = own_shift(lambda kind, o: params[1, kind, o])


def window_start(lat_count, my_lat):
    return 0 if lat_count <= WIN else jnp.clip(my_lat - REACH, 0, lat_count - WIN)


def row_of(block, j):
    return jnp.broadcast_to(block[j:j + 1, :], block.shape)


def column_of(block, j):
    return jnp.broadcast_to(block[:, j:j + 1], block.shape)


def reciprocal(value):
    guess = pl.reciprocal(value, approx=True)
    return guess * (2.0 - value * guess)


def pivot_rows(block, k, between):
    sub = lax.broadcasted_iota(jnp.int32, block.shape, 0)
    lane = lax.broadcasted_iota(jnp.int32, block.shape, 1) - k * SUB
    rows = [row_of(block, r) for r in range(SUB)]
    at = {(r, n): column_of(rows[r], k * SUB + n) for r in range(SUB) for n in range(r + 1)}
    here = (lane >= 0) & (lane < SUB)
    rows = [jnp.where(here, jnp.where(lane == r, 1.0, 0.0), row) for r, row in enumerate(rows)]
    inverse, scale = (jnp.zeros(block.shape, F32), jnp.ones(block.shape, F32))
    for j in range(0, SUB, 2):
        a, b, c = (at[j, j], at[j + 1, j], at[j + 1, j + 1])
        det = a * c - b * b
        over_det = reciprocal(det)
        top, bottom = (rows[j], rows[j + 1])
        rest = range(j + 2, SUB)
        upper = {n: (at[n, j], at[n, j + 1]) for n in rest}
        for r in rest:
            first = (at[r, j] * c - at[r, j + 1] * b) * over_det
            second = (at[r, j + 1] * a - at[r, j] * b) * over_det
            for n in range(j + 2, r + 1):
                at[r, n] = at[r, n] - (first * upper[n][0] + second * upper[n][1])
            rows[r] = rows[r] - (first * top + second * bottom)
        a_part, b_part, c_part = (a * over_det, b * over_det, c * over_det)
        for r in range(j):
            first = at[r, j] * c_part - at[r, j + 1] * b_part
            second = at[r, j + 1] * a_part - at[r, j] * b_part
            for n in rest:
                at[r, n] = at[r, n] - (first * upper[n][0] + second * upper[n][1])
            rows[r] = rows[r] - (first * top + second * bottom)
        for n in rest:
            at[j, n] = c_part * upper[n][0] - b_part * upper[n][1]
            at[j + 1, n] = a_part * upper[n][1] - b_part * upper[n][0]
        rows[j] = c_part * top - b_part * bottom
        rows[j + 1] = a_part * bottom - b_part * top
        inverse = jnp.where(sub == j, top, jnp.where(sub == j + 1, a * bottom - b * top, inverse))
        scale = jnp.where(sub == j, a, jnp.where(sub == j + 1, a * det, scale))
        between()
    return rows, jnp.where(lane < SUB, inverse * lax.rsqrt(scale), 0.0)


def eliminate(blocks):
    count = len(blocks) - 1
    blocks = list(blocks)
    lane = lax.broadcasted_iota(jnp.int32, blocks[0].shape, 1)
    inverse, waiting = ([], [])

    def update(i, k, pivot):
        terms = [column_of(blocks[i], k * SUB + j) * pivot[j] for j in range(SUB)]
        while len(terms) > 1:
            terms = [terms[n] + terms[n + 1] for n in range(0, len(terms), 2)]
        here = (lane >= k * SUB) & (lane < (k + 1) * SUB)
        blocks[i] = jnp.where(here, 0.0, blocks[i]) - terms[0]

    for k in range(count):
        share_of = -(-len(waiting) // 4)

        def between():
            for task in waiting[:share_of]:
                update(*task)
            del waiting[:share_of]

        pivot, rows = pivot_rows(blocks[k], k, between)
        update(k + 1, k, pivot)
        waiting = [(i, k, pivot) for i in range(k + 2, count + 1)]
        inverse.append(rows)
    return inverse, blocks[count][:1]


def own_blocks(near_ref):
    scaled = jnp.concatenate([near_ref[:, n].astype(F32) for n in range(PAIRS - 1)], axis=1)
    innov = near_ref[:, PAIRS - 1].astype(F32)[:, :1]
    sub = lax.broadcasted_iota(jnp.int32, scaled.shape, 1)
    lane = lax.broadcasted_iota(jnp.int32, scaled.shape, 2)
    return scaled, jnp.where(lane == sub, jnp.broadcast_to(innov, scaled.shape), 0.0)


def summed_blocks(lat_count, mine, other):
    held = min(WIN, lat_count)
    far_count = mine.shape[0] // lat_count
    start = window_start(lat_count, lax.axis_index("lat"))
    values = []
    for j in range(held):
        for far in range(far_count):
            for shares in (mine, other):
                total = jnp.zeros((SUB, LANES), F32)
                for n, da in enumerate(NEAR):
                    source = start + j - da
                    part = pl.ds(n * SUB, SUB)
                    if isinstance(source, int):
                        if 0 <= source < lat_count:
                            total = total + shares[source * far_count + far, part, :]
                    else:
                        inside = (source >= 0) & (source < lat_count)
                        source = jnp.clip(source, 0, lat_count - 1)
                        total = total + jnp.where(inside, shares[source * far_count + far, part, :], 0.0)
                values.append(total[None])
    value = jnp.concatenate(values, axis=0)
    mean = jnp.mean(value, axis=-1, keepdims=True)
    sub = lax.broadcasted_iota(jnp.int32, value.shape, 1)
    lane = lax.broadcasted_iota(jnp.int32, value.shape, 2)
    innov = jnp.where(lane == sub, jnp.broadcast_to(-mean, value.shape), 0.0)
    return (value - mean).astype(BF16).astype(F32), innov


def batch_map(batch, lat_count, blocks, pattern, swapped):
    scaled, innov = blocks
    held = min(WIN, lat_count)
    count = scaled.shape[0]
    my_lat = lax.axis_index("lat")
    start = window_start(lat_count, my_lat)
    picked = []
    for j in range(held):
        offset = start + j - my_lat + REACH
        inside = (offset >= 0) & (offset < WIN)
        row = pattern[batch, 0, 0, pl.ds(jnp.clip(offset, 0, WIN - 1), 1), :].astype(F32)
        row = jnp.where(inside, row, 0.0)
        marks = [jnp.broadcast_to(row[:, e:e + 1], (1, SUB, LANES)) for e in range(count // held)]
        for e in range(0, len(marks), 2):
            first, second = marks[e:e + 2]
            if swapped is not None:
                first, second = (jnp.where(swapped, second, first), jnp.where(swapped, first, second))
            picked.extend((first, second))
    weighted = scaled * jnp.concatenate(picked, axis=0)
    both = jnp.concatenate([scaled, innov], axis=2).reshape(count * SUB, 2 * LANES).astype(BF16)
    product = lax.dot_general(
        both,
        weighted.reshape(count * SUB, LANES).astype(BF16),
        (((0,), (0,)), ((), ())),
        preferred_element_type=F32,
    )
    sub = lax.broadcasted_iota(jnp.int32, (SUB, LANES), 0)
    lane = lax.broadcasted_iota(jnp.int32, (SUB, LANES), 1)
    members = LANES
    blocks = []
    for k in range(members // SUB):
        block = product[k * SUB:(k + 1) * SUB, :]
        blocks.append(block + jnp.where(lane - k * SUB == sub, members - 1.0, 0.0))
    proj = jnp.sum(product[members:members + SUB, :], axis=0, keepdims=True)
    blocks.append(jnp.broadcast_to(proj, (SUB, LANES)))
    inverse, weights = eliminate(blocks)
    flipped = jnp.concatenate(inverse, axis=0) * (members - 1.0) ** 0.5 - weights
    return flipped - jnp.mean(flipped, axis=-1, keepdims=True) + 1.0 / members


def exact_dot(a, b, contract_b):
    return lax.dot_general(
        a, b, (((1,), (contract_b,)), ((), ())), precision=lax.Precision.HIGHEST, preferred_element_type=F32
    )


def first_kernel(lat_count, near_ref, pattern, later, map_ref, mid_ref, out_0, out_1):
    flipped = batch_map(0, lat_count, own_blocks(near_ref), pattern, None)
    map_ref[...] = flipped
    count = len(NEAR) ** 2
    moved = exact_dot(later[pl.ds(0, count)].reshape(-1, LANES), flipped, 1)
    size = len(NEAR) * SUB
    left, mid, right = (moved[:size], moved[size:2 * size], moved[2 * size:])
    mid_ref[...] = mid
    own = pl.ds(SUB, SUB)
    mid_ref[own, :] = mid[SUB:2 * SUB] - later[count]
    forward = next_first("core")
    out_0[...] = jnp.where(forward, right, left)
    out_1[...] = jnp.where(forward, left, right)


def last_kernel(lat_count, mine, other, pattern, map_ref, pad, out_ref, result, out_sem):
    parts = out_sem.shape[0]
    rows, cols = (pad.shape[0] - 4, pad.shape[1] - 2 * SUB)
    swapped = lax.axis_index("core") == 1
    blocks = summed_blocks(lat_count, mine, other)
    flipped = exact_dot(batch_map(1, lat_count, blocks, pattern, swapped), map_ref[...], 0)
    high = flipped.astype(BF16)
    low = (flipped - high.astype(F32)).astype(BF16)
    right = jnp.concatenate(
        [jnp.concatenate([high, high], axis=1), jnp.concatenate([low, jnp.zeros_like(low)], axis=1)], axis=0
    )
    copies = []
    size = rows // parts
    for n in range(parts):
        part = pl.ds(n * size * cols, size * cols)
        value = pad[pl.ds(2 + n * size, size), pl.ds(SUB, cols), :].reshape(size * cols, LANES)
        upper = value.astype(BF16)
        rest = (value - upper.astype(F32)).astype(BF16)
        both = lax.dot_general(
            jnp.concatenate([upper, rest], axis=1), right, (((1,), (1,)), ((), ())), preferred_element_type=F32
        )
        result[part, :] = both[:, :LANES] + both[:, LANES:]
        copies.append(pltpu.make_async_copy(result.at[part], out_ref.at[part], out_sem.at[n]))
        copies[-1].start()
    for out_copy in copies:
        out_copy.wait()


def window(tiles, lat_count, lon_count):
    held = min(WIN, lat_count)
    if held == lat_count:
        return tiles
    start = jnp.clip(lax.axis_index("lat") - REACH, 0, lat_count - held)
    return lax.dynamic_slice_in_dim(tiles, start * lon_count, held * lon_count, axis=0)


def local(ensemble, observed, precision, interp_weight, stencil, owned, pattern):
    rows, cols, members = ensemble.shape
    batches = observed.shape[0]
    lat_count, lon_count = (lax.axis_size("lat"), lax.axis_size(LON))
    tiles = lat_count * lon_count
    vmem = pl.BlockSpec(memory_space=pltpu.VMEM)
    anywhere = pl.BlockSpec(memory_space=pl.ANY)
    hbm = pl.BlockSpec(memory_space=pltpu.HBM)
    megabyte = 1024 * 1024

    def shape(*dims, dtype=F32):
        return jax.ShapeDtypeStruct(dims, dtype)

    def call(kernel, name, specs, out_shape, scratch, *operands, out_specs=None, limit=48):
        return pl.pallas_call(
            kernel,
            out_shape=out_shape,
            in_specs=specs,
            out_specs=out_specs or jax.tree.map(lambda _: vmem, out_shape),
            scratch_shapes=scratch,
            compiler_params=pltpu.CompilerParams(vmem_limit_bytes=limit * megabyte),
            name=name,
        )(*operands)

    def exchange(blocks):
        return lax.all_to_all(blocks, ("lat",) + LON, split_axis=0, concat_axis=0, tiled=True)

    small = (observed, precision, interp_weight, stencil, owned)
    side = shape(rows + SUB, members)
    mine, side_1, side_0 = call(
        functools.partial(start_kernel, cols + 2),
        "start",
        [hbm] * 6,
        (shape(batches, SUB, LANES), side, side),
        [pltpu.VMEM(array.shape, array.dtype) for array in small]
        + [pltpu.VMEM((rows, SUB, members), F32)] * 2
        + [pltpu.SemaphoreType.DMA((7,))],
        *small,
        ensemble,
        limit=63,
    )
    sides = trade((side_0, side_1), LON, True)
    padded = shape(rows + 4, cols + 2 * SUB, members)
    pad = call(pad_kernel, "pad", [hbm], padded, [pltpu.SemaphoreType.DMA], ensemble)
    end = shape(cols + 3 * SUB, members)
    left, right, *ends = call(rows_kernel, "edge_rows", [vmem] * 4, (side, side, end, end), [], mine, *sides, pad)
    ends = trade(ends, "lat", False)
    slots = shape(tiles, PAIRS, 2, members, dtype=BF16)
    numbers = [pltpu.SMEM((SUB, LANES), F32), pltpu.SemaphoreType.DMA]
    block = shape(SUB, members)
    held_sides = pltpu.VMEM((2, rows + 2 * SUB, members), F32)
    own = call(row_kernel, "row_shares", [vmem] * 4, block, [held_sides] + numbers, mine, left, right, pad)
    blocks = call(
        functools.partial(prior_kernel, rows),
        "prior",
        [vmem] * 4,
        slots,
        [pltpu.VMEM((2,) + end.shape, F32), pltpu.VMEM((SUB, members), F32)] + numbers,
        mine,
        own,
        *ends,
    )
    near = window(exchange(blocks), lat_count, lon_count)
    count = len(NEAR) ** 2
    later = call(
        later_kernel,
        "later_shares",
        [vmem] * 6,
        shape(count + 1, SUB, members),
        [pltpu.SMEM((5, SUB, LANES), F32), pltpu.SemaphoreType.DMA((5,))],
        mine,
        left,
        right,
        *ends,
        pad,
    )
    column = shape(len(NEAR) * SUB, members)
    first_map, mid, *sides = call(
        functools.partial(first_kernel, lat_count),
        "first_batch",
        [vmem] * 3,
        (shape(members, members), column, column, column),
        [],
        near,
        pattern,
        later,
    )
    sides = trade(sides, LON, True)
    shares = call(meet_kernel, "meet", [vmem] * 3, shape(tiles // 2, *column.shape), [], mid, *sides)
    shares = lax.all_to_all(shares, ("lat", "far"), split_axis=0, concat_axis=0, tiled=True)
    other = lax.ppermute(shares, "core", [(0, 1), (1, 0)])
    parts = 8
    result = call(
        functools.partial(last_kernel, lat_count),
        "second_batch",
        [vmem] * 5,
        shape(rows * cols, members),
        [
            pltpu.VMEM((rows * cols, members), F32),
            pltpu.SemaphoreType.DMA((parts,)),
        ],
        shares,
        other,
        pattern,
        first_map,
        pad,
        out_specs=anywhere,
    )
    return result.reshape(rows, cols, members)


def solution(mesh):
    lat_count, lon_count = (mesh.shape["lat"], mesh.shape["lon"])
    pairs = jax.sharding.Mesh(mesh.devices.reshape(lat_count, lon_count // 2, 2), ("lat",) + LON)
    placed = (
        P("lat", LON, None),
        P(None, "lat", LON, None),
        P(None, "lat", LON, None),
        P(None, "lat", LON, None, None),
        P(None, "lat", LON, None, None),
        P(None, "lat", LON, None),
        P(None, "lat", LON, None, None),
    )
    return jax.shard_map(
        local, mesh=pairs, in_specs=placed, out_specs=P("lat", LON, None), check_vma=False
    )
```

```python
import functools
import jax
import jax.numpy as jnp
from jax import lax
from jax.experimental import pallas as pl
from jax.experimental.pallas import tpu as pltpu
from jax.sharding import PartitionSpec as P

REACH = 2
WIN = 2 * REACH + 1
SUB = 8
LANES = 128
NEAR = (-1, 0, 1)
AT_ROW, AT_COL, AT_OBS = (4, 5, 6)
PAIRS = SUB // 2 + 1
F32 = jnp.float32
BF16 = jnp.bfloat16
LON = ("far", "core")


def partner(place, turn):
    return place + (-1 if place % 2 == turn else 1)


def trade(blocks, axis, wraps):
    count = lax.axis_size(axis)
    results = []
    for turn, block in enumerate(blocks):
        route = [(place, partner(place, turn)) for place in range(count)]
        route = [(source, target % count) for source, target in route if wraps or 0 <= target < count]
        results.append(lax.ppermute(block, axis, route))
    return results


def next_first(axis):
    return lax.rem(lax.axis_index(axis), 2) == 1


def start_kernel(
    width, observed, precision, weight, stencil, owned, cells, params_ref, sides_1, sides_0,
    observed_v, precision_v, weight_v, stencil_v, owned_v, left_v, right_v, sems
):
    batches, cols = (observed.shape[0], cells.shape[1])
    pairs = (
        (observed, observed_v),
        (precision, precision_v),
        (weight, weight_v),
        (stencil, stencil_v),
        (owned, owned_v),
        (cells.at[:, pl.ds(0, SUB)], left_v),
        (cells.at[:, pl.ds(cols - SUB, SUB)], right_v),
    )
    copies = [pltpu.make_async_copy(source, target, sems.at[n]) for n, (source, target) in enumerate(pairs)]
    for copy in copies:
        copy.start()
    for copy in copies:
        copy.wait()
    params_ref[...] = jnp.zeros_like(params_ref)
    for b in range(batches):
        root = jnp.sqrt(precision_v[b, 0]) * owned_v[b, 0].astype(F32)
        corner = stencil_v[b, 0, 0, pl.ds(0, 1)].astype(F32)
        row = jnp.floor((corner + 0.5) * (1.0 / width))
        params_ref[b, pl.ds(0, 4), pl.ds(0, SUB)] = weight_v[b, 0, 0] * root
        params_ref[b, pl.ds(AT_ROW, 1), pl.ds(0, SUB)] = row
        params_ref[b, pl.ds(AT_COL, 1), pl.ds(0, SUB)] = corner - row * width
        params_ref[b, pl.ds(AT_OBS, 1), pl.ds(0, SUB)] = observed_v[b, 0] * root
    rows = cells.shape[0]
    forward = next_first("core")
    left, right = (left_v[:, 0, :], right_v[:, SUB - 1, :])
    sides_0[pl.ds(0, rows), :] = jnp.where(forward, right, left)
    sides_1[pl.ds(0, rows), :] = jnp.where(forward, left, right)
    sides_0[pl.ds(rows, SUB), :] = params_ref[1]
    sides_1[pl.ds(rows, SUB), :] = params_ref[1]


def clear_rim(pad, rows, cols):
    edge = jnp.zeros((2, cols + 2 * SUB, LANES), F32)
    pad[pl.ds(0, 2)] = edge
    pad[pl.ds(rows + 2, 2)] = edge
    side = jnp.zeros((rows, SUB, LANES), F32)
    pad[pl.ds(2, rows), pl.ds(0, SUB)] = side
    pad[pl.ds(2, rows), pl.ds(SUB + cols, SUB)] = side


def share(pad, number, rows, cols, da, dc, o):
    row = number(AT_ROW, o).astype(jnp.int32) - 1 + da * rows
    col = number(AT_COL, o).astype(jnp.int32) - 1 + dc * cols
    row = jnp.clip(row, -2, rows) + 2
    col = jnp.clip(col, -2, cols) + SUB
    terms = [number(k, o) * pad[row + k // 2, pl.ds(col + k % 2, 1), :] for k in range(4)]
    return (terms[0] + terms[1]) + (terms[2] + terms[3])


def own_shift(number):
    sub = lax.broadcasted_iota(jnp.int32, (SUB, LANES), 0)
    shift = jnp.zeros((SUB, LANES), F32)
    for o in range(SUB):
        shift = jnp.where(sub == o, number(AT_OBS, o), shift)
    return shift


def pad_kernel(cells, pad, sem):
    rows, cols = (cells.shape[0], cells.shape[1])
    copy = pltpu.make_async_copy(cells, pad.at[pl.ds(2, rows), pl.ds(SUB, cols)], sem)
    copy.start()
    clear_rim(pad, rows, cols)
    copy.wait()


def hold_sides(left, right, sides):
    rows = left.shape[0] - SUB
    sides[...] = jnp.zeros_like(sides)
    sides[0, pl.ds(SUB, rows), :] = left[pl.ds(0, rows), :]
    sides[1, pl.ds(SUB, rows), :] = right[pl.ds(0, rows), :]


def side_share(sides, side, number, rows, cols, da, o):
    row = number(AT_ROW, o).astype(jnp.int32) - 1 + da * rows
    row = jnp.clip(row, -2, rows) + SUB
    used = number(AT_COL, o).astype(jnp.int32) == (0, cols)[side]
    terms = [jnp.where(used, number(side + 2 * k, o), 0.0) * sides[side, pl.ds(row + k, 1), :] for k in range(2)]
    return terms[0] + terms[1]


def send_block(value, out_ref):
    mean = jnp.mean(value, axis=-1, keepdims=True)
    sub = lax.broadcasted_iota(jnp.int32, (SUB, LANES), 0)
    lane = lax.broadcasted_iota(jnp.int32, (SUB, LANES), 1)
    innov = jnp.sum(jnp.where(lane == sub, -mean, 0.0), axis=0, keepdims=True)
    rows = jnp.concatenate([value - mean, jnp.broadcast_to(innov, (2, LANES))], axis=0).astype(BF16)
    for n in range(PAIRS):
        pair = rows[2 * n:2 * n + 2]
        out_ref[:, n] = jnp.broadcast_to(pair, (out_ref.shape[0],) + pair.shape)


def rows_kernel(mine, sides_0, sides_1, pad, left_ref, right_ref, out_0, out_1):
    rows, cols = (pad.shape[0] - 4, pad.shape[1] - 2 * SUB)
    forward = next_first("core")
    left_ref[...] = jnp.where(forward, sides_1[...], sides_0[...])
    right_ref[...] = jnp.where(forward, sides_0[...], sides_1[...])
    lane = lax.broadcasted_iota(jnp.int32, (SUB, LANES), 1)
    block = pl.ds(rows, SUB)
    packed = jnp.where(lane < SUB, left_ref[block, :], pltpu.roll(mine[1], SUB, 1))
    packed = jnp.where(lane < 2 * SUB, packed, pltpu.roll(right_ref[block, :], 2 * SUB, 1))
    forward = next_first("lat")
    for turn, out in enumerate((out_0, out_1)):
        row = jnp.where(forward, (1 - turn) * (rows - 1), turn * (rows - 1))
        out[pl.ds(0, SUB), :] = jnp.broadcast_to(left_ref[pl.ds(row, 1), :], (SUB, LANES))
        out[pl.ds(SUB, cols), :] = pad[2 + row, pl.ds(SUB, cols), :]
        out[pl.ds(SUB + cols, SUB), :] = jnp.broadcast_to(right_ref[pl.ds(row, 1), :], (SUB, LANES))
        out[pl.ds(2 * SUB + cols, SUB), :] = packed


def row_kernel(mine, left, right, pad, out_ref, sides, params, sem):
    rows, cols = (pad.shape[0] - 4, pad.shape[1] - 2 * SUB)
    copy = pltpu.make_async_copy(mine.at[0], params, sem)
    copy.start()
    hold_sides(left, right, sides)
    copy.wait()
    number = lambda kind, o: params[kind, o]
    for o in range(SUB):
        total = share(pad, number, rows, cols, 0, 0, o)
        for side in range(2):
            total = total + side_share(sides, side, number, rows, cols, 0, o)
        out_ref[pl.ds(o, 1), :] = total
    out_ref[...] = out_ref[...] - own_shift(number)


def prior_kernel(rows, mine, own, ends_0, ends_1, out_ref, ends, value, params, sem):
    copy = pltpu.make_async_copy(mine.at[0], params, sem)
    copy.start()
    forward = next_first("lat")
    ends[0] = jnp.where(forward, ends_1[...], ends_0[...])
    ends[1] = jnp.where(forward, ends_0[...], ends_1[...])
    copy.wait()
    for o in range(SUB):
        row, col = (params[AT_ROW, o].astype(jnp.int32), params[AT_COL, o].astype(jnp.int32))
        total = own[pl.ds(o, 1), :]
        for n, at in enumerate((0, rows)):
            for k in range(2):
                weight = jnp.where(row == at, params[2 * n + k, o], 0.0)
                total = total + weight * ends[n, pl.ds(col + SUB - 1 + k, 1), :]
        value[pl.ds(o, 1), :] = total
    send_block(value[...], out_ref)


def meet_kernel(mid, sides_0, sides_1, out_ref):
    out_ref[...] = jnp.broadcast_to(mid[...] + sides_0[...] + sides_1[...], out_ref.shape)


def later_kernel(mine, left, right, ends_0, ends_1, pad, out_ref, params, sems):
    rows, cols = (pad.shape[0] - 4, pad.shape[1] - 2 * SUB)
    side, end = (pl.ds(rows, SUB), pl.ds(cols + 2 * SUB, SUB))
    sources = (left.at[side], mine.at[1], right.at[side], ends_0.at[end], ends_1.at[end])
    copies = []
    for n, source in enumerate(sources):
        copies.append(pltpu.make_async_copy(source, params.at[n], sems.at[n]))
        copies[-1].start()
    for copy in copies:
        copy.wait()
    forward = next_first("lat")
    ends = {-1: jnp.where(forward, 4, 3), 1: jnp.where(forward, 3, 4)}
    for n, dc in enumerate(NEAR):
        for m, da in enumerate(NEAR):
            spot, lane = (n, 0) if da == 0 else (ends[da], n * SUB)
            number = lambda kind, o: params[spot, kind, lane + o]
            for o in range(SUB):
                out_ref[n * len(NEAR) + m, pl.ds(o, 1), :] = share(pad, number, rows, cols, da, dc, o)
    out_ref[len(NEAR) ** 2] = own_shift(lambda kind, o: params[1, kind, o])


def window_start(lat_count, my_lat):
    return 0 if lat_count <= WIN else jnp.clip(my_lat - REACH, 0, lat_count - WIN)


def column_of(block, j):
    return jnp.broadcast_to(block[:, j:j + 1], block.shape)


def reciprocal(value):
    guess = pl.reciprocal(value, approx=True)
    return guess * (2.0 - value * guess)


def pivot_rows(block, k, held, between):
    sub = lax.broadcasted_iota(jnp.int32, block.shape, 0)
    lane = lax.broadcasted_iota(jnp.int32, block.shape, 1) - k * SUB
    held[pl.ds(k * SUB, SUB), :] = block
    rows = [held[pl.ds(k * SUB + r, SUB, stride=0), :] for r in range(SUB)]
    at = {(r, n): column_of(rows[r], k * SUB + n) for r in range(SUB) for n in range(r + 1)}
    here = (lane >= 0) & (lane < SUB)
    rows = [jnp.where(here, jnp.where(lane == r, 1.0, 0.0), row) for r, row in enumerate(rows)]
    inverse, scale = (jnp.zeros(block.shape, F32), jnp.ones(block.shape, F32))
    for j in range(0, SUB, 2):
        a, b, c = (at[j, j], at[j + 1, j], at[j + 1, j + 1])
        det = a * c - b * b
        over_det = reciprocal(det)
        top, bottom = (rows[j], rows[j + 1])
        rest = range(j + 2, SUB)
        upper = {n: (at[n, j], at[n, j + 1]) for n in rest}
        for r in rest:
            first = (at[r, j] * c - at[r, j + 1] * b) * over_det
            second = (at[r, j + 1] * a - at[r, j] * b) * over_det
            for n in range(j + 2, r + 1):
                at[r, n] = at[r, n] - (first * upper[n][0] + second * upper[n][1])
            rows[r] = rows[r] - (first * top + second * bottom)
        a_part, b_part, c_part = (a * over_det, b * over_det, c * over_det)
        for r in range(j):
            first = at[r, j] * c_part - at[r, j + 1] * b_part
            second = at[r, j + 1] * a_part - at[r, j] * b_part
            for n in rest:
                at[r, n] = at[r, n] - (first * upper[n][0] + second * upper[n][1])
            rows[r] = rows[r] - (first * top + second * bottom)
        for n in rest:
            at[j, n] = c_part * upper[n][0] - b_part * upper[n][1]
            at[j + 1, n] = a_part * upper[n][1] - b_part * upper[n][0]
        rows[j] = c_part * top - b_part * bottom
        rows[j + 1] = a_part * bottom - b_part * top
        inverse = jnp.where(sub == j, top, jnp.where(sub == j + 1, a * bottom - b * top, inverse))
        scale = jnp.where(sub == j, a, jnp.where(sub == j + 1, a * det, scale))
        between()
    return rows, jnp.where(lane < SUB, inverse * lax.rsqrt(scale), 0.0)


def eliminate(blocks, held):
    count = len(blocks) - 1
    blocks = list(blocks)
    lane = lax.broadcasted_iota(jnp.int32, blocks[0].shape, 1)
    inverse, waiting = ([], [])

    def update(i, k, pivot):
        terms = [column_of(blocks[i], k * SUB + j) * pivot[j] for j in range(SUB)]
        while len(terms) > 1:
            terms = [terms[n] + terms[n + 1] for n in range(0, len(terms), 2)]
        here = (lane >= k * SUB) & (lane < (k + 1) * SUB)
        blocks[i] = jnp.where(here, 0.0, blocks[i]) - terms[0]

    for k in range(count):
        share_of = -(-len(waiting) // 4)

        def between():
            for task in waiting[:share_of]:
                update(*task)
            del waiting[:share_of]

        pivot, rows = pivot_rows(blocks[k], k, held, between)
        update(k + 1, k, pivot)
        waiting = [(i, k, pivot) for i in range(k + 2, count + 1)]
        inverse.append(rows)
    return inverse, blocks[count][:1]


def own_blocks(near_ref):
    scaled = jnp.concatenate([near_ref[:, n].astype(F32) for n in range(PAIRS - 1)], axis=1)
    innov = near_ref[:, PAIRS - 1].astype(F32)[:, :1]
    sub = lax.broadcasted_iota(jnp.int32, scaled.shape, 1)
    lane = lax.broadcasted_iota(jnp.int32, scaled.shape, 2)
    return scaled, jnp.where(lane == sub, jnp.broadcast_to(innov, scaled.shape), 0.0)


def summed_blocks(lat_count, mine, other):
    held = min(WIN, lat_count)
    far_count = mine.shape[0] // lat_count
    start = window_start(lat_count, lax.axis_index("lat"))
    values = []
    for j in range(held):
        for far in range(far_count):
            for shares in (mine, other):
                total = jnp.zeros((SUB, LANES), F32)
                for n, da in enumerate(NEAR):
                    source = start + j - da
                    part = pl.ds(n * SUB, SUB)
                    if isinstance(source, int):
                        if 0 <= source < lat_count:
                            total = total + shares[source * far_count + far, part, :]
                    else:
                        inside = (source >= 0) & (source < lat_count)
                        source = jnp.clip(source, 0, lat_count - 1)
                        total = total + jnp.where(inside, shares[source * far_count + far, part, :], 0.0)
                values.append(total[None])
    value = jnp.concatenate(values, axis=0)
    mean = jnp.mean(value, axis=-1, keepdims=True)
    sub = lax.broadcasted_iota(jnp.int32, value.shape, 1)
    lane = lax.broadcasted_iota(jnp.int32, value.shape, 2)
    innov = jnp.where(lane == sub, jnp.broadcast_to(-mean, value.shape), 0.0)
    return (value - mean).astype(BF16).astype(F32), innov


def batch_map(batch, lat_count, blocks, pattern, swapped, held_rows):
    scaled, innov = blocks
    held = min(WIN, lat_count)
    count = scaled.shape[0]
    my_lat = lax.axis_index("lat")
    start = window_start(lat_count, my_lat)
    picked = []
    for j in range(held):
        offset = start + j - my_lat + REACH
        inside = (offset >= 0) & (offset < WIN)
        row = pattern[batch, 0, 0, pl.ds(jnp.clip(offset, 0, WIN - 1), 1), :].astype(F32)
        row = jnp.where(inside, row, 0.0)
        marks = [jnp.broadcast_to(row[:, e:e + 1], (1, SUB, LANES)) for e in range(count // held)]
        for e in range(0, len(marks), 2):
            first, second = marks[e:e + 2]
            if swapped is not None:
                first, second = (jnp.where(swapped, second, first), jnp.where(swapped, first, second))
            picked.extend((first, second))
    weighted = scaled * jnp.concatenate(picked, axis=0)
    both = jnp.concatenate([scaled, innov], axis=2).reshape(count * SUB, 2 * LANES).astype(BF16)
    product = lax.dot_general(
        both,
        weighted.reshape(count * SUB, LANES).astype(BF16),
        (((0,), (0,)), ((), ())),
        preferred_element_type=F32,
    )
    sub = lax.broadcasted_iota(jnp.int32, (SUB, LANES), 0)
    lane = lax.broadcasted_iota(jnp.int32, (SUB, LANES), 1)
    members = LANES
    blocks = []
    for k in range(members // SUB):
        block = product[k * SUB:(k + 1) * SUB, :]
        blocks.append(block + jnp.where(lane - k * SUB == sub, members - 1.0, 0.0))
    proj = jnp.sum(product[members:members + SUB, :], axis=0, keepdims=True)
    blocks.append(jnp.broadcast_to(proj, (SUB, LANES)))
    inverse, weights = eliminate(blocks, held_rows)
    flipped = jnp.concatenate(inverse, axis=0) * (members - 1.0) ** 0.5 - weights
    return flipped - jnp.mean(flipped, axis=-1, keepdims=True) + 1.0 / members


def exact_dot(a, b, contract_b):
    return lax.dot_general(
        a, b, (((1,), (contract_b,)), ((), ())), precision=lax.Precision.HIGHEST, preferred_element_type=F32
    )


def first_kernel(lat_count, near_ref, pattern, later, map_ref, mid_ref, out_0, out_1, held_rows):
    flipped = batch_map(0, lat_count, own_blocks(near_ref), pattern, None, held_rows)
    map_ref[...] = flipped
    count = len(NEAR) ** 2
    moved = exact_dot(later[pl.ds(0, count)].reshape(-1, LANES), flipped, 1)
    size = len(NEAR) * SUB
    left, mid, right = (moved[:size], moved[size:2 * size], moved[2 * size:])
    mid_ref[...] = mid
    own = pl.ds(SUB, SUB)
    mid_ref[own, :] = mid[SUB:2 * SUB] - later[count]
    forward = next_first("core")
    out_0[...] = jnp.where(forward, right, left)
    out_1[...] = jnp.where(forward, left, right)


def last_kernel(lat_count, mine, other, pattern, map_ref, pad, out_ref, result, held_rows, out_sem):
    parts = out_sem.shape[0]
    rows, cols = (pad.shape[0] - 4, pad.shape[1] - 2 * SUB)
    swapped = lax.axis_index("core") == 1
    blocks = summed_blocks(lat_count, mine, other)
    flipped = exact_dot(batch_map(1, lat_count, blocks, pattern, swapped, held_rows), map_ref[...], 0)
    high = flipped.astype(BF16)
    low = (flipped - high.astype(F32)).astype(BF16)
    right = jnp.concatenate(
        [jnp.concatenate([high, high], axis=1), jnp.concatenate([low, jnp.zeros_like(low)], axis=1)], axis=0
    )
    copies = []
    size = rows // parts
    for n in range(parts):
        part = pl.ds(n * size * cols, size * cols)
        value = pad[pl.ds(2 + n * size, size), pl.ds(SUB, cols), :].reshape(size * cols, LANES)
        upper = value.astype(BF16)
        rest = (value - upper.astype(F32)).astype(BF16)
        both = lax.dot_general(
            jnp.concatenate([upper, rest], axis=1), right, (((1,), (1,)), ((), ())), preferred_element_type=F32
        )
        result[part, :] = both[:, :LANES] + both[:, LANES:]
        copies.append(pltpu.make_async_copy(result.at[part], out_ref.at[part], out_sem.at[n]))
        copies[-1].start()
    for out_copy in copies:
        out_copy.wait()


def window(tiles, lat_count, lon_count):
    held = min(WIN, lat_count)
    if held == lat_count:
        return tiles
    start = jnp.clip(lax.axis_index("lat") - REACH, 0, lat_count - held)
    return lax.dynamic_slice_in_dim(tiles, start * lon_count, held * lon_count, axis=0)


def local(ensemble, observed, precision, interp_weight, stencil, owned, pattern):
    rows, cols, members = ensemble.shape
    batches = observed.shape[0]
    lat_count, lon_count = (lax.axis_size("lat"), lax.axis_size(LON))
    tiles = lat_count * lon_count
    vmem = pl.BlockSpec(memory_space=pltpu.VMEM)
    anywhere = pl.BlockSpec(memory_space=pl.ANY)
    hbm = pl.BlockSpec(memory_space=pltpu.HBM)
    megabyte = 1024 * 1024

    def shape(*dims, dtype=F32):
        return jax.ShapeDtypeStruct(dims, dtype)

    def call(kernel, name, specs, out_shape, scratch, *operands, out_specs=None, limit=48):
        return pl.pallas_call(
            kernel,
            out_shape=out_shape,
            in_specs=specs,
            out_specs=out_specs or jax.tree.map(lambda _: vmem, out_shape),
            scratch_shapes=scratch,
            compiler_params=pltpu.CompilerParams(vmem_limit_bytes=limit * megabyte),
            name=name,
        )(*operands)

    def exchange(blocks):
        return lax.all_to_all(blocks, ("lat",) + LON, split_axis=0, concat_axis=0, tiled=True)

    small = (observed, precision, interp_weight, stencil, owned)
    side = shape(rows + SUB, members)
    mine, side_1, side_0 = call(
        functools.partial(start_kernel, cols + 2),
        "start",
        [hbm] * 6,
        (shape(batches, SUB, LANES), side, side),
        [pltpu.VMEM(array.shape, array.dtype) for array in small]
        + [pltpu.VMEM((rows, SUB, members), F32)] * 2
        + [pltpu.SemaphoreType.DMA((7,))],
        *small,
        ensemble,
        limit=63,
    )
    sides = trade((side_0, side_1), LON, True)
    padded = shape(rows + 4, cols + 2 * SUB, members)
    pad = call(pad_kernel, "pad", [hbm], padded, [pltpu.SemaphoreType.DMA], ensemble)
    end = shape(cols + 3 * SUB, members)
    left, right, *ends = call(rows_kernel, "edge_rows", [vmem] * 4, (side, side, end, end), [], mine, *sides, pad)
    ends = trade(ends, "lat", False)
    slots = shape(tiles, PAIRS, 2, members, dtype=BF16)
    numbers = [pltpu.SMEM((SUB, LANES), F32), pltpu.SemaphoreType.DMA]
    block = shape(SUB, members)
    held_sides = pltpu.VMEM((2, rows + 2 * SUB, members), F32)
    own = call(row_kernel, "row_shares", [vmem] * 4, block, [held_sides] + numbers, mine, left, right, pad)
    blocks = call(
        functools.partial(prior_kernel, rows),
        "prior",
        [vmem] * 4,
        slots,
        [pltpu.VMEM((2,) + end.shape, F32), pltpu.VMEM((SUB, members), F32)] + numbers,
        mine,
        own,
        *ends,
    )
    near = window(exchange(blocks), lat_count, lon_count)
    count = len(NEAR) ** 2
    later = call(
        later_kernel,
        "later_shares",
        [vmem] * 6,
        shape(count + 1, SUB, members),
        [pltpu.SMEM((5, SUB, LANES), F32), pltpu.SemaphoreType.DMA((5,))],
        mine,
        left,
        right,
        *ends,
        pad,
    )
    column = shape(len(NEAR) * SUB, members)
    held_rows = pltpu.VMEM((members + SUB, members), F32)
    first_map, mid, *sides = call(
        functools.partial(first_kernel, lat_count),
        "first_batch",
        [vmem] * 3,
        (shape(members, members), column, column, column),
        [held_rows],
        near,
        pattern,
        later,
    )
    sides = trade(sides, LON, True)
    shares = call(meet_kernel, "meet", [vmem] * 3, shape(tiles // 2, *column.shape), [], mid, *sides)
    shares = lax.all_to_all(shares, ("lat", "far"), split_axis=0, concat_axis=0, tiled=True)
    other = lax.ppermute(shares, "core", [(0, 1), (1, 0)])
    parts = 8
    result = call(
        functools.partial(last_kernel, lat_count),
        "second_batch",
        [vmem] * 5,
        shape(rows * cols, members),
        [
            pltpu.VMEM((rows * cols, members), F32),
            held_rows,
            pltpu.SemaphoreType.DMA((parts,)),
        ],
        shares,
        other,
        pattern,
        first_map,
        pad,
        out_specs=anywhere,
    )
    return result.reshape(rows, cols, members)


def solution(mesh):
    lat_count, lon_count = (mesh.shape["lat"], mesh.shape["lon"])
    pairs = jax.sharding.Mesh(mesh.devices.reshape(lat_count, lon_count // 2, 2), ("lat",) + LON)
    placed = (
        P("lat", LON, None),
        P(None, "lat", LON, None),
        P(None, "lat", LON, None),
        P(None, "lat", LON, None, None),
        P(None, "lat", LON, None, None),
        P(None, "lat", LON, None),
        P(None, "lat", LON, None, None),
    )
    return jax.shard_map(
        local, mesh=pairs, in_specs=placed, out_specs=P("lat", LON, None), check_vma=False
    )
```

```python
import functools
import jax
import jax.numpy as jnp
from jax import lax
from jax.experimental import pallas as pl
from jax.experimental.pallas import tpu as pltpu
from jax.sharding import PartitionSpec as P

REACH = 2
WIN = 2 * REACH + 1
SUB = 8
LANES = 128
NEAR = (-1, 0, 1)
AT_ROW, AT_COL, AT_OBS = (4, 5, 6)
PAIRS = SUB // 2 + 1
F32 = jnp.float32
BF16 = jnp.bfloat16
LON = ("far", "core")


def partner(place, turn):
    return place + (-1 if place % 2 == turn else 1)


def trade(blocks, axis, wraps):
    count = lax.axis_size(axis)
    results = []
    for turn, block in enumerate(blocks):
        route = [(place, partner(place, turn)) for place in range(count)]
        route = [(source, target % count) for source, target in route if wraps or 0 <= target < count]
        results.append(lax.ppermute(block, axis, route))
    return results


def next_first(axis):
    return lax.rem(lax.axis_index(axis), 2) == 1


def start_kernel(
    width, observed, precision, weight, stencil, owned, cells, params_ref, sides_1, sides_0,
    observed_v, precision_v, weight_v, stencil_v, owned_v, left_v, right_v, sems
):
    batches, cols = (observed.shape[0], cells.shape[1])
    pairs = (
        (observed, observed_v),
        (precision, precision_v),
        (weight, weight_v),
        (stencil, stencil_v),
        (owned, owned_v),
        (cells.at[:, pl.ds(0, SUB)], left_v),
        (cells.at[:, pl.ds(cols - SUB, SUB)], right_v),
    )
    copies = [pltpu.make_async_copy(source, target, sems.at[n]) for n, (source, target) in enumerate(pairs)]
    for copy in copies:
        copy.start()
    for copy in copies:
        copy.wait()
    params_ref[...] = jnp.zeros_like(params_ref)
    for b in range(batches):
        root = jnp.sqrt(precision_v[b, 0]) * owned_v[b, 0].astype(F32)
        corner = stencil_v[b, 0, 0, pl.ds(0, 1)].astype(F32)
        row = jnp.floor((corner + 0.5) * (1.0 / width))
        params_ref[b, pl.ds(0, 4), pl.ds(0, SUB)] = weight_v[b, 0, 0] * root
        params_ref[b, pl.ds(AT_ROW, 1), pl.ds(0, SUB)] = row
        params_ref[b, pl.ds(AT_COL, 1), pl.ds(0, SUB)] = corner - row * width
        params_ref[b, pl.ds(AT_OBS, 1), pl.ds(0, SUB)] = observed_v[b, 0] * root
    rows = cells.shape[0]
    forward = next_first("core")
    left, right = (left_v[:, 0, :], right_v[:, SUB - 1, :])
    sides_0[pl.ds(0, rows), :] = jnp.where(forward, right, left)
    sides_1[pl.ds(0, rows), :] = jnp.where(forward, left, right)
    sides_0[pl.ds(rows, SUB), :] = params_ref[1]
    sides_1[pl.ds(rows, SUB), :] = params_ref[1]


def clear_rim(pad, rows, cols):
    edge = jnp.zeros((2, cols + 2 * SUB, LANES), F32)
    pad[pl.ds(0, 2)] = edge
    pad[pl.ds(rows + 2, 2)] = edge
    side = jnp.zeros((rows, SUB, LANES), F32)
    pad[pl.ds(2, rows), pl.ds(0, SUB)] = side
    pad[pl.ds(2, rows), pl.ds(SUB + cols, SUB)] = side


def share(pad, number, rows, cols, da, dc, o):
    row = number(AT_ROW, o).astype(jnp.int32) - 1 + da * rows
    col = number(AT_COL, o).astype(jnp.int32) - 1 + dc * cols
    row = jnp.clip(row, -2, rows) + 2
    col = jnp.clip(col, -2, cols) + SUB
    terms = [number(k, o) * pad[row + k // 2, pl.ds(col + k % 2, 1), :] for k in range(4)]
    return (terms[0] + terms[1]) + (terms[2] + terms[3])


def own_shift(number):
    sub = lax.broadcasted_iota(jnp.int32, (SUB, LANES), 0)
    shift = jnp.zeros((SUB, LANES), F32)
    for o in range(SUB):
        shift = jnp.where(sub == o, number(AT_OBS, o), shift)
    return shift


def pad_kernel(cells, pad, sem):
    rows, cols = (cells.shape[0], cells.shape[1])
    copy = pltpu.make_async_copy(cells, pad.at[pl.ds(2, rows), pl.ds(SUB, cols)], sem)
    copy.start()
    clear_rim(pad, rows, cols)
    copy.wait()


def hold_sides(left, right, sides):
    rows = left.shape[0] - SUB
    sides[...] = jnp.zeros_like(sides)
    sides[0, pl.ds(SUB, rows), :] = left[pl.ds(0, rows), :]
    sides[1, pl.ds(SUB, rows), :] = right[pl.ds(0, rows), :]


def side_share(sides, side, number, rows, cols, da, o):
    row = number(AT_ROW, o).astype(jnp.int32) - 1 + da * rows
    row = jnp.clip(row, -2, rows) + SUB
    used = number(AT_COL, o).astype(jnp.int32) == (0, cols)[side]
    terms = [jnp.where(used, number(side + 2 * k, o), 0.0) * sides[side, pl.ds(row + k, 1), :] for k in range(2)]
    return terms[0] + terms[1]


def send_block(value, out_ref):
    mean = jnp.mean(value, axis=-1, keepdims=True)
    sub = lax.broadcasted_iota(jnp.int32, (SUB, LANES), 0)
    lane = lax.broadcasted_iota(jnp.int32, (SUB, LANES), 1)
    innov = jnp.sum(jnp.where(lane == sub, -mean, 0.0), axis=0, keepdims=True)
    rows = jnp.concatenate([value - mean, jnp.broadcast_to(innov, (2, LANES))], axis=0).astype(BF16)
    for n in range(PAIRS):
        pair = rows[2 * n:2 * n + 2]
        out_ref[:, n] = jnp.broadcast_to(pair, (out_ref.shape[0],) + pair.shape)


def rows_kernel(mine, sides_0, sides_1, pad, left_ref, right_ref, out_0, out_1):
    rows, cols = (pad.shape[0] - 4, pad.shape[1] - 2 * SUB)
    forward = next_first("core")
    left_ref[...] = jnp.where(forward, sides_1[...], sides_0[...])
    right_ref[...] = jnp.where(forward, sides_0[...], sides_1[...])
    lane = lax.broadcasted_iota(jnp.int32, (SUB, LANES), 1)
    block = pl.ds(rows, SUB)
    packed = jnp.where(lane < SUB, left_ref[block, :], pltpu.roll(mine[1], SUB, 1))
    packed = jnp.where(lane < 2 * SUB, packed, pltpu.roll(right_ref[block, :], 2 * SUB, 1))
    forward = next_first("lat")
    for turn, out in enumerate((out_0, out_1)):
        row = jnp.where(forward, (1 - turn) * (rows - 1), turn * (rows - 1))
        out[pl.ds(0, SUB), :] = jnp.broadcast_to(left_ref[pl.ds(row, 1), :], (SUB, LANES))
        out[pl.ds(SUB, cols), :] = pad[2 + row, pl.ds(SUB, cols), :]
        out[pl.ds(SUB + cols, SUB), :] = jnp.broadcast_to(right_ref[pl.ds(row, 1), :], (SUB, LANES))
        out[pl.ds(2 * SUB + cols, SUB), :] = packed


def row_kernel(mine, left, right, pad, out_ref, sides, params, sem):
    rows, cols = (pad.shape[0] - 4, pad.shape[1] - 2 * SUB)
    copy = pltpu.make_async_copy(mine.at[0], params, sem)
    copy.start()
    hold_sides(left, right, sides)
    copy.wait()
    number = lambda kind, o: params[kind, o]
    for o in range(SUB):
        total = share(pad, number, rows, cols, 0, 0, o)
        for side in range(2):
            total = total + side_share(sides, side, number, rows, cols, 0, o)
        out_ref[pl.ds(o, 1), :] = total
    out_ref[...] = out_ref[...] - own_shift(number)


def prior_kernel(rows, mine, own, ends_0, ends_1, out_ref, ends, value, params, sem):
    copy = pltpu.make_async_copy(mine.at[0], params, sem)
    copy.start()
    forward = next_first("lat")
    ends[0] = jnp.where(forward, ends_1[...], ends_0[...])
    ends[1] = jnp.where(forward, ends_0[...], ends_1[...])
    copy.wait()
    for o in range(SUB):
        row, col = (params[AT_ROW, o].astype(jnp.int32), params[AT_COL, o].astype(jnp.int32))
        total = own[pl.ds(o, 1), :]
        for n, at in enumerate((0, rows)):
            for k in range(2):
                weight = jnp.where(row == at, params[2 * n + k, o], 0.0)
                total = total + weight * ends[n, pl.ds(col + SUB - 1 + k, 1), :]
        value[pl.ds(o, 1), :] = total
    send_block(value[...], out_ref)


def meet_kernel(mid, sides_0, sides_1, out_ref):
    out_ref[...] = jnp.broadcast_to(mid[...] + sides_0[...] + sides_1[...], out_ref.shape)


def later_kernel(mine, left, right, ends_0, ends_1, pad, out_ref, params, sems):
    rows, cols = (pad.shape[0] - 4, pad.shape[1] - 2 * SUB)
    side, end = (pl.ds(rows, SUB), pl.ds(cols + 2 * SUB, SUB))
    sources = (left.at[side], mine.at[1], right.at[side], ends_0.at[end], ends_1.at[end])
    copies = []
    for n, source in enumerate(sources):
        copies.append(pltpu.make_async_copy(source, params.at[n], sems.at[n]))
        copies[-1].start()
    for copy in copies:
        copy.wait()
    forward = next_first("lat")
    ends = {-1: jnp.where(forward, 4, 3), 1: jnp.where(forward, 3, 4)}
    for n, dc in enumerate(NEAR):
        for m, da in enumerate(NEAR):
            spot, lane = (n, 0) if da == 0 else (ends[da], n * SUB)
            number = lambda kind, o: params[spot, kind, lane + o]
            for o in range(SUB):
                out_ref[n * len(NEAR) + m, pl.ds(o, 1), :] = share(pad, number, rows, cols, da, dc, o)
    out_ref[len(NEAR) ** 2] = own_shift(lambda kind, o: params[1, kind, o])


def window_start(lat_count, my_lat):
    return 0 if lat_count <= WIN else jnp.clip(my_lat - REACH, 0, lat_count - WIN)


def column_of(block, j):
    return jnp.broadcast_to(block[:, j:j + 1], block.shape)


def pivot_rows(block, k, held, between):
    sub = lax.broadcasted_iota(jnp.int32, block.shape, 0)
    lane = lax.broadcasted_iota(jnp.int32, block.shape, 1) - k * SUB
    held[pl.ds(k * SUB, SUB), :] = block
    rows = [held[pl.ds(k * SUB + r, SUB, stride=0), :] for r in range(SUB)]
    at = {(r, n): column_of(rows[r], k * SUB + n) for r in range(SUB) for n in range(r + 1)}
    here = (lane >= 0) & (lane < SUB)
    rows = [jnp.where(here, jnp.where(lane == r, 1.0, 0.0), row) for r, row in enumerate(rows)]
    inverse, scale = (jnp.zeros(block.shape, F32), jnp.ones(block.shape, F32))
    for j in range(0, SUB, 2):
        a, b, c = (at[j, j], at[j + 1, j], at[j + 1, j + 1])
        det = a * c - b * b
        guess = pl.reciprocal(det, approx=True)
        better = 2.0 - det * guess
        over_det = guess * better
        top, bottom = (rows[j], rows[j + 1])
        rest = range(j + 2, SUB)
        upper = {n: (at[n, j], at[n, j + 1]) for n in rest}
        for r in rest:
            first, second = (at[r, j] * c - at[r, j + 1] * b, at[r, j + 1] * a - at[r, j] * b)
            if r < j + 4:
                for n in range(j + 2, r + 1):
                    taken = first * upper[n][0] + second * upper[n][1]
                    at[r, n] = at[r, n] - (taken * guess) * better
            first, second = (first * over_det, second * over_det)
            if r >= j + 4:
                for n in range(j + 2, r + 1):
                    at[r, n] = at[r, n] - (first * upper[n][0] + second * upper[n][1])
            rows[r] = rows[r] - (first * top + second * bottom)
        a_part, b_part, c_part = (a * over_det, b * over_det, c * over_det)
        for r in range(j):
            first = at[r, j] * c_part - at[r, j + 1] * b_part
            second = at[r, j + 1] * a_part - at[r, j] * b_part
            for n in rest:
                at[r, n] = at[r, n] - (first * upper[n][0] + second * upper[n][1])
            rows[r] = rows[r] - (first * top + second * bottom)
        for n in rest:
            at[j, n] = c_part * upper[n][0] - b_part * upper[n][1]
            at[j + 1, n] = a_part * upper[n][1] - b_part * upper[n][0]
        rows[j] = c_part * top - b_part * bottom
        rows[j + 1] = a_part * bottom - b_part * top
        inverse = jnp.where(sub == j, top, jnp.where(sub == j + 1, a * bottom - b * top, inverse))
        scale = jnp.where(sub == j, a, jnp.where(sub == j + 1, a * det, scale))
        between()
    return rows, jnp.where(lane < SUB, inverse * lax.rsqrt(scale), 0.0)


def eliminate(blocks, held):
    count = len(blocks) - 1
    blocks = list(blocks)
    lane = lax.broadcasted_iota(jnp.int32, blocks[0].shape, 1)
    inverse, waiting = ([], [])

    def update(i, k, pivot):
        terms = [column_of(blocks[i], k * SUB + j) * pivot[j] for j in range(SUB)]
        while len(terms) > 1:
            terms = [terms[n] + terms[n + 1] for n in range(0, len(terms), 2)]
        here = (lane >= k * SUB) & (lane < (k + 1) * SUB)
        blocks[i] = jnp.where(here, 0.0, blocks[i]) - terms[0]

    for k in range(count):
        share_of = -(-len(waiting) // 4)

        def between():
            for task in waiting[:share_of]:
                update(*task)
            del waiting[:share_of]

        pivot, rows = pivot_rows(blocks[k], k, held, between)
        update(k + 1, k, pivot)
        waiting = [(i, k, pivot) for i in range(k + 2, count + 1)]
        inverse.append(rows)
    return inverse, blocks[count][:1]


def own_blocks(near_ref):
    scaled = jnp.concatenate([near_ref[:, n].astype(F32) for n in range(PAIRS - 1)], axis=1)
    innov = near_ref[:, PAIRS - 1].astype(F32)[:, :1]
    sub = lax.broadcasted_iota(jnp.int32, scaled.shape, 1)
    lane = lax.broadcasted_iota(jnp.int32, scaled.shape, 2)
    return scaled, jnp.where(lane == sub, jnp.broadcast_to(innov, scaled.shape), 0.0)


def summed_blocks(lat_count, mine, other):
    held = min(WIN, lat_count)
    far_count = mine.shape[0] // lat_count
    start = window_start(lat_count, lax.axis_index("lat"))
    values = []
    for j in range(held):
        for far in range(far_count):
            for shares in (mine, other):
                total = jnp.zeros((SUB, LANES), F32)
                for n, da in enumerate(NEAR):
                    source = start + j - da
                    part = pl.ds(n * SUB, SUB)
                    if isinstance(source, int):
                        if 0 <= source < lat_count:
                            total = total + shares[source * far_count + far, part, :]
                    else:
                        inside = (source >= 0) & (source < lat_count)
                        source = jnp.clip(source, 0, lat_count - 1)
                        total = total + jnp.where(inside, shares[source * far_count + far, part, :], 0.0)
                values.append(total[None])
    value = jnp.concatenate(values, axis=0)
    mean = jnp.mean(value, axis=-1, keepdims=True)
    sub = lax.broadcasted_iota(jnp.int32, value.shape, 1)
    lane = lax.broadcasted_iota(jnp.int32, value.shape, 2)
    innov = jnp.where(lane == sub, jnp.broadcast_to(-mean, value.shape), 0.0)
    return (value - mean).astype(BF16).astype(F32), innov


def batch_map(batch, lat_count, blocks, pattern, swapped, held_rows):
    scaled, innov = blocks
    held = min(WIN, lat_count)
    count = scaled.shape[0]
    my_lat = lax.axis_index("lat")
    start = window_start(lat_count, my_lat)
    picked = []
    for j in range(held):
        offset = start + j - my_lat + REACH
        inside = (offset >= 0) & (offset < WIN)
        row = pattern[batch, 0, 0, pl.ds(jnp.clip(offset, 0, WIN - 1), 1), :].astype(F32)
        row = jnp.where(inside, row, 0.0)
        marks = [jnp.broadcast_to(row[:, e:e + 1], (1, SUB, LANES)) for e in range(count // held)]
        for e in range(0, len(marks), 2):
            first, second = marks[e:e + 2]
            if swapped is not None:
                first, second = (jnp.where(swapped, second, first), jnp.where(swapped, first, second))
            picked.extend((first, second))
    weighted = scaled * jnp.concatenate(picked, axis=0)
    both = jnp.concatenate([scaled, innov], axis=2).reshape(count * SUB, 2 * LANES).astype(BF16)
    product = lax.dot_general(
        both,
        weighted.reshape(count * SUB, LANES).astype(BF16),
        (((0,), (0,)), ((), ())),
        preferred_element_type=F32,
    )
    sub = lax.broadcasted_iota(jnp.int32, (SUB, LANES), 0)
    lane = lax.broadcasted_iota(jnp.int32, (SUB, LANES), 1)
    members = LANES
    blocks = []
    for k in range(members // SUB):
        block = product[k * SUB:(k + 1) * SUB, :]
        blocks.append(block + jnp.where(lane - k * SUB == sub, members - 1.0, 0.0))
    proj = jnp.sum(product[members:members + SUB, :], axis=0, keepdims=True)
    blocks.append(jnp.broadcast_to(proj, (SUB, LANES)))
    inverse, weights = eliminate(blocks, held_rows)
    flipped = jnp.concatenate(inverse, axis=0) * (members - 1.0) ** 0.5 - weights
    return flipped - jnp.mean(flipped, axis=-1, keepdims=True) + 1.0 / members


def exact_dot(a, b, contract_b):
    return lax.dot_general(
        a, b, (((1,), (contract_b,)), ((), ())), precision=lax.Precision.HIGHEST, preferred_element_type=F32
    )


def first_kernel(lat_count, near_ref, pattern, later, map_ref, mid_ref, out_0, out_1, held_rows):
    flipped = batch_map(0, lat_count, own_blocks(near_ref), pattern, None, held_rows)
    map_ref[...] = flipped
    count = len(NEAR) ** 2
    moved = exact_dot(later[pl.ds(0, count)].reshape(-1, LANES), flipped, 1)
    size = len(NEAR) * SUB
    left, mid, right = (moved[:size], moved[size:2 * size], moved[2 * size:])
    mid_ref[...] = mid
    own = pl.ds(SUB, SUB)
    mid_ref[own, :] = mid[SUB:2 * SUB] - later[count]
    forward = next_first("core")
    out_0[...] = jnp.where(forward, right, left)
    out_1[...] = jnp.where(forward, left, right)


def last_kernel(lat_count, mine, other, pattern, map_ref, pad, out_ref, result, held_rows, out_sem):
    parts = out_sem.shape[0]
    rows, cols = (pad.shape[0] - 4, pad.shape[1] - 2 * SUB)
    swapped = lax.axis_index("core") == 1
    blocks = summed_blocks(lat_count, mine, other)
    flipped = exact_dot(batch_map(1, lat_count, blocks, pattern, swapped, held_rows), map_ref[...], 0)
    high = flipped.astype(BF16)
    low = (flipped - high.astype(F32)).astype(BF16)
    right = jnp.concatenate(
        [jnp.concatenate([high, high], axis=1), jnp.concatenate([low, jnp.zeros_like(low)], axis=1)], axis=0
    )
    copies = []
    size = rows // parts
    for n in range(parts):
        part = pl.ds(n * size * cols, size * cols)
        value = pad[pl.ds(2 + n * size, size), pl.ds(SUB, cols), :].reshape(size * cols, LANES)
        upper = value.astype(BF16)
        rest = (value - upper.astype(F32)).astype(BF16)
        both = lax.dot_general(
            jnp.concatenate([upper, rest], axis=1), right, (((1,), (1,)), ((), ())), preferred_element_type=F32
        )
        result[part, :] = both[:, :LANES] + both[:, LANES:]
        copies.append(pltpu.make_async_copy(result.at[part], out_ref.at[part], out_sem.at[n]))
        copies[-1].start()
    for out_copy in copies:
        out_copy.wait()


def window(tiles, lat_count, lon_count):
    held = min(WIN, lat_count)
    if held == lat_count:
        return tiles
    start = jnp.clip(lax.axis_index("lat") - REACH, 0, lat_count - held)
    return lax.dynamic_slice_in_dim(tiles, start * lon_count, held * lon_count, axis=0)


def local(ensemble, observed, precision, interp_weight, stencil, owned, pattern):
    rows, cols, members = ensemble.shape
    batches = observed.shape[0]
    lat_count, lon_count = (lax.axis_size("lat"), lax.axis_size(LON))
    tiles = lat_count * lon_count
    vmem = pl.BlockSpec(memory_space=pltpu.VMEM)
    anywhere = pl.BlockSpec(memory_space=pl.ANY)
    hbm = pl.BlockSpec(memory_space=pltpu.HBM)
    megabyte = 1024 * 1024

    def shape(*dims, dtype=F32):
        return jax.ShapeDtypeStruct(dims, dtype)

    def call(kernel, name, specs, out_shape, scratch, *operands, out_specs=None, limit=48):
        return pl.pallas_call(
            kernel,
            out_shape=out_shape,
            in_specs=specs,
            out_specs=out_specs or jax.tree.map(lambda _: vmem, out_shape),
            scratch_shapes=scratch,
            compiler_params=pltpu.CompilerParams(vmem_limit_bytes=limit * megabyte),
            name=name,
        )(*operands)

    def exchange(blocks):
        return lax.all_to_all(blocks, ("lat",) + LON, split_axis=0, concat_axis=0, tiled=True)

    small = (observed, precision, interp_weight, stencil, owned)
    side = shape(rows + SUB, members)
    mine, side_1, side_0 = call(
        functools.partial(start_kernel, cols + 2),
        "start",
        [hbm] * 6,
        (shape(batches, SUB, LANES), side, side),
        [pltpu.VMEM(array.shape, array.dtype) for array in small]
        + [pltpu.VMEM((rows, SUB, members), F32)] * 2
        + [pltpu.SemaphoreType.DMA((7,))],
        *small,
        ensemble,
        limit=63,
    )
    sides = trade((side_0, side_1), LON, True)
    padded = shape(rows + 4, cols + 2 * SUB, members)
    pad = call(pad_kernel, "pad", [hbm], padded, [pltpu.SemaphoreType.DMA], ensemble)
    end = shape(cols + 3 * SUB, members)
    left, right, *ends = call(rows_kernel, "edge_rows", [vmem] * 4, (side, side, end, end), [], mine, *sides, pad)
    ends = trade(ends, "lat", False)
    slots = shape(tiles, PAIRS, 2, members, dtype=BF16)
    numbers = [pltpu.SMEM((SUB, LANES), F32), pltpu.SemaphoreType.DMA]
    block = shape(SUB, members)
    held_sides = pltpu.VMEM((2, rows + 2 * SUB, members), F32)
    own = call(row_kernel, "row_shares", [vmem] * 4, block, [held_sides] + numbers, mine, left, right, pad)
    blocks = call(
        functools.partial(prior_kernel, rows),
        "prior",
        [vmem] * 4,
        slots,
        [pltpu.VMEM((2,) + end.shape, F32), pltpu.VMEM((SUB, members), F32)] + numbers,
        mine,
        own,
        *ends,
    )
    near = window(exchange(blocks), lat_count, lon_count)
    count = len(NEAR) ** 2
    later = call(
        later_kernel,
        "later_shares",
        [vmem] * 6,
        shape(count + 1, SUB, members),
        [pltpu.SMEM((5, SUB, LANES), F32), pltpu.SemaphoreType.DMA((5,))],
        mine,
        left,
        right,
        *ends,
        pad,
    )
    column = shape(len(NEAR) * SUB, members)
    held_rows = pltpu.VMEM((members + SUB, members), F32)
    first_map, mid, *sides = call(
        functools.partial(first_kernel, lat_count),
        "first_batch",
        [vmem] * 3,
        (shape(members, members), column, column, column),
        [held_rows],
        near,
        pattern,
        later,
    )
    sides = trade(sides, LON, True)
    shares = call(meet_kernel, "meet", [vmem] * 3, shape(tiles // 2, *column.shape), [], mid, *sides)
    shares = lax.all_to_all(shares, ("lat", "far"), split_axis=0, concat_axis=0, tiled=True)
    other = lax.ppermute(shares, "core", [(0, 1), (1, 0)])
    parts = 8
    result = call(
        functools.partial(last_kernel, lat_count),
        "second_batch",
        [vmem] * 5,
        shape(rows * cols, members),
        [
            pltpu.VMEM((rows * cols, members), F32),
            held_rows,
            pltpu.SemaphoreType.DMA((parts,)),
        ],
        shares,
        other,
        pattern,
        first_map,
        pad,
        out_specs=anywhere,
    )
    return result.reshape(rows, cols, members)


def solution(mesh):
    lat_count, lon_count = (mesh.shape["lat"], mesh.shape["lon"])
    pairs = jax.sharding.Mesh(mesh.devices.reshape(lat_count, lon_count // 2, 2), ("lat",) + LON)
    placed = (
        P("lat", LON, None),
        P(None, "lat", LON, None),
        P(None, "lat", LON, None),
        P(None, "lat", LON, None, None),
        P(None, "lat", LON, None, None),
        P(None, "lat", LON, None),
        P(None, "lat", LON, None, None),
    )
    return jax.shard_map(
        local, mesh=pairs, in_specs=placed, out_specs=P("lat", LON, None), check_vma=False
    )
```

```python
import functools
import jax
import jax.numpy as jnp
from jax import lax
from jax.experimental import pallas as pl
from jax.experimental.pallas import tpu as pltpu
from jax.sharding import PartitionSpec as P

REACH = 2
WIN = 2 * REACH + 1
SUB = 8
LANES = 128
NEAR = (-1, 0, 1)
AT_ROW, AT_COL, AT_OBS = (4, 5, 6)
PAIRS = SUB // 2 + 1
F32 = jnp.float32
BF16 = jnp.bfloat16
LON = ("far", "core")


def partner(place, turn):
    return place + (-1 if place % 2 == turn else 1)


def trade(blocks, axis, wraps):
    count = lax.axis_size(axis)
    results = []
    for turn, block in enumerate(blocks):
        route = [(place, partner(place, turn)) for place in range(count)]
        route = [(source, target % count) for source, target in route if wraps or 0 <= target < count]
        results.append(lax.ppermute(block, axis, route))
    return results


def next_first(axis):
    return lax.rem(lax.axis_index(axis), 2) == 1


def start_kernel(
    width, observed, precision, weight, stencil, owned, cells, params_ref, sides_1, sides_0,
    observed_v, precision_v, weight_v, stencil_v, owned_v, left_v, right_v, sems
):
    batches, cols = (observed.shape[0], cells.shape[1])
    pairs = (
        (observed, observed_v),
        (precision, precision_v),
        (weight, weight_v),
        (stencil, stencil_v),
        (owned, owned_v),
        (cells.at[:, pl.ds(0, SUB)], left_v),
        (cells.at[:, pl.ds(cols - SUB, SUB)], right_v),
    )
    copies = [pltpu.make_async_copy(source, target, sems.at[n]) for n, (source, target) in enumerate(pairs)]
    for copy in copies:
        copy.start()
    for copy in copies:
        copy.wait()
    params_ref[...] = jnp.zeros_like(params_ref)
    for b in range(batches):
        root = jnp.sqrt(precision_v[b, 0]) * owned_v[b, 0].astype(F32)
        corner = stencil_v[b, 0, 0, pl.ds(0, 1)].astype(F32)
        row = jnp.floor((corner + 0.5) * (1.0 / width))
        params_ref[b, pl.ds(0, 4), pl.ds(0, SUB)] = weight_v[b, 0, 0] * root
        params_ref[b, pl.ds(AT_ROW, 1), pl.ds(0, SUB)] = row
        params_ref[b, pl.ds(AT_COL, 1), pl.ds(0, SUB)] = corner - row * width
        params_ref[b, pl.ds(AT_OBS, 1), pl.ds(0, SUB)] = observed_v[b, 0] * root
    rows = cells.shape[0]
    forward = next_first("core")
    left, right = (left_v[:, 0, :], right_v[:, SUB - 1, :])
    sides_0[pl.ds(0, rows), :] = jnp.where(forward, right, left)
    sides_1[pl.ds(0, rows), :] = jnp.where(forward, left, right)
    sides_0[pl.ds(rows, SUB), :] = params_ref[1]
    sides_1[pl.ds(rows, SUB), :] = params_ref[1]


def clear_rim(pad, rows, cols):
    edge = jnp.zeros((2, cols + 2 * SUB, LANES), F32)
    pad[pl.ds(0, 2)] = edge
    pad[pl.ds(rows + 2, 2)] = edge
    side = jnp.zeros((rows, SUB, LANES), F32)
    pad[pl.ds(2, rows), pl.ds(0, SUB)] = side
    pad[pl.ds(2, rows), pl.ds(SUB + cols, SUB)] = side


def share(pad, number, rows, cols, da, dc, o):
    row = number(AT_ROW, o).astype(jnp.int32) - 1 + da * rows
    col = number(AT_COL, o).astype(jnp.int32) - 1 + dc * cols
    row = jnp.clip(row, -2, rows) + 2
    col = jnp.clip(col, -2, cols) + SUB
    terms = [number(k, o) * pad[row + k // 2, pl.ds(col + k % 2, 1), :] for k in range(4)]
    return (terms[0] + terms[1]) + (terms[2] + terms[3])


def own_shift(number):
    sub = lax.broadcasted_iota(jnp.int32, (SUB, LANES), 0)
    shift = jnp.zeros((SUB, LANES), F32)
    for o in range(SUB):
        shift = jnp.where(sub == o, number(AT_OBS, o), shift)
    return shift


def pad_kernel(cells, pad, sem):
    rows, cols = (cells.shape[0], cells.shape[1])
    copy = pltpu.make_async_copy(cells, pad.at[pl.ds(2, rows), pl.ds(SUB, cols)], sem)
    copy.start()
    clear_rim(pad, rows, cols)
    copy.wait()


def hold_sides(left, right, sides):
    rows = left.shape[0] - SUB
    sides[...] = jnp.zeros_like(sides)
    sides[0, pl.ds(SUB, rows), :] = left[pl.ds(0, rows), :]
    sides[1, pl.ds(SUB, rows), :] = right[pl.ds(0, rows), :]


def side_share(sides, side, number, rows, cols, da, o):
    row = number(AT_ROW, o).astype(jnp.int32) - 1 + da * rows
    row = jnp.clip(row, -2, rows) + SUB
    used = number(AT_COL, o).astype(jnp.int32) == (0, cols)[side]
    terms = [jnp.where(used, number(side + 2 * k, o), 0.0) * sides[side, pl.ds(row + k, 1), :] for k in range(2)]
    return terms[0] + terms[1]


def send_block(value, out_ref):
    mean = jnp.mean(value, axis=-1, keepdims=True)
    sub = lax.broadcasted_iota(jnp.int32, (SUB, LANES), 0)
    lane = lax.broadcasted_iota(jnp.int32, (SUB, LANES), 1)
    innov = jnp.sum(jnp.where(lane == sub, -mean, 0.0), axis=0, keepdims=True)
    rows = jnp.concatenate([value - mean, jnp.broadcast_to(innov, (2, LANES))], axis=0).astype(BF16)
    for n in range(PAIRS):
        pair = rows[2 * n:2 * n + 2]
        out_ref[:, n] = jnp.broadcast_to(pair, (out_ref.shape[0],) + pair.shape)


def rows_kernel(mine, sides_0, sides_1, pad, left_ref, right_ref, out_0, out_1):
    rows, cols = (pad.shape[0] - 4, pad.shape[1] - 2 * SUB)
    forward = next_first("core")
    left_ref[...] = jnp.where(forward, sides_1[...], sides_0[...])
    right_ref[...] = jnp.where(forward, sides_0[...], sides_1[...])
    lane = lax.broadcasted_iota(jnp.int32, (SUB, LANES), 1)
    block = pl.ds(rows, SUB)
    packed = jnp.where(lane < SUB, left_ref[block, :], pltpu.roll(mine[1], SUB, 1))
    packed = jnp.where(lane < 2 * SUB, packed, pltpu.roll(right_ref[block, :], 2 * SUB, 1))
    forward = next_first("lat")
    for turn, out in enumerate((out_0, out_1)):
        row = jnp.where(forward, (1 - turn) * (rows - 1), turn * (rows - 1))
        out[pl.ds(0, SUB), :] = jnp.broadcast_to(left_ref[pl.ds(row, 1), :], (SUB, LANES))
        out[pl.ds(SUB, cols), :] = pad[2 + row, pl.ds(SUB, cols), :]
        out[pl.ds(SUB + cols, SUB), :] = jnp.broadcast_to(right_ref[pl.ds(row, 1), :], (SUB, LANES))
        out[pl.ds(2 * SUB + cols, SUB), :] = packed


def row_kernel(mine, left, right, pad, out_ref, sides, params, sem):
    rows, cols = (pad.shape[0] - 4, pad.shape[1] - 2 * SUB)
    copy = pltpu.make_async_copy(mine.at[0], params, sem)
    copy.start()
    hold_sides(left, right, sides)
    copy.wait()
    number = lambda kind, o: params[kind, o]
    for o in range(SUB):
        total = share(pad, number, rows, cols, 0, 0, o)
        for side in range(2):
            total = total + side_share(sides, side, number, rows, cols, 0, o)
        out_ref[pl.ds(o, 1), :] = total
    out_ref[...] = out_ref[...] - own_shift(number)


def prior_kernel(rows, mine, own, ends_0, ends_1, out_ref, ends, value, params, sem):
    copy = pltpu.make_async_copy(mine.at[0], params, sem)
    copy.start()
    forward = next_first("lat")
    ends[0] = jnp.where(forward, ends_1[...], ends_0[...])
    ends[1] = jnp.where(forward, ends_0[...], ends_1[...])
    copy.wait()
    for o in range(SUB):
        row, col = (params[AT_ROW, o].astype(jnp.int32), params[AT_COL, o].astype(jnp.int32))
        total = own[pl.ds(o, 1), :]
        for n, at in enumerate((0, rows)):
            for k in range(2):
                weight = jnp.where(row == at, params[2 * n + k, o], 0.0)
                total = total + weight * ends[n, pl.ds(col + SUB - 1 + k, 1), :]
        value[pl.ds(o, 1), :] = total
    send_block(value[...], out_ref)


def meet_kernel(mid, sides_0, sides_1, out_ref):
    out_ref[...] = jnp.broadcast_to(mid[...] + sides_0[...] + sides_1[...], out_ref.shape)


def later_tasks(mine, left, right, ends_0, ends_1, pad, later, params, sems):
    rows, cols = (pad.shape[0] - 4, pad.shape[1] - 2 * SUB)
    side, end = (pl.ds(rows, SUB), pl.ds(cols + 2 * SUB, SUB))
    sources = (left.at[side], mine.at[1], right.at[side], ends_0.at[end], ends_1.at[end])
    copies = []
    for n, source in enumerate(sources):
        copies.append(pltpu.make_async_copy(source, params.at[n], sems.at[n]))
        copies[-1].start()

    def wait():
        for copy in copies:
            copy.wait()

    def one(spot, lane, da, dc, o, at):
        number = lambda kind, o: params[spot, kind, lane + o]
        later[pl.ds(at, 1), :] = share(pad, number, rows, cols, da, dc, o)

    def own():
        later[pl.ds(len(NEAR) ** 2 * SUB, SUB), :] = own_shift(lambda kind, o: params[1, kind, o])

    forward = next_first("lat")
    ends = {-1: jnp.where(forward, 4, 3), 1: jnp.where(forward, 3, 4)}
    tasks = [wait, own]
    for n, dc in enumerate(NEAR):
        for m, da in enumerate(NEAR):
            spot, lane = (n, 0) if da == 0 else (ends[da], n * SUB)
            for o in range(SUB):
                at = (n * len(NEAR) + m) * SUB + o
                tasks.append(functools.partial(one, spot, lane, da, dc, o, at))
    return tasks


def window_start(lat_count, my_lat):
    return 0 if lat_count <= WIN else jnp.clip(my_lat - REACH, 0, lat_count - WIN)


def column_of(block, j):
    return jnp.broadcast_to(block[:, j:j + 1], block.shape)


def pivot_rows(block, k, held, between):
    sub = lax.broadcasted_iota(jnp.int32, block.shape, 0)
    lane = lax.broadcasted_iota(jnp.int32, block.shape, 1) - k * SUB
    held[pl.ds(k * SUB, SUB), :] = block
    rows = [held[pl.ds(k * SUB + r, SUB, stride=0), :] for r in range(SUB)]
    at = {(r, n): column_of(rows[r], k * SUB + n) for r in range(SUB) for n in range(r + 1)}
    here = (lane >= 0) & (lane < SUB)
    rows = [jnp.where(here, jnp.where(lane == r, 1.0, 0.0), row) for r, row in enumerate(rows)]
    inverse, scale = (jnp.zeros(block.shape, F32), jnp.ones(block.shape, F32))
    for j in range(0, SUB, 2):
        a, b, c = (at[j, j], at[j + 1, j], at[j + 1, j + 1])
        det = a * c - b * b
        guess = pl.reciprocal(det, approx=True)
        better = 2.0 - det * guess
        over_det = guess * better
        top, bottom = (rows[j], rows[j + 1])
        rest = range(j + 2, SUB)
        upper = {n: (at[n, j], at[n, j + 1]) for n in rest}
        for r in rest:
            first, second = (at[r, j] * c - at[r, j + 1] * b, at[r, j + 1] * a - at[r, j] * b)
            if r < j + 4:
                for n in range(j + 2, r + 1):
                    taken = first * upper[n][0] + second * upper[n][1]
                    at[r, n] = at[r, n] - (taken * guess) * better
            first, second = (first * over_det, second * over_det)
            if r >= j + 4:
                for n in range(j + 2, r + 1):
                    at[r, n] = at[r, n] - (first * upper[n][0] + second * upper[n][1])
            rows[r] = rows[r] - (first * top + second * bottom)
        a_part, b_part, c_part = (a * over_det, b * over_det, c * over_det)
        for r in range(j):
            first = at[r, j] * c_part - at[r, j + 1] * b_part
            second = at[r, j + 1] * a_part - at[r, j] * b_part
            for n in rest:
                at[r, n] = at[r, n] - (first * upper[n][0] + second * upper[n][1])
            rows[r] = rows[r] - (first * top + second * bottom)
        for n in rest:
            at[j, n] = c_part * upper[n][0] - b_part * upper[n][1]
            at[j + 1, n] = a_part * upper[n][1] - b_part * upper[n][0]
        rows[j] = c_part * top - b_part * bottom
        rows[j + 1] = a_part * bottom - b_part * top
        inverse = jnp.where(sub == j, top, jnp.where(sub == j + 1, a * bottom - b * top, inverse))
        scale = jnp.where(sub == j, a, jnp.where(sub == j + 1, a * det, scale))
        between()
    return rows, jnp.where(lane < SUB, inverse * lax.rsqrt(scale), 0.0)


def eliminate(blocks, held, tasks):
    tasks = list(tasks)
    count = len(blocks) - 1
    blocks = list(blocks)
    lane = lax.broadcasted_iota(jnp.int32, blocks[0].shape, 1)
    inverse, waiting = ([], [])

    def update(i, k, pivot):
        terms = [column_of(blocks[i], k * SUB + j) * pivot[j] for j in range(SUB)]
        while len(terms) > 1:
            terms = [terms[n] + terms[n + 1] for n in range(0, len(terms), 2)]
        here = (lane >= k * SUB) & (lane < (k + 1) * SUB)
        blocks[i] = jnp.where(here, 0.0, blocks[i]) - terms[0]

    for k in range(count):
        share_of = -(-len(waiting) // 4)

        def between():
            for task in waiting[:share_of]:
                update(*task)
            del waiting[:share_of]
            if k > 0:
                for task in tasks[:2]:
                    task()
                del tasks[:2]

        pivot, rows = pivot_rows(blocks[k], k, held, between)
        update(k + 1, k, pivot)
        waiting = [(i, k, pivot) for i in range(k + 2, count + 1)]
        inverse.append(rows)
    return inverse, blocks[count][:1]


def own_blocks(near_ref):
    scaled = jnp.concatenate([near_ref[:, n].astype(F32) for n in range(PAIRS - 1)], axis=1)
    innov = near_ref[:, PAIRS - 1].astype(F32)[:, :1]
    sub = lax.broadcasted_iota(jnp.int32, scaled.shape, 1)
    lane = lax.broadcasted_iota(jnp.int32, scaled.shape, 2)
    return scaled, jnp.where(lane == sub, jnp.broadcast_to(innov, scaled.shape), 0.0)


def summed_blocks(lat_count, mine, other):
    held = min(WIN, lat_count)
    far_count = mine.shape[0] // lat_count
    start = window_start(lat_count, lax.axis_index("lat"))
    values = []
    for j in range(held):
        for far in range(far_count):
            for shares in (mine, other):
                total = jnp.zeros((SUB, LANES), F32)
                for n, da in enumerate(NEAR):
                    source = start + j - da
                    part = pl.ds(n * SUB, SUB)
                    if isinstance(source, int):
                        if 0 <= source < lat_count:
                            total = total + shares[source * far_count + far, part, :]
                    else:
                        inside = (source >= 0) & (source < lat_count)
                        source = jnp.clip(source, 0, lat_count - 1)
                        total = total + jnp.where(inside, shares[source * far_count + far, part, :], 0.0)
                values.append(total[None])
    value = jnp.concatenate(values, axis=0)
    mean = jnp.mean(value, axis=-1, keepdims=True)
    sub = lax.broadcasted_iota(jnp.int32, value.shape, 1)
    lane = lax.broadcasted_iota(jnp.int32, value.shape, 2)
    innov = jnp.where(lane == sub, jnp.broadcast_to(-mean, value.shape), 0.0)
    return (value - mean).astype(BF16).astype(F32), innov


def batch_map(batch, lat_count, blocks, pattern, swapped, held_rows, tasks):
    scaled, innov = blocks
    held = min(WIN, lat_count)
    count = scaled.shape[0]
    my_lat = lax.axis_index("lat")
    start = window_start(lat_count, my_lat)
    picked = []
    for j in range(held):
        offset = start + j - my_lat + REACH
        inside = (offset >= 0) & (offset < WIN)
        row = pattern[batch, 0, 0, pl.ds(jnp.clip(offset, 0, WIN - 1), 1), :].astype(F32)
        row = jnp.where(inside, row, 0.0)
        marks = [jnp.broadcast_to(row[:, e:e + 1], (1, SUB, LANES)) for e in range(count // held)]
        for e in range(0, len(marks), 2):
            first, second = marks[e:e + 2]
            if swapped is not None:
                first, second = (jnp.where(swapped, second, first), jnp.where(swapped, first, second))
            picked.extend((first, second))
    weighted = scaled * jnp.concatenate(picked, axis=0)
    both = jnp.concatenate([scaled, innov], axis=2).reshape(count * SUB, 2 * LANES).astype(BF16)
    product = lax.dot_general(
        both,
        weighted.reshape(count * SUB, LANES).astype(BF16),
        (((0,), (0,)), ((), ())),
        preferred_element_type=F32,
    )
    sub = lax.broadcasted_iota(jnp.int32, (SUB, LANES), 0)
    lane = lax.broadcasted_iota(jnp.int32, (SUB, LANES), 1)
    members = LANES
    blocks = []
    for k in range(members // SUB):
        block = product[k * SUB:(k + 1) * SUB, :]
        blocks.append(block + jnp.where(lane - k * SUB == sub, members - 1.0, 0.0))
    proj = jnp.sum(product[members:members + SUB, :], axis=0, keepdims=True)
    blocks.append(jnp.broadcast_to(proj, (SUB, LANES)))
    inverse, weights = eliminate(blocks, held_rows, tasks)
    flipped = jnp.concatenate(inverse, axis=0) * (members - 1.0) ** 0.5 - weights
    return flipped - jnp.mean(flipped, axis=-1, keepdims=True) + 1.0 / members


def exact_dot(a, b, contract_b):
    return lax.dot_general(
        a, b, (((1,), (contract_b,)), ((), ())), precision=lax.Precision.HIGHEST, preferred_element_type=F32
    )


def first_kernel(lat_count, near_ref, pattern, *refs):
    around, (map_ref, mid_ref, out_0, out_1, held_rows, later, params, sems) = (refs[:6], refs[6:])
    tasks = later_tasks(*around, later, params, sems)
    flipped = batch_map(0, lat_count, own_blocks(near_ref), pattern, None, held_rows, tasks)
    map_ref[...] = flipped
    count = len(NEAR) ** 2
    moved = exact_dot(later[pl.ds(0, count * SUB), :], flipped, 1)
    size = len(NEAR) * SUB
    left, mid, right = (moved[:size], moved[size:2 * size], moved[2 * size:])
    mid_ref[...] = mid
    own = pl.ds(SUB, SUB)
    mid_ref[own, :] = mid[SUB:2 * SUB] - later[pl.ds(count * SUB, SUB), :]
    forward = next_first("core")
    out_0[...] = jnp.where(forward, right, left)
    out_1[...] = jnp.where(forward, left, right)


def last_kernel(lat_count, mine, other, pattern, map_ref, pad, out_ref, result, held_rows, out_sem):
    parts = out_sem.shape[0]
    rows, cols = (pad.shape[0] - 4, pad.shape[1] - 2 * SUB)
    swapped = lax.axis_index("core") == 1
    blocks = summed_blocks(lat_count, mine, other)
    flipped = exact_dot(batch_map(1, lat_count, blocks, pattern, swapped, held_rows, ()), map_ref[...], 0)
    high = flipped.astype(BF16)
    low = (flipped - high.astype(F32)).astype(BF16)
    right = jnp.concatenate(
        [jnp.concatenate([high, high], axis=1), jnp.concatenate([low, jnp.zeros_like(low)], axis=1)], axis=0
    )
    copies = []
    size = rows // parts
    for n in range(parts):
        part = pl.ds(n * size * cols, size * cols)
        value = pad[pl.ds(2 + n * size, size), pl.ds(SUB, cols), :].reshape(size * cols, LANES)
        upper = value.astype(BF16)
        rest = (value - upper.astype(F32)).astype(BF16)
        both = lax.dot_general(
            jnp.concatenate([upper, rest], axis=1), right, (((1,), (1,)), ((), ())), preferred_element_type=F32
        )
        result[part, :] = both[:, :LANES] + both[:, LANES:]
        copies.append(pltpu.make_async_copy(result.at[part], out_ref.at[part], out_sem.at[n]))
        copies[-1].start()
    for out_copy in copies:
        out_copy.wait()


def window(tiles, lat_count, lon_count):
    held = min(WIN, lat_count)
    if held == lat_count:
        return tiles
    start = jnp.clip(lax.axis_index("lat") - REACH, 0, lat_count - held)
    return lax.dynamic_slice_in_dim(tiles, start * lon_count, held * lon_count, axis=0)


def local(ensemble, observed, precision, interp_weight, stencil, owned, pattern):
    rows, cols, members = ensemble.shape
    batches = observed.shape[0]
    lat_count, lon_count = (lax.axis_size("lat"), lax.axis_size(LON))
    tiles = lat_count * lon_count
    vmem = pl.BlockSpec(memory_space=pltpu.VMEM)
    anywhere = pl.BlockSpec(memory_space=pl.ANY)
    hbm = pl.BlockSpec(memory_space=pltpu.HBM)
    megabyte = 1024 * 1024

    def shape(*dims, dtype=F32):
        return jax.ShapeDtypeStruct(dims, dtype)

    def call(kernel, name, specs, out_shape, scratch, *operands, out_specs=None, limit=48):
        return pl.pallas_call(
            kernel,
            out_shape=out_shape,
            in_specs=specs,
            out_specs=out_specs or jax.tree.map(lambda _: vmem, out_shape),
            scratch_shapes=scratch,
            compiler_params=pltpu.CompilerParams(vmem_limit_bytes=limit * megabyte),
            name=name,
        )(*operands)

    def exchange(blocks):
        return lax.all_to_all(blocks, ("lat",) + LON, split_axis=0, concat_axis=0, tiled=True)

    small = (observed, precision, interp_weight, stencil, owned)
    side = shape(rows + SUB, members)
    mine, side_1, side_0 = call(
        functools.partial(start_kernel, cols + 2),
        "start",
        [hbm] * 6,
        (shape(batches, SUB, LANES), side, side),
        [pltpu.VMEM(array.shape, array.dtype) for array in small]
        + [pltpu.VMEM((rows, SUB, members), F32)] * 2
        + [pltpu.SemaphoreType.DMA((7,))],
        *small,
        ensemble,
        limit=63,
    )
    sides = trade((side_0, side_1), LON, True)
    padded = shape(rows + 4, cols + 2 * SUB, members)
    pad = call(pad_kernel, "pad", [hbm], padded, [pltpu.SemaphoreType.DMA], ensemble)
    end = shape(cols + 3 * SUB, members)
    left, right, *ends = call(rows_kernel, "edge_rows", [vmem] * 4, (side, side, end, end), [], mine, *sides, pad)
    ends = trade(ends, "lat", False)
    slots = shape(tiles, PAIRS, 2, members, dtype=BF16)
    numbers = [pltpu.SMEM((SUB, LANES), F32), pltpu.SemaphoreType.DMA]
    block = shape(SUB, members)
    held_sides = pltpu.VMEM((2, rows + 2 * SUB, members), F32)
    own = call(row_kernel, "row_shares", [vmem] * 4, block, [held_sides] + numbers, mine, left, right, pad)
    blocks = call(
        functools.partial(prior_kernel, rows),
        "prior",
        [vmem] * 4,
        slots,
        [pltpu.VMEM((2,) + end.shape, F32), pltpu.VMEM((SUB, members), F32)] + numbers,
        mine,
        own,
        *ends,
    )
    near = window(exchange(blocks), lat_count, lon_count)
    count = len(NEAR) ** 2
    column = shape(len(NEAR) * SUB, members)
    held_rows = pltpu.VMEM((members + SUB, members), F32)
    first_map, mid, *sides = call(
        functools.partial(first_kernel, lat_count),
        "first_batch",
        [vmem] * 8,
        (shape(members, members), column, column, column),
        [
            held_rows,
            pltpu.VMEM(((count + 1) * SUB, members), F32),
            pltpu.SMEM((5, SUB, LANES), F32),
            pltpu.SemaphoreType.DMA((5,)),
        ],
        near,
        pattern,
        mine,
        left,
        right,
        *ends,
        pad,
    )
    sides = trade(sides, LON, True)
    shares = call(meet_kernel, "meet", [vmem] * 3, shape(tiles // 2, *column.shape), [], mid, *sides)
    shares = lax.all_to_all(shares, ("lat", "far"), split_axis=0, concat_axis=0, tiled=True)
    other = lax.ppermute(shares, "core", [(0, 1), (1, 0)])
    parts = 8
    result = call(
        functools.partial(last_kernel, lat_count),
        "second_batch",
        [vmem] * 5,
        shape(rows * cols, members),
        [
            pltpu.VMEM((rows * cols, members), F32),
            held_rows,
            pltpu.SemaphoreType.DMA((parts,)),
        ],
        shares,
        other,
        pattern,
        first_map,
        pad,
        out_specs=anywhere,
    )
    return result.reshape(rows, cols, members)


def solution(mesh):
    lat_count, lon_count = (mesh.shape["lat"], mesh.shape["lon"])
    pairs = jax.sharding.Mesh(mesh.devices.reshape(lat_count, lon_count // 2, 2), ("lat",) + LON)
    placed = (
        P("lat", LON, None),
        P(None, "lat", LON, None),
        P(None, "lat", LON, None),
        P(None, "lat", LON, None, None),
        P(None, "lat", LON, None, None),
        P(None, "lat", LON, None),
        P(None, "lat", LON, None, None),
    )
    return jax.shard_map(
        local, mesh=pairs, in_specs=placed, out_specs=P("lat", LON, None), check_vma=False
    )
```

```python
import functools
import jax
import jax.numpy as jnp
from jax import lax
from jax.experimental import pallas as pl
from jax.experimental.pallas import tpu as pltpu
from jax.sharding import PartitionSpec as P

REACH = 2
WIN = 2 * REACH + 1
SUB = 8
LANES = 128
NEAR = (-1, 0, 1)
AT_ROW, AT_COL, AT_OBS = (4, 5, 6)
PAIRS = SUB // 2 + 1
F32 = jnp.float32
BF16 = jnp.bfloat16
LON = ("far", "core")


def partner(place, turn):
    return place + (-1 if place % 2 == turn else 1)


def trade(blocks, axis, wraps):
    count = lax.axis_size(axis)
    results = []
    for turn, block in enumerate(blocks):
        route = [(place, partner(place, turn)) for place in range(count)]
        route = [(source, target % count) for source, target in route if wraps or 0 <= target < count]
        results.append(lax.ppermute(block, axis, route))
    return results


def next_first(axis):
    return lax.rem(lax.axis_index(axis), 2) == 1


def start_kernel(
    width, observed, precision, weight, stencil, owned, cells, params_ref, sides_1, sides_0,
    observed_v, precision_v, weight_v, stencil_v, owned_v, left_v, right_v, sems
):
    batches, cols = (observed.shape[0], cells.shape[1])
    pairs = (
        (observed, observed_v),
        (precision, precision_v),
        (weight, weight_v),
        (stencil, stencil_v),
        (owned, owned_v),
        (cells.at[:, pl.ds(0, SUB)], left_v),
        (cells.at[:, pl.ds(cols - SUB, SUB)], right_v),
    )
    copies = [pltpu.make_async_copy(source, target, sems.at[n]) for n, (source, target) in enumerate(pairs)]
    for copy in copies:
        copy.start()
    for copy in copies:
        copy.wait()
    params_ref[...] = jnp.zeros_like(params_ref)
    for b in range(batches):
        root = jnp.sqrt(precision_v[b, 0]) * owned_v[b, 0].astype(F32)
        corner = stencil_v[b, 0, 0, pl.ds(0, 1)].astype(F32)
        row = jnp.floor((corner + 0.5) * (1.0 / width))
        params_ref[b, pl.ds(0, 4), pl.ds(0, SUB)] = weight_v[b, 0, 0] * root
        params_ref[b, pl.ds(AT_ROW, 1), pl.ds(0, SUB)] = row
        params_ref[b, pl.ds(AT_COL, 1), pl.ds(0, SUB)] = corner - row * width
        params_ref[b, pl.ds(AT_OBS, 1), pl.ds(0, SUB)] = observed_v[b, 0] * root
    rows = cells.shape[0]
    forward = next_first("core")
    left, right = (left_v[:, 0, :], right_v[:, SUB - 1, :])
    sides_0[pl.ds(0, rows), :] = jnp.where(forward, right, left)
    sides_1[pl.ds(0, rows), :] = jnp.where(forward, left, right)
    sides_0[pl.ds(rows, SUB), :] = params_ref[1]
    sides_1[pl.ds(rows, SUB), :] = params_ref[1]


def clear_rim(pad, rows, cols):
    edge = jnp.zeros((2, cols + 2 * SUB, LANES), F32)
    pad[pl.ds(0, 2)] = edge
    pad[pl.ds(rows + 2, 2)] = edge
    side = jnp.zeros((rows, SUB, LANES), F32)
    pad[pl.ds(2, rows), pl.ds(0, SUB)] = side
    pad[pl.ds(2, rows), pl.ds(SUB + cols, SUB)] = side


def share(pad, number, rows, cols, da, dc, o):
    row = number(AT_ROW, o).astype(jnp.int32) - 1 + da * rows
    col = number(AT_COL, o).astype(jnp.int32) - 1 + dc * cols
    row = jnp.clip(row, -2, rows) + 2
    col = jnp.clip(col, -2, cols) + SUB
    terms = [number(k, o) * pad[row + k // 2, pl.ds(col + k % 2, 1), :] for k in range(4)]
    return (terms[0] + terms[1]) + (terms[2] + terms[3])


def own_shift(number):
    sub = lax.broadcasted_iota(jnp.int32, (SUB, LANES), 0)
    shift = jnp.zeros((SUB, LANES), F32)
    for o in range(SUB):
        shift = jnp.where(sub == o, number(AT_OBS, o), shift)
    return shift


def pad_kernel(cells, pad, sem):
    rows, cols = (cells.shape[0], cells.shape[1])
    copy = pltpu.make_async_copy(cells, pad.at[pl.ds(2, rows), pl.ds(SUB, cols)], sem)
    copy.start()
    clear_rim(pad, rows, cols)
    copy.wait()


def hold_sides(left, right, sides):
    rows = left.shape[0] - SUB
    sides[...] = jnp.zeros_like(sides)
    sides[0, pl.ds(SUB, rows), :] = left[pl.ds(0, rows), :]
    sides[1, pl.ds(SUB, rows), :] = right[pl.ds(0, rows), :]


def side_share(sides, side, number, rows, cols, da, o):
    row = number(AT_ROW, o).astype(jnp.int32) - 1 + da * rows
    row = jnp.clip(row, -2, rows) + SUB
    used = number(AT_COL, o).astype(jnp.int32) == (0, cols)[side]
    terms = [jnp.where(used, number(side + 2 * k, o), 0.0) * sides[side, pl.ds(row + k, 1), :] for k in range(2)]
    return terms[0] + terms[1]


def send_block(value, out_ref):
    mean = jnp.mean(value, axis=-1, keepdims=True)
    sub = lax.broadcasted_iota(jnp.int32, (SUB, LANES), 0)
    lane = lax.broadcasted_iota(jnp.int32, (SUB, LANES), 1)
    innov = jnp.sum(jnp.where(lane == sub, -mean, 0.0), axis=0, keepdims=True)
    rows = jnp.concatenate([value - mean, jnp.broadcast_to(innov, (2, LANES))], axis=0).astype(BF16)
    for n in range(PAIRS):
        pair = rows[2 * n:2 * n + 2]
        out_ref[:, n] = jnp.broadcast_to(pair, (out_ref.shape[0],) + pair.shape)


def rows_kernel(mine, sides_0, sides_1, pad, left_ref, right_ref, out_0, out_1):
    rows, cols = (pad.shape[0] - 4, pad.shape[1] - 2 * SUB)
    forward = next_first("core")
    left_ref[...] = jnp.where(forward, sides_1[...], sides_0[...])
    right_ref[...] = jnp.where(forward, sides_0[...], sides_1[...])
    lane = lax.broadcasted_iota(jnp.int32, (SUB, LANES), 1)
    block = pl.ds(rows, SUB)
    packed = jnp.where(lane < SUB, left_ref[block, :], pltpu.roll(mine[1], SUB, 1))
    packed = jnp.where(lane < 2 * SUB, packed, pltpu.roll(right_ref[block, :], 2 * SUB, 1))
    forward = next_first("lat")
    for turn, out in enumerate((out_0, out_1)):
        row = jnp.where(forward, (1 - turn) * (rows - 1), turn * (rows - 1))
        out[pl.ds(0, SUB), :] = jnp.broadcast_to(left_ref[pl.ds(row, 1), :], (SUB, LANES))
        out[pl.ds(SUB, cols), :] = pad[2 + row, pl.ds(SUB, cols), :]
        out[pl.ds(SUB + cols, SUB), :] = jnp.broadcast_to(right_ref[pl.ds(row, 1), :], (SUB, LANES))
        out[pl.ds(2 * SUB + cols, SUB), :] = packed


def row_kernel(mine, left, right, pad, out_ref, sides, params, sem):
    rows, cols = (pad.shape[0] - 4, pad.shape[1] - 2 * SUB)
    copy = pltpu.make_async_copy(mine.at[0], params, sem)
    copy.start()
    hold_sides(left, right, sides)
    copy.wait()
    number = lambda kind, o: params[kind, o]
    for o in range(SUB):
        total = share(pad, number, rows, cols, 0, 0, o)
        for side in range(2):
            total = total + side_share(sides, side, number, rows, cols, 0, o)
        out_ref[pl.ds(o, 1), :] = total
    out_ref[...] = out_ref[...] - own_shift(number)


def prior_kernel(rows, mine, own, ends_0, ends_1, out_ref, ends, value, params, sem):
    copy = pltpu.make_async_copy(mine.at[0], params, sem)
    copy.start()
    forward = next_first("lat")
    ends[0] = jnp.where(forward, ends_1[...], ends_0[...])
    ends[1] = jnp.where(forward, ends_0[...], ends_1[...])
    copy.wait()
    for o in range(SUB):
        row, col = (params[AT_ROW, o].astype(jnp.int32), params[AT_COL, o].astype(jnp.int32))
        total = own[pl.ds(o, 1), :]
        for n, at in enumerate((0, rows)):
            for k in range(2):
                weight = jnp.where(row == at, params[2 * n + k, o], 0.0)
                total = total + weight * ends[n, pl.ds(col + SUB - 1 + k, 1), :]
        value[pl.ds(o, 1), :] = total
    send_block(value[...], out_ref)


def meet_kernel(mid, sides_0, sides_1, out_ref):
    out_ref[...] = jnp.broadcast_to(mid[...] + sides_0[...] + sides_1[...], out_ref.shape)


def later_kernel(mine, left, right, ends_0, ends_1, pad, out_ref, params, sems):
    rows, cols = (pad.shape[0] - 4, pad.shape[1] - 2 * SUB)
    side, end = (pl.ds(rows, SUB), pl.ds(cols + 2 * SUB, SUB))
    sources = (left.at[side], mine.at[1], right.at[side], ends_0.at[end], ends_1.at[end])
    copies = []
    for n, source in enumerate(sources):
        copies.append(pltpu.make_async_copy(source, params.at[n], sems.at[n]))
        copies[-1].start()
    for copy in copies:
        copy.wait()
    forward = next_first("lat")
    ends = {-1: jnp.where(forward, 4, 3), 1: jnp.where(forward, 3, 4)}
    for n, dc in enumerate(NEAR):
        for m, da in enumerate(NEAR):
            spot, lane = (n, 0) if da == 0 else (ends[da], n * SUB)
            number = lambda kind, o: params[spot, kind, lane + o]
            for o in range(SUB):
                out_ref[n * len(NEAR) + m, pl.ds(o, 1), :] = share(pad, number, rows, cols, da, dc, o)
    out_ref[len(NEAR) ** 2] = own_shift(lambda kind, o: params[1, kind, o])


def window_start(lat_count, my_lat):
    return 0 if lat_count <= WIN else jnp.clip(my_lat - REACH, 0, lat_count - WIN)


def column_of(block, j):
    return jnp.broadcast_to(block[:, j:j + 1], block.shape)


def pivot_rows(block, k, held, between):
    sub = lax.broadcasted_iota(jnp.int32, block.shape, 0)
    lane = lax.broadcasted_iota(jnp.int32, block.shape, 1) - k * SUB
    held[pl.ds(k * SUB, SUB), :] = block
    rows = [held[pl.ds(k * SUB + r, SUB, stride=0), :] for r in range(SUB)]
    at = {(r, n): column_of(rows[r], k * SUB + n) for r in range(SUB) for n in range(r + 1)}
    here = (lane >= 0) & (lane < SUB)
    rows = [jnp.where(here, jnp.where(lane == r, 1.0, 0.0), row) for r, row in enumerate(rows)]
    inverse, scale = (jnp.zeros(block.shape, F32), jnp.ones(block.shape, F32))
    for j in range(0, SUB, 2):
        a, b, c = (at[j, j], at[j + 1, j], at[j + 1, j + 1])
        det = a * c - b * b
        guess = pl.reciprocal(det, approx=True)
        better = 2.0 - det * guess
        over_det = guess * better
        top, bottom = (rows[j], rows[j + 1])
        rest = range(j + 2, SUB)
        upper = {n: (at[n, j], at[n, j + 1]) for n in rest}
        for r in rest:
            first, second = (at[r, j] * c - at[r, j + 1] * b, at[r, j + 1] * a - at[r, j] * b)
            if r < j + 4:
                for n in range(j + 2, r + 1):
                    taken = first * upper[n][0] + second * upper[n][1]
                    at[r, n] = at[r, n] - (taken * guess) * better
            first, second = (first * over_det, second * over_det)
            if r >= j + 4:
                for n in range(j + 2, r + 1):
                    at[r, n] = at[r, n] - (first * upper[n][0] + second * upper[n][1])
            rows[r] = rows[r] - (first * top + second * bottom)
        a_part, b_part, c_part = (a * over_det, b * over_det, c * over_det)
        for r in range(j):
            first = at[r, j] * c_part - at[r, j + 1] * b_part
            second = at[r, j + 1] * a_part - at[r, j] * b_part
            for n in rest:
                at[r, n] = at[r, n] - (first * upper[n][0] + second * upper[n][1])
            rows[r] = rows[r] - (first * top + second * bottom)
        for n in rest:
            at[j, n] = c_part * upper[n][0] - b_part * upper[n][1]
            at[j + 1, n] = a_part * upper[n][1] - b_part * upper[n][0]
        rows[j] = c_part * top - b_part * bottom
        rows[j + 1] = a_part * bottom - b_part * top
        inverse = jnp.where(sub == j, top, jnp.where(sub == j + 1, a * bottom - b * top, inverse))
        scale = jnp.where(sub == j, a, jnp.where(sub == j + 1, a * det, scale))
        between()
    return rows, jnp.where(lane < SUB, inverse * lax.rsqrt(scale), 0.0)


def eliminate(blocks, held):
    count = len(blocks) - 1
    blocks = list(blocks)
    lane = lax.broadcasted_iota(jnp.int32, blocks[0].shape, 1)
    inverse, waiting = ([], [])

    def update(i, k, pivot):
        terms = [column_of(blocks[i], k * SUB + j) * pivot[j] for j in range(SUB)]
        while len(terms) > 1:
            terms = [terms[n] + terms[n + 1] for n in range(0, len(terms), 2)]
        here = (lane >= k * SUB) & (lane < (k + 1) * SUB)
        blocks[i] = jnp.where(here, 0.0, blocks[i]) - terms[0]

    for k in range(count):
        share_of = -(-len(waiting) // 4)

        def between():
            for task in waiting[:share_of]:
                update(*task)
            del waiting[:share_of]

        pivot, rows = pivot_rows(blocks[k], k, held, between)
        update(k + 1, k, pivot)
        waiting = [(i, k, pivot) for i in range(k + 2, count + 1)]
        inverse.append(rows)
    return inverse, blocks[count][:1]


def own_blocks(mine, other):
    scaled = [jnp.concatenate([near[:, n].astype(F32) for n in range(PAIRS - 1)], axis=1) for near in (mine, other)]
    innov = [jnp.broadcast_to(near[:, PAIRS - 1].astype(F32)[:, :1], scaled[0].shape) for near in (mine, other)]
    sub = lax.broadcasted_iota(jnp.int32, scaled[0].shape, 1)
    lane = lax.broadcasted_iota(jnp.int32, scaled[0].shape, 2)
    innov = [jnp.where(lane == sub, value, 0.0) for value in innov]
    shape = (2 * mine.shape[0], SUB, LANES)
    return [jnp.stack(pair, axis=1).reshape(shape) for pair in (scaled, innov)]


def summed_blocks(lat_count, mine, other):
    held = min(WIN, lat_count)
    far_count = mine.shape[0] // lat_count
    start = window_start(lat_count, lax.axis_index("lat"))
    values = []
    for j in range(held):
        for far in range(far_count):
            for shares in (mine, other):
                total = jnp.zeros((SUB, LANES), F32)
                for n, da in enumerate(NEAR):
                    source = start + j - da
                    part = pl.ds(n * SUB, SUB)
                    if isinstance(source, int):
                        if 0 <= source < lat_count:
                            total = total + shares[source * far_count + far, part, :]
                    else:
                        inside = (source >= 0) & (source < lat_count)
                        source = jnp.clip(source, 0, lat_count - 1)
                        total = total + jnp.where(inside, shares[source * far_count + far, part, :], 0.0)
                values.append(total[None])
    value = jnp.concatenate(values, axis=0)
    mean = jnp.mean(value, axis=-1, keepdims=True)
    sub = lax.broadcasted_iota(jnp.int32, value.shape, 1)
    lane = lax.broadcasted_iota(jnp.int32, value.shape, 2)
    innov = jnp.where(lane == sub, jnp.broadcast_to(-mean, value.shape), 0.0)
    return (value - mean).astype(BF16).astype(F32), innov


def batch_map(batch, lat_count, blocks, pattern, held_rows):
    scaled, innov = blocks
    held = min(WIN, lat_count)
    count = scaled.shape[0]
    my_lat = lax.axis_index("lat")
    start = window_start(lat_count, my_lat)
    swapped = lax.axis_index("core") == 1
    picked = []
    for j in range(held):
        offset = start + j - my_lat + REACH
        inside = (offset >= 0) & (offset < WIN)
        row = pattern[batch, 0, 0, pl.ds(jnp.clip(offset, 0, WIN - 1), 1), :].astype(F32)
        row = jnp.where(inside, row, 0.0)
        marks = [jnp.broadcast_to(row[:, e:e + 1], (1, SUB, LANES)) for e in range(count // held)]
        for e in range(0, len(marks), 2):
            first, second = marks[e:e + 2]
            picked.extend((jnp.where(swapped, second, first), jnp.where(swapped, first, second)))
    weighted = scaled * jnp.concatenate(picked, axis=0)
    both = jnp.concatenate([scaled, innov], axis=2).reshape(count * SUB, 2 * LANES).astype(BF16)
    product = lax.dot_general(
        both,
        weighted.reshape(count * SUB, LANES).astype(BF16),
        (((0,), (0,)), ((), ())),
        preferred_element_type=F32,
    )
    sub = lax.broadcasted_iota(jnp.int32, (SUB, LANES), 0)
    lane = lax.broadcasted_iota(jnp.int32, (SUB, LANES), 1)
    members = LANES
    blocks = []
    for k in range(members // SUB):
        block = product[k * SUB:(k + 1) * SUB, :]
        blocks.append(block + jnp.where(lane - k * SUB == sub, members - 1.0, 0.0))
    proj = jnp.sum(product[members:members + SUB, :], axis=0, keepdims=True)
    blocks.append(jnp.broadcast_to(proj, (SUB, LANES)))
    inverse, weights = eliminate(blocks, held_rows)
    flipped = jnp.concatenate(inverse, axis=0) * (members - 1.0) ** 0.5 - weights
    return flipped - jnp.mean(flipped, axis=-1, keepdims=True) + 1.0 / members


def exact_dot(a, b, contract_b):
    return lax.dot_general(
        a, b, (((1,), (contract_b,)), ((), ())), precision=lax.Precision.HIGHEST, preferred_element_type=F32
    )


def first_kernel(lat_count, near, other, pattern, later, map_ref, mid_ref, out_0, out_1, held_rows):
    flipped = batch_map(0, lat_count, own_blocks(near, other), pattern, held_rows)
    map_ref[...] = flipped
    count = len(NEAR) ** 2
    moved = exact_dot(later[pl.ds(0, count)].reshape(-1, LANES), flipped, 1)
    size = len(NEAR) * SUB
    left, mid, right = (moved[:size], moved[size:2 * size], moved[2 * size:])
    mid_ref[...] = mid
    own = pl.ds(SUB, SUB)
    mid_ref[own, :] = mid[SUB:2 * SUB] - later[count]
    forward = next_first("core")
    out_0[...] = jnp.where(forward, right, left)
    out_1[...] = jnp.where(forward, left, right)


def last_kernel(lat_count, mine, other, pattern, map_ref, pad, out_ref, result, held_rows, out_sem):
    parts = out_sem.shape[0]
    rows, cols = (pad.shape[0] - 4, pad.shape[1] - 2 * SUB)
    blocks = summed_blocks(lat_count, mine, other)
    flipped = exact_dot(batch_map(1, lat_count, blocks, pattern, held_rows), map_ref[...], 0)
    high = flipped.astype(BF16)
    low = (flipped - high.astype(F32)).astype(BF16)
    right = jnp.concatenate(
        [jnp.concatenate([high, high], axis=1), jnp.concatenate([low, jnp.zeros_like(low)], axis=1)], axis=0
    )
    copies = []
    size = rows // parts
    for n in range(parts):
        part = pl.ds(n * size * cols, size * cols)
        value = pad[pl.ds(2 + n * size, size), pl.ds(SUB, cols), :].reshape(size * cols, LANES)
        upper = value.astype(BF16)
        rest = (value - upper.astype(F32)).astype(BF16)
        both = lax.dot_general(
            jnp.concatenate([upper, rest], axis=1), right, (((1,), (1,)), ((), ())), preferred_element_type=F32
        )
        result[part, :] = both[:, :LANES] + both[:, LANES:]
        copies.append(pltpu.make_async_copy(result.at[part], out_ref.at[part], out_sem.at[n]))
        copies[-1].start()
    for out_copy in copies:
        out_copy.wait()


def window(blocks, lat_count):
    held = min(WIN, lat_count)
    if held == lat_count:
        return blocks
    start = jnp.clip(lax.axis_index("lat") - REACH, 0, lat_count - held)
    per_row = blocks.shape[0] // lat_count
    return lax.dynamic_slice_in_dim(blocks, start * per_row, held * per_row, axis=0)


def local(ensemble, observed, precision, interp_weight, stencil, owned, pattern):
    rows, cols, members = ensemble.shape
    batches = observed.shape[0]
    lat_count, lon_count = (lax.axis_size("lat"), lax.axis_size(LON))
    tiles = lat_count * lon_count
    vmem = pl.BlockSpec(memory_space=pltpu.VMEM)
    anywhere = pl.BlockSpec(memory_space=pl.ANY)
    hbm = pl.BlockSpec(memory_space=pltpu.HBM)
    megabyte = 1024 * 1024

    def shape(*dims, dtype=F32):
        return jax.ShapeDtypeStruct(dims, dtype)

    def call(kernel, name, specs, out_shape, scratch, *operands, out_specs=None, limit=48):
        return pl.pallas_call(
            kernel,
            out_shape=out_shape,
            in_specs=specs,
            out_specs=out_specs or jax.tree.map(lambda _: vmem, out_shape),
            scratch_shapes=scratch,
            compiler_params=pltpu.CompilerParams(vmem_limit_bytes=limit * megabyte),
            name=name,
        )(*operands)

    def exchange(blocks):
        mine = lax.all_to_all(blocks, ("lat", "far"), split_axis=0, concat_axis=0, tiled=True)
        return mine, lax.ppermute(mine, "core", [(0, 1), (1, 0)])

    small = (observed, precision, interp_weight, stencil, owned)
    side = shape(rows + SUB, members)
    mine, side_1, side_0 = call(
        functools.partial(start_kernel, cols + 2),
        "start",
        [hbm] * 6,
        (shape(batches, SUB, LANES), side, side),
        [pltpu.VMEM(array.shape, array.dtype) for array in small]
        + [pltpu.VMEM((rows, SUB, members), F32)] * 2
        + [pltpu.SemaphoreType.DMA((7,))],
        *small,
        ensemble,
        limit=63,
    )
    sides = trade((side_0, side_1), LON, True)
    padded = shape(rows + 4, cols + 2 * SUB, members)
    pad = call(pad_kernel, "pad", [hbm], padded, [pltpu.SemaphoreType.DMA], ensemble)
    end = shape(cols + 3 * SUB, members)
    left, right, *ends = call(rows_kernel, "edge_rows", [vmem] * 4, (side, side, end, end), [], mine, *sides, pad)
    ends = trade(ends, "lat", False)
    slots = shape(tiles // 2, PAIRS, 2, members, dtype=BF16)
    numbers = [pltpu.SMEM((SUB, LANES), F32), pltpu.SemaphoreType.DMA]
    block = shape(SUB, members)
    held_sides = pltpu.VMEM((2, rows + 2 * SUB, members), F32)
    own = call(row_kernel, "row_shares", [vmem] * 4, block, [held_sides] + numbers, mine, left, right, pad)
    blocks = call(
        functools.partial(prior_kernel, rows),
        "prior",
        [vmem] * 4,
        slots,
        [pltpu.VMEM((2,) + end.shape, F32), pltpu.VMEM((SUB, members), F32)] + numbers,
        mine,
        own,
        *ends,
    )
    near = [window(part, lat_count) for part in exchange(blocks)]
    count = len(NEAR) ** 2
    later = call(
        later_kernel,
        "later_shares",
        [vmem] * 6,
        shape(count + 1, SUB, members),
        [pltpu.SMEM((5, SUB, LANES), F32), pltpu.SemaphoreType.DMA((5,))],
        mine,
        left,
        right,
        *ends,
        pad,
    )
    column = shape(len(NEAR) * SUB, members)
    held_rows = pltpu.VMEM((members + SUB, members), F32)
    first_map, mid, *sides = call(
        functools.partial(first_kernel, lat_count),
        "first_batch",
        [vmem] * 4,
        (shape(members, members), column, column, column),
        [held_rows],
        *near,
        pattern,
        later,
    )
    sides = trade(sides, LON, True)
    shares = call(meet_kernel, "meet", [vmem] * 3, shape(tiles // 2, *column.shape), [], mid, *sides)
    near = exchange(shares)
    parts = 16
    result = call(
        functools.partial(last_kernel, lat_count),
        "second_batch",
        [vmem] * 5,
        shape(rows * cols, members),
        [
            pltpu.VMEM((rows * cols, members), F32),
            held_rows,
            pltpu.SemaphoreType.DMA((parts,)),
        ],
        *near,
        pattern,
        first_map,
        pad,
        out_specs=anywhere,
    )
    return result.reshape(rows, cols, members)


def solution(mesh):
    lat_count, lon_count = (mesh.shape["lat"], mesh.shape["lon"])
    pairs = jax.sharding.Mesh(mesh.devices.reshape(lat_count, lon_count // 2, 2), ("lat",) + LON)
    placed = (
        P("lat", LON, None),
        P(None, "lat", LON, None),
        P(None, "lat", LON, None),
        P(None, "lat", LON, None, None),
        P(None, "lat", LON, None, None),
        P(None, "lat", LON, None),
        P(None, "lat", LON, None, None),
    )
    return jax.shard_map(
        local, mesh=pairs, in_specs=placed, out_specs=P("lat", LON, None), check_vma=False
    )
```

```python
import functools
import jax
import jax.numpy as jnp
from jax import lax
from jax.experimental import pallas as pl
from jax.experimental.pallas import tpu as pltpu
from jax.sharding import PartitionSpec as P

REACH = 2
WIN = 2 * REACH + 1
SUB = 8
LANES = 128
NEAR = (-1, 0, 1)
AT_ROW, AT_COL, AT_OBS = (4, 5, 6)
PAIRS = SUB // 2 + 1
F32 = jnp.float32
BF16 = jnp.bfloat16
LON = ("far", "core")


def partner(place, turn):
    return place + (-1 if place % 2 == turn else 1)


def trade(blocks, axis, wraps):
    count = lax.axis_size(axis)
    results = []
    for turn, block in enumerate(blocks):
        route = [(place, partner(place, turn)) for place in range(count)]
        route = [(source, target % count) for source, target in route if wraps or 0 <= target < count]
        results.append(lax.ppermute(block, axis, route))
    return results


def next_first(axis):
    return lax.rem(lax.axis_index(axis), 2) == 1


def start_kernel(
    width, observed, precision, weight, stencil, owned, cells, params_ref, sides_1, sides_0,
    observed_v, precision_v, weight_v, stencil_v, owned_v, left_v, right_v, sems
):
    batches, cols = (observed.shape[0], cells.shape[1])
    pairs = (
        (observed, observed_v),
        (precision, precision_v),
        (weight, weight_v),
        (stencil, stencil_v),
        (owned, owned_v),
        (cells.at[:, pl.ds(0, SUB)], left_v),
        (cells.at[:, pl.ds(cols - SUB, SUB)], right_v),
    )
    copies = [pltpu.make_async_copy(source, target, sems.at[n]) for n, (source, target) in enumerate(pairs)]
    for copy in copies:
        copy.start()
    for copy in copies:
        copy.wait()
    params_ref[...] = jnp.zeros_like(params_ref)
    for b in range(batches):
        root = jnp.sqrt(precision_v[b, 0]) * owned_v[b, 0].astype(F32)
        corner = stencil_v[b, 0, 0, pl.ds(0, 1)].astype(F32)
        row = jnp.floor((corner + 0.5) * (1.0 / width))
        params_ref[b, pl.ds(0, 4), pl.ds(0, SUB)] = weight_v[b, 0, 0] * root
        params_ref[b, pl.ds(AT_ROW, 1), pl.ds(0, SUB)] = row
        params_ref[b, pl.ds(AT_COL, 1), pl.ds(0, SUB)] = corner - row * width
        params_ref[b, pl.ds(AT_OBS, 1), pl.ds(0, SUB)] = observed_v[b, 0] * root
    rows = cells.shape[0]
    forward = next_first("core")
    left, right = (left_v[:, 0, :], right_v[:, SUB - 1, :])
    sides_0[pl.ds(0, rows), :] = jnp.where(forward, right, left)
    sides_1[pl.ds(0, rows), :] = jnp.where(forward, left, right)
    sides_0[pl.ds(rows, SUB), :] = params_ref[1]
    sides_1[pl.ds(rows, SUB), :] = params_ref[1]


def clear_rim(pad, rows, cols):
    edge = jnp.zeros((2, cols + 2 * SUB, LANES), F32)
    pad[pl.ds(0, 2)] = edge
    pad[pl.ds(rows + 2, 2)] = edge
    side = jnp.zeros((rows, SUB, LANES), F32)
    pad[pl.ds(2, rows), pl.ds(0, SUB)] = side
    pad[pl.ds(2, rows), pl.ds(SUB + cols, SUB)] = side


def share(pad, number, rows, cols, da, dc, o):
    row = number(AT_ROW, o).astype(jnp.int32) - 1 + da * rows
    col = number(AT_COL, o).astype(jnp.int32) - 1 + dc * cols
    row = jnp.clip(row, -2, rows) + 2
    col = jnp.clip(col, -2, cols) + SUB
    terms = [number(k, o) * pad[row + k // 2, pl.ds(col + k % 2, 1), :] for k in range(4)]
    return (terms[0] + terms[1]) + (terms[2] + terms[3])


def own_shift(number):
    sub = lax.broadcasted_iota(jnp.int32, (SUB, LANES), 0)
    shift = jnp.zeros((SUB, LANES), F32)
    for o in range(SUB):
        shift = jnp.where(sub == o, number(AT_OBS, o), shift)
    return shift


def pad_kernel(cells, pad, sem):
    rows, cols = (cells.shape[0], cells.shape[1])
    copy = pltpu.make_async_copy(cells, pad.at[pl.ds(2, rows), pl.ds(SUB, cols)], sem)
    copy.start()
    clear_rim(pad, rows, cols)
    copy.wait()


def hold_sides(left, right, sides):
    rows = left.shape[0] - SUB
    sides[...] = jnp.zeros_like(sides)
    sides[0, pl.ds(SUB, rows), :] = left[pl.ds(0, rows), :]
    sides[1, pl.ds(SUB, rows), :] = right[pl.ds(0, rows), :]


def side_share(sides, side, number, rows, cols, da, o):
    row = number(AT_ROW, o).astype(jnp.int32) - 1 + da * rows
    row = jnp.clip(row, -2, rows) + SUB
    used = number(AT_COL, o).astype(jnp.int32) == (0, cols)[side]
    terms = [jnp.where(used, number(side + 2 * k, o), 0.0) * sides[side, pl.ds(row + k, 1), :] for k in range(2)]
    return terms[0] + terms[1]


def send_block(value, out_ref):
    mean = jnp.mean(value, axis=-1, keepdims=True)
    sub = lax.broadcasted_iota(jnp.int32, (SUB, LANES), 0)
    lane = lax.broadcasted_iota(jnp.int32, (SUB, LANES), 1)
    innov = jnp.sum(jnp.where(lane == sub, -mean, 0.0), axis=0, keepdims=True)
    rows = jnp.concatenate([value - mean, jnp.broadcast_to(innov, (2, LANES))], axis=0).astype(BF16)
    for n in range(PAIRS):
        pair = rows[2 * n:2 * n + 2]
        out_ref[:, n] = jnp.broadcast_to(pair, (out_ref.shape[0],) + pair.shape)


def rows_kernel(mine, sides_0, sides_1, pad, left_ref, right_ref, out_0, out_1):
    rows, cols = (pad.shape[0] - 4, pad.shape[1] - 2 * SUB)
    forward = next_first("core")
    left_ref[...] = jnp.where(forward, sides_1[...], sides_0[...])
    right_ref[...] = jnp.where(forward, sides_0[...], sides_1[...])
    lane = lax.broadcasted_iota(jnp.int32, (SUB, LANES), 1)
    block = pl.ds(rows, SUB)
    packed = jnp.where(lane < SUB, left_ref[block, :], pltpu.roll(mine[1], SUB, 1))
    packed = jnp.where(lane < 2 * SUB, packed, pltpu.roll(right_ref[block, :], 2 * SUB, 1))
    forward = next_first("lat")
    for turn, out in enumerate((out_0, out_1)):
        row = jnp.where(forward, (1 - turn) * (rows - 1), turn * (rows - 1))
        out[pl.ds(0, SUB), :] = jnp.broadcast_to(left_ref[pl.ds(row, 1), :], (SUB, LANES))
        out[pl.ds(SUB, cols), :] = pad[2 + row, pl.ds(SUB, cols), :]
        out[pl.ds(SUB + cols, SUB), :] = jnp.broadcast_to(right_ref[pl.ds(row, 1), :], (SUB, LANES))
        out[pl.ds(2 * SUB + cols, SUB), :] = packed


def row_kernel(mine, left, right, pad, out_ref, sides, params, sem):
    rows, cols = (pad.shape[0] - 4, pad.shape[1] - 2 * SUB)
    copy = pltpu.make_async_copy(mine.at[0], params, sem)
    copy.start()
    hold_sides(left, right, sides)
    copy.wait()
    number = lambda kind, o: params[kind, o]
    for o in range(SUB):
        total = share(pad, number, rows, cols, 0, 0, o)
        for side in range(2):
            total = total + side_share(sides, side, number, rows, cols, 0, o)
        out_ref[pl.ds(o, 1), :] = total
    out_ref[...] = out_ref[...] - own_shift(number)


def prior_kernel(rows, mine, own, ends_0, ends_1, out_ref, ends, value, params, sem):
    copy = pltpu.make_async_copy(mine.at[0], params, sem)
    copy.start()
    forward = next_first("lat")
    ends[0] = jnp.where(forward, ends_1[...], ends_0[...])
    ends[1] = jnp.where(forward, ends_0[...], ends_1[...])
    copy.wait()
    for o in range(SUB):
        row, col = (params[AT_ROW, o].astype(jnp.int32), params[AT_COL, o].astype(jnp.int32))
        total = own[pl.ds(o, 1), :]
        for n, at in enumerate((0, rows)):
            for k in range(2):
                weight = jnp.where(row == at, params[2 * n + k, o], 0.0)
                total = total + weight * ends[n, pl.ds(col + SUB - 1 + k, 1), :]
        value[pl.ds(o, 1), :] = total
    send_block(value[...], out_ref)


def meet_kernel(mid, sides_0, sides_1, out_ref):
    out_ref[...] = jnp.broadcast_to(mid[...] + sides_0[...] + sides_1[...], out_ref.shape)


def later_kernel(mine, left, right, ends_0, ends_1, pad, out_ref, params, sems):
    rows, cols = (pad.shape[0] - 4, pad.shape[1] - 2 * SUB)
    side, end = (pl.ds(rows, SUB), pl.ds(cols + 2 * SUB, SUB))
    sources = (left.at[side], mine.at[1], right.at[side], ends_0.at[end], ends_1.at[end])
    copies = []
    for n, source in enumerate(sources):
        copies.append(pltpu.make_async_copy(source, params.at[n], sems.at[n]))
        copies[-1].start()
    for copy in copies:
        copy.wait()
    forward = next_first("lat")
    ends = {-1: jnp.where(forward, 4, 3), 1: jnp.where(forward, 3, 4)}
    for n, dc in enumerate(NEAR):
        for m, da in enumerate(NEAR):
            spot, lane = (n, 0) if da == 0 else (ends[da], n * SUB)
            number = lambda kind, o: params[spot, kind, lane + o]
            for o in range(SUB):
                out_ref[n * len(NEAR) + m, pl.ds(o, 1), :] = share(pad, number, rows, cols, da, dc, o)
    out_ref[len(NEAR) ** 2] = own_shift(lambda kind, o: params[1, kind, o])


def window_start(lat_count, my_lat):
    return 0 if lat_count <= WIN else jnp.clip(my_lat - REACH, 0, lat_count - WIN)


def column_of(block, j):
    return jnp.broadcast_to(block[:, j:j + 1], block.shape)


def pivot_rows(block, k, held, between):
    sub = lax.broadcasted_iota(jnp.int32, block.shape, 0)
    lane = lax.broadcasted_iota(jnp.int32, block.shape, 1) - k * SUB
    held[pl.ds(k * SUB, SUB), :] = block
    rows = [held[pl.ds(k * SUB + r, SUB, stride=0), :] for r in range(SUB)]
    at = {(r, n): column_of(rows[r], k * SUB + n) for r in range(SUB) for n in range(r + 1)}
    here = (lane >= 0) & (lane < SUB)
    rows = [jnp.where(here, jnp.where(lane == r, 1.0, 0.0), row) for r, row in enumerate(rows)]
    inverse, scale = (jnp.zeros(block.shape, F32), jnp.ones(block.shape, F32))
    for j in range(0, SUB, 2):
        a, b, c = (at[j, j], at[j + 1, j], at[j + 1, j + 1])
        det = a * c - b * b
        guess = pl.reciprocal(det, approx=True)
        better = 2.0 - det * guess
        over_det = guess * better
        top, bottom = (rows[j], rows[j + 1])
        rest = range(j + 2, SUB)
        upper = {n: (at[n, j], at[n, j + 1]) for n in rest}
        for r in rest:
            first, second = (at[r, j] * c - at[r, j + 1] * b, at[r, j + 1] * a - at[r, j] * b)
            if r < j + 4:
                for n in range(j + 2, r + 1):
                    taken = first * upper[n][0] + second * upper[n][1]
                    at[r, n] = at[r, n] - (taken * guess) * better
            first, second = (first * over_det, second * over_det)
            if r >= j + 4:
                for n in range(j + 2, r + 1):
                    at[r, n] = at[r, n] - (first * upper[n][0] + second * upper[n][1])
            rows[r] = rows[r] - (first * top + second * bottom)
        a_part, b_part, c_part = (a * over_det, b * over_det, c * over_det)
        for r in range(j):
            first = at[r, j] * c_part - at[r, j + 1] * b_part
            second = at[r, j + 1] * a_part - at[r, j] * b_part
            for n in rest:
                at[r, n] = at[r, n] - (first * upper[n][0] + second * upper[n][1])
            rows[r] = rows[r] - (first * top + second * bottom)
        for n in rest:
            at[j, n] = c_part * upper[n][0] - b_part * upper[n][1]
            at[j + 1, n] = a_part * upper[n][1] - b_part * upper[n][0]
        rows[j] = c_part * top - b_part * bottom
        rows[j + 1] = a_part * bottom - b_part * top
        inverse = jnp.where(sub == j, top, jnp.where(sub == j + 1, a * bottom - b * top, inverse))
        scale = jnp.where(sub == j, a, jnp.where(sub == j + 1, a * det, scale))
        between()
    return rows, jnp.where(lane < SUB, inverse * lax.rsqrt(scale), 0.0)


def eliminate(blocks, held):
    count = len(blocks) - 1
    blocks = list(blocks)
    lane = lax.broadcasted_iota(jnp.int32, blocks[0].shape, 1)
    inverse, waiting = ([], [])

    def update(i, k, pivot):
        terms = [column_of(blocks[i], k * SUB + j) * pivot[j] for j in range(SUB)]
        while len(terms) > 1:
            terms = [terms[n] + terms[n + 1] for n in range(0, len(terms), 2)]
        here = (lane >= k * SUB) & (lane < (k + 1) * SUB)
        blocks[i] = jnp.where(here, 0.0, blocks[i]) - terms[0]

    for k in range(count):
        share_of = -(-len(waiting) // 4)

        def between():
            for task in waiting[:share_of]:
                update(*task)
            del waiting[:share_of]

        pivot, rows = pivot_rows(blocks[k], k, held, between)
        update(k + 1, k, pivot)
        waiting = [(i, k, pivot) for i in range(k + 2, count + 1)]
        inverse.append(rows)
    return inverse, blocks[count][:1]


def own_blocks(near_ref):
    scaled = jnp.concatenate([near_ref[:, n].astype(F32) for n in range(PAIRS - 1)], axis=1)
    innov = near_ref[:, PAIRS - 1].astype(F32)[:, :1]
    sub = lax.broadcasted_iota(jnp.int32, scaled.shape, 1)
    lane = lax.broadcasted_iota(jnp.int32, scaled.shape, 2)
    return scaled, jnp.where(lane == sub, jnp.broadcast_to(innov, scaled.shape), 0.0)


def summed_blocks(lat_count, shares):
    held = min(WIN, lat_count)
    far_count = shares.shape[0] // lat_count
    start = window_start(lat_count, lax.axis_index("lat"))
    values = []
    for j in range(held):
        for far in range(far_count):
            total = jnp.zeros((SUB, LANES), F32)
            for n, da in enumerate(NEAR):
                source = start + j - da
                part = pl.ds(n * SUB, SUB)
                if isinstance(source, int):
                    if 0 <= source < lat_count:
                        total = total + shares[source * far_count + far, part, :]
                else:
                    inside = (source >= 0) & (source < lat_count)
                    source = jnp.clip(source, 0, lat_count - 1)
                    total = total + jnp.where(inside, shares[source * far_count + far, part, :], 0.0)
            values.append(total[None])
    value = jnp.concatenate(values, axis=0)
    mean = jnp.mean(value, axis=-1, keepdims=True)
    sub = lax.broadcasted_iota(jnp.int32, value.shape, 1)
    lane = lax.broadcasted_iota(jnp.int32, value.shape, 2)
    innov = jnp.where(lane == sub, jnp.broadcast_to(-mean, value.shape), 0.0)
    return (value - mean).astype(BF16).astype(F32), innov


def marked_product(batch, lat_count, blocks, pattern, place=None):
    scaled, innov = blocks
    held = min(WIN, lat_count)
    count = scaled.shape[0]
    lon_count = pattern.shape[-1]
    my_lat = lax.axis_index("lat")
    start = window_start(lat_count, my_lat)
    picked = []
    for j in range(held):
        offset = start + j - my_lat + REACH
        inside = (offset >= 0) & (offset < WIN)
        row = pattern[batch, 0, 0, pl.ds(jnp.clip(offset, 0, WIN - 1), 1), :].astype(F32)
        row = jnp.where(inside, row, 0.0)
        marks = [jnp.broadcast_to(row[:, e:e + 1], (1, SUB, LANES)) for e in range(lon_count)]
        if place is not None:
            marks = [jnp.where(place == 1, marks[e + 1], marks[e]) for e in range(0, lon_count, 2)]
        picked.extend(marks)
    weighted = scaled * jnp.concatenate(picked, axis=0)
    both = jnp.concatenate([scaled, innov], axis=2).reshape(count * SUB, 2 * LANES).astype(BF16)
    product = lax.dot_general(
        both,
        weighted.reshape(count * SUB, LANES).astype(BF16),
        (((0,), (0,)), ((), ())),
        preferred_element_type=F32,
    )
    return product[:LANES + SUB]


def solved_map(product, held_rows):
    sub = lax.broadcasted_iota(jnp.int32, (SUB, LANES), 0)
    lane = lax.broadcasted_iota(jnp.int32, (SUB, LANES), 1)
    members = LANES
    blocks = []
    for k in range(members // SUB):
        block = product[k * SUB:(k + 1) * SUB, :]
        blocks.append(block + jnp.where(lane - k * SUB == sub, members - 1.0, 0.0))
    proj = jnp.sum(product[members:members + SUB, :], axis=0, keepdims=True)
    blocks.append(jnp.broadcast_to(proj, (SUB, LANES)))
    inverse, weights = eliminate(blocks, held_rows)
    flipped = jnp.concatenate(inverse, axis=0) * (members - 1.0) ** 0.5 - weights
    return flipped - jnp.mean(flipped, axis=-1, keepdims=True) + 1.0 / members


def exact_dot(a, b, contract_b):
    return lax.dot_general(
        a, b, (((1,), (contract_b,)), ((), ())), precision=lax.Precision.HIGHEST, preferred_element_type=F32
    )


def first_kernel(lat_count, near_ref, pattern, later, map_ref, mid_ref, out_0, out_1, held_rows):
    flipped = solved_map(marked_product(0, lat_count, own_blocks(near_ref), pattern), held_rows)
    map_ref[...] = flipped
    count = len(NEAR) ** 2
    moved = exact_dot(later[pl.ds(0, count)].reshape(-1, LANES), flipped, 1)
    size = len(NEAR) * SUB
    left, mid, right = (moved[:size], moved[size:2 * size], moved[2 * size:])
    mid_ref[...] = mid
    own = pl.ds(SUB, SUB)
    mid_ref[own, :] = mid[SUB:2 * SUB] - later[count]
    forward = next_first("core")
    out_0[...] = jnp.where(forward, right, left)
    out_1[...] = jnp.where(forward, left, right)


def half_kernel(lat_count, mine, pattern, out_ref):
    out_ref[...] = marked_product(1, lat_count, summed_blocks(lat_count, mine), pattern, lax.axis_index("core"))


def last_kernel(lat_count, half, other, pattern, map_ref, pad, out_ref, result, held_rows, out_sem):
    parts = out_sem.shape[0]
    rows, cols = (pad.shape[0] - 4, pad.shape[1] - 2 * SUB)
    product = marked_product(1, lat_count, summed_blocks(lat_count, other), pattern, 1 - lax.axis_index("core"))
    flipped = exact_dot(solved_map(product + half[...], held_rows), map_ref[...], 0)
    high = flipped.astype(BF16)
    low = (flipped - high.astype(F32)).astype(BF16)
    right = jnp.concatenate(
        [jnp.concatenate([high, high], axis=1), jnp.concatenate([low, jnp.zeros_like(low)], axis=1)], axis=0
    )
    copies = []
    size = rows // parts
    for n in range(parts):
        part = pl.ds(n * size * cols, size * cols)
        value = pad[pl.ds(2 + n * size, size), pl.ds(SUB, cols), :].reshape(size * cols, LANES)
        upper = value.astype(BF16)
        rest = (value - upper.astype(F32)).astype(BF16)
        both = lax.dot_general(
            jnp.concatenate([upper, rest], axis=1), right, (((1,), (1,)), ((), ())), preferred_element_type=F32
        )
        result[part, :] = both[:, :LANES] + both[:, LANES:]
        copies.append(pltpu.make_async_copy(result.at[part], out_ref.at[part], out_sem.at[n]))
        copies[-1].start()
    for out_copy in copies:
        out_copy.wait()


def window(tiles, lat_count, lon_count):
    held = min(WIN, lat_count)
    if held == lat_count:
        return tiles
    start = jnp.clip(lax.axis_index("lat") - REACH, 0, lat_count - held)
    return lax.dynamic_slice_in_dim(tiles, start * lon_count, held * lon_count, axis=0)


def local(ensemble, observed, precision, interp_weight, stencil, owned, pattern):
    rows, cols, members = ensemble.shape
    batches = observed.shape[0]
    lat_count, lon_count = (lax.axis_size("lat"), lax.axis_size(LON))
    tiles = lat_count * lon_count
    vmem = pl.BlockSpec(memory_space=pltpu.VMEM)
    anywhere = pl.BlockSpec(memory_space=pl.ANY)
    hbm = pl.BlockSpec(memory_space=pltpu.HBM)
    megabyte = 1024 * 1024

    def shape(*dims, dtype=F32):
        return jax.ShapeDtypeStruct(dims, dtype)

    def call(kernel, name, specs, out_shape, scratch, *operands, out_specs=None, limit=48):
        return pl.pallas_call(
            kernel,
            out_shape=out_shape,
            in_specs=specs,
            out_specs=out_specs or jax.tree.map(lambda _: vmem, out_shape),
            scratch_shapes=scratch,
            compiler_params=pltpu.CompilerParams(vmem_limit_bytes=limit * megabyte),
            name=name,
        )(*operands)

    def exchange(blocks):
        return lax.all_to_all(blocks, ("lat",) + LON, split_axis=0, concat_axis=0, tiled=True)

    small = (observed, precision, interp_weight, stencil, owned)
    side = shape(rows + SUB, members)
    mine, side_1, side_0 = call(
        functools.partial(start_kernel, cols + 2),
        "start",
        [hbm] * 6,
        (shape(batches, SUB, LANES), side, side),
        [pltpu.VMEM(array.shape, array.dtype) for array in small]
        + [pltpu.VMEM((rows, SUB, members), F32)] * 2
        + [pltpu.SemaphoreType.DMA((7,))],
        *small,
        ensemble,
        limit=63,
    )
    sides = trade((side_0, side_1), LON, True)
    padded = shape(rows + 4, cols + 2 * SUB, members)
    pad = call(pad_kernel, "pad", [hbm], padded, [pltpu.SemaphoreType.DMA], ensemble)
    end = shape(cols + 3 * SUB, members)
    left, right, *ends = call(rows_kernel, "edge_rows", [vmem] * 4, (side, side, end, end), [], mine, *sides, pad)
    ends = trade(ends, "lat", False)
    slots = shape(tiles, PAIRS, 2, members, dtype=BF16)
    numbers = [pltpu.SMEM((SUB, LANES), F32), pltpu.SemaphoreType.DMA]
    block = shape(SUB, members)
    held_sides = pltpu.VMEM((2, rows + 2 * SUB, members), F32)
    own = call(row_kernel, "row_shares", [vmem] * 4, block, [held_sides] + numbers, mine, left, right, pad)
    blocks = call(
        functools.partial(prior_kernel, rows),
        "prior",
        [vmem] * 4,
        slots,
        [pltpu.VMEM((2,) + end.shape, F32), pltpu.VMEM((SUB, members), F32)] + numbers,
        mine,
        own,
        *ends,
    )
    near = window(exchange(blocks), lat_count, lon_count)
    count = len(NEAR) ** 2
    later = call(
        later_kernel,
        "later_shares",
        [vmem] * 6,
        shape(count + 1, SUB, members),
        [pltpu.SMEM((5, SUB, LANES), F32), pltpu.SemaphoreType.DMA((5,))],
        mine,
        left,
        right,
        *ends,
        pad,
    )
    column = shape(len(NEAR) * SUB, members)
    held_rows = pltpu.VMEM((members + SUB, members), F32)
    first_map, mid, *sides = call(
        functools.partial(first_kernel, lat_count),
        "first_batch",
        [vmem] * 3,
        (shape(members, members), column, column, column),
        [held_rows],
        near,
        pattern,
        later,
    )
    sides = trade(sides, LON, True)
    shares = call(meet_kernel, "meet", [vmem] * 3, shape(tiles // 2, *column.shape), [], mid, *sides)
    shares = lax.all_to_all(shares, ("lat", "far"), split_axis=0, concat_axis=0, tiled=True)
    other = lax.ppermute(shares, "core", [(0, 1), (1, 0)])
    half = call(
        functools.partial(half_kernel, lat_count),
        "half_product",
        [vmem] * 2,
        shape(members + SUB, members),
        [],
        shares,
        pattern,
    )
    parts = 8
    result = call(
        functools.partial(last_kernel, lat_count),
        "second_batch",
        [vmem] * 5,
        shape(rows * cols, members),
        [
            pltpu.VMEM((rows * cols, members), F32),
            held_rows,
            pltpu.SemaphoreType.DMA((parts,)),
        ],
        half,
        other,
        pattern,
        first_map,
        pad,
        out_specs=anywhere,
    )
    return result.reshape(rows, cols, members)


def solution(mesh):
    lat_count, lon_count = (mesh.shape["lat"], mesh.shape["lon"])
    pairs = jax.sharding.Mesh(mesh.devices.reshape(lat_count, lon_count // 2, 2), ("lat",) + LON)
    placed = (
        P("lat", LON, None),
        P(None, "lat", LON, None),
        P(None, "lat", LON, None),
        P(None, "lat", LON, None, None),
        P(None, "lat", LON, None, None),
        P(None, "lat", LON, None),
        P(None, "lat", LON, None, None),
    )
    return jax.shard_map(
        local, mesh=pairs, in_specs=placed, out_specs=P("lat", LON, None), check_vma=False
    )
```

```python
import functools
import jax
import jax.numpy as jnp
from jax import lax
from jax.experimental import pallas as pl
from jax.experimental.pallas import tpu as pltpu
from jax.sharding import PartitionSpec as P

REACH = 2
WIN = 2 * REACH + 1
SUB = 8
LANES = 128
NEAR = (-1, 0, 1)
AT_ROW, AT_COL, AT_OBS = (4, 5, 6)
PAIRS = SUB // 2 + 1
F32 = jnp.float32
BF16 = jnp.bfloat16
LON = ("far", "core")


def partner(place, turn):
    return place + (-1 if place % 2 == turn else 1)


def trade(blocks, axis, wraps):
    count = lax.axis_size(axis)
    results = []
    for turn, block in enumerate(blocks):
        route = [(place, partner(place, turn)) for place in range(count)]
        route = [(source, target % count) for source, target in route if wraps or 0 <= target < count]
        results.append(lax.ppermute(block, axis, route))
    return results


def next_first(axis):
    return lax.rem(lax.axis_index(axis), 2) == 1


def start_kernel(
    width, observed, precision, weight, stencil, owned, cells, params_ref, sides_1, sides_0,
    observed_v, precision_v, weight_v, stencil_v, owned_v, left_v, right_v, sems
):
    batches, cols = (observed.shape[0], cells.shape[1])
    pairs = (
        (observed, observed_v),
        (precision, precision_v),
        (weight, weight_v),
        (stencil, stencil_v),
        (owned, owned_v),
        (cells.at[:, pl.ds(0, SUB)], left_v),
        (cells.at[:, pl.ds(cols - SUB, SUB)], right_v),
    )
    copies = [pltpu.make_async_copy(source, target, sems.at[n]) for n, (source, target) in enumerate(pairs)]
    for n, copy in enumerate(copies):
        copy.start(priority=n % 2)
    for copy in copies:
        copy.wait()
    params_ref[...] = jnp.zeros_like(params_ref)
    for b in range(batches):
        root = jnp.sqrt(precision_v[b, 0]) * owned_v[b, 0].astype(F32)
        corner = stencil_v[b, 0, 0, pl.ds(0, 1)].astype(F32)
        row = jnp.floor((corner + 0.5) * (1.0 / width))
        params_ref[b, pl.ds(0, 4), pl.ds(0, SUB)] = weight_v[b, 0, 0] * root
        params_ref[b, pl.ds(AT_ROW, 1), pl.ds(0, SUB)] = row
        params_ref[b, pl.ds(AT_COL, 1), pl.ds(0, SUB)] = corner - row * width
        params_ref[b, pl.ds(AT_OBS, 1), pl.ds(0, SUB)] = observed_v[b, 0] * root
    rows = cells.shape[0]
    forward = next_first("core")
    left, right = (left_v[:, 0, :], right_v[:, SUB - 1, :])
    sides_0[pl.ds(0, rows), :] = jnp.where(forward, right, left)
    sides_1[pl.ds(0, rows), :] = jnp.where(forward, left, right)
    sides_0[pl.ds(rows, SUB), :] = params_ref[1]
    sides_1[pl.ds(rows, SUB), :] = params_ref[1]


def clear_rim(pad, rows, cols):
    edge = jnp.zeros((2, cols + 2 * SUB, LANES), F32)
    pad[pl.ds(0, 2)] = edge
    pad[pl.ds(rows + 2, 2)] = edge
    side = jnp.zeros((rows, SUB, LANES), F32)
    pad[pl.ds(2, rows), pl.ds(0, SUB)] = side
    pad[pl.ds(2, rows), pl.ds(SUB + cols, SUB)] = side


def share(pad, number, rows, cols, da, dc, o):
    row = number(AT_ROW, o).astype(jnp.int32) - 1 + da * rows
    col = number(AT_COL, o).astype(jnp.int32) - 1 + dc * cols
    row = jnp.clip(row, -2, rows) + 2
    col = jnp.clip(col, -2, cols) + SUB
    terms = [number(k, o) * pad[row + k // 2, pl.ds(col + k % 2, 1), :] for k in range(4)]
    return (terms[0] + terms[1]) + (terms[2] + terms[3])


def own_shift(number):
    sub = lax.broadcasted_iota(jnp.int32, (SUB, LANES), 0)
    shift = jnp.zeros((SUB, LANES), F32)
    for o in range(SUB):
        shift = jnp.where(sub == o, number(AT_OBS, o), shift)
    return shift


def pad_kernel(cells, pad, sem):
    rows, cols = (cells.shape[0], cells.shape[1])
    copy = pltpu.make_async_copy(cells, pad.at[pl.ds(2, rows), pl.ds(SUB, cols)], sem)
    copy.start()
    clear_rim(pad, rows, cols)
    copy.wait()


def hold_sides(left, right, sides):
    rows = left.shape[0] - SUB
    sides[...] = jnp.zeros_like(sides)
    sides[0, pl.ds(SUB, rows), :] = left[pl.ds(0, rows), :]
    sides[1, pl.ds(SUB, rows), :] = right[pl.ds(0, rows), :]


def side_share(sides, side, number, rows, cols, da, o):
    row = number(AT_ROW, o).astype(jnp.int32) - 1 + da * rows
    row = jnp.clip(row, -2, rows) + SUB
    used = number(AT_COL, o).astype(jnp.int32) == (0, cols)[side]
    terms = [jnp.where(used, number(side + 2 * k, o), 0.0) * sides[side, pl.ds(row + k, 1), :] for k in range(2)]
    return terms[0] + terms[1]


def send_block(value, out_ref):
    mean = jnp.mean(value, axis=-1, keepdims=True)
    sub = lax.broadcasted_iota(jnp.int32, (SUB, LANES), 0)
    lane = lax.broadcasted_iota(jnp.int32, (SUB, LANES), 1)
    innov = jnp.sum(jnp.where(lane == sub, -mean, 0.0), axis=0, keepdims=True)
    rows = jnp.concatenate([value - mean, jnp.broadcast_to(innov, (2, LANES))], axis=0).astype(BF16)
    for n in range(PAIRS):
        pair = rows[2 * n:2 * n + 2]
        out_ref[:, n] = jnp.broadcast_to(pair, (out_ref.shape[0],) + pair.shape)


def rows_kernel(mine, sides_0, sides_1, pad, left_ref, right_ref, out_0, out_1):
    rows, cols = (pad.shape[0] - 4, pad.shape[1] - 2 * SUB)
    forward = next_first("core")
    left_ref[...] = jnp.where(forward, sides_1[...], sides_0[...])
    right_ref[...] = jnp.where(forward, sides_0[...], sides_1[...])
    lane = lax.broadcasted_iota(jnp.int32, (SUB, LANES), 1)
    block = pl.ds(rows, SUB)
    packed = jnp.where(lane < SUB, left_ref[block, :], pltpu.roll(mine[1], SUB, 1))
    packed = jnp.where(lane < 2 * SUB, packed, pltpu.roll(right_ref[block, :], 2 * SUB, 1))
    forward = next_first("lat")
    for turn, out in enumerate((out_0, out_1)):
        row = jnp.where(forward, (1 - turn) * (rows - 1), turn * (rows - 1))
        out[pl.ds(0, SUB), :] = jnp.broadcast_to(left_ref[pl.ds(row, 1), :], (SUB, LANES))
        out[pl.ds(SUB, cols), :] = pad[2 + row, pl.ds(SUB, cols), :]
        out[pl.ds(SUB + cols, SUB), :] = jnp.broadcast_to(right_ref[pl.ds(row, 1), :], (SUB, LANES))
        out[pl.ds(2 * SUB + cols, SUB), :] = packed


def row_kernel(mine, left, right, pad, out_ref, sides, params, sem):
    rows, cols = (pad.shape[0] - 4, pad.shape[1] - 2 * SUB)
    copy = pltpu.make_async_copy(mine.at[0], params, sem)
    copy.start()
    hold_sides(left, right, sides)
    copy.wait()
    number = lambda kind, o: params[kind, o]
    for o in range(SUB):
        total = share(pad, number, rows, cols, 0, 0, o)
        for side in range(2):
            total = total + side_share(sides, side, number, rows, cols, 0, o)
        out_ref[pl.ds(o, 1), :] = total
    out_ref[...] = out_ref[...] - own_shift(number)


def prior_kernel(rows, mine, own, ends_0, ends_1, out_ref, ends, value, params, sem):
    copy = pltpu.make_async_copy(mine.at[0], params, sem)
    copy.start()
    forward = next_first("lat")
    ends[0] = jnp.where(forward, ends_1[...], ends_0[...])
    ends[1] = jnp.where(forward, ends_0[...], ends_1[...])
    copy.wait()
    for o in range(SUB):
        row, col = (params[AT_ROW, o].astype(jnp.int32), params[AT_COL, o].astype(jnp.int32))
        total = own[pl.ds(o, 1), :]
        for n, at in enumerate((0, rows)):
            for k in range(2):
                weight = jnp.where(row == at, params[2 * n + k, o], 0.0)
                total = total + weight * ends[n, pl.ds(col + SUB - 1 + k, 1), :]
        value[pl.ds(o, 1), :] = total
    send_block(value[...], out_ref)


def meet_kernel(mid, sides_0, sides_1, out_ref):
    out_ref[...] = jnp.broadcast_to(mid[...] + sides_0[...] + sides_1[...], out_ref.shape)


def later_kernel(mine, left, right, ends_0, ends_1, pad, out_ref, params, sems):
    rows, cols = (pad.shape[0] - 4, pad.shape[1] - 2 * SUB)
    side, end = (pl.ds(rows, SUB), pl.ds(cols + 2 * SUB, SUB))
    sources = (left.at[side], mine.at[1], right.at[side], ends_0.at[end], ends_1.at[end])
    copies = []
    for n, source in enumerate(sources):
        copies.append(pltpu.make_async_copy(source, params.at[n], sems.at[n]))
        copies[-1].start()
    for copy in copies:
        copy.wait()
    forward = next_first("lat")
    ends = {-1: jnp.where(forward, 4, 3), 1: jnp.where(forward, 3, 4)}
    for n, dc in enumerate(NEAR):
        for m, da in enumerate(NEAR):
            spot, lane = (n, 0) if da == 0 else (ends[da], n * SUB)
            number = lambda kind, o: params[spot, kind, lane + o]
            for o in range(SUB):
                out_ref[n * len(NEAR) + m, pl.ds(o, 1), :] = share(pad, number, rows, cols, da, dc, o)
    out_ref[len(NEAR) ** 2] = own_shift(lambda kind, o: params[1, kind, o])


def window_start(lat_count, my_lat):
    return 0 if lat_count <= WIN else jnp.clip(my_lat - REACH, 0, lat_count - WIN)


def column_of(block, j):
    return jnp.broadcast_to(block[:, j:j + 1], block.shape)


def pivot_rows(block, k, held, between):
    sub = lax.broadcasted_iota(jnp.int32, block.shape, 0)
    lane = lax.broadcasted_iota(jnp.int32, block.shape, 1) - k * SUB
    held[pl.ds(k * SUB, SUB), :] = block
    rows = [held[pl.ds(k * SUB + r, SUB, stride=0), :] for r in range(SUB)]
    at = {(r, n): column_of(rows[r], k * SUB + n) for r in range(SUB) for n in range(r + 1)}
    here = (lane >= 0) & (lane < SUB)
    rows = [jnp.where(here, jnp.where(lane == r, 1.0, 0.0), row) for r, row in enumerate(rows)]
    inverse, scale = (jnp.zeros(block.shape, F32), jnp.ones(block.shape, F32))
    for j in range(0, SUB, 2):
        a, b, c = (at[j, j], at[j + 1, j], at[j + 1, j + 1])
        det = a * c - b * b
        guess = pl.reciprocal(det, approx=True)
        better = 2.0 - det * guess
        over_det = guess * better
        top, bottom = (rows[j], rows[j + 1])
        rest = range(j + 2, SUB)
        upper = {n: (at[n, j], at[n, j + 1]) for n in rest}
        for r in rest:
            first, second = (at[r, j] * c - at[r, j + 1] * b, at[r, j + 1] * a - at[r, j] * b)
            if r < j + 4:
                for n in range(j + 2, r + 1):
                    taken = first * upper[n][0] + second * upper[n][1]
                    at[r, n] = at[r, n] - (taken * guess) * better
            first, second = (first * over_det, second * over_det)
            if r >= j + 4:
                for n in range(j + 2, r + 1):
                    at[r, n] = at[r, n] - (first * upper[n][0] + second * upper[n][1])
            rows[r] = rows[r] - (first * top + second * bottom)
        a_part, b_part, c_part = (a * over_det, b * over_det, c * over_det)
        for r in range(j):
            first = at[r, j] * c_part - at[r, j + 1] * b_part
            second = at[r, j + 1] * a_part - at[r, j] * b_part
            for n in rest:
                at[r, n] = at[r, n] - (first * upper[n][0] + second * upper[n][1])
            rows[r] = rows[r] - (first * top + second * bottom)
        for n in rest:
            at[j, n] = c_part * upper[n][0] - b_part * upper[n][1]
            at[j + 1, n] = a_part * upper[n][1] - b_part * upper[n][0]
        rows[j] = c_part * top - b_part * bottom
        rows[j + 1] = a_part * bottom - b_part * top
        inverse = jnp.where(sub == j, top, jnp.where(sub == j + 1, a * bottom - b * top, inverse))
        scale = jnp.where(sub == j, a, jnp.where(sub == j + 1, a * det, scale))
        between()
    return rows, jnp.where(lane < SUB, inverse * lax.rsqrt(scale), 0.0)


def eliminate(blocks, held):
    count = len(blocks) - 1
    blocks = list(blocks)
    lane = lax.broadcasted_iota(jnp.int32, blocks[0].shape, 1)
    inverse, waiting = ([], [])

    def update(i, k, pivot):
        terms = [column_of(blocks[i], k * SUB + j) * pivot[j] for j in range(SUB)]
        while len(terms) > 1:
            terms = [terms[n] + terms[n + 1] for n in range(0, len(terms), 2)]
        here = (lane >= k * SUB) & (lane < (k + 1) * SUB)
        blocks[i] = jnp.where(here, 0.0, blocks[i]) - terms[0]

    for k in range(count):
        share_of = -(-len(waiting) // 4)

        def between():
            for task in waiting[:share_of]:
                update(*task)
            del waiting[:share_of]

        pivot, rows = pivot_rows(blocks[k], k, held, between)
        update(k + 1, k, pivot)
        waiting = [(i, k, pivot) for i in range(k + 2, count + 1)]
        inverse.append(rows)
    return inverse, blocks[count][:1]


def own_blocks(near_ref):
    scaled = jnp.concatenate([near_ref[:, n].astype(F32) for n in range(PAIRS - 1)], axis=1)
    innov = near_ref[:, PAIRS - 1].astype(F32)[:, :1]
    sub = lax.broadcasted_iota(jnp.int32, scaled.shape, 1)
    lane = lax.broadcasted_iota(jnp.int32, scaled.shape, 2)
    return scaled, jnp.where(lane == sub, jnp.broadcast_to(innov, scaled.shape), 0.0)


def summed_blocks(lat_count, shares):
    held = min(WIN, lat_count)
    far_count = shares.shape[0] // lat_count
    start = window_start(lat_count, lax.axis_index("lat"))
    values = []
    for j in range(held):
        for far in range(far_count):
            total = jnp.zeros((SUB, LANES), F32)
            for n, da in enumerate(NEAR):
                source = start + j - da
                part = pl.ds(n * SUB, SUB)
                if isinstance(source, int):
                    if 0 <= source < lat_count:
                        total = total + shares[source * far_count + far, part, :]
                else:
                    inside = (source >= 0) & (source < lat_count)
                    source = jnp.clip(source, 0, lat_count - 1)
                    total = total + jnp.where(inside, shares[source * far_count + far, part, :], 0.0)
            values.append(total[None])
    value = jnp.concatenate(values, axis=0)
    mean = jnp.mean(value, axis=-1, keepdims=True)
    sub = lax.broadcasted_iota(jnp.int32, value.shape, 1)
    lane = lax.broadcasted_iota(jnp.int32, value.shape, 2)
    innov = jnp.where(lane == sub, jnp.broadcast_to(-mean, value.shape), 0.0)
    return (value - mean).astype(BF16).astype(F32), innov


def marked_product(batch, lat_count, blocks, pattern, place=None):
    scaled, innov = blocks
    held = min(WIN, lat_count)
    count = scaled.shape[0]
    lon_count = pattern.shape[-1]
    my_lat = lax.axis_index("lat")
    start = window_start(lat_count, my_lat)
    picked = []
    for j in range(held):
        offset = start + j - my_lat + REACH
        inside = (offset >= 0) & (offset < WIN)
        row = pattern[batch, 0, 0, pl.ds(jnp.clip(offset, 0, WIN - 1), 1), :].astype(F32)
        row = jnp.where(inside, row, 0.0)
        marks = [jnp.broadcast_to(row[:, e:e + 1], (1, SUB, LANES)) for e in range(lon_count)]
        if place is not None:
            marks = [jnp.where(place == 1, marks[e + 1], marks[e]) for e in range(0, lon_count, 2)]
        picked.extend(marks)
    weighted = scaled * jnp.concatenate(picked, axis=0)
    both = jnp.concatenate([scaled, innov], axis=2).reshape(count * SUB, 2 * LANES).astype(BF16)
    product = lax.dot_general(
        both,
        weighted.reshape(count * SUB, LANES).astype(BF16),
        (((0,), (0,)), ((), ())),
        preferred_element_type=F32,
    )
    return product[:LANES + SUB]


def solved_map(product, held_rows):
    sub = lax.broadcasted_iota(jnp.int32, (SUB, LANES), 0)
    lane = lax.broadcasted_iota(jnp.int32, (SUB, LANES), 1)
    members = LANES
    blocks = []
    for k in range(members // SUB):
        block = product[k * SUB:(k + 1) * SUB, :]
        blocks.append(block + jnp.where(lane - k * SUB == sub, members - 1.0, 0.0))
    proj = jnp.sum(product[members:members + SUB, :], axis=0, keepdims=True)
    blocks.append(jnp.broadcast_to(proj, (SUB, LANES)))
    inverse, weights = eliminate(blocks, held_rows)
    flipped = jnp.concatenate(inverse, axis=0) * (members - 1.0) ** 0.5 - weights
    return flipped - jnp.mean(flipped, axis=-1, keepdims=True) + 1.0 / members


def exact_dot(a, b, contract_b):
    return lax.dot_general(
        a, b, (((1,), (contract_b,)), ((), ())), precision=lax.Precision.HIGHEST, preferred_element_type=F32
    )


def first_kernel(lat_count, near_ref, pattern, later, map_ref, mid_ref, out_0, out_1, held_rows):
    flipped = solved_map(marked_product(0, lat_count, own_blocks(near_ref), pattern), held_rows)
    map_ref[...] = flipped
    count = len(NEAR) ** 2
    moved = exact_dot(later[pl.ds(0, count)].reshape(-1, LANES), flipped, 1)
    size = len(NEAR) * SUB
    left, mid, right = (moved[:size], moved[size:2 * size], moved[2 * size:])
    mid_ref[...] = mid
    own = pl.ds(SUB, SUB)
    mid_ref[own, :] = mid[SUB:2 * SUB] - later[count]
    forward = next_first("core")
    out_0[...] = jnp.where(forward, right, left)
    out_1[...] = jnp.where(forward, left, right)


def half_kernel(lat_count, mine, pattern, out_ref):
    out_ref[...] = marked_product(1, lat_count, summed_blocks(lat_count, mine), pattern, lax.axis_index("core"))


def last_kernel(lat_count, half, other, pattern, map_ref, pad, out_ref, result, held_rows, out_sem):
    parts = out_sem.shape[0]
    rows, cols = (pad.shape[0] - 4, pad.shape[1] - 2 * SUB)
    product = marked_product(1, lat_count, summed_blocks(lat_count, other), pattern, 1 - lax.axis_index("core"))
    flipped = exact_dot(solved_map(product + half[...], held_rows), map_ref[...], 0)
    high = flipped.astype(BF16)
    low = (flipped - high.astype(F32)).astype(BF16)
    right = jnp.concatenate(
        [jnp.concatenate([high, high], axis=1), jnp.concatenate([low, jnp.zeros_like(low)], axis=1)], axis=0
    )
    copies = []
    size = rows // parts
    for n in range(parts):
        part = pl.ds(n * size * cols, size * cols)
        value = pad[pl.ds(2 + n * size, size), pl.ds(SUB, cols), :].reshape(size * cols, LANES)
        upper = value.astype(BF16)
        rest = (value - upper.astype(F32)).astype(BF16)
        both = lax.dot_general(
            jnp.concatenate([upper, rest], axis=1), right, (((1,), (1,)), ((), ())), preferred_element_type=F32
        )
        result[part, :] = both[:, :LANES] + both[:, LANES:]
        copies.append(pltpu.make_async_copy(result.at[part], out_ref.at[part], out_sem.at[n]))
        copies[-1].start(priority=n % 2)
    for out_copy in copies:
        out_copy.wait()


def window(tiles, lat_count, lon_count):
    held = min(WIN, lat_count)
    if held == lat_count:
        return tiles
    start = jnp.clip(lax.axis_index("lat") - REACH, 0, lat_count - held)
    return lax.dynamic_slice_in_dim(tiles, start * lon_count, held * lon_count, axis=0)


def local(ensemble, observed, precision, interp_weight, stencil, owned, pattern):
    rows, cols, members = ensemble.shape
    batches = observed.shape[0]
    lat_count, lon_count = (lax.axis_size("lat"), lax.axis_size(LON))
    tiles = lat_count * lon_count
    vmem = pl.BlockSpec(memory_space=pltpu.VMEM)
    anywhere = pl.BlockSpec(memory_space=pl.ANY)
    hbm = pl.BlockSpec(memory_space=pltpu.HBM)
    megabyte = 1024 * 1024

    def shape(*dims, dtype=F32):
        return jax.ShapeDtypeStruct(dims, dtype)

    def call(kernel, name, specs, out_shape, scratch, *operands, out_specs=None, limit=48):
        return pl.pallas_call(
            kernel,
            out_shape=out_shape,
            in_specs=specs,
            out_specs=out_specs or jax.tree.map(lambda _: vmem, out_shape),
            scratch_shapes=scratch,
            compiler_params=pltpu.CompilerParams(vmem_limit_bytes=limit * megabyte),
            name=name,
        )(*operands)

    def exchange(blocks):
        return lax.all_to_all(blocks, ("lat",) + LON, split_axis=0, concat_axis=0, tiled=True)

    small = (observed, precision, interp_weight, stencil, owned)
    side = shape(rows + SUB, members)
    mine, side_1, side_0 = call(
        functools.partial(start_kernel, cols + 2),
        "start",
        [hbm] * 6,
        (shape(batches, SUB, LANES), side, side),
        [pltpu.VMEM(array.shape, array.dtype) for array in small]
        + [pltpu.VMEM((rows, SUB, members), F32)] * 2
        + [pltpu.SemaphoreType.DMA((7,))],
        *small,
        ensemble,
        limit=63,
    )
    sides = trade((side_0, side_1), LON, True)
    padded = shape(rows + 4, cols + 2 * SUB, members)
    pad = call(pad_kernel, "pad", [hbm], padded, [pltpu.SemaphoreType.DMA], ensemble)
    end = shape(cols + 3 * SUB, members)
    left, right, *ends = call(rows_kernel, "edge_rows", [vmem] * 4, (side, side, end, end), [], mine, *sides, pad)
    ends = trade(ends, "lat", False)
    slots = shape(tiles, PAIRS, 2, members, dtype=BF16)
    numbers = [pltpu.SMEM((SUB, LANES), F32), pltpu.SemaphoreType.DMA]
    block = shape(SUB, members)
    held_sides = pltpu.VMEM((2, rows + 2 * SUB, members), F32)
    own = call(row_kernel, "row_shares", [vmem] * 4, block, [held_sides] + numbers, mine, left, right, pad)
    blocks = call(
        functools.partial(prior_kernel, rows),
        "prior",
        [vmem] * 4,
        slots,
        [pltpu.VMEM((2,) + end.shape, F32), pltpu.VMEM((SUB, members), F32)] + numbers,
        mine,
        own,
        *ends,
    )
    near = window(exchange(blocks), lat_count, lon_count)
    count = len(NEAR) ** 2
    later = call(
        later_kernel,
        "later_shares",
        [vmem] * 6,
        shape(count + 1, SUB, members),
        [pltpu.SMEM((5, SUB, LANES), F32), pltpu.SemaphoreType.DMA((5,))],
        mine,
        left,
        right,
        *ends,
        pad,
    )
    column = shape(len(NEAR) * SUB, members)
    held_rows = pltpu.VMEM((members + SUB, members), F32)
    first_map, mid, *sides = call(
        functools.partial(first_kernel, lat_count),
        "first_batch",
        [vmem] * 3,
        (shape(members, members), column, column, column),
        [held_rows],
        near,
        pattern,
        later,
    )
    sides = trade(sides, LON, True)
    shares = call(meet_kernel, "meet", [vmem] * 3, shape(tiles // 2, *column.shape), [], mid, *sides)
    shares = lax.all_to_all(shares, ("lat", "far"), split_axis=0, concat_axis=0, tiled=True)
    other = lax.ppermute(shares, "core", [(0, 1), (1, 0)])
    half = call(
        functools.partial(half_kernel, lat_count),
        "half_product",
        [vmem] * 2,
        shape(members + SUB, members),
        [],
        shares,
        pattern,
    )
    parts = 8
    result = call(
        functools.partial(last_kernel, lat_count),
        "second_batch",
        [vmem] * 5,
        shape(rows * cols, members),
        [
            pltpu.VMEM((rows * cols, members), F32),
            held_rows,
            pltpu.SemaphoreType.DMA((parts,)),
        ],
        half,
        other,
        pattern,
        first_map,
        pad,
        out_specs=anywhere,
    )
    return result.reshape(rows, cols, members)


def solution(mesh):
    lat_count, lon_count = (mesh.shape["lat"], mesh.shape["lon"])
    pairs = jax.sharding.Mesh(mesh.devices.reshape(lat_count, lon_count // 2, 2), ("lat",) + LON)
    placed = (
        P("lat", LON, None),
        P(None, "lat", LON, None),
        P(None, "lat", LON, None),
        P(None, "lat", LON, None, None),
        P(None, "lat", LON, None, None),
        P(None, "lat", LON, None),
        P(None, "lat", LON, None, None),
    )
    return jax.shard_map(
        local, mesh=pairs, in_specs=placed, out_specs=P("lat", LON, None), check_vma=False
    )
```

```python
import functools
import jax
import jax.numpy as jnp
from jax import lax
from jax.experimental import pallas as pl
from jax.experimental.pallas import tpu as pltpu
from jax.sharding import PartitionSpec as P

REACH = 2
WIN = 2 * REACH + 1
SUB = 8
LANES = 128
NEAR = (-1, 0, 1)
AT_ROW, AT_COL, AT_OBS = (4, 5, 6)
PAIRS = SUB // 2 + 1
F32 = jnp.float32
BF16 = jnp.bfloat16
LON = ("far", "core")


def partner(place, turn):
    return place + (-1 if place % 2 == turn else 1)


def trade(blocks, axis, wraps):
    count = lax.axis_size(axis)
    results = []
    for turn, block in enumerate(blocks):
        route = [(place, partner(place, turn)) for place in range(count)]
        route = [(source, target % count) for source, target in route if wraps or 0 <= target < count]
        results.append(lax.ppermute(block, axis, route))
    return results


def next_first(axis):
    return lax.rem(lax.axis_index(axis), 2) == 1


def start_kernel(
    width, observed, precision, weight, stencil, owned, cells, params_ref, sides_1, sides_0,
    observed_v, precision_v, weight_v, stencil_v, owned_v, left_v, right_v, sems
):
    batches, cols = (observed.shape[0], cells.shape[1])
    pairs = (
        (observed, observed_v),
        (precision, precision_v),
        (weight, weight_v),
        (stencil, stencil_v),
        (owned, owned_v),
        (cells.at[:, pl.ds(0, SUB)], left_v),
        (cells.at[:, pl.ds(cols - SUB, SUB)], right_v),
    )
    copies = [pltpu.make_async_copy(source, target, sems.at[n]) for n, (source, target) in enumerate(pairs)]
    for copy in copies:
        copy.start()
    for copy in copies:
        copy.wait()
    params_ref[...] = jnp.zeros_like(params_ref)
    for b in range(batches):
        root = jnp.sqrt(precision_v[b, 0]) * owned_v[b, 0].astype(F32)
        corner = stencil_v[b, 0, 0, pl.ds(0, 1)].astype(F32)
        row = jnp.floor((corner + 0.5) * (1.0 / width))
        params_ref[b, pl.ds(0, 4), pl.ds(0, SUB)] = weight_v[b, 0, 0] * root
        params_ref[b, pl.ds(AT_ROW, 1), pl.ds(0, SUB)] = row
        params_ref[b, pl.ds(AT_COL, 1), pl.ds(0, SUB)] = corner - row * width
        params_ref[b, pl.ds(AT_OBS, 1), pl.ds(0, SUB)] = observed_v[b, 0] * root
    rows = cells.shape[0]
    forward = next_first("core")
    left, right = (left_v[:, 0, :], right_v[:, SUB - 1, :])
    sides_0[pl.ds(0, rows), :] = jnp.where(forward, right, left)
    sides_1[pl.ds(0, rows), :] = jnp.where(forward, left, right)
    sides_0[pl.ds(rows, SUB), :] = params_ref[1]
    sides_1[pl.ds(rows, SUB), :] = params_ref[1]


def clear_rim(pad, rows, cols):
    edge = jnp.zeros((2, cols + 2 * SUB, LANES), F32)
    pad[pl.ds(0, 2)] = edge
    pad[pl.ds(rows + 2, 2)] = edge
    side = jnp.zeros((rows, SUB, LANES), F32)
    pad[pl.ds(2, rows), pl.ds(0, SUB)] = side
    pad[pl.ds(2, rows), pl.ds(SUB + cols, SUB)] = side


def share(pad, number, rows, cols, da, dc, o):
    row = number(AT_ROW, o).astype(jnp.int32) - 1 + da * rows
    col = number(AT_COL, o).astype(jnp.int32) - 1 + dc * cols
    row = jnp.clip(row, -2, rows) + 2
    col = jnp.clip(col, -2, cols) + SUB
    terms = [number(k, o) * pad[row + k // 2, pl.ds(col + k % 2, 1), :] for k in range(4)]
    return (terms[0] + terms[1]) + (terms[2] + terms[3])


def own_shift(number):
    sub = lax.broadcasted_iota(jnp.int32, (SUB, LANES), 0)
    shift = jnp.zeros((SUB, LANES), F32)
    for o in range(SUB):
        shift = jnp.where(sub == o, number(AT_OBS, o), shift)
    return shift


def pad_kernel(cells, pad, sem):
    rows, cols = (cells.shape[0], cells.shape[1])
    copy = pltpu.make_async_copy(cells, pad.at[pl.ds(2, rows), pl.ds(SUB, cols)], sem)
    copy.start()
    clear_rim(pad, rows, cols)
    copy.wait()


def hold_sides(left, right, sides):
    rows = left.shape[0] - SUB
    sides[...] = jnp.zeros_like(sides)
    sides[0, pl.ds(SUB, rows), :] = left[pl.ds(0, rows), :]
    sides[1, pl.ds(SUB, rows), :] = right[pl.ds(0, rows), :]


def side_share(sides, side, number, rows, cols, da, o):
    row = number(AT_ROW, o).astype(jnp.int32) - 1 + da * rows
    row = jnp.clip(row, -2, rows) + SUB
    used = number(AT_COL, o).astype(jnp.int32) == (0, cols)[side]
    terms = [jnp.where(used, number(side + 2 * k, o), 0.0) * sides[side, pl.ds(row + k, 1), :] for k in range(2)]
    return terms[0] + terms[1]


def send_block(value, out_ref):
    mean = jnp.mean(value, axis=-1, keepdims=True)
    sub = lax.broadcasted_iota(jnp.int32, (SUB, LANES), 0)
    lane = lax.broadcasted_iota(jnp.int32, (SUB, LANES), 1)
    innov = jnp.sum(jnp.where(lane == sub, -mean, 0.0), axis=0, keepdims=True)
    rows = jnp.concatenate([value - mean, jnp.broadcast_to(innov, (2, LANES))], axis=0).astype(BF16)
    for n in range(PAIRS):
        pair = rows[2 * n:2 * n + 2]
        out_ref[:, n] = jnp.broadcast_to(pair, (out_ref.shape[0],) + pair.shape)


def rows_kernel(mine, sides_0, sides_1, pad, left_ref, right_ref, out_0, out_1):
    rows, cols = (pad.shape[0] - 4, pad.shape[1] - 2 * SUB)
    forward = next_first("core")
    left_ref[...] = jnp.where(forward, sides_1[...], sides_0[...])
    right_ref[...] = jnp.where(forward, sides_0[...], sides_1[...])
    lane = lax.broadcasted_iota(jnp.int32, (SUB, LANES), 1)
    block = pl.ds(rows, SUB)
    packed = jnp.where(lane < SUB, left_ref[block, :], pltpu.roll(mine[1], SUB, 1))
    packed = jnp.where(lane < 2 * SUB, packed, pltpu.roll(right_ref[block, :], 2 * SUB, 1))
    forward = next_first("lat")
    for turn, out in enumerate((out_0, out_1)):
        row = jnp.where(forward, (1 - turn) * (rows - 1), turn * (rows - 1))
        out[pl.ds(0, SUB), :] = jnp.broadcast_to(left_ref[pl.ds(row, 1), :], (SUB, LANES))
        out[pl.ds(SUB, cols), :] = pad[2 + row, pl.ds(SUB, cols), :]
        out[pl.ds(SUB + cols, SUB), :] = jnp.broadcast_to(right_ref[pl.ds(row, 1), :], (SUB, LANES))
        out[pl.ds(2 * SUB + cols, SUB), :] = packed


def row_kernel(mine, left, right, pad, out_ref, sides, params, sem):
    rows, cols = (pad.shape[0] - 4, pad.shape[1] - 2 * SUB)
    copy = pltpu.make_async_copy(mine.at[0], params, sem)
    copy.start()
    hold_sides(left, right, sides)
    copy.wait()
    number = lambda kind, o: params[kind, o]
    for o in range(SUB):
        total = share(pad, number, rows, cols, 0, 0, o)
        for side in range(2):
            total = total + side_share(sides, side, number, rows, cols, 0, o)
        out_ref[pl.ds(o, 1), :] = total
    out_ref[...] = out_ref[...] - own_shift(number)


def prior_kernel(rows, mine, own, ends_0, ends_1, out_ref, ends, value, params, sem):
    copy = pltpu.make_async_copy(mine.at[0], params, sem)
    copy.start()
    forward = next_first("lat")
    ends[0] = jnp.where(forward, ends_1[...], ends_0[...])
    ends[1] = jnp.where(forward, ends_0[...], ends_1[...])
    copy.wait()
    for o in range(SUB):
        row, col = (params[AT_ROW, o].astype(jnp.int32), params[AT_COL, o].astype(jnp.int32))
        total = own[pl.ds(o, 1), :]
        for n, at in enumerate((0, rows)):
            for k in range(2):
                weight = jnp.where(row == at, params[2 * n + k, o], 0.0)
                total = total + weight * ends[n, pl.ds(col + SUB - 1 + k, 1), :]
        value[pl.ds(o, 1), :] = total
    send_block(value[...], out_ref)


def meet_kernel(mid, sides_0, sides_1, done, out_ref):
    total = mid[...] + sides_0[...] + sides_1[...] + done[pl.ds(0, 1), :]
    out_ref[...] = jnp.broadcast_to(total, out_ref.shape)


def later_kernel(mine, left, right, ends_0, ends_1, pad, out_ref, params, sems):
    rows, cols = (pad.shape[0] - 4, pad.shape[1] - 2 * SUB)
    side, end = (pl.ds(rows, SUB), pl.ds(cols + 2 * SUB, SUB))
    sources = (left.at[side], mine.at[1], right.at[side], ends_0.at[end], ends_1.at[end])
    copies = []
    for n, source in enumerate(sources):
        copies.append(pltpu.make_async_copy(source, params.at[n], sems.at[n]))
        copies[-1].start()
    for copy in copies:
        copy.wait()
    forward = next_first("lat")
    ends = {-1: jnp.where(forward, 4, 3), 1: jnp.where(forward, 3, 4)}
    for n, dc in enumerate(NEAR):
        for m, da in enumerate(NEAR):
            spot, lane = (n, 0) if da == 0 else (ends[da], n * SUB)
            number = lambda kind, o: params[spot, kind, lane + o]
            for o in range(SUB):
                out_ref[n * len(NEAR) + m, pl.ds(o, 1), :] = share(pad, number, rows, cols, da, dc, o)
    out_ref[len(NEAR) ** 2] = own_shift(lambda kind, o: params[1, kind, o])


def window_start(lat_count, my_lat):
    return 0 if lat_count <= WIN else jnp.clip(my_lat - REACH, 0, lat_count - WIN)


def column_of(block, j):
    return jnp.broadcast_to(block[:, j:j + 1], block.shape)


def pivot_rows(block, k, held, between):
    sub = lax.broadcasted_iota(jnp.int32, block.shape, 0)
    lane = lax.broadcasted_iota(jnp.int32, block.shape, 1) - k * SUB
    held[pl.ds(k * SUB, SUB), :] = block
    rows = [held[pl.ds(k * SUB + r, SUB, stride=0), :] for r in range(SUB)]
    at = {(r, n): column_of(rows[r], k * SUB + n) for r in range(SUB) for n in range(r + 1)}
    here = (lane >= 0) & (lane < SUB)
    rows = [jnp.where(here, jnp.where(lane == r, 1.0, 0.0), row) for r, row in enumerate(rows)]
    inverse, scale = (jnp.zeros(block.shape, F32), jnp.ones(block.shape, F32))
    for j in range(0, SUB, 2):
        a, b, c = (at[j, j], at[j + 1, j], at[j + 1, j + 1])
        det = a * c - b * b
        guess = pl.reciprocal(det, approx=True)
        better = 2.0 - det * guess
        over_det = guess * better
        top, bottom = (rows[j], rows[j + 1])
        rest = range(j + 2, SUB)
        upper = {n: (at[n, j], at[n, j + 1]) for n in rest}
        for r in rest:
            first, second = (at[r, j] * c - at[r, j + 1] * b, at[r, j + 1] * a - at[r, j] * b)
            if r < j + 4:
                for n in range(j + 2, r + 1):
                    taken = first * upper[n][0] + second * upper[n][1]
                    at[r, n] = at[r, n] - (taken * guess) * better
            first, second = (first * over_det, second * over_det)
            if r >= j + 4:
                for n in range(j + 2, r + 1):
                    at[r, n] = at[r, n] - (first * upper[n][0] + second * upper[n][1])
            rows[r] = rows[r] - (first * top + second * bottom)
        a_part, b_part, c_part = (a * over_det, b * over_det, c * over_det)
        for r in range(j):
            first = at[r, j] * c_part - at[r, j + 1] * b_part
            second = at[r, j + 1] * a_part - at[r, j] * b_part
            for n in rest:
                at[r, n] = at[r, n] - (first * upper[n][0] + second * upper[n][1])
            rows[r] = rows[r] - (first * top + second * bottom)
        for n in rest:
            at[j, n] = c_part * upper[n][0] - b_part * upper[n][1]
            at[j + 1, n] = a_part * upper[n][1] - b_part * upper[n][0]
        rows[j] = c_part * top - b_part * bottom
        rows[j + 1] = a_part * bottom - b_part * top
        inverse = jnp.where(sub == j, top, jnp.where(sub == j + 1, a * bottom - b * top, inverse))
        scale = jnp.where(sub == j, a, jnp.where(sub == j + 1, a * det, scale))
        between()
    return rows, jnp.where(lane < SUB, inverse * lax.rsqrt(scale), 0.0)


def eliminate(blocks, held):
    count = len(blocks) - 1
    blocks = list(blocks)
    lane = lax.broadcasted_iota(jnp.int32, blocks[0].shape, 1)
    inverse, waiting = ([], [])

    def update(i, k, pivot):
        terms = [column_of(blocks[i], k * SUB + j) * pivot[j] for j in range(SUB)]
        while len(terms) > 1:
            terms = [terms[n] + terms[n + 1] for n in range(0, len(terms), 2)]
        here = (lane >= k * SUB) & (lane < (k + 1) * SUB)
        blocks[i] = jnp.where(here, 0.0, blocks[i]) - terms[0]

    for k in range(count):
        share_of = -(-len(waiting) // 4)

        def between():
            for task in waiting[:share_of]:
                update(*task)
            del waiting[:share_of]

        pivot, rows = pivot_rows(blocks[k], k, held, between)
        update(k + 1, k, pivot)
        waiting = [(i, k, pivot) for i in range(k + 2, count + 1)]
        inverse.append(rows)
    return inverse, blocks[count][:1]


def own_blocks(near_ref):
    scaled = jnp.concatenate([near_ref[:, n].astype(F32) for n in range(PAIRS - 1)], axis=1)
    innov = near_ref[:, PAIRS - 1].astype(F32)[:, :1]
    sub = lax.broadcasted_iota(jnp.int32, scaled.shape, 1)
    lane = lax.broadcasted_iota(jnp.int32, scaled.shape, 2)
    return scaled, jnp.where(lane == sub, jnp.broadcast_to(innov, scaled.shape), 0.0)


def summed_blocks(lat_count, shares):
    held = min(WIN, lat_count)
    far_count = shares.shape[0] // lat_count
    start = window_start(lat_count, lax.axis_index("lat"))
    values = []
    for j in range(held):
        for far in range(far_count):
            total = jnp.zeros((SUB, LANES), F32)
            for n, da in enumerate(NEAR):
                source = start + j - da
                part = pl.ds(n * SUB, SUB)
                if isinstance(source, int):
                    if 0 <= source < lat_count:
                        total = total + shares[source * far_count + far, part, :]
                else:
                    inside = (source >= 0) & (source < lat_count)
                    source = jnp.clip(source, 0, lat_count - 1)
                    total = total + jnp.where(inside, shares[source * far_count + far, part, :], 0.0)
            values.append(total[None])
    value = jnp.concatenate(values, axis=0)
    mean = jnp.mean(value, axis=-1, keepdims=True)
    sub = lax.broadcasted_iota(jnp.int32, value.shape, 1)
    lane = lax.broadcasted_iota(jnp.int32, value.shape, 2)
    innov = jnp.where(lane == sub, jnp.broadcast_to(-mean, value.shape), 0.0)
    return (value - mean).astype(BF16).astype(F32), innov


def marked_product(batch, lat_count, blocks, pattern, place=None):
    scaled, innov = blocks
    held = min(WIN, lat_count)
    count = scaled.shape[0]
    lon_count = pattern.shape[-1]
    my_lat = lax.axis_index("lat")
    start = window_start(lat_count, my_lat)
    picked = []
    for j in range(held):
        offset = start + j - my_lat + REACH
        inside = (offset >= 0) & (offset < WIN)
        row = pattern[batch, 0, 0, pl.ds(jnp.clip(offset, 0, WIN - 1), 1), :].astype(F32)
        row = jnp.where(inside, row, 0.0)
        marks = [jnp.broadcast_to(row[:, e:e + 1], (1, SUB, LANES)) for e in range(lon_count)]
        if place is not None:
            marks = [jnp.where(place == 1, marks[e + 1], marks[e]) for e in range(0, lon_count, 2)]
        picked.extend(marks)
    weighted = scaled * jnp.concatenate(picked, axis=0)
    both = jnp.concatenate([scaled, innov], axis=2).reshape(count * SUB, 2 * LANES).astype(BF16)
    product = lax.dot_general(
        both,
        weighted.reshape(count * SUB, LANES).astype(BF16),
        (((0,), (0,)), ((), ())),
        preferred_element_type=F32,
    )
    return product[:LANES + SUB]


def solved_map(product, held_rows):
    sub = lax.broadcasted_iota(jnp.int32, (SUB, LANES), 0)
    lane = lax.broadcasted_iota(jnp.int32, (SUB, LANES), 1)
    members = LANES
    blocks = []
    for k in range(members // SUB):
        block = product[k * SUB:(k + 1) * SUB, :]
        blocks.append(block + jnp.where(lane - k * SUB == sub, members - 1.0, 0.0))
    proj = jnp.sum(product[members:members + SUB, :], axis=0, keepdims=True)
    blocks.append(jnp.broadcast_to(proj, (SUB, LANES)))
    inverse, weights = eliminate(blocks, held_rows)
    flipped = jnp.concatenate(inverse, axis=0) * (members - 1.0) ** 0.5 - weights
    return flipped - jnp.mean(flipped, axis=-1, keepdims=True) + 1.0 / members


def exact_dot(a, b, contract_b):
    return lax.dot_general(
        a, b, (((1,), (contract_b,)), ((), ())), precision=lax.Precision.HIGHEST, preferred_element_type=F32
    )


def first_kernel(lat_count, near_ref, pattern, later, map_ref, mid_ref, out_0, out_1, held_rows):
    flipped = solved_map(marked_product(0, lat_count, own_blocks(near_ref), pattern), held_rows)
    map_ref[...] = flipped
    count = len(NEAR) ** 2
    moved = exact_dot(later[pl.ds(0, count)].reshape(-1, LANES), flipped, 1)
    size = len(NEAR) * SUB
    left, mid, right = (moved[:size], moved[size:2 * size], moved[2 * size:])
    mid_ref[...] = mid
    own = pl.ds(SUB, SUB)
    mid_ref[own, :] = mid[SUB:2 * SUB] - later[count]
    forward = next_first("core")
    out_0[...] = jnp.where(forward, right, left)
    out_1[...] = jnp.where(forward, left, right)


def half_kernel(lat_count, mine, pattern, out_ref):
    out_ref[...] = marked_product(1, lat_count, summed_blocks(lat_count, mine), pattern, lax.axis_index("core"))


def halves(value):
    upper = value.astype(BF16)
    return jnp.concatenate([upper, (value - upper.astype(F32)).astype(BF16)], axis=1)


def mapped(both, flipped):
    high = flipped.astype(BF16)
    low = (flipped - high.astype(F32)).astype(BF16)
    right = jnp.concatenate(
        [jnp.concatenate([high, high], axis=1), jnp.concatenate([low, jnp.zeros_like(low)], axis=1)], axis=0
    )
    product = lax.dot_general(both, right, (((1,), (1,)), ((), ())), preferred_element_type=F32)
    return product[:, :LANES] + product[:, LANES:]


def apply_kernel(map_ref, pad, out_ref, done_ref):
    rows, cols = (pad.shape[0] - 4, pad.shape[1] - 2 * SUB)
    size = 4
    for n in range(0, rows, size):
        value = pad[pl.ds(2 + n, size), pl.ds(SUB, cols), :].reshape(size * cols, LANES)
        out_ref[pl.ds(n * cols, size * cols), :] = halves(mapped(halves(value), map_ref[...]))
    done_ref[...] = jnp.zeros_like(done_ref)


def last_kernel(lat_count, half, other, pattern, cells, out_ref, result, held_rows, out_sem):
    parts = out_sem.shape[0]
    size = result.shape[0] // parts
    product = marked_product(1, lat_count, summed_blocks(lat_count, other), pattern, 1 - lax.axis_index("core"))
    flipped = solved_map(product + half[...], held_rows)
    copies = []
    for n in range(parts):
        part = pl.ds(n * size, size)
        result[part, :] = mapped(cells[part, :], flipped)
        copies.append(pltpu.make_async_copy(result.at[part], out_ref.at[part], out_sem.at[n]))
        copies[-1].start()
    for out_copy in copies:
        out_copy.wait()


def window(tiles, lat_count, lon_count):
    held = min(WIN, lat_count)
    if held == lat_count:
        return tiles
    start = jnp.clip(lax.axis_index("lat") - REACH, 0, lat_count - held)
    return lax.dynamic_slice_in_dim(tiles, start * lon_count, held * lon_count, axis=0)


def local(ensemble, observed, precision, interp_weight, stencil, owned, pattern):
    rows, cols, members = ensemble.shape
    batches = observed.shape[0]
    lat_count, lon_count = (lax.axis_size("lat"), lax.axis_size(LON))
    tiles = lat_count * lon_count
    vmem = pl.BlockSpec(memory_space=pltpu.VMEM)
    anywhere = pl.BlockSpec(memory_space=pl.ANY)
    hbm = pl.BlockSpec(memory_space=pltpu.HBM)
    megabyte = 1024 * 1024

    def shape(*dims, dtype=F32):
        return jax.ShapeDtypeStruct(dims, dtype)

    def call(kernel, name, specs, out_shape, scratch, *operands, out_specs=None, limit=48):
        return pl.pallas_call(
            kernel,
            out_shape=out_shape,
            in_specs=specs,
            out_specs=out_specs or jax.tree.map(lambda _: vmem, out_shape),
            scratch_shapes=scratch,
            compiler_params=pltpu.CompilerParams(vmem_limit_bytes=limit * megabyte),
            name=name,
        )(*operands)

    def exchange(blocks):
        return lax.all_to_all(blocks, ("lat",) + LON, split_axis=0, concat_axis=0, tiled=True)

    small = (observed, precision, interp_weight, stencil, owned)
    side = shape(rows + SUB, members)
    mine, side_1, side_0 = call(
        functools.partial(start_kernel, cols + 2),
        "start",
        [hbm] * 6,
        (shape(batches, SUB, LANES), side, side),
        [pltpu.VMEM(array.shape, array.dtype) for array in small]
        + [pltpu.VMEM((rows, SUB, members), F32)] * 2
        + [pltpu.SemaphoreType.DMA((7,))],
        *small,
        ensemble,
        limit=63,
    )
    sides = trade((side_0, side_1), LON, True)
    padded = shape(rows + 4, cols + 2 * SUB, members)
    pad = call(pad_kernel, "pad", [hbm], padded, [pltpu.SemaphoreType.DMA], ensemble)
    end = shape(cols + 3 * SUB, members)
    left, right, *ends = call(rows_kernel, "edge_rows", [vmem] * 4, (side, side, end, end), [], mine, *sides, pad)
    ends = trade(ends, "lat", False)
    slots = shape(tiles, PAIRS, 2, members, dtype=BF16)
    numbers = [pltpu.SMEM((SUB, LANES), F32), pltpu.SemaphoreType.DMA]
    block = shape(SUB, members)
    held_sides = pltpu.VMEM((2, rows + 2 * SUB, members), F32)
    own = call(row_kernel, "row_shares", [vmem] * 4, block, [held_sides] + numbers, mine, left, right, pad)
    blocks = call(
        functools.partial(prior_kernel, rows),
        "prior",
        [vmem] * 4,
        slots,
        [pltpu.VMEM((2,) + end.shape, F32), pltpu.VMEM((SUB, members), F32)] + numbers,
        mine,
        own,
        *ends,
    )
    near = window(exchange(blocks), lat_count, lon_count)
    count = len(NEAR) ** 2
    later = call(
        later_kernel,
        "later_shares",
        [vmem] * 6,
        shape(count + 1, SUB, members),
        [pltpu.SMEM((5, SUB, LANES), F32), pltpu.SemaphoreType.DMA((5,))],
        mine,
        left,
        right,
        *ends,
        pad,
    )
    column = shape(len(NEAR) * SUB, members)
    held_rows = pltpu.VMEM((members + SUB, members), F32)
    first_map, mid, *sides = call(
        functools.partial(first_kernel, lat_count),
        "first_batch",
        [vmem] * 3,
        (shape(members, members), column, column, column),
        [held_rows],
        near,
        pattern,
        later,
    )
    sides = trade(sides, LON, True)
    cells, done = call(
        apply_kernel,
        "apply_first",
        [vmem] * 2,
        (shape(rows * cols, 2 * members, dtype=BF16), shape(SUB, members)),
        [],
        first_map,
        pad,
    )
    shares = call(meet_kernel, "meet", [vmem] * 4, shape(tiles // 2, *column.shape), [], mid, *sides, done)
    shares = lax.all_to_all(shares, ("lat", "far"), split_axis=0, concat_axis=0, tiled=True)
    other = lax.ppermute(shares, "core", [(0, 1), (1, 0)])
    half = call(
        functools.partial(half_kernel, lat_count),
        "half_product",
        [vmem] * 2,
        shape(members + SUB, members),
        [],
        shares,
        pattern,
    )
    parts = 8
    result = call(
        functools.partial(last_kernel, lat_count),
        "second_batch",
        [vmem] * 4,
        shape(rows * cols, members),
        [
            pltpu.VMEM((rows * cols, members), F32),
            held_rows,
            pltpu.SemaphoreType.DMA((parts,)),
        ],
        half,
        other,
        pattern,
        cells,
        out_specs=anywhere,
    )
    return result.reshape(rows, cols, members)


def solution(mesh):
    lat_count, lon_count = (mesh.shape["lat"], mesh.shape["lon"])
    pairs = jax.sharding.Mesh(mesh.devices.reshape(lat_count, lon_count // 2, 2), ("lat",) + LON)
    placed = (
        P("lat", LON, None),
        P(None, "lat", LON, None),
        P(None, "lat", LON, None),
        P(None, "lat", LON, None, None),
        P(None, "lat", LON, None, None),
        P(None, "lat", LON, None),
        P(None, "lat", LON, None, None),
    )
    return jax.shard_map(
        local, mesh=pairs, in_specs=placed, out_specs=P("lat", LON, None), check_vma=False
    )
```

```python
import functools
import jax
import jax.numpy as jnp
from jax import lax
from jax.experimental import pallas as pl
from jax.experimental.pallas import tpu as pltpu
from jax.sharding import PartitionSpec as P

REACH = 2
WIN = 2 * REACH + 1
SUB = 8
LANES = 128
NEAR = (-1, 0, 1)
AT_ROW, AT_COL, AT_OBS = (4, 5, 6)
PAIRS = SUB // 2 + 1
F32 = jnp.float32
BF16 = jnp.bfloat16
LON = ("far", "core")


def partner(place, turn):
    return place + (-1 if place % 2 == turn else 1)


def trade(blocks, axis, wraps):
    count = lax.axis_size(axis)
    results = []
    for turn, block in enumerate(blocks):
        route = [(place, partner(place, turn)) for place in range(count)]
        route = [(source, target % count) for source, target in route if wraps or 0 <= target < count]
        results.append(lax.ppermute(block, axis, route))
    return results


def next_first(axis):
    return lax.rem(lax.axis_index(axis), 2) == 1


def start_kernel(
    width, observed, precision, weight, stencil, owned, cells, params_ref, sides_1, sides_0,
    observed_v, precision_v, weight_v, stencil_v, owned_v, left_v, right_v, sems
):
    batches, cols = (observed.shape[0], cells.shape[1])
    pairs = (
        (observed, observed_v),
        (precision, precision_v),
        (weight, weight_v),
        (stencil, stencil_v),
        (owned, owned_v),
        (cells.at[:, pl.ds(0, 1)], left_v),
        (cells.at[:, pl.ds(cols - 1, 1)], right_v),
    )
    copies = [pltpu.make_async_copy(source, target, sems.at[n]) for n, (source, target) in enumerate(pairs)]
    for copy in copies:
        copy.start()
    for copy in copies:
        copy.wait()
    params_ref[...] = jnp.zeros_like(params_ref)
    for b in range(batches):
        root = jnp.sqrt(precision_v[b, 0]) * owned_v[b, 0].astype(F32)
        corner = stencil_v[b, 0, 0, pl.ds(0, 1)].astype(F32)
        row = jnp.floor((corner + 0.5) * (1.0 / width))
        params_ref[b, pl.ds(0, 4), pl.ds(0, SUB)] = weight_v[b, 0, 0] * root
        params_ref[b, pl.ds(AT_ROW, 1), pl.ds(0, SUB)] = row
        params_ref[b, pl.ds(AT_COL, 1), pl.ds(0, SUB)] = corner - row * width
        params_ref[b, pl.ds(AT_OBS, 1), pl.ds(0, SUB)] = observed_v[b, 0] * root
    rows = cells.shape[0]
    forward = next_first("core")
    left, right = (left_v[:, 0, :], right_v[:, 0, :])
    sides_0[pl.ds(0, rows), :] = jnp.where(forward, right, left)
    sides_1[pl.ds(0, rows), :] = jnp.where(forward, left, right)
    sides_0[pl.ds(rows, SUB), :] = params_ref[1]
    sides_1[pl.ds(rows, SUB), :] = params_ref[1]


def clear_rim(pad, rows, cols):
    edge = jnp.zeros((2, cols + 2 * SUB, LANES), F32)
    pad[pl.ds(0, 2)] = edge
    pad[pl.ds(rows + 2, 2)] = edge
    side = jnp.zeros((rows, SUB, LANES), F32)
    pad[pl.ds(2, rows), pl.ds(0, SUB)] = side
    pad[pl.ds(2, rows), pl.ds(SUB + cols, SUB)] = side


def share(pad, number, rows, cols, da, dc, o):
    row = number(AT_ROW, o).astype(jnp.int32) - 1 + da * rows
    col = number(AT_COL, o).astype(jnp.int32) - 1 + dc * cols
    row = jnp.clip(row, -2, rows) + 2
    col = jnp.clip(col, -2, cols) + SUB
    terms = [number(k, o) * pad[row + k // 2, pl.ds(col + k % 2, 1), :] for k in range(4)]
    return (terms[0] + terms[1]) + (terms[2] + terms[3])


def own_shift(number):
    sub = lax.broadcasted_iota(jnp.int32, (SUB, LANES), 0)
    shift = jnp.zeros((SUB, LANES), F32)
    for o in range(SUB):
        shift = jnp.where(sub == o, number(AT_OBS, o), shift)
    return shift


def pad_kernel(cells, pad, sem):
    rows, cols = (cells.shape[0], cells.shape[1])
    copy = pltpu.make_async_copy(cells, pad.at[pl.ds(2, rows), pl.ds(SUB, cols)], sem)
    copy.start()
    clear_rim(pad, rows, cols)
    copy.wait()


def hold_sides(left, right, sides):
    rows = left.shape[0] - SUB
    sides[...] = jnp.zeros_like(sides)
    sides[0, pl.ds(SUB, rows), :] = left[pl.ds(0, rows), :]
    sides[1, pl.ds(SUB, rows), :] = right[pl.ds(0, rows), :]


def side_share(sides, side, number, rows, cols, da, o):
    row = number(AT_ROW, o).astype(jnp.int32) - 1 + da * rows
    row = jnp.clip(row, -2, rows) + SUB
    used = number(AT_COL, o).astype(jnp.int32) == (0, cols)[side]
    terms = [jnp.where(used, number(side + 2 * k, o), 0.0) * sides[side, pl.ds(row + k, 1), :] for k in range(2)]
    return terms[0] + terms[1]


def send_block(value, out_ref):
    mean = jnp.mean(value, axis=-1, keepdims=True)
    sub = lax.broadcasted_iota(jnp.int32, (SUB, LANES), 0)
    lane = lax.broadcasted_iota(jnp.int32, (SUB, LANES), 1)
    innov = jnp.sum(jnp.where(lane == sub, -mean, 0.0), axis=0, keepdims=True)
    rows = jnp.concatenate([value - mean, jnp.broadcast_to(innov, (2, LANES))], axis=0).astype(BF16)
    for n in range(PAIRS):
        pair = rows[2 * n:2 * n + 2]
        out_ref[:, n] = jnp.broadcast_to(pair, (out_ref.shape[0],) + pair.shape)


def rows_kernel(mine, sides_0, sides_1, pad, left_ref, right_ref, out_0, out_1):
    rows, cols = (pad.shape[0] - 4, pad.shape[1] - 2 * SUB)
    forward = next_first("core")
    left_ref[...] = jnp.where(forward, sides_1[...], sides_0[...])
    right_ref[...] = jnp.where(forward, sides_0[...], sides_1[...])
    lane = lax.broadcasted_iota(jnp.int32, (SUB, LANES), 1)
    block = pl.ds(rows, SUB)
    packed = jnp.where(lane < SUB, left_ref[block, :], pltpu.roll(mine[1], SUB, 1))
    packed = jnp.where(lane < 2 * SUB, packed, pltpu.roll(right_ref[block, :], 2 * SUB, 1))
    forward = next_first("lat")
    for turn, out in enumerate((out_0, out_1)):
        row = jnp.where(forward, (1 - turn) * (rows - 1), turn * (rows - 1))
        out[pl.ds(0, SUB), :] = jnp.broadcast_to(left_ref[pl.ds(row, 1), :], (SUB, LANES))
        out[pl.ds(SUB, cols), :] = pad[2 + row, pl.ds(SUB, cols), :]
        out[pl.ds(SUB + cols, SUB), :] = jnp.broadcast_to(right_ref[pl.ds(row, 1), :], (SUB, LANES))
        out[pl.ds(2 * SUB + cols, SUB), :] = packed


def row_kernel(mine, left, right, pad, out_ref, sides, params, sem):
    rows, cols = (pad.shape[0] - 4, pad.shape[1] - 2 * SUB)
    copy = pltpu.make_async_copy(mine.at[0], params, sem)
    copy.start()
    hold_sides(left, right, sides)
    copy.wait()
    number = lambda kind, o: params[kind, o]
    for o in range(SUB):
        total = share(pad, number, rows, cols, 0, 0, o)
        for side in range(2):
            total = total + side_share(sides, side, number, rows, cols, 0, o)
        out_ref[pl.ds(o, 1), :] = total
    out_ref[...] = out_ref[...] - own_shift(number)


def prior_kernel(rows, mine, own, ends_0, ends_1, out_ref, ends, value, params, sem):
    copy = pltpu.make_async_copy(mine.at[0], params, sem)
    copy.start()
    forward = next_first("lat")
    ends[0] = jnp.where(forward, ends_1[...], ends_0[...])
    ends[1] = jnp.where(forward, ends_0[...], ends_1[...])
    copy.wait()
    for o in range(SUB):
        row, col = (params[AT_ROW, o].astype(jnp.int32), params[AT_COL, o].astype(jnp.int32))
        total = own[pl.ds(o, 1), :]
        for n, at in enumerate((0, rows)):
            for k in range(2):
                weight = jnp.where(row == at, params[2 * n + k, o], 0.0)
                total = total + weight * ends[n, pl.ds(col + SUB - 1 + k, 1), :]
        value[pl.ds(o, 1), :] = total
    send_block(value[...], out_ref)


def meet_kernel(mid, sides_0, sides_1, done, out_ref):
    total = mid[...] + sides_0[...] + sides_1[...] + done[pl.ds(0, 1), :]
    out_ref[...] = jnp.broadcast_to(total, out_ref.shape)


def later_kernel(mine, left, right, ends_0, ends_1, pad, out_ref, params, sems):
    rows, cols = (pad.shape[0] - 4, pad.shape[1] - 2 * SUB)
    side, end = (pl.ds(rows, SUB), pl.ds(cols + 2 * SUB, SUB))
    sources = (left.at[side], mine.at[1], right.at[side], ends_0.at[end], ends_1.at[end])
    copies = []
    for n, source in enumerate(sources):
        copies.append(pltpu.make_async_copy(source, params.at[n], sems.at[n]))
        copies[-1].start()
    for copy in copies:
        copy.wait()
    forward = next_first("lat")
    ends = {-1: jnp.where(forward, 4, 3), 1: jnp.where(forward, 3, 4)}
    for n, dc in enumerate(NEAR):
        for m, da in enumerate(NEAR):
            spot, lane = (n, 0) if da == 0 else (ends[da], n * SUB)
            number = lambda kind, o: params[spot, kind, lane + o]
            for o in range(SUB):
                out_ref[n * len(NEAR) + m, pl.ds(o, 1), :] = share(pad, number, rows, cols, da, dc, o)
    out_ref[len(NEAR) ** 2] = own_shift(lambda kind, o: params[1, kind, o])


def window_start(lat_count, my_lat):
    return 0 if lat_count <= WIN else jnp.clip(my_lat - REACH, 0, lat_count - WIN)


def column_of(block, j):
    return jnp.broadcast_to(block[:, j:j + 1], block.shape)


def pivot_rows(block, after, k, held, between):
    sub = lax.broadcasted_iota(jnp.int32, block.shape, 0)
    lane = lax.broadcasted_iota(jnp.int32, block.shape, 1) - k * SUB
    held[pl.ds(k * SUB, SUB), :] = block
    rows = [held[pl.ds(k * SUB + r, SUB, stride=0), :] for r in range(SUB)]
    at = {(r, n): column_of(rows[r], k * SUB + n) for r in range(SUB) for n in range(r + 1)}
    here = (lane >= 0) & (lane < SUB)
    rows = [jnp.where(here, jnp.where(lane == r, 1.0, 0.0), row) for r, row in enumerate(rows)]
    inverse, scale = (jnp.zeros(block.shape, F32), jnp.ones(block.shape, F32))
    beside = [column_of(after, k * SUB + n) for n in range(SUB)]
    after = jnp.where(here, 0.0, after)
    for j in range(0, SUB, 2):
        a, b, c = (at[j, j], at[j + 1, j], at[j + 1, j + 1])
        det = a * c - b * b
        guess = pl.reciprocal(det, approx=True)
        better = 2.0 - det * guess
        over_det = guess * better
        top, bottom = (rows[j], rows[j + 1])
        rest = range(j + 2, SUB)
        upper = {n: (at[n, j], at[n, j + 1]) for n in rest}
        for r in rest:
            first, second = (at[r, j] * c - at[r, j + 1] * b, at[r, j + 1] * a - at[r, j] * b)
            if r < j + 4:
                for n in range(j + 2, r + 1):
                    taken = first * upper[n][0] + second * upper[n][1]
                    at[r, n] = at[r, n] - (taken * guess) * better
            first, second = (first * over_det, second * over_det)
            if r >= j + 4:
                for n in range(j + 2, r + 1):
                    at[r, n] = at[r, n] - (first * upper[n][0] + second * upper[n][1])
            rows[r] = rows[r] - (first * top + second * bottom)
        first, second = (beside[j] * c - beside[j + 1] * b, beside[j + 1] * a - beside[j] * b)
        first, second = (first * over_det, second * over_det)
        for n in rest:
            beside[n] = beside[n] - (first * upper[n][0] + second * upper[n][1])
        after = after - (first * top + second * bottom)
        a_part, b_part, c_part = (a * over_det, b * over_det, c * over_det)
        for r in range(j):
            first = at[r, j] * c_part - at[r, j + 1] * b_part
            second = at[r, j + 1] * a_part - at[r, j] * b_part
            for n in rest:
                at[r, n] = at[r, n] - (first * upper[n][0] + second * upper[n][1])
            rows[r] = rows[r] - (first * top + second * bottom)
        for n in rest:
            at[j, n] = c_part * upper[n][0] - b_part * upper[n][1]
            at[j + 1, n] = a_part * upper[n][1] - b_part * upper[n][0]
        rows[j] = c_part * top - b_part * bottom
        rows[j + 1] = a_part * bottom - b_part * top
        inverse = jnp.where(sub == j, top, jnp.where(sub == j + 1, a * bottom - b * top, inverse))
        scale = jnp.where(sub == j, a, jnp.where(sub == j + 1, a * det, scale))
        between()
    return rows, jnp.where(lane < SUB, inverse * lax.rsqrt(scale), 0.0), after


def eliminate(blocks, held):
    count = len(blocks) - 1
    blocks = list(blocks)
    lane = lax.broadcasted_iota(jnp.int32, blocks[0].shape, 1)
    inverse, waiting = ([], [])

    def update(i, k, pivot):
        terms = [column_of(blocks[i], k * SUB + j) * pivot[j] for j in range(SUB)]
        while len(terms) > 1:
            terms = [terms[n] + terms[n + 1] for n in range(0, len(terms), 2)]
        here = (lane >= k * SUB) & (lane < (k + 1) * SUB)
        blocks[i] = jnp.where(here, 0.0, blocks[i]) - terms[0]

    for k in range(count):
        if waiting:
            update(*waiting.pop(0))
        share_of = -(-len(waiting) // 4)

        def between():
            for task in waiting[:share_of]:
                update(*task)
            del waiting[:share_of]

        pivot, rows, blocks[k + 1] = pivot_rows(blocks[k], blocks[k + 1], k, held, between)
        waiting = [(i, k, pivot) for i in range(k + 2, count + 1)]
        inverse.append(rows)
    return inverse, blocks[count][:1]


def own_blocks(near_ref):
    scaled = jnp.concatenate([near_ref[:, n].astype(F32) for n in range(PAIRS - 1)], axis=1)
    innov = near_ref[:, PAIRS - 1].astype(F32)[:, :1]
    sub = lax.broadcasted_iota(jnp.int32, scaled.shape, 1)
    lane = lax.broadcasted_iota(jnp.int32, scaled.shape, 2)
    return scaled, jnp.where(lane == sub, jnp.broadcast_to(innov, scaled.shape), 0.0)


def summed_blocks(lat_count, shares):
    held = min(WIN, lat_count)
    far_count = shares.shape[0] // lat_count
    start = window_start(lat_count, lax.axis_index("lat"))
    values = []
    for j in range(held):
        for far in range(far_count):
            total = jnp.zeros((SUB, LANES), F32)
            for n, da in enumerate(NEAR):
                source = start + j - da
                part = pl.ds(n * SUB, SUB)
                if isinstance(source, int):
                    if 0 <= source < lat_count:
                        total = total + shares[source * far_count + far, part, :]
                else:
                    inside = (source >= 0) & (source < lat_count)
                    source = jnp.clip(source, 0, lat_count - 1)
                    total = total + jnp.where(inside, shares[source * far_count + far, part, :], 0.0)
            values.append(total[None])
    value = jnp.concatenate(values, axis=0)
    mean = jnp.mean(value, axis=-1, keepdims=True)
    sub = lax.broadcasted_iota(jnp.int32, value.shape, 1)
    lane = lax.broadcasted_iota(jnp.int32, value.shape, 2)
    innov = jnp.where(lane == sub, jnp.broadcast_to(-mean, value.shape), 0.0)
    return (value - mean).astype(BF16).astype(F32), innov


def marked_product(batch, lat_count, blocks, pattern, place=None):
    scaled, innov = blocks
    held = min(WIN, lat_count)
    count = scaled.shape[0]
    lon_count = pattern.shape[-1]
    my_lat = lax.axis_index("lat")
    start = window_start(lat_count, my_lat)
    picked = []
    for j in range(held):
        offset = start + j - my_lat + REACH
        inside = (offset >= 0) & (offset < WIN)
        row = pattern[batch, 0, 0, pl.ds(jnp.clip(offset, 0, WIN - 1), 1), :].astype(F32)
        row = jnp.where(inside, row, 0.0)
        marks = [jnp.broadcast_to(row[:, e:e + 1], (1, SUB, LANES)) for e in range(lon_count)]
        if place is not None:
            marks = [jnp.where(place == 1, marks[e + 1], marks[e]) for e in range(0, lon_count, 2)]
        picked.extend(marks)
    weighted = scaled * jnp.concatenate(picked, axis=0)
    both = jnp.concatenate([scaled, innov], axis=2).reshape(count * SUB, 2 * LANES).astype(BF16)
    product = lax.dot_general(
        both,
        weighted.reshape(count * SUB, LANES).astype(BF16),
        (((0,), (0,)), ((), ())),
        preferred_element_type=F32,
    )
    return product[:LANES + SUB]


def solved_map(product, held_rows):
    sub = lax.broadcasted_iota(jnp.int32, (SUB, LANES), 0)
    lane = lax.broadcasted_iota(jnp.int32, (SUB, LANES), 1)
    members = LANES
    blocks = []
    for k in range(members // SUB):
        block = product[k * SUB:(k + 1) * SUB, :]
        blocks.append(block + jnp.where(lane - k * SUB == sub, members - 1.0, 0.0))
    proj = jnp.sum(product[members:members + SUB, :], axis=0, keepdims=True)
    blocks.append(jnp.broadcast_to(proj, (SUB, LANES)))
    inverse, weights = eliminate(blocks, held_rows)
    flipped = jnp.concatenate(inverse, axis=0) * (members - 1.0) ** 0.5 - weights
    return flipped - jnp.mean(flipped, axis=-1, keepdims=True) + 1.0 / members


def exact_dot(a, b, contract_b):
    return lax.dot_general(
        a, b, (((1,), (contract_b,)), ((), ())), precision=lax.Precision.HIGHEST, preferred_element_type=F32
    )


def first_kernel(lat_count, near_ref, pattern, later, map_ref, mid_ref, out_0, out_1, held_rows):
    flipped = solved_map(marked_product(0, lat_count, own_blocks(near_ref), pattern), held_rows)
    map_ref[...] = flipped
    count = len(NEAR) ** 2
    moved = exact_dot(later[pl.ds(0, count)].reshape(-1, LANES), flipped, 1)
    size = len(NEAR) * SUB
    left, mid, right = (moved[:size], moved[size:2 * size], moved[2 * size:])
    mid_ref[...] = mid
    own = pl.ds(SUB, SUB)
    mid_ref[own, :] = mid[SUB:2 * SUB] - later[count]
    forward = next_first("core")
    out_0[...] = jnp.where(forward, right, left)
    out_1[...] = jnp.where(forward, left, right)


def half_kernel(lat_count, mine, pattern, out_ref):
    out_ref[...] = marked_product(1, lat_count, summed_blocks(lat_count, mine), pattern, lax.axis_index("core"))


def halves(value):
    upper = value.astype(BF16)
    return jnp.concatenate([upper, (value - upper.astype(F32)).astype(BF16)], axis=1)


def mapped(both, flipped):
    high = flipped.astype(BF16)
    low = (flipped - high.astype(F32)).astype(BF16)
    right = jnp.concatenate(
        [jnp.concatenate([high, high], axis=1), jnp.concatenate([low, jnp.zeros_like(low)], axis=1)], axis=0
    )
    product = lax.dot_general(both, right, (((1,), (1,)), ((), ())), preferred_element_type=F32)
    return product[:, :LANES] + product[:, LANES:]


def apply_kernel(map_ref, pad, out_ref, done_ref):
    rows, cols = (pad.shape[0] - 4, pad.shape[1] - 2 * SUB)
    size = 4
    for n in range(0, rows, size):
        value = pad[pl.ds(2 + n, size), pl.ds(SUB, cols), :].reshape(size * cols, LANES)
        out_ref[pl.ds(n * cols, size * cols), :] = halves(mapped(halves(value), map_ref[...]))
    done_ref[...] = jnp.zeros_like(done_ref)


def last_kernel(lat_count, half, other, pattern, cells, out_ref, result, held_rows, out_sem):
    parts = out_sem.shape[0]
    size = result.shape[0] // parts
    product = marked_product(1, lat_count, summed_blocks(lat_count, other), pattern, 1 - lax.axis_index("core"))
    flipped = solved_map(product + half[...], held_rows)
    copies = []
    for n in range(parts):
        part = pl.ds(n * size, size)
        result[part, :] = mapped(cells[part, :], flipped)
        copies.append(pltpu.make_async_copy(result.at[part], out_ref.at[part], out_sem.at[n]))
        copies[-1].start()
    for out_copy in copies:
        out_copy.wait()


def window(tiles, lat_count, lon_count):
    held = min(WIN, lat_count)
    if held == lat_count:
        return tiles
    start = jnp.clip(lax.axis_index("lat") - REACH, 0, lat_count - held)
    return lax.dynamic_slice_in_dim(tiles, start * lon_count, held * lon_count, axis=0)


def local(ensemble, observed, precision, interp_weight, stencil, owned, pattern):
    rows, cols, members = ensemble.shape
    batches = observed.shape[0]
    lat_count, lon_count = (lax.axis_size("lat"), lax.axis_size(LON))
    tiles = lat_count * lon_count
    vmem = pl.BlockSpec(memory_space=pltpu.VMEM)
    anywhere = pl.BlockSpec(memory_space=pl.ANY)
    hbm = pl.BlockSpec(memory_space=pltpu.HBM)
    megabyte = 1024 * 1024

    def shape(*dims, dtype=F32):
        return jax.ShapeDtypeStruct(dims, dtype)

    def call(kernel, name, specs, out_shape, scratch, *operands, out_specs=None, limit=48):
        return pl.pallas_call(
            kernel,
            out_shape=out_shape,
            in_specs=specs,
            out_specs=out_specs or jax.tree.map(lambda _: vmem, out_shape),
            scratch_shapes=scratch,
            compiler_params=pltpu.CompilerParams(vmem_limit_bytes=limit * megabyte),
            name=name,
        )(*operands)

    def exchange(blocks):
        return lax.all_to_all(blocks, ("lat",) + LON, split_axis=0, concat_axis=0, tiled=True)

    small = (observed, precision, interp_weight, stencil, owned)
    side = shape(rows + SUB, members)
    mine, side_1, side_0 = call(
        functools.partial(start_kernel, cols + 2),
        "start",
        [hbm] * 6,
        (shape(batches, SUB, LANES), side, side),
        [pltpu.VMEM(array.shape, array.dtype) for array in small]
        + [pltpu.VMEM((rows, 1, members), F32)] * 2
        + [pltpu.SemaphoreType.DMA((7,))],
        *small,
        ensemble,
        limit=63,
    )
    sides = trade((side_0, side_1), LON, True)
    padded = shape(rows + 4, cols + 2 * SUB, members)
    pad = call(pad_kernel, "pad", [hbm], padded, [pltpu.SemaphoreType.DMA], ensemble)
    end = shape(cols + 3 * SUB, members)
    left, right, *ends = call(rows_kernel, "edge_rows", [vmem] * 4, (side, side, end, end), [], mine, *sides, pad)
    ends = trade(ends, "lat", False)
    slots = shape(tiles, PAIRS, 2, members, dtype=BF16)
    numbers = [pltpu.SMEM((SUB, LANES), F32), pltpu.SemaphoreType.DMA]
    block = shape(SUB, members)
    held_sides = pltpu.VMEM((2, rows + 2 * SUB, members), F32)
    own = call(row_kernel, "row_shares", [vmem] * 4, block, [held_sides] + numbers, mine, left, right, pad)
    blocks = call(
        functools.partial(prior_kernel, rows),
        "prior",
        [vmem] * 4,
        slots,
        [pltpu.VMEM((2,) + end.shape, F32), pltpu.VMEM((SUB, members), F32)] + numbers,
        mine,
        own,
        *ends,
    )
    near = window(exchange(blocks), lat_count, lon_count)
    count = len(NEAR) ** 2
    later = call(
        later_kernel,
        "later_shares",
        [vmem] * 6,
        shape(count + 1, SUB, members),
        [pltpu.SMEM((5, SUB, LANES), F32), pltpu.SemaphoreType.DMA((5,))],
        mine,
        left,
        right,
        *ends,
        pad,
    )
    column = shape(len(NEAR) * SUB, members)
    held_rows = pltpu.VMEM((members + SUB, members), F32)
    first_map, mid, *sides = call(
        functools.partial(first_kernel, lat_count),
        "first_batch",
        [vmem] * 3,
        (shape(members, members), column, column, column),
        [held_rows],
        near,
        pattern,
        later,
    )
    sides = trade(sides, LON, True)
    cells, done = call(
        apply_kernel,
        "apply_first",
        [vmem] * 2,
        (shape(rows * cols, 2 * members, dtype=BF16), shape(SUB, members)),
        [],
        first_map,
        pad,
    )
    shares = call(meet_kernel, "meet", [vmem] * 4, shape(tiles // 2, *column.shape), [], mid, *sides, done)
    shares = lax.all_to_all(shares, ("lat", "far"), split_axis=0, concat_axis=0, tiled=True)
    other = lax.ppermute(shares, "core", [(0, 1), (1, 0)])
    half = call(
        functools.partial(half_kernel, lat_count),
        "half_product",
        [vmem] * 2,
        shape(members + SUB, members),
        [],
        shares,
        pattern,
    )
    parts = 8
    result = call(
        functools.partial(last_kernel, lat_count),
        "second_batch",
        [vmem] * 4,
        shape(rows * cols, members),
        [
            pltpu.VMEM((rows * cols, members), F32),
            held_rows,
            pltpu.SemaphoreType.DMA((parts,)),
        ],
        half,
        other,
        pattern,
        cells,
        out_specs=anywhere,
    )
    return result.reshape(rows, cols, members)


def solution(mesh):
    lat_count, lon_count = (mesh.shape["lat"], mesh.shape["lon"])
    pairs = jax.sharding.Mesh(mesh.devices.reshape(lat_count, lon_count // 2, 2), ("lat",) + LON)
    placed = (
        P("lat", LON, None),
        P(None, "lat", LON, None),
        P(None, "lat", LON, None),
        P(None, "lat", LON, None, None),
        P(None, "lat", LON, None, None),
        P(None, "lat", LON, None),
        P(None, "lat", LON, None, None),
    )
    return jax.shard_map(
        local, mesh=pairs, in_specs=placed, out_specs=P("lat", LON, None), check_vma=False
    )
```

```python
import functools
import jax
import jax.numpy as jnp
from jax import lax
from jax.experimental import pallas as pl
from jax.experimental.pallas import tpu as pltpu
from jax.sharding import PartitionSpec as P

REACH = 2
WIN = 2 * REACH + 1
SUB = 8
LANES = 128
NEAR = (-1, 0, 1)
AT_ROW, AT_COL, AT_OBS = (4, 5, 6)
PAIRS = SUB // 2 + 1
F32 = jnp.float32
BF16 = jnp.bfloat16
LON = ("far", "core")


def partner(place, turn):
    return place + (-1 if place % 2 == turn else 1)


def trade(blocks, axis, wraps):
    count = lax.axis_size(axis)
    results = []
    for turn, block in enumerate(blocks):
        route = [(place, partner(place, turn)) for place in range(count)]
        route = [(source, target % count) for source, target in route if wraps or 0 <= target < count]
        results.append(lax.ppermute(block, axis, route))
    return results


def next_first(axis):
    return lax.rem(lax.axis_index(axis), 2) == 1


def start_kernel(
    width, observed, precision, weight, stencil, owned, cells, params_ref, sides_1, sides_0,
    observed_v, precision_v, weight_v, stencil_v, owned_v, left_v, right_v, sems
):
    batches, cols = (observed.shape[0], cells.shape[1])
    pairs = (
        (observed, observed_v),
        (precision, precision_v),
        (weight, weight_v),
        (stencil, stencil_v),
        (owned, owned_v),
        (cells.at[:, pl.ds(0, 1)], left_v),
        (cells.at[:, pl.ds(cols - 1, 1)], right_v),
    )
    copies = [pltpu.make_async_copy(source, target, sems.at[n]) for n, (source, target) in enumerate(pairs)]
    for copy in copies:
        copy.start()
    for copy in copies:
        copy.wait()
    params_ref[...] = jnp.zeros_like(params_ref)
    for b in range(batches):
        root = jnp.sqrt(precision_v[b, 0]) * owned_v[b, 0].astype(F32)
        corner = stencil_v[b, 0, 0, pl.ds(0, 1)].astype(F32)
        row = jnp.floor((corner + 0.5) * (1.0 / width))
        params_ref[b, pl.ds(0, 4), pl.ds(0, SUB)] = weight_v[b, 0, 0] * root
        params_ref[b, pl.ds(AT_ROW, 1), pl.ds(0, SUB)] = row
        params_ref[b, pl.ds(AT_COL, 1), pl.ds(0, SUB)] = corner - row * width
        params_ref[b, pl.ds(AT_OBS, 1), pl.ds(0, SUB)] = observed_v[b, 0] * root
    rows = cells.shape[0]
    forward = next_first("core")
    left, right = (left_v[:, 0, :], right_v[:, 0, :])
    sides_0[pl.ds(0, rows), :] = jnp.where(forward, right, left)
    sides_1[pl.ds(0, rows), :] = jnp.where(forward, left, right)
    sides_0[pl.ds(rows, SUB), :] = params_ref[1]
    sides_1[pl.ds(rows, SUB), :] = params_ref[1]


def clear_rim(pad, rows, cols):
    edge = jnp.zeros((2, cols + 2 * SUB, LANES), F32)
    pad[pl.ds(0, 2)] = edge
    pad[pl.ds(rows + 2, 2)] = edge
    side = jnp.zeros((rows, SUB, LANES), F32)
    pad[pl.ds(2, rows), pl.ds(0, SUB)] = side
    pad[pl.ds(2, rows), pl.ds(SUB + cols, SUB)] = side


def share(pad, number, rows, cols, da, dc, o):
    row = number(AT_ROW, o).astype(jnp.int32) - 1 + da * rows
    col = number(AT_COL, o).astype(jnp.int32) - 1 + dc * cols
    row = jnp.clip(row, -2, rows) + 2
    col = jnp.clip(col, -2, cols) + SUB
    terms = [number(k, o) * pad[row + k // 2, pl.ds(col + k % 2, 1), :] for k in range(4)]
    return (terms[0] + terms[1]) + (terms[2] + terms[3])


def own_shift(number):
    sub = lax.broadcasted_iota(jnp.int32, (SUB, LANES), 0)
    shift = jnp.zeros((SUB, LANES), F32)
    for o in range(SUB):
        shift = jnp.where(sub == o, number(AT_OBS, o), shift)
    return shift


def pad_kernel(cells, pad, sem):
    rows, cols = (cells.shape[0], cells.shape[1])
    copy = pltpu.make_async_copy(cells, pad.at[pl.ds(2, rows), pl.ds(SUB, cols)], sem)
    copy.start()
    clear_rim(pad, rows, cols)
    copy.wait()


def hold_sides(left, right, sides):
    rows = left.shape[0] - SUB
    sides[...] = jnp.zeros_like(sides)
    sides[0, pl.ds(SUB, rows), :] = left[pl.ds(0, rows), :]
    sides[1, pl.ds(SUB, rows), :] = right[pl.ds(0, rows), :]


def side_share(sides, side, number, rows, cols, da, o):
    row = number(AT_ROW, o).astype(jnp.int32) - 1 + da * rows
    row = jnp.clip(row, -2, rows) + SUB
    used = number(AT_COL, o).astype(jnp.int32) == (0, cols)[side]
    terms = [jnp.where(used, number(side + 2 * k, o), 0.0) * sides[side, pl.ds(row + k, 1), :] for k in range(2)]
    return terms[0] + terms[1]


def send_block(value, out_ref):
    mean = jnp.mean(value, axis=-1, keepdims=True)
    sub = lax.broadcasted_iota(jnp.int32, (SUB, LANES), 0)
    lane = lax.broadcasted_iota(jnp.int32, (SUB, LANES), 1)
    innov = jnp.sum(jnp.where(lane == sub, -mean, 0.0), axis=0, keepdims=True)
    rows = jnp.concatenate([value - mean, jnp.broadcast_to(innov, (2, LANES))], axis=0).astype(BF16)
    for n in range(PAIRS):
        pair = rows[2 * n:2 * n + 2]
        out_ref[:, n] = jnp.broadcast_to(pair, (out_ref.shape[0],) + pair.shape)


def rows_kernel(mine, sides_0, sides_1, pad, left_ref, right_ref, out_0, out_1):
    rows, cols = (pad.shape[0] - 4, pad.shape[1] - 2 * SUB)
    forward = next_first("core")
    left_ref[...] = jnp.where(forward, sides_1[...], sides_0[...])
    right_ref[...] = jnp.where(forward, sides_0[...], sides_1[...])
    lane = lax.broadcasted_iota(jnp.int32, (SUB, LANES), 1)
    block = pl.ds(rows, SUB)
    packed = jnp.where(lane < SUB, left_ref[block, :], pltpu.roll(mine[1], SUB, 1))
    packed = jnp.where(lane < 2 * SUB, packed, pltpu.roll(right_ref[block, :], 2 * SUB, 1))
    forward = next_first("lat")
    for turn, out in enumerate((out_0, out_1)):
        row = jnp.where(forward, (1 - turn) * (rows - 1), turn * (rows - 1))
        out[pl.ds(0, SUB), :] = jnp.broadcast_to(left_ref[pl.ds(row, 1), :], (SUB, LANES))
        out[pl.ds(SUB, cols), :] = pad[2 + row, pl.ds(SUB, cols), :]
        out[pl.ds(SUB + cols, SUB), :] = jnp.broadcast_to(right_ref[pl.ds(row, 1), :], (SUB, LANES))
        out[pl.ds(2 * SUB + cols, SUB), :] = packed


def row_kernel(mine, left, right, pad, out_ref, sides, params, sem):
    rows, cols = (pad.shape[0] - 4, pad.shape[1] - 2 * SUB)
    copy = pltpu.make_async_copy(mine.at[0], params, sem)
    copy.start()
    hold_sides(left, right, sides)
    copy.wait()
    number = lambda kind, o: params[kind, o]
    for o in range(SUB):
        total = share(pad, number, rows, cols, 0, 0, o)
        for side in range(2):
            total = total + side_share(sides, side, number, rows, cols, 0, o)
        out_ref[pl.ds(o, 1), :] = total
    out_ref[...] = out_ref[...] - own_shift(number)


def prior_kernel(rows, mine, own, ends_0, ends_1, out_ref, ends, value, params, sem):
    copy = pltpu.make_async_copy(mine.at[0], params, sem)
    copy.start()
    forward = next_first("lat")
    ends[0] = jnp.where(forward, ends_1[...], ends_0[...])
    ends[1] = jnp.where(forward, ends_0[...], ends_1[...])
    copy.wait()
    for o in range(SUB):
        row, col = (params[AT_ROW, o].astype(jnp.int32), params[AT_COL, o].astype(jnp.int32))
        total = own[pl.ds(o, 1), :]
        for n, at in enumerate((0, rows)):
            for k in range(2):
                weight = jnp.where(row == at, params[2 * n + k, o], 0.0)
                total = total + weight * ends[n, pl.ds(col + SUB - 1 + k, 1), :]
        value[pl.ds(o, 1), :] = total
    send_block(value[...], out_ref)


def meet_kernel(mid, sides_0, sides_1, done, out_ref):
    total = mid[...] + sides_0[...] + sides_1[...] + done[pl.ds(0, 1), :]
    out_ref[...] = jnp.broadcast_to(total, out_ref.shape)


def later_kernel(mine, left, right, ends_0, ends_1, pad, out_ref, params, sems):
    rows, cols = (pad.shape[0] - 4, pad.shape[1] - 2 * SUB)
    side, end = (pl.ds(rows, SUB), pl.ds(cols + 2 * SUB, SUB))
    sources = (left.at[side], mine.at[1], right.at[side], ends_0.at[end], ends_1.at[end])
    copies = []
    for n, source in enumerate(sources):
        copies.append(pltpu.make_async_copy(source, params.at[n], sems.at[n]))
        copies[-1].start()
    for copy in copies:
        copy.wait()
    forward = next_first("lat")
    ends = {-1: jnp.where(forward, 4, 3), 1: jnp.where(forward, 3, 4)}
    for n, dc in enumerate(NEAR):
        for m, da in enumerate(NEAR):
            spot, lane = (n, 0) if da == 0 else (ends[da], n * SUB)
            number = lambda kind, o: params[spot, kind, lane + o]
            for o in range(SUB):
                out_ref[n * len(NEAR) + m, pl.ds(o, 1), :] = share(pad, number, rows, cols, da, dc, o)
    out_ref[len(NEAR) ** 2] = own_shift(lambda kind, o: params[1, kind, o])


def window_start(lat_count, my_lat):
    return 0 if lat_count <= WIN else jnp.clip(my_lat - REACH, 0, lat_count - WIN)


def column_of(block, j):
    return jnp.broadcast_to(block[:, j:j + 1], block.shape)


def pivot_rows(block, after, k, held, between):
    sub = lax.broadcasted_iota(jnp.int32, block.shape, 0)
    lane = lax.broadcasted_iota(jnp.int32, block.shape, 1) - k * SUB
    held[pl.ds(k * SUB, SUB), :] = block
    rows = [held[pl.ds(k * SUB + r, SUB, stride=0), :] for r in range(SUB)]
    at = {(r, n): column_of(rows[r], k * SUB + n) for r in range(SUB) for n in range(r + 1)}
    here = (lane >= 0) & (lane < SUB)
    rows = [jnp.where(here, jnp.where(lane == r, 1.0, 0.0), row) for r, row in enumerate(rows)]
    inverse, scale = (jnp.zeros(block.shape, F32), jnp.ones(block.shape, F32))
    beside = [column_of(after, k * SUB + n) for n in range(SUB)]
    after = jnp.where(here, 0.0, after)
    for j in range(0, SUB, 2):
        a, b, c = (at[j, j], at[j + 1, j], at[j + 1, j + 1])
        det = a * c - b * b
        guess = pl.reciprocal(det, approx=True)
        better = 2.0 - det * guess
        over_det = guess * better
        top, bottom = (rows[j], rows[j + 1])
        rest = range(j + 2, SUB)
        upper = {n: (at[n, j], at[n, j + 1]) for n in rest}
        for r in rest:
            first, second = (at[r, j] * c - at[r, j + 1] * b, at[r, j + 1] * a - at[r, j] * b)
            if r < j + 4:
                for n in range(j + 2, r + 1):
                    taken = first * upper[n][0] + second * upper[n][1]
                    at[r, n] = at[r, n] - (taken * guess) * better
            first, second = (first * over_det, second * over_det)
            if r >= j + 4:
                for n in range(j + 2, r + 1):
                    at[r, n] = at[r, n] - (first * upper[n][0] + second * upper[n][1])
            rows[r] = rows[r] - (first * top + second * bottom)
        first, second = (beside[j] * c - beside[j + 1] * b, beside[j + 1] * a - beside[j] * b)
        after = after - ((first * top + second * bottom) * guess) * better
        first, second = (first * over_det, second * over_det)
        for n in rest:
            beside[n] = beside[n] - (first * upper[n][0] + second * upper[n][1])
        a_part, b_part, c_part = (a * over_det, b * over_det, c * over_det)
        for r in range(j):
            first = at[r, j] * c_part - at[r, j + 1] * b_part
            second = at[r, j + 1] * a_part - at[r, j] * b_part
            for n in rest:
                at[r, n] = at[r, n] - (first * upper[n][0] + second * upper[n][1])
            rows[r] = rows[r] - (first * top + second * bottom)
        for n in rest:
            at[j, n] = c_part * upper[n][0] - b_part * upper[n][1]
            at[j + 1, n] = a_part * upper[n][1] - b_part * upper[n][0]
        rows[j] = c_part * top - b_part * bottom
        rows[j + 1] = a_part * bottom - b_part * top
        inverse = jnp.where(sub == j, top, jnp.where(sub == j + 1, a * bottom - b * top, inverse))
        scale = jnp.where(sub == j, a, jnp.where(sub == j + 1, a * det, scale))
        between()
    return rows, jnp.where(lane < SUB, inverse * lax.rsqrt(scale), 0.0), after


def eliminate(blocks, held):
    count = len(blocks) - 1
    blocks = list(blocks)
    lane = lax.broadcasted_iota(jnp.int32, blocks[0].shape, 1)
    inverse, waiting = ([], [])

    def update(i, k, pivot):
        terms = [column_of(blocks[i], k * SUB + j) * pivot[j] for j in range(SUB)]
        while len(terms) > 1:
            terms = [terms[n] + terms[n + 1] for n in range(0, len(terms), 2)]
        here = (lane >= k * SUB) & (lane < (k + 1) * SUB)
        blocks[i] = jnp.where(here, 0.0, blocks[i]) - terms[0]

    for k in range(count):
        if waiting:
            update(*waiting.pop(0))
        share_of = -(-len(waiting) // 4)

        def between():
            for task in waiting[:share_of]:
                update(*task)
            del waiting[:share_of]

        pivot, rows, blocks[k + 1] = pivot_rows(blocks[k], blocks[k + 1], k, held, between)
        waiting = [(i, k, pivot) for i in range(k + 2, count + 1)]
        inverse.append(rows)
    return inverse, blocks[count][:1]


def own_blocks(near_ref):
    scaled = jnp.concatenate([near_ref[:, n].astype(F32) for n in range(PAIRS - 1)], axis=1)
    innov = near_ref[:, PAIRS - 1].astype(F32)[:, :1]
    sub = lax.broadcasted_iota(jnp.int32, scaled.shape, 1)
    lane = lax.broadcasted_iota(jnp.int32, scaled.shape, 2)
    return scaled, jnp.where(lane == sub, jnp.broadcast_to(innov, scaled.shape), 0.0)


def summed_blocks(lat_count, shares):
    held = min(WIN, lat_count)
    far_count = shares.shape[0] // lat_count
    start = window_start(lat_count, lax.axis_index("lat"))
    values = []
    for j in range(held):
        for far in range(far_count):
            total = jnp.zeros((SUB, LANES), F32)
            for n, da in enumerate(NEAR):
                source = start + j - da
                part = pl.ds(n * SUB, SUB)
                if isinstance(source, int):
                    if 0 <= source < lat_count:
                        total = total + shares[source * far_count + far, part, :]
                else:
                    inside = (source >= 0) & (source < lat_count)
                    source = jnp.clip(source, 0, lat_count - 1)
                    total = total + jnp.where(inside, shares[source * far_count + far, part, :], 0.0)
            values.append(total[None])
    value = jnp.concatenate(values, axis=0)
    mean = jnp.mean(value, axis=-1, keepdims=True)
    sub = lax.broadcasted_iota(jnp.int32, value.shape, 1)
    lane = lax.broadcasted_iota(jnp.int32, value.shape, 2)
    innov = jnp.where(lane == sub, jnp.broadcast_to(-mean, value.shape), 0.0)
    return (value - mean).astype(BF16).astype(F32), innov


def marked_product(batch, lat_count, blocks, pattern, place=None):
    scaled, innov = blocks
    held = min(WIN, lat_count)
    count = scaled.shape[0]
    lon_count = pattern.shape[-1]
    my_lat = lax.axis_index("lat")
    start = window_start(lat_count, my_lat)
    picked = []
    for j in range(held):
        offset = start + j - my_lat + REACH
        inside = (offset >= 0) & (offset < WIN)
        row = pattern[batch, 0, 0, pl.ds(jnp.clip(offset, 0, WIN - 1), 1), :].astype(F32)
        row = jnp.where(inside, row, 0.0)
        marks = [jnp.broadcast_to(row[:, e:e + 1], (1, SUB, LANES)) for e in range(lon_count)]
        if place is not None:
            marks = [jnp.where(place == 1, marks[e + 1], marks[e]) for e in range(0, lon_count, 2)]
        picked.extend(marks)
    weighted = scaled * jnp.concatenate(picked, axis=0)
    both = jnp.concatenate([scaled, innov], axis=2).reshape(count * SUB, 2 * LANES).astype(BF16)
    product = lax.dot_general(
        both,
        weighted.reshape(count * SUB, LANES).astype(BF16),
        (((0,), (0,)), ((), ())),
        preferred_element_type=F32,
    )
    return product[:LANES + SUB]


def solved_map(product, held_rows):
    sub = lax.broadcasted_iota(jnp.int32, (SUB, LANES), 0)
    lane = lax.broadcasted_iota(jnp.int32, (SUB, LANES), 1)
    members = LANES
    blocks = []
    for k in range(members // SUB):
        block = product[k * SUB:(k + 1) * SUB, :]
        blocks.append(block + jnp.where(lane - k * SUB == sub, members - 1.0, 0.0))
    proj = jnp.sum(product[members:members + SUB, :], axis=0, keepdims=True)
    blocks.append(jnp.broadcast_to(proj, (SUB, LANES)))
    inverse, weights = eliminate(blocks, held_rows)
    flipped = jnp.concatenate(inverse, axis=0) * (members - 1.0) ** 0.5 - weights
    return flipped - jnp.mean(flipped, axis=-1, keepdims=True) + 1.0 / members


def exact_dot(a, b, contract_b):
    return lax.dot_general(
        a, b, (((1,), (contract_b,)), ((), ())), precision=lax.Precision.HIGHEST, preferred_element_type=F32
    )


def first_kernel(lat_count, near_ref, pattern, later, map_ref, mid_ref, out_0, out_1, held_rows):
    flipped = solved_map(marked_product(0, lat_count, own_blocks(near_ref), pattern), held_rows)
    map_ref[...] = flipped
    count = len(NEAR) ** 2
    moved = exact_dot(later[pl.ds(0, count)].reshape(-1, LANES), flipped, 1)
    size = len(NEAR) * SUB
    left, mid, right = (moved[:size], moved[size:2 * size], moved[2 * size:])
    mid_ref[...] = mid
    own = pl.ds(SUB, SUB)
    mid_ref[own, :] = mid[SUB:2 * SUB] - later[count]
    forward = next_first("core")
    out_0[...] = jnp.where(forward, right, left)
    out_1[...] = jnp.where(forward, left, right)


def half_kernel(lat_count, mine, pattern, out_ref):
    out_ref[...] = marked_product(1, lat_count, summed_blocks(lat_count, mine), pattern, lax.axis_index("core"))


def halves(value):
    upper = value.astype(BF16)
    return jnp.concatenate([upper, (value - upper.astype(F32)).astype(BF16)], axis=1)


def mapped(both, flipped):
    high = flipped.astype(BF16)
    low = (flipped - high.astype(F32)).astype(BF16)
    right = jnp.concatenate(
        [jnp.concatenate([high, high], axis=1), jnp.concatenate([low, jnp.zeros_like(low)], axis=1)], axis=0
    )
    product = lax.dot_general(both, right, (((1,), (1,)), ((), ())), preferred_element_type=F32)
    return product[:, :LANES] + product[:, LANES:]


def apply_kernel(map_ref, pad, out_ref, done_ref):
    rows, cols = (pad.shape[0] - 4, pad.shape[1] - 2 * SUB)
    size = 4
    for n in range(0, rows, size):
        value = pad[pl.ds(2 + n, size), pl.ds(SUB, cols), :].reshape(size * cols, LANES)
        out_ref[pl.ds(n * cols, size * cols), :] = halves(mapped(halves(value), map_ref[...]))
    done_ref[...] = jnp.zeros_like(done_ref)


def last_kernel(lat_count, half, other, pattern, cells, out_ref, result, held_rows, out_sem):
    parts = out_sem.shape[0]
    size = result.shape[0] // parts
    product = marked_product(1, lat_count, summed_blocks(lat_count, other), pattern, 1 - lax.axis_index("core"))
    flipped = solved_map(product + half[...], held_rows)
    copies = []
    for n in range(parts):
        part = pl.ds(n * size, size)
        result[part, :] = mapped(cells[part, :], flipped)
        copies.append(pltpu.make_async_copy(result.at[part], out_ref.at[part], out_sem.at[n]))
        copies[-1].start()
    for out_copy in copies:
        out_copy.wait()


def window(tiles, lat_count, lon_count):
    held = min(WIN, lat_count)
    if held == lat_count:
        return tiles
    start = jnp.clip(lax.axis_index("lat") - REACH, 0, lat_count - held)
    return lax.dynamic_slice_in_dim(tiles, start * lon_count, held * lon_count, axis=0)


def local(ensemble, observed, precision, interp_weight, stencil, owned, pattern):
    rows, cols, members = ensemble.shape
    batches = observed.shape[0]
    lat_count, lon_count = (lax.axis_size("lat"), lax.axis_size(LON))
    tiles = lat_count * lon_count
    vmem = pl.BlockSpec(memory_space=pltpu.VMEM)
    anywhere = pl.BlockSpec(memory_space=pl.ANY)
    hbm = pl.BlockSpec(memory_space=pltpu.HBM)
    megabyte = 1024 * 1024

    def shape(*dims, dtype=F32):
        return jax.ShapeDtypeStruct(dims, dtype)

    def call(kernel, name, specs, out_shape, scratch, *operands, out_specs=None, limit=48):
        return pl.pallas_call(
            kernel,
            out_shape=out_shape,
            in_specs=specs,
            out_specs=out_specs or jax.tree.map(lambda _: vmem, out_shape),
            scratch_shapes=scratch,
            compiler_params=pltpu.CompilerParams(vmem_limit_bytes=limit * megabyte),
            name=name,
        )(*operands)

    def exchange(blocks):
        return lax.all_to_all(blocks, ("lat",) + LON, split_axis=0, concat_axis=0, tiled=True)

    small = (observed, precision, interp_weight, stencil, owned)
    side = shape(rows + SUB, members)
    mine, side_1, side_0 = call(
        functools.partial(start_kernel, cols + 2),
        "start",
        [hbm] * 6,
        (shape(batches, SUB, LANES), side, side),
        [pltpu.VMEM(array.shape, array.dtype) for array in small]
        + [pltpu.VMEM((rows, 1, members), F32)] * 2
        + [pltpu.SemaphoreType.DMA((7,))],
        *small,
        ensemble,
        limit=63,
    )
    sides = trade((side_0, side_1), LON, True)
    padded = shape(rows + 4, cols + 2 * SUB, members)
    pad = call(pad_kernel, "pad", [hbm], padded, [pltpu.SemaphoreType.DMA], ensemble)
    end = shape(cols + 3 * SUB, members)
    left, right, *ends = call(rows_kernel, "edge_rows", [vmem] * 4, (side, side, end, end), [], mine, *sides, pad)
    ends = trade(ends, "lat", False)
    slots = shape(tiles, PAIRS, 2, members, dtype=BF16)
    numbers = [pltpu.SMEM((SUB, LANES), F32), pltpu.SemaphoreType.DMA]
    block = shape(SUB, members)
    held_sides = pltpu.VMEM((2, rows + 2 * SUB, members), F32)
    own = call(row_kernel, "row_shares", [vmem] * 4, block, [held_sides] + numbers, mine, left, right, pad)
    blocks = call(
        functools.partial(prior_kernel, rows),
        "prior",
        [vmem] * 4,
        slots,
        [pltpu.VMEM((2,) + end.shape, F32), pltpu.VMEM((SUB, members), F32)] + numbers,
        mine,
        own,
        *ends,
    )
    near = window(exchange(blocks), lat_count, lon_count)
    count = len(NEAR) ** 2
    later = call(
        later_kernel,
        "later_shares",
        [vmem] * 6,
        shape(count + 1, SUB, members),
        [pltpu.SMEM((5, SUB, LANES), F32), pltpu.SemaphoreType.DMA((5,))],
        mine,
        left,
        right,
        *ends,
        pad,
    )
    column = shape(len(NEAR) * SUB, members)
    held_rows = pltpu.VMEM((members + SUB, members), F32)
    first_map, mid, *sides = call(
        functools.partial(first_kernel, lat_count),
        "first_batch",
        [vmem] * 3,
        (shape(members, members), column, column, column),
        [held_rows],
        near,
        pattern,
        later,
    )
    sides = trade(sides, LON, True)
    cells, done = call(
        apply_kernel,
        "apply_first",
        [vmem] * 2,
        (shape(rows * cols, 2 * members, dtype=BF16), shape(SUB, members)),
        [],
        first_map,
        pad,
    )
    shares = call(meet_kernel, "meet", [vmem] * 4, shape(tiles // 2, *column.shape), [], mid, *sides, done)
    shares = lax.all_to_all(shares, ("lat", "far"), split_axis=0, concat_axis=0, tiled=True)
    other = lax.ppermute(shares, "core", [(0, 1), (1, 0)])
    half = call(
        functools.partial(half_kernel, lat_count),
        "half_product",
        [vmem] * 2,
        shape(members + SUB, members),
        [],
        shares,
        pattern,
    )
    parts = 8
    result = call(
        functools.partial(last_kernel, lat_count),
        "second_batch",
        [vmem] * 4,
        shape(rows * cols, members),
        [
            pltpu.VMEM((rows * cols, members), F32),
            held_rows,
            pltpu.SemaphoreType.DMA((parts,)),
        ],
        half,
        other,
        pattern,
        cells,
        out_specs=anywhere,
    )
    return result.reshape(rows, cols, members)


def solution(mesh):
    lat_count, lon_count = (mesh.shape["lat"], mesh.shape["lon"])
    pairs = jax.sharding.Mesh(mesh.devices.reshape(lat_count, lon_count // 2, 2), ("lat",) + LON)
    placed = (
        P("lat", LON, None),
        P(None, "lat", LON, None),
        P(None, "lat", LON, None),
        P(None, "lat", LON, None, None),
        P(None, "lat", LON, None, None),
        P(None, "lat", LON, None),
        P(None, "lat", LON, None, None),
    )
    return jax.shard_map(
        local, mesh=pairs, in_specs=placed, out_specs=P("lat", LON, None), check_vma=False
    )
```

```python
import functools
import jax
import jax.numpy as jnp
from jax import lax
from jax.experimental import pallas as pl
from jax.experimental.pallas import tpu as pltpu
from jax.sharding import PartitionSpec as P

REACH = 2
WIN = 2 * REACH + 1
SUB = 8
LANES = 128
NEAR = (-1, 0, 1)
AT_ROW, AT_COL, AT_OBS = (4, 5, 6)
PAIRS = SUB // 2 + 1
F32 = jnp.float32
BF16 = jnp.bfloat16
LON = ("far", "core")


def partner(place, turn):
    return place + (-1 if place % 2 == turn else 1)


def trade(blocks, axis, wraps):
    count = lax.axis_size(axis)
    results = []
    for turn, block in enumerate(blocks):
        route = [(place, partner(place, turn)) for place in range(count)]
        route = [(source, target % count) for source, target in route if wraps or 0 <= target < count]
        results.append(lax.ppermute(block, axis, route))
    return results


def next_first(axis):
    return lax.rem(lax.axis_index(axis), 2) == 1


def start_kernel(
    width, observed, precision, weight, stencil, owned, cells, params_ref, sides_1, sides_0,
    observed_v, precision_v, weight_v, stencil_v, owned_v, left_v, right_v, sems
):
    batches, cols = (observed.shape[0], cells.shape[1])
    pairs = (
        (observed, observed_v),
        (precision, precision_v),
        (weight, weight_v),
        (stencil, stencil_v),
        (owned, owned_v),
        (cells.at[:, pl.ds(0, 1)], left_v),
        (cells.at[:, pl.ds(cols - 1, 1)], right_v),
    )
    copies = [pltpu.make_async_copy(source, target, sems.at[n]) for n, (source, target) in enumerate(pairs)]
    for copy in copies:
        copy.start()
    for copy in copies:
        copy.wait()
    params_ref[...] = jnp.zeros_like(params_ref)
    for b in range(batches):
        root = jnp.sqrt(precision_v[b, 0]) * owned_v[b, 0].astype(F32)
        corner = stencil_v[b, 0, 0, pl.ds(0, 1)].astype(F32)
        row = jnp.floor((corner + 0.5) * (1.0 / width))
        params_ref[b, pl.ds(0, 4), pl.ds(0, SUB)] = weight_v[b, 0, 0] * root
        params_ref[b, pl.ds(AT_ROW, 1), pl.ds(0, SUB)] = row
        params_ref[b, pl.ds(AT_COL, 1), pl.ds(0, SUB)] = corner - row * width
        params_ref[b, pl.ds(AT_OBS, 1), pl.ds(0, SUB)] = observed_v[b, 0] * root
    rows = cells.shape[0]
    forward = next_first("core")
    left, right = (left_v[:, 0, :], right_v[:, 0, :])
    sides_0[pl.ds(0, rows), :] = jnp.where(forward, right, left)
    sides_1[pl.ds(0, rows), :] = jnp.where(forward, left, right)
    sides_0[pl.ds(rows, SUB), :] = params_ref[1]
    sides_1[pl.ds(rows, SUB), :] = params_ref[1]


def clear_rim(pad, rows, cols):
    edge = jnp.zeros((2, cols + 2 * SUB, LANES), F32)
    pad[pl.ds(0, 2)] = edge
    pad[pl.ds(rows + 2, 2)] = edge
    side = jnp.zeros((rows, SUB, LANES), F32)
    pad[pl.ds(2, rows), pl.ds(0, SUB)] = side
    pad[pl.ds(2, rows), pl.ds(SUB + cols, SUB)] = side


def share(pad, number, rows, cols, da, dc, o):
    row = number(AT_ROW, o).astype(jnp.int32) - 1 + da * rows
    col = number(AT_COL, o).astype(jnp.int32) - 1 + dc * cols
    row = jnp.clip(row, -2, rows) + 2
    col = jnp.clip(col, -2, cols) + SUB
    terms = [number(k, o) * pad[row + k // 2, pl.ds(col + k % 2, 1), :] for k in range(4)]
    return (terms[0] + terms[1]) + (terms[2] + terms[3])


def own_shift(number):
    sub = lax.broadcasted_iota(jnp.int32, (SUB, LANES), 0)
    shift = jnp.zeros((SUB, LANES), F32)
    for o in range(SUB):
        shift = jnp.where(sub == o, number(AT_OBS, o), shift)
    return shift


def pad_kernel(cells, pad, sem):
    rows, cols = (cells.shape[0], cells.shape[1])
    copy = pltpu.make_async_copy(cells, pad.at[pl.ds(2, rows), pl.ds(SUB, cols)], sem)
    copy.start()
    clear_rim(pad, rows, cols)
    copy.wait()


def hold_sides(left, right, sides):
    rows = left.shape[0] - SUB
    sides[...] = jnp.zeros_like(sides)
    sides[0, pl.ds(SUB, rows), :] = left[pl.ds(0, rows), :]
    sides[1, pl.ds(SUB, rows), :] = right[pl.ds(0, rows), :]


def side_share(sides, side, number, rows, cols, da, o):
    row = number(AT_ROW, o).astype(jnp.int32) - 1 + da * rows
    row = jnp.clip(row, -2, rows) + SUB
    used = number(AT_COL, o).astype(jnp.int32) == (0, cols)[side]
    terms = [jnp.where(used, number(side + 2 * k, o), 0.0) * sides[side, pl.ds(row + k, 1), :] for k in range(2)]
    return terms[0] + terms[1]


def send_block(value, out_ref):
    mean = jnp.mean(value, axis=-1, keepdims=True)
    sub = lax.broadcasted_iota(jnp.int32, (SUB, LANES), 0)
    lane = lax.broadcasted_iota(jnp.int32, (SUB, LANES), 1)
    innov = jnp.sum(jnp.where(lane == sub, -mean, 0.0), axis=0, keepdims=True)
    rows = jnp.concatenate([value - mean, jnp.broadcast_to(innov, (2, LANES))], axis=0).astype(BF16)
    for n in range(PAIRS):
        pair = rows[2 * n:2 * n + 2]
        out_ref[:, n] = jnp.broadcast_to(pair, (out_ref.shape[0],) + pair.shape)


def rows_kernel(mine, sides_0, sides_1, pad, left_ref, right_ref, out_0, out_1):
    rows, cols = (pad.shape[0] - 4, pad.shape[1] - 2 * SUB)
    forward = next_first("core")
    left_ref[...] = jnp.where(forward, sides_1[...], sides_0[...])
    right_ref[...] = jnp.where(forward, sides_0[...], sides_1[...])
    lane = lax.broadcasted_iota(jnp.int32, (SUB, LANES), 1)
    block = pl.ds(rows, SUB)
    packed = jnp.where(lane < SUB, left_ref[block, :], pltpu.roll(mine[1], SUB, 1))
    packed = jnp.where(lane < 2 * SUB, packed, pltpu.roll(right_ref[block, :], 2 * SUB, 1))
    forward = next_first("lat")
    for turn, out in enumerate((out_0, out_1)):
        row = jnp.where(forward, (1 - turn) * (rows - 1), turn * (rows - 1))
        out[pl.ds(0, SUB), :] = jnp.broadcast_to(left_ref[pl.ds(row, 1), :], (SUB, LANES))
        out[pl.ds(SUB, cols), :] = pad[2 + row, pl.ds(SUB, cols), :]
        out[pl.ds(SUB + cols, SUB), :] = jnp.broadcast_to(right_ref[pl.ds(row, 1), :], (SUB, LANES))
        out[pl.ds(2 * SUB + cols, SUB), :] = packed


def row_kernel(mine, left, right, pad, out_ref, sides, params, sem):
    rows, cols = (pad.shape[0] - 4, pad.shape[1] - 2 * SUB)
    copy = pltpu.make_async_copy(mine.at[0], params, sem)
    copy.start()
    hold_sides(left, right, sides)
    copy.wait()
    number = lambda kind, o: params[kind, o]
    for o in range(SUB):
        total = share(pad, number, rows, cols, 0, 0, o)
        for side in range(2):
            total = total + side_share(sides, side, number, rows, cols, 0, o)
        out_ref[pl.ds(o, 1), :] = total
    out_ref[...] = out_ref[...] - own_shift(number)


def prior_kernel(rows, mine, own, ends_0, ends_1, out_ref, ends, value, params, sem):
    copy = pltpu.make_async_copy(mine.at[0], params, sem)
    copy.start()
    forward = next_first("lat")
    ends[0] = jnp.where(forward, ends_1[...], ends_0[...])
    ends[1] = jnp.where(forward, ends_0[...], ends_1[...])
    copy.wait()
    for o in range(SUB):
        row, col = (params[AT_ROW, o].astype(jnp.int32), params[AT_COL, o].astype(jnp.int32))
        total = own[pl.ds(o, 1), :]
        for n, at in enumerate((0, rows)):
            for k in range(2):
                weight = jnp.where(row == at, params[2 * n + k, o], 0.0)
                total = total + weight * ends[n, pl.ds(col + SUB - 1 + k, 1), :]
        value[pl.ds(o, 1), :] = total
    send_block(value[...], out_ref)


def meet_kernel(mid, sides_0, sides_1, done, out_ref):
    total = mid[...] + sides_0[...] + sides_1[...] + done[pl.ds(0, 1), :]
    out_ref[...] = jnp.broadcast_to(total, out_ref.shape)


def later_kernel(mine, left, right, ends_0, ends_1, pad, out_ref, params, sems):
    rows, cols = (pad.shape[0] - 4, pad.shape[1] - 2 * SUB)
    side, end = (pl.ds(rows, SUB), pl.ds(cols + 2 * SUB, SUB))
    sources = (left.at[side], mine.at[1], right.at[side], ends_0.at[end], ends_1.at[end])
    copies = []
    for n, source in enumerate(sources):
        copies.append(pltpu.make_async_copy(source, params.at[n], sems.at[n]))
        copies[-1].start()
    for copy in copies:
        copy.wait()
    forward = next_first("lat")
    ends = {-1: jnp.where(forward, 4, 3), 1: jnp.where(forward, 3, 4)}
    for n, dc in enumerate(NEAR):
        for m, da in enumerate(NEAR):
            spot, lane = (n, 0) if da == 0 else (ends[da], n * SUB)
            number = lambda kind, o: params[spot, kind, lane + o]
            for o in range(SUB):
                out_ref[n * len(NEAR) + m, pl.ds(o, 1), :] = share(pad, number, rows, cols, da, dc, o)
    out_ref[len(NEAR) ** 2] = own_shift(lambda kind, o: params[1, kind, o])


def window_start(lat_count, my_lat):
    return 0 if lat_count <= WIN else jnp.clip(my_lat - REACH, 0, lat_count - WIN)


def column_of(block, j):
    return jnp.broadcast_to(block[:, j:j + 1], block.shape)


def pivot_rows(block, after, k, held, between):
    sub = lax.broadcasted_iota(jnp.int32, block.shape, 0)
    lane = lax.broadcasted_iota(jnp.int32, block.shape, 1) - k * SUB
    held[pl.ds(k * SUB, SUB), :] = block
    rows = [held[pl.ds(k * SUB + r, SUB, stride=0), :] for r in range(SUB)]
    at = {(r, n): column_of(rows[r], k * SUB + n) for r in range(SUB) for n in range(r + 1)}
    here = (lane >= 0) & (lane < SUB)
    rows = [jnp.where(here, jnp.where(lane == r, 1.0, 0.0), row) for r, row in enumerate(rows)]
    inverse, scale = (jnp.zeros(block.shape, F32), jnp.ones(block.shape, F32))
    beside = [column_of(after, k * SUB + n) for n in range(SUB)]
    after = jnp.where(here, 0.0, after)
    for j in range(0, SUB, 2):
        a, b, c = (at[j, j], at[j + 1, j], at[j + 1, j + 1])
        det = a * c - b * b
        guess = pl.reciprocal(det, approx=True)
        better = 2.0 - det * guess
        over_det = guess * better
        top, bottom = (rows[j], rows[j + 1])
        rest = range(j + 2, SUB)
        upper = {n: (at[n, j], at[n, j + 1]) for n in rest}
        for r in rest:
            first, second = (at[r, j] * c - at[r, j + 1] * b, at[r, j + 1] * a - at[r, j] * b)
            if r < j + 4:
                for n in range(j + 2, r + 1):
                    taken = first * upper[n][0] + second * upper[n][1]
                    at[r, n] = at[r, n] - (taken * guess) * better
            first, second = (first * over_det, second * over_det)
            if r >= j + 4:
                for n in range(j + 2, r + 1):
                    at[r, n] = at[r, n] - (first * upper[n][0] + second * upper[n][1])
            rows[r] = rows[r] - (first * top + second * bottom)
        first, second = (beside[j] * c - beside[j + 1] * b, beside[j + 1] * a - beside[j] * b)
        after = after - ((first * top + second * bottom) * guess) * better
        first, second = (first * over_det, second * over_det)
        for n in rest:
            beside[n] = beside[n] - (first * upper[n][0] + second * upper[n][1])
        a_part, b_part, c_part = (a * over_det, b * over_det, c * over_det)
        for r in range(j):
            first = at[r, j] * c_part - at[r, j + 1] * b_part
            second = at[r, j + 1] * a_part - at[r, j] * b_part
            for n in rest:
                at[r, n] = at[r, n] - (first * upper[n][0] + second * upper[n][1])
            rows[r] = rows[r] - (first * top + second * bottom)
        for n in rest:
            at[j, n] = c_part * upper[n][0] - b_part * upper[n][1]
            at[j + 1, n] = a_part * upper[n][1] - b_part * upper[n][0]
        rows[j] = c_part * top - b_part * bottom
        rows[j + 1] = a_part * bottom - b_part * top
        inverse = jnp.where(sub == j, top, jnp.where(sub == j + 1, a * bottom - b * top, inverse))
        scale = jnp.where(sub == j, a, jnp.where(sub == j + 1, a * det, scale))
        between()
    return rows, jnp.where(lane < SUB, inverse * lax.rsqrt(scale), 0.0), after


def eliminate(blocks, held):
    count = len(blocks) - 1
    blocks = list(blocks)
    lane = lax.broadcasted_iota(jnp.int32, blocks[0].shape, 1)
    inverse, waiting = ([], [])

    def update(i, k, pivot):
        terms = [column_of(blocks[i], k * SUB + j) * pivot[j] for j in range(SUB)]
        while len(terms) > 1:
            terms = [terms[n] + terms[n + 1] for n in range(0, len(terms), 2)]
        here = (lane >= k * SUB) & (lane < (k + 1) * SUB)
        blocks[i] = jnp.where(here, 0.0, blocks[i]) - terms[0]

    for k in range(count):
        if waiting:
            update(*waiting.pop(0))
        share_of = -(-len(waiting) // 4)

        def between():
            for task in waiting[:share_of]:
                update(*task)
            del waiting[:share_of]

        pivot, rows, blocks[k + 1] = pivot_rows(blocks[k], blocks[k + 1], k, held, between)
        waiting = [(i, k, pivot) for i in range(k + 2, count + 1)]
        inverse.append(rows)
    return inverse, blocks[count][:1]


def own_blocks(near_ref):
    scaled = jnp.concatenate([near_ref[:, n].astype(F32) for n in range(PAIRS - 1)], axis=1)
    innov = near_ref[:, PAIRS - 1].astype(F32)[:, :1]
    sub = lax.broadcasted_iota(jnp.int32, scaled.shape, 1)
    lane = lax.broadcasted_iota(jnp.int32, scaled.shape, 2)
    return scaled, jnp.where(lane == sub, jnp.broadcast_to(innov, scaled.shape), 0.0)


def summed_blocks(lat_count, shares):
    held = min(WIN, lat_count)
    far_count = shares.shape[0] // lat_count
    start = window_start(lat_count, lax.axis_index("lat"))
    values = []
    for j in range(held):
        for far in range(far_count):
            total = jnp.zeros((SUB, LANES), F32)
            for n, da in enumerate(NEAR):
                source = start + j - da
                part = pl.ds(n * SUB, SUB)
                if isinstance(source, int):
                    if 0 <= source < lat_count:
                        total = total + shares[source * far_count + far, part, :]
                else:
                    inside = (source >= 0) & (source < lat_count)
                    source = jnp.clip(source, 0, lat_count - 1)
                    total = total + jnp.where(inside, shares[source * far_count + far, part, :], 0.0)
            values.append(total[None])
    value = jnp.concatenate(values, axis=0)
    mean = jnp.mean(value, axis=-1, keepdims=True)
    sub = lax.broadcasted_iota(jnp.int32, value.shape, 1)
    lane = lax.broadcasted_iota(jnp.int32, value.shape, 2)
    innov = jnp.where(lane == sub, jnp.broadcast_to(-mean, value.shape), 0.0)
    return (value - mean).astype(BF16).astype(F32), innov


def marked_product(batch, lat_count, blocks, pattern, place=None):
    scaled, innov = blocks
    held = min(WIN, lat_count)
    count = scaled.shape[0]
    lon_count = pattern.shape[-1]
    my_lat = lax.axis_index("lat")
    start = window_start(lat_count, my_lat)
    picked = []
    for j in range(held):
        offset = start + j - my_lat + REACH
        inside = (offset >= 0) & (offset < WIN)
        row = pattern[batch, 0, 0, pl.ds(jnp.clip(offset, 0, WIN - 1), 1), :].astype(F32)
        row = jnp.where(inside, row, 0.0)
        marks = [jnp.broadcast_to(row[:, e:e + 1], (1, SUB, LANES)) for e in range(lon_count)]
        if place is not None:
            marks = [jnp.where(place == 1, marks[e + 1], marks[e]) for e in range(0, lon_count, 2)]
        picked.extend(marks)
    weighted = scaled * jnp.concatenate(picked, axis=0)
    both = jnp.concatenate([scaled, innov], axis=2).reshape(count * SUB, 2 * LANES).astype(BF16)
    product = lax.dot_general(
        both,
        weighted.reshape(count * SUB, LANES).astype(BF16),
        (((0,), (0,)), ((), ())),
        preferred_element_type=F32,
    )
    return product[:LANES + SUB]


def solved_map(product, held_rows):
    sub = lax.broadcasted_iota(jnp.int32, (SUB, LANES), 0)
    lane = lax.broadcasted_iota(jnp.int32, (SUB, LANES), 1)
    members = LANES
    blocks = []
    for k in range(members // SUB):
        block = product[k * SUB:(k + 1) * SUB, :]
        blocks.append(block + jnp.where(lane - k * SUB == sub, members - 1.0, 0.0))
    proj = jnp.sum(product[members:members + SUB, :], axis=0, keepdims=True)
    blocks.append(jnp.broadcast_to(proj, (SUB, LANES)))
    inverse, weights = eliminate(blocks, held_rows)
    flipped = jnp.concatenate(inverse, axis=0) * (members - 1.0) ** 0.5 - weights
    return flipped - jnp.mean(flipped, axis=-1, keepdims=True) + 1.0 / members


def exact_dot(a, b, contract_b):
    return lax.dot_general(
        a, b, (((1,), (contract_b,)), ((), ())), precision=lax.Precision.HIGHEST, preferred_element_type=F32
    )


def first_kernel(lat_count, near_ref, pattern, later, map_ref, mid_ref, out_0, out_1, held_rows):
    flipped = solved_map(marked_product(0, lat_count, own_blocks(near_ref), pattern), held_rows)
    map_ref[...] = flipped
    count = len(NEAR) ** 2
    moved = exact_dot(later[pl.ds(0, count)].reshape(-1, LANES), flipped, 1)
    size = len(NEAR) * SUB
    left, mid, right = (moved[:size], moved[size:2 * size], moved[2 * size:])
    mid_ref[...] = mid
    own = pl.ds(SUB, SUB)
    mid_ref[own, :] = mid[SUB:2 * SUB] - later[count]
    forward = next_first("core")
    out_0[...] = jnp.where(forward, right, left)
    out_1[...] = jnp.where(forward, left, right)


def half_kernel(lat_count, mine, pattern, out_ref):
    out_ref[...] = marked_product(1, lat_count, summed_blocks(lat_count, mine), pattern, lax.axis_index("core"))


def halves(value):
    upper = value.astype(BF16)
    return jnp.concatenate([upper, (value - upper.astype(F32)).astype(BF16)], axis=1)


def mapped(both, flipped):
    high = flipped.astype(BF16)
    low = (flipped - high.astype(F32)).astype(BF16)
    right = jnp.concatenate(
        [jnp.concatenate([high, high], axis=1), jnp.concatenate([low, jnp.zeros_like(low)], axis=1)], axis=0
    )
    product = lax.dot_general(both, right, (((1,), (1,)), ((), ())), preferred_element_type=F32)
    return product[:, :LANES] + product[:, LANES:]


def apply_kernel(map_ref, pad, out_ref, done_ref):
    rows, cols = (pad.shape[0] - 4, pad.shape[1] - 2 * SUB)
    size = 4
    for n in range(0, rows, size):
        value = pad[pl.ds(2 + n, size), pl.ds(SUB, cols), :].reshape(size * cols, LANES)
        out_ref[pl.ds(n * cols, size * cols), :] = halves(mapped(halves(value), map_ref[...]))
    done_ref[...] = jnp.zeros_like(done_ref)


def last_kernel(lat_count, half, other, pattern, cells, out_ref, result, held_rows, out_sem):
    parts = out_sem.shape[0]
    unit = result.shape[0] // 2 ** parts
    product = marked_product(1, lat_count, summed_blocks(lat_count, other), pattern, 1 - lax.axis_index("core"))
    flipped = solved_map(product + half[...], held_rows)
    copies = []
    for n in range(parts):
        size = unit * 2 ** max(n - 1, 0) * 2
        part = pl.ds(size if n else 0, size)
        result[part, :] = mapped(cells[part, :], flipped)
        copies.append(pltpu.make_async_copy(result.at[part], out_ref.at[part], out_sem.at[n]))
        copies[-1].start()
    for out_copy in copies:
        out_copy.wait()


def window(tiles, lat_count, lon_count):
    held = min(WIN, lat_count)
    if held == lat_count:
        return tiles
    start = jnp.clip(lax.axis_index("lat") - REACH, 0, lat_count - held)
    return lax.dynamic_slice_in_dim(tiles, start * lon_count, held * lon_count, axis=0)


def local(ensemble, observed, precision, interp_weight, stencil, owned, pattern):
    rows, cols, members = ensemble.shape
    batches = observed.shape[0]
    lat_count, lon_count = (lax.axis_size("lat"), lax.axis_size(LON))
    tiles = lat_count * lon_count
    vmem = pl.BlockSpec(memory_space=pltpu.VMEM)
    anywhere = pl.BlockSpec(memory_space=pl.ANY)
    hbm = pl.BlockSpec(memory_space=pltpu.HBM)
    megabyte = 1024 * 1024

    def shape(*dims, dtype=F32):
        return jax.ShapeDtypeStruct(dims, dtype)

    def call(kernel, name, specs, out_shape, scratch, *operands, out_specs=None, limit=48):
        return pl.pallas_call(
            kernel,
            out_shape=out_shape,
            in_specs=specs,
            out_specs=out_specs or jax.tree.map(lambda _: vmem, out_shape),
            scratch_shapes=scratch,
            compiler_params=pltpu.CompilerParams(vmem_limit_bytes=limit * megabyte),
            name=name,
        )(*operands)

    def exchange(blocks):
        return lax.all_to_all(blocks, ("lat",) + LON, split_axis=0, concat_axis=0, tiled=True)

    small = (observed, precision, interp_weight, stencil, owned)
    side = shape(rows + SUB, members)
    mine, side_1, side_0 = call(
        functools.partial(start_kernel, cols + 2),
        "start",
        [hbm] * 6,
        (shape(batches, SUB, LANES), side, side),
        [pltpu.VMEM(array.shape, array.dtype) for array in small]
        + [pltpu.VMEM((rows, 1, members), F32)] * 2
        + [pltpu.SemaphoreType.DMA((7,))],
        *small,
        ensemble,
        limit=63,
    )
    sides = trade((side_0, side_1), LON, True)
    padded = shape(rows + 4, cols + 2 * SUB, members)
    pad = call(pad_kernel, "pad", [hbm], padded, [pltpu.SemaphoreType.DMA], ensemble)
    end = shape(cols + 3 * SUB, members)
    left, right, *ends = call(rows_kernel, "edge_rows", [vmem] * 4, (side, side, end, end), [], mine, *sides, pad)
    ends = trade(ends, "lat", False)
    slots = shape(tiles, PAIRS, 2, members, dtype=BF16)
    numbers = [pltpu.SMEM((SUB, LANES), F32), pltpu.SemaphoreType.DMA]
    block = shape(SUB, members)
    held_sides = pltpu.VMEM((2, rows + 2 * SUB, members), F32)
    own = call(row_kernel, "row_shares", [vmem] * 4, block, [held_sides] + numbers, mine, left, right, pad)
    blocks = call(
        functools.partial(prior_kernel, rows),
        "prior",
        [vmem] * 4,
        slots,
        [pltpu.VMEM((2,) + end.shape, F32), pltpu.VMEM((SUB, members), F32)] + numbers,
        mine,
        own,
        *ends,
    )
    near = window(exchange(blocks), lat_count, lon_count)
    count = len(NEAR) ** 2
    later = call(
        later_kernel,
        "later_shares",
        [vmem] * 6,
        shape(count + 1, SUB, members),
        [pltpu.SMEM((5, SUB, LANES), F32), pltpu.SemaphoreType.DMA((5,))],
        mine,
        left,
        right,
        *ends,
        pad,
    )
    column = shape(len(NEAR) * SUB, members)
    held_rows = pltpu.VMEM((members + SUB, members), F32)
    first_map, mid, *sides = call(
        functools.partial(first_kernel, lat_count),
        "first_batch",
        [vmem] * 3,
        (shape(members, members), column, column, column),
        [held_rows],
        near,
        pattern,
        later,
    )
    sides = trade(sides, LON, True)
    cells, done = call(
        apply_kernel,
        "apply_first",
        [vmem] * 2,
        (shape(rows * cols, 2 * members, dtype=BF16), shape(SUB, members)),
        [],
        first_map,
        pad,
    )
    shares = call(meet_kernel, "meet", [vmem] * 4, shape(tiles // 2, *column.shape), [], mid, *sides, done)
    shares = lax.all_to_all(shares, ("lat", "far"), split_axis=0, concat_axis=0, tiled=True)
    other = lax.ppermute(shares, "core", [(0, 1), (1, 0)])
    half = call(
        functools.partial(half_kernel, lat_count),
        "half_product",
        [vmem] * 2,
        shape(members + SUB, members),
        [],
        shares,
        pattern,
    )
    parts = 5
    result = call(
        functools.partial(last_kernel, lat_count),
        "second_batch",
        [vmem] * 4,
        shape(rows * cols, members),
        [
            pltpu.VMEM((rows * cols, members), F32),
            held_rows,
            pltpu.SemaphoreType.DMA((parts,)),
        ],
        half,
        other,
        pattern,
        cells,
        out_specs=anywhere,
    )
    return result.reshape(rows, cols, members)


def solution(mesh):
    lat_count, lon_count = (mesh.shape["lat"], mesh.shape["lon"])
    pairs = jax.sharding.Mesh(mesh.devices.reshape(lat_count, lon_count // 2, 2), ("lat",) + LON)
    placed = (
        P("lat", LON, None),
        P(None, "lat", LON, None),
        P(None, "lat", LON, None),
        P(None, "lat", LON, None, None),
        P(None, "lat", LON, None, None),
        P(None, "lat", LON, None),
        P(None, "lat", LON, None, None),
    )
    return jax.shard_map(
        local, mesh=pairs, in_specs=placed, out_specs=P("lat", LON, None), check_vma=False
    )
```
